32 devices in a mesh: rows: 8 (over z, y), cols: 4 (over x, core).
Axes of the slice: x: 2, y: 2, z: 4, core: 2. Of those that a mesh axis runs over, the one named last changes fastest.
Arguments:
- kernel: bfloat16 [128, 64, 128, 128], P('rows', 'cols'), may hold values from -0.0625 to 0.0625
- pattern: int32 [128, 64], P('rows', 'cols'), may hold values from 0 to 23, as said below
- counts: int32 [128, 4], P('rows', 'cols'), may hold values from 1 to 16, as said below
- delays: float32 [16384, 128], P('rows'), may hold values from -6 to 6
Outputs:
- model: float32 [12288, 128], P('cols')
- gradient: float32 [12288, 128], P('cols')
- misfit: float32 [128], replicated
The draws below stay inside these ranges and needn't reach their ends.
Inputs may be any that keep to these rules, and one draw needn't show every extreme that they name: `pattern`: within one row block and one column shard the 16 slots name different column blocks; slots at or beyond the count hold valid indices that take no part. `counts`: some row block uses all 16 slots of some column shard.
All inputs are finite; a program needn't handle non-finite values.
Results may differ from the reference program's by a relative error of at most 0.0087.
Values sent between devices are 32-bit elements; how exact they have to be, the bound alone decides.
No kernel may reach another device: no remote copies, remote signals or barrier semaphores. Data moves between devices by JAX's collectives and lax.ppermute only.
A program may use at most 128 MiB of HBM per device.

```python
import jax
import jax.numpy as jnp
from jax import lax

RB_DEV = 16
CB_DEV = 24
KT = 16
BANDS = 128
ITERS = 2
RBLK = 128
SLOTS = 64
MODEL_BLOCKS = 96
DATA_ROWS = 16384
MODEL_CELLS = 12288


def draw_pattern(key, part):
    key = jax.random.fold_in(key, 11)
    col_shards = SLOTS // KT
    keys = jax.random.split(key, RBLK * col_shards)
    picks = jax.vmap(lambda one_key: jax.random.permutation(one_key, CB_DEV)[:KT])(keys)
    return picks.reshape(RBLK, SLOTS).astype(jnp.int32)


def draw_counts(key, part):
    key = jax.random.fold_in(key, 23)
    key_base, key_level, key_spot = jax.random.split(key, 3)
    col_shards = SLOTS // KT
    base = jax.random.randint(key_base, (RBLK // RB_DEV, RB_DEV, col_shards), 1, KT + 1)
    level = jax.random.randint(key_level, (RBLK // RB_DEV, 1, 1), 1, 5)
    scaled = jnp.maximum(base * level // 4, 1).reshape(-1)
    spot = jax.random.randint(key_spot, (), 0, RBLK * col_shards)
    filled = jnp.where(jnp.arange(RBLK * col_shards) == spot, KT, scaled)
    return filled.reshape(RBLK, col_shards).astype(jnp.int32)


def block_levels(own_key, shape, cuts, low, high):
    level, own = 1.0, jax.random.fold_in(own_key, 6)
    for position, parts in cuts:
        draws = jnp.exp(jax.random.uniform(jax.random.fold_in(own, position), (parts,), jnp.float32, low / len(cuts), high / len(cuts)))
        level = level * jnp.repeat(draws, shape[position] // parts).reshape([-1 if axis == position else 1 for axis in range(len(shape))])
    return level


def bell_draw(own_key, dims, spread, limit, cuts=(), held_as=jnp.bfloat16):
    entries = jax.random.normal(own_key, dims, jnp.float32) * spread
    if len(cuts) > 0:
        entries = block_levels(own_key, dims, cuts, -0.22, 0.18) * entries
    return jnp.clip(entries, min=-limit, max=limit).astype(held_as)


def setup_inputs(seed: int = 0) -> dict:
    streams_of = jax.random.split(jax.random.key(seed), 5)
    return {
        "kernel": bell_draw(streams_of[0], (RBLK, SLOTS, 128, 128), (128 * SLOTS) ** -0.5, 0.0625, ((0, 8), (1, 4))),
        "pattern": draw_pattern(jax.random.fold_in(streams_of[4], 71), 0),
        "counts": draw_counts(jax.random.fold_in(streams_of[4], 71), 0),
        "delays": bell_draw(streams_of[3], (DATA_ROWS, BANDS), 1.0, 6.0, ((0, 8),), jnp.float32),
    }


def reference(kernel, pattern, counts, delays):
    slot_ids = jnp.arange(SLOTS)
    shard_of = slot_ids // KT
    col_index = (pattern + (shard_of * CB_DEV)[None, :]).astype(jnp.int32)
    alive = slot_ids[None, :] % KT < counts[:, shard_of]
    alive_f = alive.astype(jnp.float32)
    width = delays.shape[1]
    tiny_eps = 1e-06

    def forward(vec_bf):
        tiles_v = vec_bf.astype(jnp.float32).reshape(MODEL_BLOCKS, 128, width)

        def one_block(items):
            tile_row, index_row, alive_row = items
            picked = tiles_v[index_row] * alive_row[:, None, None]
            return jnp.einsum('kij,kjr->ir', tile_row.astype(jnp.float32), picked)
        return lax.map(one_block, (kernel, col_index, alive_f)).reshape(-1, width)

    def backward(vec_bf):
        rows_v = vec_bf.astype(jnp.float32).reshape(RBLK, 128, width)

        def add_block(acc, items):
            tile_row, index_row, alive_row, row_vec = items
            prods = jnp.einsum('kij,ir->kjr', tile_row.astype(jnp.float32), row_vec)
            prods = prods * alive_row[:, None, None]
            return (acc.at[index_row].add(prods), None)
        start = jnp.zeros((MODEL_BLOCKS, 128, width), jnp.float32)
        summed, _ = lax.scan(add_block, start, (kernel, col_index, alive_f, rows_v))
        return summed.reshape(-1, width)

    def back_step(left_raw, right_prev):
        beta_norm = jnp.sqrt(lax.optimization_barrier(jnp.sum(left_raw * left_raw, axis=0)) + tiny_eps)
        right_raw = backward(left_raw.astype(jnp.bfloat16)) / beta_norm - beta_norm * right_prev
        return (beta_norm, left_raw / beta_norm, right_raw)

    def fore_step(right_raw, left_vec):
        alpha_norm = jnp.sqrt(lax.optimization_barrier(jnp.sum(right_raw * right_raw, axis=0)) + tiny_eps)
        left_raw = forward(right_raw.astype(jnp.bfloat16)) / alpha_norm - alpha_norm * left_vec
        return (alpha_norm, right_raw / alpha_norm, left_raw)
    right_zero = jnp.zeros((MODEL_CELLS, width), jnp.float32)
    beta_first, left_vec, right_raw = back_step(delays, right_zero)
    resid_bar = beta_first
    model = jnp.zeros((MODEL_CELLS, width), jnp.float32)
    search = right_zero
    diag_bar = beta_first
    rotate_cos = beta_first
    rotate_sin = beta_first
    radius = beta_first
    for iteration in range(ITERS):
        alpha_norm, right_vec, left_raw = fore_step(right_raw, left_vec)
        if iteration == 0:
            diag_bar = alpha_norm
            search = right_vec
        else:
            coupling = rotate_sin * alpha_norm
            diag_bar = -rotate_cos * alpha_norm
            search = right_vec - coupling / radius * search
        beta_norm, left_vec, right_raw = back_step(left_raw, right_vec)
        radius = jnp.sqrt(diag_bar * diag_bar + beta_norm * beta_norm)
        rotate_cos = diag_bar / radius
        rotate_sin = beta_norm / radius
        step_size = rotate_cos * resid_bar
        resid_bar = rotate_sin * resid_bar
        model = model + step_size / radius * search
    misfit = resid_bar / beta_first
    gradient = misfit * rotate_cos * right_raw
    return (model, gradient, misfit)
```

```python
import jax
import jax.numpy as jnp
from jax import lax
from jax.sharding import PartitionSpec as P

CB_DEV = 24
ITERS = 2


tiny_eps = 1e-06


def column_norm(values):
    return jnp.sum(values * values, axis=0)


def build_dense(kernel, pattern, counts):
    row_blocks = kernel.shape[0]
    slot_count = kernel.shape[1]
    alive_bool = jnp.arange(slot_count)[None, :] < counts
    selector = (
        (pattern[:, :, None] == jnp.arange(CB_DEV)[None, None, :]) & alive_bool[:, :, None]
    ).astype(jnp.bfloat16)
    placed = jnp.einsum("bkc,bkij->bicj", selector, kernel, preferred_element_type=jnp.float32)
    return placed.astype(jnp.bfloat16).reshape(row_blocks * 128, CB_DEV * 128)


def local_forward(dense_kernel, vec_bf):
    return jnp.dot(dense_kernel, vec_bf, preferred_element_type=jnp.float32)


def local_backward(dense_kernel, vec_bf):
    return lax.dot_general(
        dense_kernel, vec_bf, (((0,), (0,)), ((), ())), preferred_element_type=jnp.float32
    )


def swap(value, axis, count, bit):
    return lax.ppermute(value, axis, [(i, i ^ (1 << bit)) for i in range(count)])


def reduce_streams(streams, norm, axis, count, orders):
    index = lax.axis_index(axis)
    levels = len(orders[0])
    streams = list(streams)
    for level in range(levels):
        for s, order in enumerate(orders):
            bit = order[level]
            side = (index >> bit) & 1
            if level < levels - 1:
                half = streams[s].shape[0] // 2
                keep = lax.dynamic_slice_in_dim(streams[s], side * half, half)
                send = lax.dynamic_slice_in_dim(streams[s], (1 - side) * half, half)
            else:
                keep = send = streams[s]
            if s == 0:
                send = jnp.concatenate([send, norm])
            got = swap(send, axis, count, bit)
            streams[s] = keep + got[: keep.shape[0]]
            if s == 0:
                norm = norm + got[keep.shape[0] :]
    for level in reversed(range(levels - 1)):
        for s, order in enumerate(orders):
            bit = order[level]
            side = (index >> bit) & 1
            got = swap(streams[s], axis, count, bit)
            low = jnp.where(side == 0, streams[s], got)
            high = jnp.where(side == 0, got, streams[s])
            streams[s] = jnp.concatenate([low, high])
    return streams, norm


def bit_orders(count):
    bits = list(range(count.bit_length() - 1))
    other = [bits[1], bits[0], *bits[2:]] if len(bits) > 2 else bits
    return [bits, other]


def on_device(row_count, col_count, kernel, pattern, counts, delays):
    width = delays.shape[1]
    dense_kernel = build_dense(kernel, pattern, counts)

    def summed_with_norm(partial, values, axis, count):
        norm = jnp.broadcast_to(column_norm(values)[None, :], (8, width))
        half = partial.shape[0] // 2
        pieces, norm = reduce_streams(
            [partial[:half], partial[half:]], norm, axis, count, bit_orders(count)
        )
        return jnp.concatenate(pieces), norm[0]

    def back_step(left_raw, right_prev):
        left_bf = left_raw.astype(jnp.bfloat16)
        partial_sum = local_backward(dense_kernel, left_bf)
        summed, squares = summed_with_norm(partial_sum, left_raw, "rows", row_count)
        beta_norm = jnp.sqrt(squares + tiny_eps)
        right_raw = summed / beta_norm - beta_norm * right_prev
        return (beta_norm, left_raw / beta_norm, right_raw)

    right_zero = jnp.zeros((CB_DEV * 128, width), jnp.float32)
    beta_first, left_vec, right_raw = back_step(delays, right_zero)
    resid_bar = beta_first
    model = right_zero
    search = right_zero
    diag_bar = beta_first
    rotate_cos = beta_first
    rotate_sin = beta_first
    radius = beta_first
    for iteration in range(ITERS):
        right_bf = right_raw.astype(jnp.bfloat16)
        fore_partial_sum = local_forward(dense_kernel, right_bf)
        fore_summed, fore_squares = summed_with_norm(fore_partial_sum, right_raw, "cols", col_count)
        alpha_norm = jnp.sqrt(fore_squares + tiny_eps)
        fore_left_raw = fore_summed / alpha_norm - alpha_norm * left_vec
        alpha_norm, right_vec, left_raw = (alpha_norm, right_raw / alpha_norm, fore_left_raw)
        if iteration == 0:
            diag_bar = alpha_norm
            search = right_vec
        else:
            coupling = rotate_sin * alpha_norm
            diag_bar = -rotate_cos * alpha_norm
            search = right_vec - coupling / radius * search
        beta_norm, left_vec, right_raw = back_step(left_raw, right_vec)
        radius = jnp.sqrt(diag_bar * diag_bar + beta_norm * beta_norm)
        rotate_cos = diag_bar / radius
        rotate_sin = beta_norm / radius
        step_size = rotate_cos * resid_bar
        resid_bar = rotate_sin * resid_bar
        model = model + step_size / radius * search
    misfit = resid_bar / beta_first
    gradient = misfit * rotate_cos * right_raw
    return (model, gradient, misfit)


def solution(mesh):
    placed = (P("rows", "cols", None, None), P("rows", "cols"), P("rows", "cols"), P("rows", None))

    def local(kernel, pattern, counts, delays):
        return on_device(
            mesh.shape["rows"], mesh.shape["cols"], kernel, pattern, counts, delays
        )

    return jax.shard_map(
        local,
        mesh=mesh,
        in_specs=placed,
        out_specs=(P("cols", None), P("cols", None), P()),
        check_vma=False,
    )
```

```python
import jax
import jax.numpy as jnp
from jax import lax
from jax.experimental import pallas as pl
from jax.experimental.pallas import tpu as pltpu
from jax.sharding import PartitionSpec as P

CB_DEV = 24
ITERS = 2
TILE = 128
ROW_STREAMS = ((8, False), (8, True), (8, False))
COL_STREAMS = (8, 8)

tiny_eps = 1e-06


def fill_kernel(slot_ref, flip_ref, tile_ref, *out_refs):
    block = pl.program_id(0) ^ flip_ref[0]
    position = 0
    for out_ref in out_refs:
        for place in range(out_ref.shape[1] // TILE):
            slot = slot_ref[block * CB_DEV + position]
            lanes = slice(place * TILE, (place + 1) * TILE)

            @pl.when(slot >= 0)
            def _():
                out_ref[:, lanes] = tile_ref[0, jnp.maximum(slot, 0)]

            @pl.when(slot < 0)
            def _():
                out_ref[:, lanes] = jnp.zeros((TILE, TILE), out_ref.dtype)

            position += 1


def fill_dense(kernel, slots, flip, widths):
    row_blocks, slot_count = kernel.shape[:2]
    return pl.pallas_call(
        fill_kernel,
        grid_spec=pltpu.PrefetchScalarGridSpec(
            num_scalar_prefetch=2,
            grid=(row_blocks,),
            in_specs=[
                pl.BlockSpec(
                    (1, slot_count, TILE, TILE), lambda i, slots, flip: (i ^ flip[0], 0, 0, 0)
                )
            ],
            out_specs=[
                pl.BlockSpec((TILE, width * TILE), lambda i, slots, flip: (i, 0))
                for width in widths
            ],
        ),
        out_shape=[
            jax.ShapeDtypeStruct((row_blocks * TILE, width * TILE), kernel.dtype)
            for width in widths
        ],
        compiler_params=pltpu.CompilerParams(vmem_limit_bytes=16 * 1024 * 1024),
    )(slots, flip, kernel)


def swap(value, axis, count, bit):
    return lax.ppermute(value, axis, [(i, i ^ (1 << bit)) for i in range(count)])


def swap_with(value, extra, axis, count, bit):
    got = swap(jnp.concatenate([value, extra]), axis, count, bit)
    return got[: value.shape[0]], got[value.shape[0] :]


def after(value, other):
    return lax.optimization_barrier((value, other))[0]


def column_norm(pieces):
    sums = []
    for piece in pieces:
        blocks = piece.reshape(-1, TILE, piece.shape[-1])
        sums.append(jnp.sum(blocks * blocks, axis=1))
    sums = jnp.concatenate(sums)
    parts = [sums[i] for i in range(sums.shape[0])]
    while len(parts) > 1:
        paired = [parts[i] + parts[i + 1] for i in range(0, len(parts) - 1, 2)]
        parts = paired + parts[len(parts) - len(parts) % 2 :]
    return parts[0]


def on_device(row_count, col_count, kernel, pattern, counts, delays):
    width = delays.shape[1]
    row_blocks, slot_count = pattern.shape
    row_bits = list(range(row_count.bit_length() - 1))
    col_bits = list(range(col_count.bit_length() - 1))
    row_index = lax.axis_index("rows")
    col_index = lax.axis_index("cols")

    def side(index, bit):
        return (index >> bit) & 1

    orders = [
        [row_bits[1], row_bits[0], *row_bits[2:]] if turned else row_bits
        for _, turned in ROW_STREAMS
    ]

    position_of = []
    start = 0
    for (blocks, _), order in zip(ROW_STREAMS, orders):
        mask = (1 - side(row_index, order[0])) * (blocks // 2) + (
            1 - side(row_index, order[1])
        ) * (blocks // 4)
        quarter = jnp.arange(blocks) // (blocks // 4)
        rest = jnp.arange(blocks) % (blocks // 4)
        quarter_mask = (1 - side(row_index, order[0])) * 2 + (1 - side(row_index, order[1]))
        position_of.append(start + (quarter ^ quarter_mask) * (blocks // 4) + rest)
        start += blocks
    block_at = jnp.concatenate(position_of)
    flip = (1 - side(col_index, 0)) * (COL_STREAMS[0] // 2)

    alive = jnp.arange(slot_count)[None, :] < counts
    hits = (pattern[:, :, None] == block_at[None, None, :]) & alive[:, :, None]
    slots = jnp.sum(hits * (jnp.arange(slot_count) + 1)[None, :, None], axis=1) - 1
    widths = [half for blocks, _ in ROW_STREAMS for half in (blocks // 2, blocks // 2)]
    dense = fill_dense(
        kernel,
        slots.reshape(-1).astype(jnp.int32),
        flip.reshape(1).astype(jnp.int32),
        widths,
    )

    kept_first = side(col_index, 0) == 0
    left_pieces = []
    start = 0
    for blocks in COL_STREAMS:
        half = blocks // 2 * TILE
        low = delays[start : start + half]
        high = delays[start + half : start + 2 * half]
        left_pieces += [jnp.where(kept_first, high, low), jnp.where(kept_first, low, high)]
        start += 2 * half

    def reduce_rows(partials, norm):
        keeps = []
        first_got = []
        for s, order in enumerate(orders):
            send, keep = partials[s]
            if s >= 2:
                send = after(send, first_got[s - 2])
            if s == 1:
                got, other = swap_with(send, norm, "rows", row_count, order[0])
                norm = norm + other
            else:
                got = swap(send, "rows", row_count, order[0])
            first_got.append(got)
            keeps.append(keep + got)
        for level in range(1, len(row_bits)):
            for s, order in enumerate(orders):
                mine = keeps[s]
                if level == 1:
                    half = mine.shape[0] // 2
                    send, mine = mine[:half], mine[half:]
                else:
                    send = mine
                if s == 1:
                    got, other = swap_with(send, norm, "rows", row_count, order[level])
                    norm = norm + other
                else:
                    got = swap(send, "rows", row_count, order[level])
                keeps[s] = mine + got
        pieces = []
        for s, order in enumerate(orders):
            inner = swap(keeps[s], "rows", row_count, order[1])
            own = jnp.concatenate([inner, keeps[s]])
            outer = swap(own, "rows", row_count, order[0])
            pieces += [outer, own]
        return pieces, norm[0]

    def reduce_cols(partials, norm):
        keeps = []
        for s in range(len(COL_STREAMS)):
            send, keep = partials[2 * s], partials[2 * s + 1]
            if s == 0:
                got, other = swap_with(send, norm, "cols", col_count, 0)
                norm = norm + other
            else:
                got = swap(send, "cols", col_count, 0)
            keeps.append(keep + got)
        for bit in col_bits[1:]:
            for s in range(len(COL_STREAMS)):
                if s == 0:
                    got, other = swap_with(keeps[s], norm, "cols", col_count, bit)
                    norm = norm + other
                else:
                    got = swap(keeps[s], "cols", col_count, bit)
                keeps[s] = keeps[s] + got
        pieces = []
        for s in range(len(COL_STREAMS)):
            pieces += [swap(keeps[s], "cols", col_count, 0), keeps[s]]
        return pieces, norm[0]

    def spread(norm):
        return jnp.broadcast_to(norm[None, :], (8, width))

    def back_step(left_raw, right_prev):
        left_bf = jnp.concatenate([piece.astype(jnp.bfloat16) for piece in left_raw])
        products = [
            lax.dot_general(
                chunk, left_bf, (((0,), (0,)), ((), ())), preferred_element_type=jnp.float32
            )
            for chunk in dense
        ]
        partials = list(zip(products[0::2], products[1::2]))
        summed, squares = reduce_rows(partials, spread(column_norm(left_raw)))
        beta_norm = jnp.sqrt(squares + tiny_eps)
        right_raw = [
            total / beta_norm - beta_norm * prev for total, prev in zip(summed, right_prev)
        ]
        return (beta_norm, [piece / beta_norm for piece in left_raw], right_raw)

    def fore_products(right_raw):
        totals = None
        for chunk, piece in zip(dense, right_raw):
            part = jnp.dot(chunk, piece.astype(jnp.bfloat16), preferred_element_type=jnp.float32)
            totals = part if totals is None else totals + part
        pieces = []
        start = 0
        for blocks in COL_STREAMS:
            half = blocks // 2 * TILE
            pieces += [totals[start : start + half], totals[start + half : start + 2 * half]]
            start += 2 * half
        return pieces

    right_zero = [jnp.zeros((chunk.shape[1], width), jnp.float32) for chunk in dense]
    beta_first, left_vec, right_raw = back_step(left_pieces, right_zero)
    resid_bar = beta_first
    model = right_zero
    search = right_zero
    diag_bar = beta_first
    rotate_cos = beta_first
    rotate_sin = beta_first
    radius = beta_first
    for iteration in range(ITERS):
        fore_summed, fore_squares = reduce_cols(
            fore_products(right_raw), spread(column_norm(right_raw))
        )
        alpha_norm = jnp.sqrt(fore_squares + tiny_eps)
        left_raw = [
            total / alpha_norm - alpha_norm * prev for total, prev in zip(fore_summed, left_vec)
        ]
        right_vec = [piece / alpha_norm for piece in right_raw]
        if iteration == 0:
            diag_bar = alpha_norm
            search = right_vec
        else:
            coupling = rotate_sin * alpha_norm
            diag_bar = -rotate_cos * alpha_norm
            search = [now - coupling / radius * old for now, old in zip(right_vec, search)]
        beta_norm, left_vec, right_raw = back_step(left_raw, right_vec)
        radius = jnp.sqrt(diag_bar * diag_bar + beta_norm * beta_norm)
        rotate_cos = diag_bar / radius
        rotate_sin = beta_norm / radius
        step_size = rotate_cos * resid_bar
        resid_bar = rotate_sin * resid_bar
        model = [old + step_size / radius * way for old, way in zip(model, search)]
    misfit = resid_bar / beta_first
    gradient = [misfit * rotate_cos * piece for piece in right_raw]

    def in_block_order(pieces):
        out = []
        for s, order in enumerate(orders):
            outer, own = pieces[2 * s], pieces[2 * s + 1]
            half = outer.shape[0] // 2
            straight = side(row_index, order[1]) == 1
            outer, own = (
                jnp.where(straight, v, jnp.concatenate([v[half:], v[:half]]))
                for v in (outer, own)
            )
            straight = side(row_index, order[0]) == 1
            out += [jnp.where(straight, outer, own), jnp.where(straight, own, outer)]
        return jnp.concatenate(out)

    return (in_block_order(model), in_block_order(gradient), misfit)


def solution(mesh):
    placed = (P("rows", "cols", None, None), P("rows", "cols"), P("rows", "cols"), P("rows", None))

    def local(kernel, pattern, counts, delays):
        return on_device(
            mesh.shape["rows"], mesh.shape["cols"], kernel, pattern, counts, delays
        )

    return jax.shard_map(
        local,
        mesh=mesh,
        in_specs=placed,
        out_specs=(P("cols", None), P("cols", None), P()),
        check_vma=False,
    )
```

```python
import jax
import jax.numpy as jnp
from jax import lax
from jax.experimental import pallas as pl
from jax.experimental.pallas import tpu as pltpu
from jax.sharding import PartitionSpec as P

CB_DEV = 24
ITERS = 2
TILE = 128
ROW_STREAMS = (12, 12)
COL_STREAMS = (16,)

tiny_eps = 1e-06


def fill_kernel(slot_ref, flip_ref, tile_ref, *out_refs):
    block = pl.program_id(0) ^ flip_ref[0]
    position = 0
    for out_ref in out_refs:
        for place in range(out_ref.shape[1] // TILE):
            slot = slot_ref[block * CB_DEV + position]
            lanes = slice(place * TILE, (place + 1) * TILE)

            @pl.when(slot >= 0)
            def _():
                out_ref[:, lanes] = tile_ref[0, jnp.maximum(slot, 0)]

            @pl.when(slot < 0)
            def _():
                out_ref[:, lanes] = jnp.zeros((TILE, TILE), out_ref.dtype)

            position += 1


def fill_dense(kernel, slots, flip, widths):
    row_blocks, slot_count = kernel.shape[:2]
    return pl.pallas_call(
        fill_kernel,
        grid_spec=pltpu.PrefetchScalarGridSpec(
            num_scalar_prefetch=2,
            grid=(row_blocks,),
            in_specs=[
                pl.BlockSpec(
                    (1, slot_count, TILE, TILE), lambda i, slots, flip: (i ^ flip[0], 0, 0, 0)
                )
            ],
            out_specs=[
                pl.BlockSpec((TILE, width * TILE), lambda i, slots, flip: (i, 0))
                for width in widths
            ],
        ),
        out_shape=[
            jax.ShapeDtypeStruct((row_blocks * TILE, width * TILE), kernel.dtype)
            for width in widths
        ],
        compiler_params=pltpu.CompilerParams(vmem_limit_bytes=16 * 1024 * 1024),
    )(slots, flip, kernel)


def after(value, other):
    return lax.optimization_barrier((value, other))[0]


def column_norm(pieces, unit):
    parts = []
    for piece in pieces:
        squares = (piece * piece).reshape(-1, unit, piece.shape[-1])
        sums = jnp.sum(squares, axis=1)
        parts += [sums[i] for i in range(sums.shape[0])]
    while len(parts) > 1:
        paired = [parts[i] + parts[i + 1] for i in range(0, len(parts) - 1, 2)]
        parts = paired + parts[len(parts) - len(parts) % 2 :]
    return parts[0]


def on_device(row_count, col_count, kernel, pattern, counts, delays):
    width = delays.shape[1]
    row_blocks, slot_count = pattern.shape
    row_bits = list(range(row_count.bit_length() - 1))
    col_bits = list(range(col_count.bit_length() - 1))
    row_index = lax.axis_index("rows")
    col_index = lax.axis_index("cols")

    def side(index, bit):
        return (index >> bit) & 1

    core = side(col_index, 0)
    orders = [row_bits, [row_bits[1], row_bits[0], *row_bits[2:]]]
    outer_side, inner_side = (
        jnp.where(core == 0, side(row_index, orders[0][level]), side(row_index, orders[1][level]))
        for level in range(2)
    )

    def swap_rows(value, level):
        pairs = []
        for row in range(row_count):
            for col in range(col_count):
                partner = row ^ (1 << orders[col & 1][level])
                pairs.append((row * col_count + col, partner * col_count + col))
        return lax.ppermute(value, ("rows", "cols"), pairs)

    def swap_cols(value, level):
        return lax.ppermute(value, "cols", [(i, i ^ (1 << level)) for i in range(col_count)])

    position_of = []
    start = 0
    for blocks in ROW_STREAMS:
        quarter = jnp.arange(blocks) // (blocks // 4)
        rest = jnp.arange(blocks) % (blocks // 4)
        mask = (1 - outer_side) * 2 + (1 - inner_side)
        position_of.append(start + (quarter ^ mask) * (blocks // 4) + rest)
        start += blocks
    block_at = jnp.concatenate(position_of)
    flip = (1 - core) * (COL_STREAMS[0] // 2)

    alive = jnp.arange(slot_count)[None, :] < counts
    hits = (pattern[:, :, None] == block_at[None, None, :]) & alive[:, :, None]
    slots = jnp.sum(hits * (jnp.arange(slot_count) + 1)[None, :, None], axis=1) - 1
    widths = [half for blocks in ROW_STREAMS for half in (blocks // 2, blocks // 2)]
    dense = fill_dense(
        kernel,
        slots.reshape(-1).astype(jnp.int32),
        flip.reshape(1).astype(jnp.int32),
        widths,
    )

    kept_first = core == 0
    left_pieces = []
    start = 0
    for blocks in COL_STREAMS:
        half = blocks // 2 * TILE
        low = delays[start : start + half]
        high = delays[start + half : start + 2 * half]
        left_pieces += [jnp.where(kept_first, high, low), jnp.where(kept_first, low, high)]
        start += 2 * half

    def staggered(sends, norm, swap):
        got = []
        for s, send in enumerate(sends):
            if s > 0:
                send = after(send, got[s - 1])
            elif norm is not None:
                send = jnp.concatenate([send, norm])
            got.append(swap(send))
        if norm is not None:
            split = sends[0].shape[0]
            norm = norm + got[0][split:]
            got[0] = got[0][:split]
        return got, norm

    def reduce_rows(partials, norm):
        sends, keeps = [list(part) for part in zip(*partials)]
        for level in range(len(row_bits)):
            got, norm = staggered(sends, norm, lambda value: swap_rows(value, level))
            keeps = [keep + other for keep, other in zip(keeps, got)]
            if level == 0:
                halves = [keep.shape[0] // 2 for keep in keeps]
                sends = [keep[:half] for keep, half in zip(keeps, halves)]
                keeps = [keep[half:] for keep, half in zip(keeps, halves)]
            else:
                sends = keeps
        inner, _ = staggered(keeps, None, lambda value: swap_rows(value, 1))
        own = [jnp.concatenate(pair) for pair in zip(inner, keeps)]
        outer, _ = staggered(own, None, lambda value: swap_rows(value, 0))
        return [piece for pair in zip(outer, own) for piece in pair], norm[0]

    def reduce_cols(partials, norm):
        sends, keeps = partials[0::2], partials[1::2]
        for level in range(len(col_bits)):
            got, norm = staggered(sends, norm, lambda value: swap_cols(value, level))
            sends = keeps = [keep + other for keep, other in zip(keeps, got)]
        other, _ = staggered(keeps, None, lambda value: swap_cols(value, 0))
        return [piece for pair in zip(other, keeps) for piece in pair], norm[0]

    def spread(norm):
        return jnp.broadcast_to(norm[None, :], (8, width))

    def back_step(left_raw, right_prev):
        left_bf = jnp.concatenate([piece.astype(jnp.bfloat16) for piece in left_raw])
        products = [
            lax.dot_general(
                chunk, left_bf, (((0,), (0,)), ((), ())), preferred_element_type=jnp.float32
            )
            for chunk in dense
        ]
        partials = list(zip(products[0::2], products[1::2]))
        summed, squares = reduce_rows(partials, spread(column_norm(left_raw, left_raw[0].shape[0])))
        beta_norm = jnp.sqrt(squares + tiny_eps)
        right_raw = [
            total / beta_norm - beta_norm * prev for total, prev in zip(summed, right_prev)
        ]
        return (beta_norm, [piece / beta_norm for piece in left_raw], right_raw)

    def fore_products(right_raw):
        totals = None
        for chunk, piece in zip(dense, right_raw):
            part = jnp.dot(chunk, piece.astype(jnp.bfloat16), preferred_element_type=jnp.float32)
            totals = part if totals is None else totals + part
        pieces = []
        start = 0
        for blocks in COL_STREAMS:
            half = blocks // 2 * TILE
            pieces += [totals[start : start + half], totals[start + half : start + 2 * half]]
            start += 2 * half
        return pieces

    right_zero = [jnp.zeros((chunk.shape[1], width), jnp.float32) for chunk in dense]
    beta_first, left_vec, right_raw = back_step(left_pieces, right_zero)
    resid_bar = beta_first
    model = right_zero
    search = right_zero
    diag_bar = beta_first
    rotate_cos = beta_first
    rotate_sin = beta_first
    radius = beta_first
    for iteration in range(ITERS):
        fore_summed, fore_squares = reduce_cols(
            fore_products(right_raw), spread(column_norm(right_raw, right_raw[0].shape[0] // 2))
        )
        alpha_norm = jnp.sqrt(fore_squares + tiny_eps)
        left_raw = [
            total / alpha_norm - alpha_norm * prev for total, prev in zip(fore_summed, left_vec)
        ]
        right_vec = [piece / alpha_norm for piece in right_raw]
        if iteration == 0:
            diag_bar = alpha_norm
            search = right_vec
        else:
            coupling = rotate_sin * alpha_norm
            diag_bar = -rotate_cos * alpha_norm
            search = [now - coupling / radius * old for now, old in zip(right_vec, search)]
        beta_norm, left_vec, right_raw = back_step(left_raw, right_vec)
        radius = jnp.sqrt(diag_bar * diag_bar + beta_norm * beta_norm)
        rotate_cos = diag_bar / radius
        rotate_sin = beta_norm / radius
        step_size = rotate_cos * resid_bar
        resid_bar = rotate_sin * resid_bar
        model = [old + step_size / radius * way for old, way in zip(model, search)]
    misfit = resid_bar / beta_first
    gradient = [misfit * rotate_cos * piece for piece in right_raw]

    def in_block_order(pieces):
        out = []
        for outer, own in zip(pieces[0::2], pieces[1::2]):
            half = outer.shape[0] // 2
            outer, own = (
                jnp.where(inner_side == 1, v, jnp.concatenate([v[half:], v[:half]]))
                for v in (outer, own)
            )
            out += [jnp.where(outer_side == 1, outer, own), jnp.where(outer_side == 1, own, outer)]
        return jnp.concatenate(out)

    return (in_block_order(model), in_block_order(gradient), misfit)


def solution(mesh):
    placed = (P("rows", "cols", None, None), P("rows", "cols"), P("rows", "cols"), P("rows", None))

    def local(kernel, pattern, counts, delays):
        return on_device(
            mesh.shape["rows"], mesh.shape["cols"], kernel, pattern, counts, delays
        )

    return jax.shard_map(
        local,
        mesh=mesh,
        in_specs=placed,
        out_specs=(P("cols", None), P("cols", None), P()),
        check_vma=False,
    )
```

```python
import jax
import jax.numpy as jnp
from jax import lax
from jax.experimental import pallas as pl
from jax.experimental.pallas import tpu as pltpu
from jax.sharding import PartitionSpec as P

CB_DEV = 24
ITERS = 2
TILE = 128
PIECE = 4
ROW_STREAMS = (4, 2)
COL_STREAMS = (16,)

tiny_eps = 1e-06


def fill_kernel(slot_ref, flip_ref, tile_ref, *out_refs):
    block = pl.program_id(0) ^ flip_ref[0]
    position = 0
    for out_ref in out_refs:
        for place in range(out_ref.shape[1] // TILE):
            slot = slot_ref[block * CB_DEV + position]
            lanes = slice(place * TILE, (place + 1) * TILE)

            @pl.when(slot >= 0)
            def _():
                out_ref[:, lanes] = tile_ref[0, jnp.maximum(slot, 0)]

            @pl.when(slot < 0)
            def _():
                out_ref[:, lanes] = jnp.zeros((TILE, TILE), out_ref.dtype)

            position += 1


def fill_dense(kernel, slots, flip, widths):
    row_blocks, slot_count = kernel.shape[:2]
    return pl.pallas_call(
        fill_kernel,
        grid_spec=pltpu.PrefetchScalarGridSpec(
            num_scalar_prefetch=2,
            grid=(row_blocks,),
            in_specs=[
                pl.BlockSpec(
                    (1, slot_count, TILE, TILE), lambda i, slots, flip: (i ^ flip[0], 0, 0, 0)
                )
            ],
            out_specs=[
                pl.BlockSpec((TILE, width * TILE), lambda i, slots, flip: (i, 0))
                for width in widths
            ],
        ),
        out_shape=[
            jax.ShapeDtypeStruct((row_blocks * TILE, width * TILE), kernel.dtype)
            for width in widths
        ],
        compiler_params=pltpu.CompilerParams(vmem_limit_bytes=16 * 1024 * 1024),
    )(slots, flip, kernel)


def column_norm(pieces, unit):
    parts = []
    for piece in pieces:
        blocks = piece.reshape(-1, TILE, piece.shape[-1])
        sums = jnp.sum(blocks * blocks, axis=1)
        parts += [sums[i] for i in range(sums.shape[0])]
    parts = [sum(parts[i + 1 : i + unit], parts[i]) for i in range(0, len(parts), unit)]
    while len(parts) > 1:
        paired = [parts[i] + parts[i + 1] for i in range(0, len(parts) - 1, 2)]
        parts = paired + parts[len(parts) - len(parts) % 2 :]
    return parts[0]


def on_device(row_count, col_count, kernel, pattern, counts, delays):
    width = delays.shape[1]
    row_blocks, slot_count = pattern.shape
    row_bits = list(range(row_count.bit_length() - 1))
    col_bits = list(range(col_count.bit_length() - 1))
    row_index = lax.axis_index("rows")
    col_index = lax.axis_index("cols")

    def side(index, bit):
        return (index >> bit) & 1

    core = side(col_index, 0)
    first, second, third, *more = row_bits
    orders = [
        [[first, second, third, *more], [second, first, third, *more]],
        [[first, third, second, *more], [third, first, second, *more]],
    ]
    sides = [
        [
            jnp.where(core == 0, side(row_index, by_core[0][level]), side(row_index, by_core[1][level]))
            for level in range(2)
        ]
        for by_core in orders
    ]

    def swap_rows(value, stream, level):
        pairs = []
        for row in range(row_count):
            for col in range(col_count):
                partner = row ^ (1 << orders[stream][col & 1][level])
                pairs.append((row * col_count + col, partner * col_count + col))
        return lax.ppermute(value, ("rows", "cols"), pairs)

    def swap_cols(value, level):
        return lax.ppermute(value, "cols", [(i, i ^ (1 << level)) for i in range(col_count)])

    position_of = []
    start = 0
    for pieces, (outer_side, inner_side) in zip(ROW_STREAMS, sides):
        blocks = pieces * PIECE
        quarter = jnp.arange(blocks) // (blocks // 4)
        rest = jnp.arange(blocks) % (blocks // 4)
        mask = (1 - outer_side) * 2 + (1 - inner_side)
        position_of.append(start + (quarter ^ mask) * (blocks // 4) + rest)
        start += blocks
    block_at = jnp.concatenate(position_of)
    flip = (1 - core) * (COL_STREAMS[0] // 2)

    alive = jnp.arange(slot_count)[None, :] < counts
    hits = (pattern[:, :, None] == block_at[None, None, :]) & alive[:, :, None]
    slots = jnp.sum(hits * (jnp.arange(slot_count) + 1)[None, :, None], axis=1) - 1
    widths = [PIECE] * sum(ROW_STREAMS)
    dense = fill_dense(
        kernel,
        slots.reshape(-1).astype(jnp.int32),
        flip.reshape(1).astype(jnp.int32),
        widths,
    )

    kept_first = core == 0
    left_pieces = []
    start = 0
    for blocks in COL_STREAMS:
        half = blocks // 2 * TILE
        low = delays[start : start + half]
        high = delays[start + half : start + 2 * half]
        left_pieces += [jnp.where(kept_first, high, low), jnp.where(kept_first, low, high)]
        start += 2 * half

    def swap_normed(value, norm, swap):
        got = swap(jnp.concatenate([value, norm]))
        return got[: value.shape[0]], norm + got[value.shape[0] :]

    def reduce_rows(products, norm):
        streams = []
        start = 0
        for pieces in ROW_STREAMS:
            half = pieces // 2
            streams.append(
                [jnp.concatenate(products[start : start + half]), products[start + half : start + pieces]]
            )
            start += pieces
        keeps = []
        for s, (send, keep) in enumerate(streams):
            if s == 0:
                got, norm = swap_normed(send, norm, lambda value: swap_rows(value, 0, 0))
            else:
                got = swap_rows(send, s, 0)
            keep = jnp.concatenate(keep) + got
            half = keep.shape[0] // 2
            keeps.append((keep[:half], keep[half:]))
        for level in range(1, len(row_bits)):
            for s, (send, keep) in enumerate(keeps):
                if s == 0:
                    got, norm = swap_normed(send, norm, lambda value: swap_rows(value, 0, level))
                else:
                    got = swap_rows(send, s, level)
                keeps[s] = (keep + got, keep + got)
        own = []
        for s, (keep, _) in enumerate(keeps):
            own.append([swap_rows(keep, s, 1), keep])
        pieces = []
        for s, pair in enumerate(own):
            own_all = jnp.concatenate(pair)
            both = jnp.concatenate([swap_rows(own_all, s, 0), own_all])
            step = both.shape[0] // ROW_STREAMS[s]
            pieces += [both[i * step : (i + 1) * step] for i in range(ROW_STREAMS[s])]
        return pieces, norm[0]

    def reduce_cols(partials, norm):
        sends, keeps = partials[0::2], partials[1::2]
        for level in range(len(col_bits)):
            got = []
            for s, send in enumerate(sends):
                if s == 0:
                    other, norm = swap_normed(send, norm, lambda value: swap_cols(value, level))
                else:
                    other = swap_cols(send, level)
                got.append(other)
            sends = keeps = [keep + other for keep, other in zip(keeps, got)]
        other = [swap_cols(keep, 0) for keep in keeps]
        return [piece for pair in zip(other, keeps) for piece in pair], norm[0]

    def spread(norm):
        return jnp.broadcast_to(norm[None, :], (8, width))

    def back_step(left_raw, right_prev):
        left_bf = jnp.concatenate([piece.astype(jnp.bfloat16) for piece in left_raw])
        products = [
            lax.dot_general(
                chunk, left_bf, (((0,), (0,)), ((), ())), preferred_element_type=jnp.float32
            )
            for chunk in dense
        ]
        squares = column_norm(left_raw, left_raw[0].shape[0] // TILE)
        summed, squares = reduce_rows(products, spread(squares))
        beta_norm = jnp.sqrt(squares + tiny_eps)
        right_raw = [
            total / beta_norm - beta_norm * prev for total, prev in zip(summed, right_prev)
        ]
        return (beta_norm, [piece / beta_norm for piece in left_raw], right_raw)

    def fore_products(right_raw):
        totals = None
        for chunk, piece in zip(dense, right_raw):
            part = jnp.dot(chunk, piece.astype(jnp.bfloat16), preferred_element_type=jnp.float32)
            totals = part if totals is None else totals + part
        pieces = []
        start = 0
        for blocks in COL_STREAMS:
            half = blocks // 2 * TILE
            pieces += [totals[start : start + half], totals[start + half : start + 2 * half]]
            start += 2 * half
        return pieces

    right_zero = [jnp.zeros((chunk.shape[1], width), jnp.float32) for chunk in dense]
    beta_first, left_vec, right_raw = back_step(left_pieces, right_zero)
    resid_bar = beta_first
    model = right_zero
    search = right_zero
    diag_bar = beta_first
    rotate_cos = beta_first
    rotate_sin = beta_first
    radius = beta_first
    for iteration in range(ITERS):
        fore_summed, fore_squares = reduce_cols(
            fore_products(right_raw), spread(column_norm(right_raw, ROW_STREAMS[1] * PIECE // 4))
        )
        alpha_norm = jnp.sqrt(fore_squares + tiny_eps)
        left_raw = [
            total / alpha_norm - alpha_norm * prev for total, prev in zip(fore_summed, left_vec)
        ]
        right_vec = [piece / alpha_norm for piece in right_raw]
        if iteration == 0:
            diag_bar = alpha_norm
            search = right_vec
        else:
            coupling = rotate_sin * alpha_norm
            diag_bar = -rotate_cos * alpha_norm
            search = [now - coupling / radius * old for now, old in zip(right_vec, search)]
        beta_norm, left_vec, right_raw = back_step(left_raw, right_vec)
        radius = jnp.sqrt(diag_bar * diag_bar + beta_norm * beta_norm)
        rotate_cos = diag_bar / radius
        rotate_sin = beta_norm / radius
        step_size = rotate_cos * resid_bar
        resid_bar = rotate_sin * resid_bar
        model = [old + step_size / radius * way for old, way in zip(model, search)]
    misfit = resid_bar / beta_first
    gradient = [misfit * rotate_cos * piece for piece in right_raw]

    def in_block_order(pieces):
        out = []
        start = 0
        for count, (outer_side, inner_side) in zip(ROW_STREAMS, sides):
            whole = jnp.concatenate(pieces[start : start + count])
            quarter = whole.shape[0] // 4
            parts = [whole[i * quarter : (i + 1) * quarter] for i in range(4)]
            straight = inner_side == 1
            parts = [jnp.where(straight, parts[i], parts[i ^ 1]) for i in range(4)]
            straight = outer_side == 1
            out += [jnp.where(straight, parts[i], parts[i ^ 2]) for i in range(4)]
            start += count
        return jnp.concatenate(out)

    return (in_block_order(model), in_block_order(gradient), misfit)


def solution(mesh):
    placed = (P("rows", "cols", None, None), P("rows", "cols"), P("rows", "cols"), P("rows", None))

    def local(kernel, pattern, counts, delays):
        return on_device(
            mesh.shape["rows"], mesh.shape["cols"], kernel, pattern, counts, delays
        )

    return jax.shard_map(
        local,
        mesh=mesh,
        in_specs=placed,
        out_specs=(P("cols", None), P("cols", None), P()),
        check_vma=False,
    )
```

```python
import functools

import jax
import jax.numpy as jnp
from jax import lax
from jax.experimental import pallas as pl
from jax.experimental.pallas import tpu as pltpu
from jax.sharding import PartitionSpec as P

CB_DEV = 24
ITERS = 2
TILE = 128
PAIR = 2 * TILE
UNITS = 4
NORM_ROWS = 8
BUFFERS = 4

tiny_eps = 1e-06

WHOLE = pl.BlockSpec(memory_space=pltpu.VMEM)
SCALARS = pl.BlockSpec(memory_space=pltpu.SMEM)


def low_lanes(shape):
    return lax.broadcasted_iota(jnp.int32, shape, 1) < shape[1] // 2


def turned(value):
    return pltpu.roll(value, value.shape[1] // 2, 1)


def rows_of(pair, size=TILE):
    return slice(pair * size, (pair + 1) * size)


def fill_kernel(
    pattern_ref, count_ref, place_ref, flip_ref, delays_ref, tiles_ref,
    dense_ref, *rest,
):
    left_refs, (buffer_ref, arrived) = rest[:-2], rest[-2:]
    row_blocks = tiles_ref.shape[0]
    flip = flip_ref[0]

    def fetch(position, slot):
        return pltpu.make_async_copy(
            tiles_ref.at[position ^ flip], buffer_ref.at[slot], arrived.at[slot]
        )

    for position in range(BUFFERS):
        fetch(position, position).start()

    low = low_lanes((TILE, TILE))
    for pair in range(row_blocks // 2):
        source = (pair ^ (flip // 2)) * PAIR
        even = delays_ref[pl.ds(pl.multiple_of(source, TILE), TILE), :]
        odd = delays_ref[pl.ds(pl.multiple_of(source + TILE, TILE), TILE), :]
        left_refs[0][rows_of(pair), :] = jnp.where(low, even, turned(odd))
        left_refs[1][rows_of(pair), :] = jnp.where(low, turned(even), odd)

    @pl.loop(0, row_blocks)
    def _(position):
        slot = lax.rem(position, BUFFERS)
        rows = pl.ds(pl.multiple_of(position * TILE, TILE), TILE)
        dense_ref[rows, :] = jnp.zeros((TILE, dense_ref.shape[1]), dense_ref.dtype)
        fetch(position, slot).wait()
        block = position ^ flip

        @pl.loop(0, count_ref[block, 0])
        def _(tile):
            place = place_ref[pattern_ref[block, tile]]
            lanes = pl.ds(pl.multiple_of(place * TILE, TILE), TILE)
            dense_ref[rows, lanes] = buffer_ref[slot, tile]

        @pl.when(position + BUFFERS < row_blocks)
        def _():
            fetch(position + BUFFERS, slot).start()


def fill_dense(kernel, pattern, counts, places, flip, delays):
    row_blocks, slot_count = kernel.shape[:2]
    rows = row_blocks * TILE
    left = jax.ShapeDtypeStruct((rows // 2, TILE), jnp.float32)
    return pl.pallas_call(
        fill_kernel,
        in_specs=[SCALARS] * 4 + [WHOLE, pl.BlockSpec(memory_space=pl.ANY)],
        out_specs=[WHOLE] * 3,
        out_shape=[jax.ShapeDtypeStruct((rows, CB_DEV * TILE), kernel.dtype), left, left],
        scratch_shapes=[
            pltpu.VMEM((BUFFERS, slot_count, TILE, TILE), kernel.dtype),
            pltpu.SemaphoreType.DMA((BUFFERS,)),
        ],
        compiler_params=pltpu.CompilerParams(vmem_limit_bytes=46 * 1024 * 1024),
        cost_estimate=pl.CostEstimate(
            flops=0, bytes_accessed=2 * kernel.size, transcendentals=0
        ),
    )(pattern, counts, places, flip, delays, kernel)


def norm_of(ref):
    return jnp.sqrt(ref[0:1, :] + tiny_eps)


def squares_row(sums):
    while len(sums) > 1:
        sums = [sums[i] + sums[i + 1] for i in range(0, len(sums), 2)]
    row = jnp.sum(sums[0], axis=0, keepdims=True)
    return row + turned(row)


def next_vector(parts, raw_ref, scale_ref, past_ref, past_scale_ref):
    if scale_ref is not None:
        scale = norm_of(scale_ref)
    if past_ref is not None:
        past_scale = norm_of(past_scale_ref)
    position = 0
    for part, units in parts:
        pairs = part.shape[0] // TILE // units
        for unit in range(units):
            squares = jnp.zeros((NORM_ROWS, TILE), jnp.float32)
            for pair in range(pairs):
                value = part[rows_of(unit * pairs + pair), :]
                if scale_ref is not None:
                    value = value / scale
                if past_ref is not None:
                    value = value - scale * (past_ref[rows_of(position), :] / past_scale)
                if raw_ref is not None:
                    raw_ref[rows_of(position), :] = value
                squares += jnp.sum((value * value).reshape(-1, NORM_ROWS, TILE), axis=0)
                yield position, value, squares if pair == pairs - 1 else None
                position += 1


def store_message(pair, value, send_ref, keep_ref):
    half = keep_ref.shape[0] // TILE
    if pair < half:
        send_ref[rows_of(pair), :] = value
    else:
        keep_ref[rows_of(pair - half), :] = value


def back_kernel(first, *refs):
    if first:
        dense_ref, own_ref, send_ref, keep_ref, turned_ref = refs
        parts, raw_ref, scales = [(own_ref, 2)], None, (None, None, None)
    else:
        (dense_ref, other_ref, own_ref, scale_ref, past_ref, past_scale_ref,
         send_ref, keep_ref, raw_ref, turned_ref) = refs
        parts, scales = [(other_ref, 1), (own_ref, 1)], (scale_ref, past_ref, past_scale_ref)
    sums = []
    half = turned_ref.shape[0]
    for pair, value, squares in next_vector(parts, raw_ref, *scales):
        flat = value.T.astype(turned_ref.dtype)
        turned_ref[:, rows_of(2 * pair)] = flat[:half]
        turned_ref[:, rows_of(2 * pair + 1)] = flat[half:]
        if squares is not None:
            sums.append(squares)
    send_ref[keep_ref.shape[0] :, :] = jnp.broadcast_to(squares_row(sums), (NORM_ROWS, TILE))
    for pair in range(dense_ref.shape[1] // PAIR):
        product = jnp.dot(
            turned_ref[...], dense_ref[:, rows_of(pair, PAIR)], preferred_element_type=jnp.float32
        )
        stacked = jnp.concatenate([product[:, :TILE], product[:, TILE:]], axis=0)
        store_message(pair, stacked.T, send_ref, keep_ref)


def fore_kernel(first, *refs):
    if first:
        (dense_ref, outer_ref, inner_ref, mine_ref, scale_ref,
         send_ref, keep_ref, raw_ref, wide_ref) = refs
        scales = (scale_ref, None, None)
    else:
        (dense_ref, outer_ref, inner_ref, mine_ref, scale_ref, past_ref, past_scale_ref,
         send_ref, keep_ref, raw_ref, wide_ref) = refs
        scales = (scale_ref, past_ref, past_scale_ref)
    parts = [(outer_ref, 2), (inner_ref, 1), (mine_ref, 1)]
    low = low_lanes((TILE, TILE))
    sums = []
    for pair, value, squares in next_vector(parts, raw_ref, *scales):
        other = turned(value)
        wide_ref[rows_of(2 * pair), :] = jnp.where(low, value, other).astype(wide_ref.dtype)
        wide_ref[rows_of(2 * pair + 1), :] = jnp.where(low, other, value).astype(wide_ref.dtype)
        if squares is not None:
            sums.append(squares)
    send_ref[keep_ref.shape[0] :, :] = jnp.broadcast_to(squares_row(sums), (NORM_ROWS, TILE))
    step = 4
    for start in range(0, dense_ref.shape[0] // TILE, step):
        product = jnp.dot(
            dense_ref[start * TILE : (start + step) * TILE, :],
            wide_ref[...],
            preferred_element_type=jnp.float32,
        )
        for pair in range(step // 2):
            even, odd = product[rows_of(2 * pair), :], product[rows_of(2 * pair + 1), :]
            store_message(start // 2 + pair, jnp.where(low, even, odd), send_ref, keep_ref)


def product_call(body, dense, operands, half, raw_rows, scratch):
    message = jax.ShapeDtypeStruct((half + NORM_ROWS, TILE), jnp.float32)
    kept = jax.ShapeDtypeStruct((half, TILE), jnp.float32)
    shapes = [message, kept]
    if raw_rows:
        shapes.append(jax.ShapeDtypeStruct((raw_rows, TILE), jnp.float32))
    return pl.pallas_call(
        body,
        in_specs=[WHOLE] * (1 + len(operands)),
        out_specs=[WHOLE] * len(shapes),
        out_shape=shapes,
        scratch_shapes=[scratch],
        compiler_params=pltpu.CompilerParams(vmem_limit_bytes=12 * 1024 * 1024),
        cost_estimate=pl.CostEstimate(
            flops=4 * TILE * dense.size, bytes_accessed=2 * dense.size, transcendentals=0
        ),
    )(dense, *operands)


def back_product(dense, operands, first):
    scratch = pltpu.VMEM((TILE // 2, dense.shape[0]), dense.dtype)
    raw_rows = 0 if first else dense.shape[0] // 2
    return product_call(
        functools.partial(back_kernel, first), dense, operands, dense.shape[1] // 4, raw_rows, scratch
    )


def fore_product(dense, operands, first):
    scratch = pltpu.VMEM((dense.shape[1], TILE), dense.dtype)
    return product_call(
        functools.partial(fore_kernel, first),
        dense, operands, dense.shape[0] // 4, dense.shape[1] // 2, scratch,
    )


def rotation(norms):
    betas, alphas = [norm_of(ref) for ref in norms[0::2]], [norm_of(ref) for ref in norms[1::2]]
    resid_bar, diag_bar = betas[0], alphas[0]
    steps = []
    for j in range(len(alphas)):
        radius = jnp.sqrt(diag_bar * diag_bar + betas[j + 1] * betas[j + 1])
        rotate_cos = diag_bar / radius
        rotate_sin = betas[j + 1] / radius
        step_size = rotate_cos * resid_bar
        resid_bar = rotate_sin * resid_bar
        coupling = None
        if j + 1 < len(alphas):
            coupling = rotate_sin * alphas[j + 1] / radius
            diag_bar = -rotate_cos * alphas[j + 1]
        steps.append((step_size / radius, coupling))
    misfit = resid_bar / betas[0]
    return alphas, betas, steps, misfit, misfit * rotate_cos


def store_in_order(out_ref, mask, pair, low, values):
    pairs = out_ref.shape[0] // PAIR // UNITS
    start = (((pair // pairs) ^ mask) * pairs + pair % pairs) * PAIR
    ours, theirs = values
    even = pl.ds(pl.multiple_of(start, TILE), TILE)
    odd = pl.ds(pl.multiple_of(start + TILE, TILE), TILE)
    out_ref[even, :] = jnp.where(low, ours, turned(theirs))
    out_ref[odd, :] = jnp.where(low, turned(ours), theirs)


def model_kernel(count, mask_ref, *refs):
    ins, (model_ref, misfit_ref) = refs[:-2], refs[-2:]
    chains = [ins[: len(ins) // 2], ins[len(ins) // 2 :]]
    low = low_lanes((TILE, TILE))
    rotations = [rotation(refs_[count:]) for refs_ in chains]
    misfits = [jnp.broadcast_to(r[3], misfit_ref.shape) for r in rotations]
    misfit_ref[...] = jnp.where(low_lanes(misfit_ref.shape), misfits[0], misfits[1])
    for pair in range(model_ref.shape[0] // PAIR):
        values = []
        for refs_, (alphas, _, steps, _, _) in zip(chains, rotations):
            search = total = None
            for j in range(count):
                right = refs_[j][rows_of(pair), :] / alphas[j]
                search = right if j == 0 else right - steps[j - 1][1] * search
                total = steps[j][0] * search if j == 0 else total + steps[j][0] * search
            values.append(total)
        store_in_order(model_ref, mask_ref[0], pair, low, values)


def gradient_kernel(mask_ref, *refs):
    ins, gradient_ref = refs[:-1], refs[-1]
    chains = [ins[: len(ins) // 2], ins[len(ins) // 2 :]]
    low = low_lanes((TILE, TILE))
    vectors = []
    factors = []
    for outer_ref, inner_ref, mine_ref, past_ref, *norms in chains:
        alphas, betas, _, _, factor = rotation(norms)
        parts = [(outer_ref, 2), (inner_ref, 1), (mine_ref, 1)]
        vectors.append(next_vector(parts, None, norms[-1], past_ref, norms[-2]))
        factors.append(factor)
    for ours, theirs in zip(*vectors):
        values = [factors[0] * ours[1], factors[1] * theirs[1]]
        store_in_order(gradient_ref, mask_ref[0], ours[0], low, values)


def last_call(body, mask, operands, shapes):
    return pl.pallas_call(
        body,
        in_specs=[SCALARS] + [WHOLE] * len(operands),
        out_specs=[WHOLE] * len(shapes),
        out_shape=[jax.ShapeDtypeStruct(shape, jnp.float32) for shape in shapes],
        compiler_params=pltpu.CompilerParams(vmem_limit_bytes=12 * 1024 * 1024),
        cost_estimate=pl.CostEstimate(
            flops=0, bytes_accessed=8 * shapes[0][0] * TILE, transcendentals=0
        ),
    )(mask, *operands)


def on_device(row_count, col_count, kernel, pattern, counts, delays):
    row_bits = list(range(row_count.bit_length() - 1))
    col_bits = list(range(col_count.bit_length() - 1))
    row_index = lax.axis_index("rows")
    core = lax.axis_index("cols") & 1

    orders = [row_bits, [row_bits[1], row_bits[0], *row_bits[2:]]]

    def swap_rows(value, level):
        pairs = []
        for row in range(row_count):
            for col in range(col_count):
                partner = row ^ (1 << orders[col & 1][level])
                pairs.append((row * col_count + col, partner * col_count + col))
        return lax.ppermute(value, ("rows", "cols"), pairs)

    def swap_cols(value, level):
        return lax.ppermute(value, "cols", [(i, i ^ (1 << level)) for i in range(col_count)])

    bits = [(row_index >> bit) & 1 for bit in row_bits[:2]]
    outer_side = jnp.where(core == 0, bits[0], bits[1])
    inner_side = jnp.where(core == 0, bits[1], bits[0])
    mask = ((1 - outer_side) * 2 + (1 - inner_side)).astype(jnp.int32)
    blocks = jnp.arange(CB_DEV, dtype=jnp.int32)
    unit = CB_DEV // UNITS
    places = ((blocks // unit) ^ mask) * unit + blocks % unit
    flip = ((1 - core) * (kernel.shape[0] // 2)).astype(jnp.int32).reshape(1)
    mask = mask.reshape(1)

    dense, *lefts = fill_dense(kernel, pattern, counts, places, flip, delays)

    def swap_normed(value, norm, swap):
        got = swap(jnp.concatenate([value, norm]))
        return got[: value.shape[0]], norm + got[value.shape[0] :]

    def reduce_rows(send, keep):
        half = keep.shape[0]
        got = swap_rows(send, 0)
        keep = keep + got[:half]
        norm = send[half:] + got[half:]
        send, mine = keep[: half // 2], keep[half // 2 :]
        for level in range(1, len(row_bits)):
            got, norm = swap_normed(send, norm, lambda value: swap_rows(value, level))
            mine = mine + got
            send = mine
        inner = swap_rows(mine, 1)
        outer = swap_rows(jnp.concatenate([inner, mine]), 0)
        return [outer, inner, mine], norm

    def reduce_cols(send, keep):
        half = keep.shape[0]
        got = swap_cols(send, 0)
        own = keep + got[:half]
        norm = send[half:] + got[half:]
        for bit in col_bits[1:]:
            got, norm = swap_normed(own, norm, lambda value: swap_cols(value, bit))
            own = own + got
        return [swap_cols(own, 0), own], norm

    def chain(left):
        send, keep = back_product(dense, [left], True)
        totals, norm = reduce_rows(send, keep)
        norms = [norm]
        rights = []
        for iteration in range(ITERS):
            past = [rights[-1], norms[-2]] if rights else []
            send, keep, right = fore_product(dense, [*totals, norms[-1], *past], not rights)
            rights.append(right)
            halves, norm = reduce_cols(send, keep)
            norms.append(norm)
            send, keep, left = back_product(
                dense, [*halves, norms[-1], left, norms[-2]], False
            )
            totals, norm = reduce_rows(send, keep)
            norms.append(norm)
        return rights, norms, totals

    chains = [chain(left) for left in lefts]
    cells = dense.shape[1]
    model, misfit = last_call(
        functools.partial(model_kernel, ITERS),
        mask,
        [operand for rights, norms, _ in chains for operand in [*rights, *norms]],
        [(cells, TILE), (NORM_ROWS, TILE)],
    )
    (gradient,) = last_call(
        gradient_kernel,
        mask,
        [operand for rights, norms, totals in chains for operand in [*totals, rights[-1], *norms]],
        [(cells, TILE)],
    )
    return (model, gradient, misfit[0])


def solution(mesh):
    placed = (P("rows", "cols", None, None), P("rows", "cols"), P("rows", "cols"), P("rows", None))

    def local(kernel, pattern, counts, delays):
        return on_device(
            mesh.shape["rows"], mesh.shape["cols"], kernel, pattern, counts, delays
        )

    return jax.shard_map(
        local,
        mesh=mesh,
        in_specs=placed,
        out_specs=(P("cols", None), P("cols", None), P()),
        check_vma=False,
    )
```

```python
import functools

import jax
import jax.numpy as jnp
from jax import lax
from jax.experimental import pallas as pl
from jax.experimental.pallas import tpu as pltpu
from jax.sharding import PartitionSpec as P

CB_DEV = 24
ITERS = 2
TILE = 128
PAIR = 2 * TILE
UNITS = 4
NORM_ROWS = 8
BEHIND = 2

tiny_eps = 1e-06

WHOLE = pl.BlockSpec(memory_space=pltpu.VMEM)
SCALARS = pl.BlockSpec(memory_space=pltpu.SMEM)


def low_lanes(shape):
    return lax.broadcasted_iota(jnp.int32, shape, 1) < shape[1] // 2


def turned(value):
    return pltpu.roll(value, value.shape[1] // 2, 1)


def rows_of(pair, size=TILE):
    return slice(pair * size, (pair + 1) * size)


def fill_kernel(
    pattern_ref, count_ref, place_ref, flip_ref, delays_ref, tiles_ref, dense_ref, *left_refs
):
    flip = flip_ref[0]
    low = low_lanes((TILE, TILE))
    for pair in range(delays_ref.shape[0] // PAIR):
        source = (pair ^ (flip // 2)) * PAIR
        even = delays_ref[pl.ds(pl.multiple_of(source, TILE), TILE), :]
        odd = delays_ref[pl.ds(pl.multiple_of(source + TILE, TILE), TILE), :]
        left_refs[0][rows_of(pair), :] = jnp.where(low, even, turned(odd))
        left_refs[1][rows_of(pair), :] = jnp.where(low, turned(even), odd)

    @pl.loop(0, tiles_ref.shape[0])
    def _(position):
        rows = pl.ds(pl.multiple_of(position * TILE, TILE), TILE)
        dense_ref[rows, :] = jnp.zeros((TILE, dense_ref.shape[1]), dense_ref.dtype)
        block = position ^ flip

        @pl.loop(0, count_ref[block])
        def _(tile):
            place = place_ref[pattern_ref[block, tile]]
            lanes = pl.ds(pl.multiple_of(place * TILE, TILE), TILE)
            dense_ref[rows, lanes] = tiles_ref[block, tile]


def fill_dense(kernel, pattern, counts, places, flip, delays):
    rows = kernel.shape[0] * TILE
    left = jax.ShapeDtypeStruct((rows // 2, TILE), jnp.float32)
    return pl.pallas_call(
        fill_kernel,
        in_specs=[SCALARS] * 4 + [WHOLE] * 2,
        out_specs=[WHOLE] * 3,
        out_shape=[jax.ShapeDtypeStruct((rows, CB_DEV * TILE), kernel.dtype), left, left],
        compiler_params=pltpu.CompilerParams(vmem_limit_bytes=12 * 1024 * 1024),
        cost_estimate=pl.CostEstimate(
            flops=0, bytes_accessed=2 * kernel.size, transcendentals=0
        ),
    )(pattern, counts.reshape(-1), places, flip, delays, kernel)


def norm_of(ref):
    return jnp.sqrt(ref[0:1, :] + tiny_eps)


def squares_row(sums):
    while len(sums) > 1:
        sums = [sums[i] + sums[i + 1] for i in range(0, len(sums), 2)]
    row = jnp.sum(sums[0], axis=0, keepdims=True)
    return row + turned(row)


def next_vector(parts, raw_ref, scale_ref, past_ref, past_scale_ref):
    if scale_ref is not None:
        scale = norm_of(scale_ref)
    if past_ref is not None:
        past_scale = norm_of(past_scale_ref)
    position = 0
    for part, units in parts:
        pairs = part.shape[0] // TILE // units
        for unit in range(units):
            squares = jnp.zeros((NORM_ROWS, TILE), jnp.float32)
            for pair in range(pairs):
                value = part[rows_of(unit * pairs + pair), :]
                if scale_ref is not None:
                    value = value / scale
                if past_ref is not None:
                    value = value - scale * (past_ref[rows_of(position), :] / past_scale)
                if raw_ref is not None:
                    raw_ref[rows_of(position), :] = value
                squares += jnp.sum((value * value).reshape(-1, NORM_ROWS, TILE), axis=0)
                yield position, value, squares if pair == pairs - 1 else None
                position += 1


def store_message(pair, value, send_ref, keep_ref):
    half = keep_ref.shape[0] // TILE
    if pair < half:
        send_ref[rows_of(pair), :] = value
    else:
        keep_ref[rows_of(pair - half), :] = value


def back_kernel(first, *refs):
    if first:
        dense_ref, own_ref, send_ref, keep_ref, turned_ref = refs
        parts, raw_ref, scales = [(own_ref, 2)], None, (None, None, None)
    else:
        (dense_ref, other_ref, own_ref, scale_ref, past_ref, past_scale_ref,
         send_ref, keep_ref, raw_ref, turned_ref) = refs
        parts, scales = [(other_ref, 1), (own_ref, 1)], (scale_ref, past_ref, past_scale_ref)
    sums = []
    half = turned_ref.shape[0]
    for pair, value, squares in next_vector(parts, raw_ref, *scales):
        flat = value.T.astype(turned_ref.dtype)
        turned_ref[:, rows_of(2 * pair)] = flat[:half]
        turned_ref[:, rows_of(2 * pair + 1)] = flat[half:]
        if squares is not None:
            sums.append(squares)
    send_ref[keep_ref.shape[0] :, :] = jnp.broadcast_to(squares_row(sums), (NORM_ROWS, TILE))
    for pair in range(dense_ref.shape[1] // PAIR):
        product = jnp.dot(
            turned_ref[...], dense_ref[:, rows_of(pair, PAIR)], preferred_element_type=jnp.float32
        )
        stacked = jnp.concatenate([product[:, :TILE], product[:, TILE:]], axis=0)
        store_message(pair, stacked.T, send_ref, keep_ref)


def fore_kernel(first, *refs):
    if first:
        (dense_ref, outer_ref, inner_ref, mine_ref, scale_ref,
         send_ref, keep_ref, raw_ref, wide_ref) = refs
        scales = (scale_ref, None, None)
    else:
        (dense_ref, outer_ref, inner_ref, mine_ref, scale_ref, past_ref, past_scale_ref,
         send_ref, keep_ref, raw_ref, wide_ref) = refs
        scales = (scale_ref, past_ref, past_scale_ref)
    parts = [(outer_ref, 2), (inner_ref, 1), (mine_ref, 1)]
    low = low_lanes((TILE, TILE))
    sums = []
    for pair, value, squares in next_vector(parts, raw_ref, *scales):
        other = turned(value)
        wide_ref[rows_of(2 * pair), :] = jnp.where(low, value, other).astype(wide_ref.dtype)
        wide_ref[rows_of(2 * pair + 1), :] = jnp.where(low, other, value).astype(wide_ref.dtype)
        if squares is not None:
            sums.append(squares)
    send_ref[keep_ref.shape[0] :, :] = jnp.broadcast_to(squares_row(sums), (NORM_ROWS, TILE))
    step = 4
    for start in range(0, dense_ref.shape[0] // TILE, step):
        product = jnp.dot(
            dense_ref[start * TILE : (start + step) * TILE, :],
            wide_ref[...],
            preferred_element_type=jnp.float32,
        )
        for pair in range(step // 2):
            even, odd = product[rows_of(2 * pair), :], product[rows_of(2 * pair + 1), :]
            store_message(start // 2 + pair, jnp.where(low, even, odd), send_ref, keep_ref)


def product_call(body, dense, operands, half, raw_rows, scratch):
    message = jax.ShapeDtypeStruct((half + NORM_ROWS, TILE), jnp.float32)
    kept = jax.ShapeDtypeStruct((half, TILE), jnp.float32)
    shapes = [message, kept]
    if raw_rows:
        shapes.append(jax.ShapeDtypeStruct((raw_rows, TILE), jnp.float32))
    return pl.pallas_call(
        body,
        in_specs=[WHOLE] * (1 + len(operands)),
        out_specs=[WHOLE] * len(shapes),
        out_shape=shapes,
        scratch_shapes=[scratch],
        compiler_params=pltpu.CompilerParams(vmem_limit_bytes=12 * 1024 * 1024),
        cost_estimate=pl.CostEstimate(
            flops=4 * TILE * dense.size, bytes_accessed=2 * dense.size, transcendentals=0
        ),
    )(dense, *operands)


def back_product(dense, operands, first):
    scratch = pltpu.VMEM((TILE // 2, dense.shape[0]), dense.dtype)
    raw_rows = 0 if first else dense.shape[0] // 2
    return product_call(
        functools.partial(back_kernel, first), dense, operands, dense.shape[1] // 4, raw_rows, scratch
    )


def fore_product(dense, operands, first):
    scratch = pltpu.VMEM((dense.shape[1], TILE), dense.dtype)
    return product_call(
        functools.partial(fore_kernel, first),
        dense, operands, dense.shape[0] // 4, dense.shape[1] // 2, scratch,
    )


def rotation(norms):
    betas, alphas = [norm_of(ref) for ref in norms[0::2]], [norm_of(ref) for ref in norms[1::2]]
    resid_bar, diag_bar = betas[0], alphas[0]
    steps = []
    for j in range(len(alphas)):
        radius = jnp.sqrt(diag_bar * diag_bar + betas[j + 1] * betas[j + 1])
        rotate_cos = diag_bar / radius
        rotate_sin = betas[j + 1] / radius
        step_size = rotate_cos * resid_bar
        resid_bar = rotate_sin * resid_bar
        coupling = None
        if j + 1 < len(alphas):
            coupling = rotate_sin * alphas[j + 1] / radius
            diag_bar = -rotate_cos * alphas[j + 1]
        steps.append((step_size / radius, coupling))
    misfit = resid_bar / betas[0]
    return alphas, betas, steps, misfit, misfit * rotate_cos


def store_in_order(out_ref, mask, pair, low, values):
    pairs = out_ref.shape[0] // PAIR // UNITS
    start = (((pair // pairs) ^ mask) * pairs + pair % pairs) * PAIR
    ours, theirs = values
    even = pl.ds(pl.multiple_of(start, TILE), TILE)
    odd = pl.ds(pl.multiple_of(start + TILE, TILE), TILE)
    out_ref[even, :] = jnp.where(low, ours, turned(theirs))
    out_ref[odd, :] = jnp.where(low, turned(ours), theirs)


def model_kernel(count, mask_ref, *refs):
    ins, (model_ref, misfit_ref) = refs[:-2], refs[-2:]
    chains = [ins[: len(ins) // 2], ins[len(ins) // 2 :]]
    low = low_lanes((TILE, TILE))
    rotations = [rotation(refs_[count:]) for refs_ in chains]
    misfits = [jnp.broadcast_to(r[3], misfit_ref.shape) for r in rotations]
    misfit_ref[...] = jnp.where(low_lanes(misfit_ref.shape), misfits[0], misfits[1])
    for pair in range(model_ref.shape[0] // PAIR):
        values = []
        for refs_, (alphas, _, steps, _, _) in zip(chains, rotations):
            search = total = None
            for j in range(count):
                right = refs_[j][rows_of(pair), :] / alphas[j]
                search = right if j == 0 else right - steps[j - 1][1] * search
                total = steps[j][0] * search if j == 0 else total + steps[j][0] * search
            values.append(total)
        store_in_order(model_ref, mask_ref[0], pair, low, values)


def gradient_kernel(mask_ref, *refs):
    ins, gradient_ref = refs[:-1], refs[-1]
    chains = [ins[: len(ins) // 2], ins[len(ins) // 2 :]]
    low = low_lanes((TILE, TILE))
    vectors = []
    factors = []
    for outer_ref, inner_ref, mine_ref, past_ref, *norms in chains:
        alphas, betas, _, _, factor = rotation(norms)
        parts = [(outer_ref, 2), (inner_ref, 1), (mine_ref, 1)]
        vectors.append(next_vector(parts, None, norms[-1], past_ref, norms[-2]))
        factors.append(factor)
    for ours, theirs in zip(*vectors):
        values = [factors[0] * ours[1], factors[1] * theirs[1]]
        store_in_order(gradient_ref, mask_ref[0], ours[0], low, values)


def last_call(body, mask, operands, shapes):
    return pl.pallas_call(
        body,
        in_specs=[SCALARS] + [WHOLE] * len(operands),
        out_specs=[WHOLE] * len(shapes),
        out_shape=[jax.ShapeDtypeStruct(shape, jnp.float32) for shape in shapes],
        compiler_params=pltpu.CompilerParams(vmem_limit_bytes=12 * 1024 * 1024),
        cost_estimate=pl.CostEstimate(
            flops=0, bytes_accessed=8 * shapes[0][0] * TILE, transcendentals=0
        ),
    )(mask, *operands)


def on_device(row_count, col_count, kernel, pattern, counts, delays):
    row_bits = list(range(row_count.bit_length() - 1))
    col_bits = list(range(col_count.bit_length() - 1))
    row_index = lax.axis_index("rows")
    core = lax.axis_index("cols") & 1

    orders = [row_bits, [row_bits[1], row_bits[0], *row_bits[2:]]]

    def swap_rows(value, level):
        pairs = []
        for row in range(row_count):
            for col in range(col_count):
                partner = row ^ (1 << orders[col & 1][level])
                pairs.append((row * col_count + col, partner * col_count + col))
        return lax.ppermute(value, ("rows", "cols"), pairs)

    def swap_cols(value, level):
        return lax.ppermute(value, "cols", [(i, i ^ (1 << level)) for i in range(col_count)])

    bits = [(row_index >> bit) & 1 for bit in row_bits[:2]]
    outer_side = jnp.where(core == 0, bits[0], bits[1])
    inner_side = jnp.where(core == 0, bits[1], bits[0])
    mask = ((1 - outer_side) * 2 + (1 - inner_side)).astype(jnp.int32)
    blocks = jnp.arange(CB_DEV, dtype=jnp.int32)
    unit = CB_DEV // UNITS
    places = ((blocks // unit) ^ mask) * unit + blocks % unit
    flip = ((1 - core) * (kernel.shape[0] // 2)).astype(jnp.int32).reshape(1)
    mask = mask.reshape(1)

    dense, *lefts = fill_dense(kernel, pattern, counts, places, flip, delays)

    def swap_normed(value, norm, swap):
        got = swap(jnp.concatenate([value, norm]))
        return got[: value.shape[0]], norm + got[value.shape[0] :]

    def reduce_rows(send, keep, swap_rows):
        half = keep.shape[0]
        got = swap_rows(send, 0)
        keep = keep + got[:half]
        norm = send[half:] + got[half:]
        send, mine = keep[: half // 2], keep[half // 2 :]
        for level in range(1, len(row_bits)):
            got, norm = swap_normed(send, norm, lambda value: swap_rows(value, level))
            mine = mine + got
            send = mine
        inner = swap_rows(mine, 1)
        outer = swap_rows(jnp.concatenate([inner, mine]), 0)
        return [outer, inner, mine], norm

    def reduce_cols(send, keep, swap_cols):
        half = keep.shape[0]
        got = swap_cols(send, 0)
        own = keep + got[:half]
        norm = send[half:] + got[half:]
        for bit in col_bits[1:]:
            got, norm = swap_normed(own, norm, lambda value: swap_cols(value, bit))
            own = own + got
        return [swap_cols(own, 0), own], norm

    def chain(left, leader):
        gots = []

        def follow(swap):
            def one(value, level):
                ahead = len(gots) + BEHIND - 1
                if ahead < len(leader):
                    value = lax.optimization_barrier((value, leader[ahead]))[0]
                gots.append(swap(value, level))
                return gots[-1]

            return one

        rows, cols = follow(swap_rows), follow(swap_cols)
        send, keep = back_product(dense, [left], True)
        totals, norm = reduce_rows(send, keep, rows)
        norms = [norm]
        rights = []
        for iteration in range(ITERS):
            past = [rights[-1], norms[-2]] if rights else []
            send, keep, right = fore_product(dense, [*totals, norms[-1], *past], not rights)
            rights.append(right)
            halves, norm = reduce_cols(send, keep, cols)
            norms.append(norm)
            send, keep, left = back_product(
                dense, [*halves, norms[-1], left, norms[-2]], False
            )
            totals, norm = reduce_rows(send, keep, rows)
            norms.append(norm)
        return (rights, norms, totals), gots

    ahead, gots = chain(lefts[0], [])
    behind, _ = chain(lefts[1], gots)
    chains = [ahead, behind]
    cells = dense.shape[1]
    model, misfit = last_call(
        functools.partial(model_kernel, ITERS),
        mask,
        [operand for rights, norms, _ in chains for operand in [*rights, *norms]],
        [(cells, TILE), (NORM_ROWS, TILE)],
    )
    (gradient,) = last_call(
        gradient_kernel,
        mask,
        [operand for rights, norms, totals in chains for operand in [*totals, rights[-1], *norms]],
        [(cells, TILE)],
    )
    return (model, gradient, misfit[0])


def solution(mesh):
    placed = (P("rows", "cols", None, None), P("rows", "cols"), P("rows", "cols"), P("rows", None))

    def local(kernel, pattern, counts, delays):
        return on_device(
            mesh.shape["rows"], mesh.shape["cols"], kernel, pattern, counts, delays
        )

    return jax.shard_map(
        local,
        mesh=mesh,
        in_specs=placed,
        out_specs=(P("cols", None), P("cols", None), P()),
        check_vma=False,
    )
```

```python
import functools

import jax
import jax.numpy as jnp
from jax import lax
from jax.experimental import pallas as pl
from jax.experimental.pallas import tpu as pltpu
from jax.sharding import PartitionSpec as P

CB_DEV = 24
ITERS = 2
TILE = 128
PAIR = 2 * TILE
UNITS = 4
NORM_ROWS = 8
BEHIND = 0

tiny_eps = 1e-06

WHOLE = pl.BlockSpec(memory_space=pltpu.VMEM)
SCALARS = pl.BlockSpec(memory_space=pltpu.SMEM)


def low_lanes(shape):
    return lax.broadcasted_iota(jnp.int32, shape, 1) < shape[1] // 2


def turned(value):
    return pltpu.roll(value, value.shape[1] // 2, 1)


def rows_of(pair, size=TILE):
    return slice(pair * size, (pair + 1) * size)


def fill_kernel(
    place_ref, flip_ref, pattern_in, counts_in, delays_in, tiles_in,
    dense_ref, even_left_ref, odd_left_ref, pattern_ref, counts_ref, delays_ref, tiles_ref, arrived,
):
    flip = flip_ref[0]
    row_blocks = tiles_in.shape[0]
    small = [
        pltpu.make_async_copy(source, target, arrived.at[row_blocks + i])
        for i, (source, target) in enumerate(
            [(pattern_in, pattern_ref), (counts_in, counts_ref), (delays_in, delays_ref)]
        )
    ]
    for copy in small:
        copy.start()

    def fetch(position):
        return pltpu.make_async_copy(
            tiles_in.at[position ^ flip], tiles_ref.at[position], arrived.at[position]
        )

    for position in range(row_blocks):
        fetch(position).start()
    for copy in small:
        copy.wait()

    low = low_lanes((TILE, TILE))
    for pair in range(row_blocks // 2):
        source = (pair ^ (flip // 2)) * PAIR
        even = delays_ref[pl.ds(pl.multiple_of(source, TILE), TILE), :]
        odd = delays_ref[pl.ds(pl.multiple_of(source + TILE, TILE), TILE), :]
        even_left_ref[rows_of(pair), :] = jnp.where(low, even, turned(odd))
        odd_left_ref[rows_of(pair), :] = jnp.where(low, turned(even), odd)

    @pl.loop(0, row_blocks)
    def _(position):
        rows = pl.ds(pl.multiple_of(position * TILE, TILE), TILE)
        dense_ref[rows, :] = jnp.zeros((TILE, dense_ref.shape[1]), dense_ref.dtype)
        fetch(position).wait()
        block = position ^ flip

        @pl.loop(0, counts_ref[block])
        def _(tile):
            place = place_ref[pattern_ref[block, tile]]
            lanes = pl.ds(pl.multiple_of(place * TILE, TILE), TILE)
            dense_ref[rows, lanes] = tiles_ref[position, tile]


def fill_dense(kernel, pattern, counts, places, flip, delays):
    row_blocks = kernel.shape[0]
    rows = row_blocks * TILE
    left = jax.ShapeDtypeStruct((rows // 2, TILE), jnp.float32)
    return pl.pallas_call(
        fill_kernel,
        in_specs=[SCALARS] * 2 + [pl.BlockSpec(memory_space=pltpu.HBM)] * 4,
        out_specs=[WHOLE] * 3,
        out_shape=[jax.ShapeDtypeStruct((rows, CB_DEV * TILE), kernel.dtype), left, left],
        scratch_shapes=[
            pltpu.SMEM(pattern.shape, jnp.int32),
            pltpu.SMEM((row_blocks,), jnp.int32),
            pltpu.VMEM(delays.shape, delays.dtype),
            pltpu.VMEM(kernel.shape, kernel.dtype),
            pltpu.SemaphoreType.DMA((row_blocks + 3,)),
        ],
        compiler_params=pltpu.CompilerParams(vmem_limit_bytes=16 * 1024 * 1024),
        cost_estimate=pl.CostEstimate(
            flops=0, bytes_accessed=2 * kernel.size, transcendentals=0
        ),
    )(
        places,
        flip,
        *(pltpu.with_memory_space_constraint(x, pltpu.HBM) for x in (pattern, counts.reshape(-1), delays, kernel)),
    )


def norm_of(ref):
    return jnp.sqrt(ref[0:1, :] + tiny_eps)


def squares_row(sums):
    while len(sums) > 1:
        sums = [sums[i] + sums[i + 1] for i in range(0, len(sums), 2)]
    row = jnp.sum(sums[0], axis=0, keepdims=True)
    return row + turned(row)


def next_vector(parts, raw_ref, scale_ref, past_ref, past_scale_ref):
    if scale_ref is not None:
        scale = norm_of(scale_ref)
    if past_ref is not None:
        past_scale = norm_of(past_scale_ref)
    position = 0
    for part, units in parts:
        pairs = part.shape[0] // TILE // units
        for unit in range(units):
            squares = jnp.zeros((NORM_ROWS, TILE), jnp.float32)
            for pair in range(pairs):
                value = part[rows_of(unit * pairs + pair), :]
                if scale_ref is not None:
                    value = value / scale
                if past_ref is not None:
                    value = value - scale * (past_ref[rows_of(position), :] / past_scale)
                if raw_ref is not None:
                    raw_ref[rows_of(position), :] = value
                squares += jnp.sum((value * value).reshape(-1, NORM_ROWS, TILE), axis=0)
                yield position, value, squares if pair == pairs - 1 else None
                position += 1


def store_message(pair, value, send_ref, keep_ref):
    half = keep_ref.shape[0] // TILE
    if pair < half:
        send_ref[rows_of(pair), :] = value
    else:
        keep_ref[rows_of(pair - half), :] = value


def back_kernel(first, *refs):
    if first:
        dense_ref, own_ref, send_ref, keep_ref, turned_ref = refs
        parts, raw_ref, scales = [(own_ref, 2)], None, (None, None, None)
    else:
        (dense_ref, other_ref, own_ref, scale_ref, past_ref, past_scale_ref,
         send_ref, keep_ref, raw_ref, turned_ref) = refs
        parts, scales = [(other_ref, 1), (own_ref, 1)], (scale_ref, past_ref, past_scale_ref)
    sums = []
    half = turned_ref.shape[0]
    for pair, value, squares in next_vector(parts, raw_ref, *scales):
        flat = value.T.astype(turned_ref.dtype)
        turned_ref[:, rows_of(2 * pair)] = flat[:half]
        turned_ref[:, rows_of(2 * pair + 1)] = flat[half:]
        if squares is not None:
            sums.append(squares)
    send_ref[keep_ref.shape[0] :, :] = jnp.broadcast_to(squares_row(sums), (NORM_ROWS, TILE))
    for pair in range(dense_ref.shape[1] // PAIR):
        product = jnp.dot(
            turned_ref[...], dense_ref[:, rows_of(pair, PAIR)], preferred_element_type=jnp.float32
        )
        stacked = jnp.concatenate([product[:, :TILE], product[:, TILE:]], axis=0)
        store_message(pair, stacked.T, send_ref, keep_ref)


def fore_kernel(first, *refs):
    if first:
        (dense_ref, outer_ref, inner_ref, mine_ref, scale_ref,
         send_ref, keep_ref, raw_ref, wide_ref) = refs
        scales = (scale_ref, None, None)
    else:
        (dense_ref, outer_ref, inner_ref, mine_ref, scale_ref, past_ref, past_scale_ref,
         send_ref, keep_ref, raw_ref, wide_ref) = refs
        scales = (scale_ref, past_ref, past_scale_ref)
    parts = [(outer_ref, 2), (inner_ref, 1), (mine_ref, 1)]
    low = low_lanes((TILE, TILE))
    sums = []
    for pair, value, squares in next_vector(parts, raw_ref, *scales):
        other = turned(value)
        wide_ref[rows_of(2 * pair), :] = jnp.where(low, value, other).astype(wide_ref.dtype)
        wide_ref[rows_of(2 * pair + 1), :] = jnp.where(low, other, value).astype(wide_ref.dtype)
        if squares is not None:
            sums.append(squares)
    send_ref[keep_ref.shape[0] :, :] = jnp.broadcast_to(squares_row(sums), (NORM_ROWS, TILE))
    step = 4
    for start in range(0, dense_ref.shape[0] // TILE, step):
        product = jnp.dot(
            dense_ref[start * TILE : (start + step) * TILE, :],
            wide_ref[...],
            preferred_element_type=jnp.float32,
        )
        for pair in range(step // 2):
            even, odd = product[rows_of(2 * pair), :], product[rows_of(2 * pair + 1), :]
            store_message(start // 2 + pair, jnp.where(low, even, odd), send_ref, keep_ref)


def product_call(body, dense, operands, half, raw_rows, scratch):
    message = jax.ShapeDtypeStruct((half + NORM_ROWS, TILE), jnp.float32)
    kept = jax.ShapeDtypeStruct((half, TILE), jnp.float32)
    shapes = [message, kept]
    if raw_rows:
        shapes.append(jax.ShapeDtypeStruct((raw_rows, TILE), jnp.float32))
    return pl.pallas_call(
        body,
        in_specs=[WHOLE] * (1 + len(operands)),
        out_specs=[WHOLE] * len(shapes),
        out_shape=shapes,
        scratch_shapes=[scratch],
        compiler_params=pltpu.CompilerParams(vmem_limit_bytes=12 * 1024 * 1024),
        cost_estimate=pl.CostEstimate(
            flops=4 * TILE * dense.size, bytes_accessed=2 * dense.size, transcendentals=0
        ),
    )(dense, *operands)


def back_product(dense, operands, first):
    scratch = pltpu.VMEM((TILE // 2, dense.shape[0]), dense.dtype)
    raw_rows = 0 if first else dense.shape[0] // 2
    return product_call(
        functools.partial(back_kernel, first), dense, operands, dense.shape[1] // 4, raw_rows, scratch
    )


def fore_product(dense, operands, first):
    scratch = pltpu.VMEM((dense.shape[1], TILE), dense.dtype)
    return product_call(
        functools.partial(fore_kernel, first),
        dense, operands, dense.shape[0] // 4, dense.shape[1] // 2, scratch,
    )


def rotation(norms):
    betas, alphas = [norm_of(ref) for ref in norms[0::2]], [norm_of(ref) for ref in norms[1::2]]
    resid_bar, diag_bar = betas[0], alphas[0]
    steps = []
    for j in range(len(alphas)):
        radius = jnp.sqrt(diag_bar * diag_bar + betas[j + 1] * betas[j + 1])
        rotate_cos = diag_bar / radius
        rotate_sin = betas[j + 1] / radius
        step_size = rotate_cos * resid_bar
        resid_bar = rotate_sin * resid_bar
        coupling = None
        if j + 1 < len(alphas):
            coupling = rotate_sin * alphas[j + 1] / radius
            diag_bar = -rotate_cos * alphas[j + 1]
        steps.append((step_size / radius, coupling))
    misfit = resid_bar / betas[0]
    return alphas, betas, steps, misfit, misfit * rotate_cos


def store_in_order(out_ref, mask, pair, low, values):
    pairs = out_ref.shape[0] // PAIR // UNITS
    start = (((pair // pairs) ^ mask) * pairs + pair % pairs) * PAIR
    ours, theirs = values
    even = pl.ds(pl.multiple_of(start, TILE), TILE)
    odd = pl.ds(pl.multiple_of(start + TILE, TILE), TILE)
    out_ref[even, :] = jnp.where(low, ours, turned(theirs))
    out_ref[odd, :] = jnp.where(low, turned(ours), theirs)


def model_kernel(count, mask_ref, *refs):
    ins, (model_ref, misfit_ref) = refs[:-2], refs[-2:]
    chains = [ins[: len(ins) // 2], ins[len(ins) // 2 :]]
    low = low_lanes((TILE, TILE))
    rotations = [rotation(refs_[count:]) for refs_ in chains]
    misfits = [jnp.broadcast_to(r[3], misfit_ref.shape) for r in rotations]
    misfit_ref[...] = jnp.where(low_lanes(misfit_ref.shape), misfits[0], misfits[1])
    for pair in range(model_ref.shape[0] // PAIR):
        values = []
        for refs_, (alphas, _, steps, _, _) in zip(chains, rotations):
            search = total = None
            for j in range(count):
                right = refs_[j][rows_of(pair), :] / alphas[j]
                search = right if j == 0 else right - steps[j - 1][1] * search
                total = steps[j][0] * search if j == 0 else total + steps[j][0] * search
            values.append(total)
        store_in_order(model_ref, mask_ref[0], pair, low, values)


def gradient_kernel(mask_ref, *refs):
    ins, gradient_ref = refs[:-1], refs[-1]
    chains = [ins[: len(ins) // 2], ins[len(ins) // 2 :]]
    low = low_lanes((TILE, TILE))
    vectors = []
    factors = []
    for outer_ref, inner_ref, mine_ref, past_ref, *norms in chains:
        alphas, betas, _, _, factor = rotation(norms)
        parts = [(outer_ref, 2), (inner_ref, 1), (mine_ref, 1)]
        vectors.append(next_vector(parts, None, norms[-1], past_ref, norms[-2]))
        factors.append(factor)
    for ours, theirs in zip(*vectors):
        values = [factors[0] * ours[1], factors[1] * theirs[1]]
        store_in_order(gradient_ref, mask_ref[0], ours[0], low, values)


def last_call(body, mask, operands, shapes):
    return pl.pallas_call(
        body,
        in_specs=[SCALARS] + [WHOLE] * len(operands),
        out_specs=[WHOLE] * len(shapes),
        out_shape=[jax.ShapeDtypeStruct(shape, jnp.float32) for shape in shapes],
        compiler_params=pltpu.CompilerParams(vmem_limit_bytes=12 * 1024 * 1024),
        cost_estimate=pl.CostEstimate(
            flops=0, bytes_accessed=8 * shapes[0][0] * TILE, transcendentals=0
        ),
    )(mask, *operands)


def on_device(row_count, col_count, kernel, pattern, counts, delays):
    row_bits = list(range(row_count.bit_length() - 1))
    col_bits = list(range(col_count.bit_length() - 1))
    row_index = lax.axis_index("rows")
    core = lax.axis_index("cols") & 1

    orders = [row_bits, [row_bits[1], row_bits[0], *row_bits[2:]]]

    def swap_rows(value, level):
        pairs = []
        for row in range(row_count):
            for col in range(col_count):
                partner = row ^ (1 << orders[col & 1][level])
                pairs.append((row * col_count + col, partner * col_count + col))
        return lax.ppermute(value, ("rows", "cols"), pairs)

    def swap_cols(value, level):
        return lax.ppermute(value, "cols", [(i, i ^ (1 << level)) for i in range(col_count)])

    bits = [(row_index >> bit) & 1 for bit in row_bits[:2]]
    outer_side = jnp.where(core == 0, bits[0], bits[1])
    inner_side = jnp.where(core == 0, bits[1], bits[0])
    mask = ((1 - outer_side) * 2 + (1 - inner_side)).astype(jnp.int32)
    blocks = jnp.arange(CB_DEV, dtype=jnp.int32)
    unit = CB_DEV // UNITS
    places = ((blocks // unit) ^ mask) * unit + blocks % unit
    flip = ((1 - core) * (kernel.shape[0] // 2)).astype(jnp.int32).reshape(1)
    mask = mask.reshape(1)

    dense, *lefts = fill_dense(kernel, pattern, counts, places, flip, delays)

    def reduce_rows(send, keep):
        half = keep.shape[0]
        got = yield swap_rows, send, 0
        keep = keep + got[:half]
        norm = send[half:] + got[half:]
        send, mine = keep[: half // 2], keep[half // 2 :]
        for level in range(1, len(row_bits)):
            got = yield swap_rows, jnp.concatenate([send, norm]), level
            norm = norm + got[half // 2 :]
            send = mine = mine + got[: half // 2]
        inner = yield swap_rows, mine, 1
        outer = yield swap_rows, jnp.concatenate([inner, mine]), 0
        return [outer, inner, mine], norm

    def reduce_cols(send, keep):
        half = keep.shape[0]
        got = yield swap_cols, send, 0
        own = keep + got[:half]
        norm = send[half:] + got[half:]
        for bit in col_bits[1:]:
            got = yield swap_cols, jnp.concatenate([own, norm]), bit
            norm = norm + got[half:]
            own = own + got[:half]
        other = yield swap_cols, own, 0
        return [other, own], norm

    def chain(left):
        send, keep = back_product(dense, [left], True)
        totals, norm = yield from reduce_rows(send, keep)
        norms = [norm]
        rights = []
        for iteration in range(ITERS):
            past = [rights[-1], norms[-2]] if rights else []
            send, keep, right = fore_product(dense, [*totals, norms[-1], *past], not rights)
            rights.append(right)
            halves, norm = yield from reduce_cols(send, keep)
            norms.append(norm)
            send, keep, left = back_product(
                dense, [*halves, norms[-1], left, norms[-2]], False
            )
            totals, norm = yield from reduce_rows(send, keep)
            norms.append(norm)
        return rights, norms, totals

    def tied(value, other):
        return lax.optimization_barrier((value, other))[0]

    runs = [chain(left) for left in lefts]
    wanted = [next(run) for run in runs]
    chains = [None] * len(runs)
    gots = [None] * len(runs)
    swap, latest, level = wanted[0]
    gots[0] = swap(latest, level)
    turn = 0
    while None in chains:
        mine = 0 if turn < BEHIND else (turn - BEHIND) % 2
        turn += 1
        if chains[mine] is not None:
            continue
        if gots[mine] is None:
            swap, value, level = wanted[mine]
            latest = tied(value, latest)
        else:
            try:
                swap, latest, level = runs[mine].send(tied(gots[mine], latest))
            except StopIteration as stop:
                chains[mine] = stop.value
                continue
        gots[mine] = swap(latest, level)

    cells = dense.shape[1]
    model, misfit = last_call(
        functools.partial(model_kernel, ITERS),
        mask,
        [operand for rights, norms, _ in chains for operand in [*rights, *norms]],
        [(cells, TILE), (NORM_ROWS, TILE)],
    )
    (gradient,) = last_call(
        gradient_kernel,
        mask,
        [operand for rights, norms, totals in chains for operand in [*totals, rights[-1], *norms]],
        [(cells, TILE)],
    )
    return (model, gradient, misfit[0])


def solution(mesh):
    placed = (P("rows", "cols", None, None), P("rows", "cols"), P("rows", "cols"), P("rows", None))

    def local(kernel, pattern, counts, delays):
        return on_device(
            mesh.shape["rows"], mesh.shape["cols"], kernel, pattern, counts, delays
        )

    return jax.shard_map(
        local,
        mesh=mesh,
        in_specs=placed,
        out_specs=(P("cols", None), P("cols", None), P()),
        check_vma=False,
    )
```

```python
import functools

import jax
import jax.numpy as jnp
from jax import lax
from jax.experimental import pallas as pl
from jax.experimental.pallas import tpu as pltpu
from jax.sharding import PartitionSpec as P

CB_DEV = 24
ITERS = 2
TILE = 128
PAIR = 2 * TILE
UNITS = 4
NORM_ROWS = 8
ROW_TIMES = (8, 6, 11)
COL_TIME = 22

tiny_eps = 1e-06

WHOLE = pl.BlockSpec(memory_space=pltpu.VMEM)
SCALARS = pl.BlockSpec(memory_space=pltpu.SMEM)


def low_lanes(shape):
    return lax.broadcasted_iota(jnp.int32, shape, 1) < shape[1] // 2


def turned(value):
    return pltpu.roll(value, value.shape[1] // 2, 1)


def rows_of(pair, size=TILE):
    return slice(pair * size, (pair + 1) * size)


def fill_kernel(
    place_ref, pattern_in, counts_in, delays_in, tiles_in,
    dense_ref, even_left_ref, odd_left_ref, pattern_ref, counts_ref, delays_ref, tiles_ref, arrived,
):
    row_blocks = tiles_in.shape[0]
    small = [
        pltpu.make_async_copy(source, target, arrived.at[row_blocks + i])
        for i, (source, target) in enumerate(
            [(pattern_in, pattern_ref), (counts_in, counts_ref), (delays_in, delays_ref)]
        )
    ]
    for copy in small:
        copy.start()

    def fetch(position):
        return pltpu.make_async_copy(
            tiles_in.at[position], tiles_ref.at[position], arrived.at[position]
        )

    for position in range(row_blocks):
        fetch(position).start()
    for copy in small:
        copy.wait()

    low = low_lanes((TILE, TILE))
    for pair in range(row_blocks // 2):
        even, odd = delays_ref[rows_of(2 * pair), :], delays_ref[rows_of(2 * pair + 1), :]
        even_left_ref[rows_of(pair), :] = jnp.where(low, even, turned(odd))
        odd_left_ref[rows_of(pair), :] = jnp.where(low, turned(even), odd)

    @pl.loop(0, row_blocks)
    def _(position):
        rows = pl.ds(pl.multiple_of(position * TILE, TILE), TILE)
        dense_ref[rows, :] = jnp.zeros((TILE, dense_ref.shape[1]), dense_ref.dtype)
        fetch(position).wait()

        @pl.loop(0, counts_ref[position])
        def _(tile):
            place = place_ref[pattern_ref[position, tile]]
            lanes = pl.ds(pl.multiple_of(place * TILE, TILE), TILE)
            dense_ref[rows, lanes] = tiles_ref[position, tile]


def fill_dense(kernel, pattern, counts, places, delays):
    row_blocks = kernel.shape[0]
    rows = row_blocks * TILE
    left = jax.ShapeDtypeStruct((rows // 2, TILE), jnp.float32)
    return pl.pallas_call(
        fill_kernel,
        in_specs=[SCALARS] + [pl.BlockSpec(memory_space=pltpu.HBM)] * 4,
        out_specs=[WHOLE] * 3,
        out_shape=[jax.ShapeDtypeStruct((rows, CB_DEV * TILE), kernel.dtype), left, left],
        scratch_shapes=[
            pltpu.SMEM(pattern.shape, jnp.int32),
            pltpu.SMEM((row_blocks,), jnp.int32),
            pltpu.VMEM(delays.shape, delays.dtype),
            pltpu.VMEM(kernel.shape, kernel.dtype),
            pltpu.SemaphoreType.DMA((row_blocks + 3,)),
        ],
        compiler_params=pltpu.CompilerParams(vmem_limit_bytes=16 * 1024 * 1024),
        cost_estimate=pl.CostEstimate(
            flops=0, bytes_accessed=2 * kernel.size, transcendentals=0
        ),
    )(
        places,
        *(pltpu.with_memory_space_constraint(x, pltpu.HBM) for x in (pattern, counts.reshape(-1), delays, kernel)),
    )


def norm_of(ref):
    return jnp.sqrt(ref[0:1, :] + tiny_eps)


def squares_row(sums):
    while len(sums) > 1:
        sums = [sums[i] + sums[i + 1] for i in range(0, len(sums), 2)]
    row = jnp.sum(sums[0], axis=0, keepdims=True)
    return row + turned(row)


def next_vector(parts, raw_ref, scale_ref, past_ref, past_scale_ref):
    if scale_ref is not None:
        scale = norm_of(scale_ref)
    if past_ref is not None:
        past_scale = norm_of(past_scale_ref)
    position = 0
    for part, units in parts:
        pairs = part.shape[0] // TILE // units
        for unit in range(units):
            squares = jnp.zeros((NORM_ROWS, TILE), jnp.float32)
            for pair in range(pairs):
                value = part[rows_of(unit * pairs + pair), :]
                if scale_ref is not None:
                    value = value / scale
                if past_ref is not None:
                    value = value - scale * (past_ref[rows_of(position), :] / past_scale)
                if raw_ref is not None:
                    raw_ref[rows_of(position), :] = value
                squares += jnp.sum((value * value).reshape(-1, NORM_ROWS, TILE), axis=0)
                yield position, value, squares if pair == pairs - 1 else None
                position += 1


def store_message(pair, value, send_ref, keep_ref):
    half = keep_ref.shape[0] // TILE
    if pair < half:
        send_ref[rows_of(pair), :] = value
    else:
        keep_ref[rows_of(pair - half), :] = value


def back_kernel(first, *refs):
    if first:
        dense_ref, total_ref, send_ref, keep_ref, turned_ref = refs
        raw_ref, scales = None, (None, None, None)
    else:
        (dense_ref, total_ref, scale_ref, past_ref, past_scale_ref,
         send_ref, keep_ref, raw_ref, turned_ref) = refs
        scales = (scale_ref, past_ref, past_scale_ref)
    parts = [(total_ref, 1)]
    sums = []
    half = turned_ref.shape[0]
    for pair, value, squares in next_vector(parts, raw_ref, *scales):
        flat = value.T.astype(turned_ref.dtype)
        turned_ref[:, rows_of(2 * pair)] = flat[:half]
        turned_ref[:, rows_of(2 * pair + 1)] = flat[half:]
        if squares is not None:
            sums.append(squares)
    send_ref[keep_ref.shape[0] :, :] = jnp.broadcast_to(squares_row(sums), (NORM_ROWS, TILE))
    for pair in range(dense_ref.shape[1] // PAIR):
        product = jnp.dot(
            turned_ref[...], dense_ref[:, rows_of(pair, PAIR)], preferred_element_type=jnp.float32
        )
        stacked = jnp.concatenate([product[:, :TILE], product[:, TILE:]], axis=0)
        store_message(pair, stacked.T, send_ref, keep_ref)


def fore_kernel(first, *refs):
    if first:
        dense_ref, outer_ref, inner_ref, mine_ref, scale_ref, send_ref, raw_ref, wide_ref = refs
        scales = (scale_ref, None, None)
    else:
        (dense_ref, outer_ref, inner_ref, mine_ref, scale_ref, past_ref, past_scale_ref,
         send_ref, raw_ref, wide_ref) = refs
        scales = (scale_ref, past_ref, past_scale_ref)
    parts = [(outer_ref, 2), (inner_ref, 1), (mine_ref, 1)]
    low = low_lanes((TILE, TILE))
    sums = []
    for pair, value, squares in next_vector(parts, raw_ref, *scales):
        other = turned(value)
        wide_ref[rows_of(2 * pair), :] = jnp.where(low, value, other).astype(wide_ref.dtype)
        wide_ref[rows_of(2 * pair + 1), :] = jnp.where(low, other, value).astype(wide_ref.dtype)
        if squares is not None:
            sums.append(squares)
    send_ref[dense_ref.shape[0] // 2 :, :] = jnp.broadcast_to(squares_row(sums), (NORM_ROWS, TILE))
    step = 4
    for start in range(0, dense_ref.shape[0] // TILE, step):
        product = jnp.dot(
            dense_ref[start * TILE : (start + step) * TILE, :],
            wide_ref[...],
            preferred_element_type=jnp.float32,
        )
        for pair in range(step // 2):
            even, odd = product[rows_of(2 * pair), :], product[rows_of(2 * pair + 1), :]
            send_ref[rows_of(start // 2 + pair), :] = jnp.where(low, even, odd)


def product_call(body, dense, operands, out_rows, scratch):
    return pl.pallas_call(
        body,
        in_specs=[WHOLE] * (1 + len(operands)),
        out_specs=[WHOLE] * len(out_rows),
        out_shape=[jax.ShapeDtypeStruct((rows, TILE), jnp.float32) for rows in out_rows],
        scratch_shapes=[scratch],
        compiler_params=pltpu.CompilerParams(vmem_limit_bytes=12 * 1024 * 1024),
        cost_estimate=pl.CostEstimate(
            flops=4 * TILE * dense.size, bytes_accessed=2 * dense.size, transcendentals=0
        ),
    )(dense, *operands)


def back_product(dense, operands, first):
    rows, cells = dense.shape
    scratch = pltpu.VMEM((TILE // 2, rows), dense.dtype)
    out_rows = [cells // 4 + NORM_ROWS, cells // 4] + ([] if first else [rows // 2])
    return product_call(functools.partial(back_kernel, first), dense, operands, out_rows, scratch)


def fore_product(dense, operands, first):
    rows, cells = dense.shape
    scratch = pltpu.VMEM((cells, TILE), dense.dtype)
    out_rows = [rows // 2 + NORM_ROWS, cells // 2]
    return product_call(functools.partial(fore_kernel, first), dense, operands, out_rows, scratch)


def rotation(norms):
    betas, alphas = [norm_of(ref) for ref in norms[0::2]], [norm_of(ref) for ref in norms[1::2]]
    resid_bar, diag_bar = betas[0], alphas[0]
    steps = []
    for j in range(len(alphas)):
        radius = jnp.sqrt(diag_bar * diag_bar + betas[j + 1] * betas[j + 1])
        rotate_cos = diag_bar / radius
        rotate_sin = betas[j + 1] / radius
        step_size = rotate_cos * resid_bar
        resid_bar = rotate_sin * resid_bar
        coupling = None
        if j + 1 < len(alphas):
            coupling = rotate_sin * alphas[j + 1] / radius
            diag_bar = -rotate_cos * alphas[j + 1]
        steps.append((step_size / radius, coupling))
    misfit = resid_bar / betas[0]
    return alphas, betas, steps, misfit, misfit * rotate_cos


def store_in_order(out_ref, mask, pair, low, values):
    pairs = out_ref.shape[0] // PAIR // UNITS
    start = (((pair // pairs) ^ mask) * pairs + pair % pairs) * PAIR
    ours, theirs = values
    even = pl.ds(pl.multiple_of(start, TILE), TILE)
    odd = pl.ds(pl.multiple_of(start + TILE, TILE), TILE)
    out_ref[even, :] = jnp.where(low, ours, turned(theirs))
    out_ref[odd, :] = jnp.where(low, turned(ours), theirs)


def model_kernel(count, mask_ref, *refs):
    ins, (model_ref, misfit_ref) = refs[:-2], refs[-2:]
    chains = [ins[: len(ins) // 2], ins[len(ins) // 2 :]]
    low = low_lanes((TILE, TILE))
    rotations = [rotation(refs_[count:]) for refs_ in chains]
    misfits = [jnp.broadcast_to(r[3], misfit_ref.shape) for r in rotations]
    misfit_ref[...] = jnp.where(low_lanes(misfit_ref.shape), misfits[0], misfits[1])
    for pair in range(model_ref.shape[0] // PAIR):
        values = []
        for refs_, (alphas, _, steps, _, _) in zip(chains, rotations):
            search = total = None
            for j in range(count):
                right = refs_[j][rows_of(pair), :] / alphas[j]
                search = right if j == 0 else right - steps[j - 1][1] * search
                total = steps[j][0] * search if j == 0 else total + steps[j][0] * search
            values.append(total)
        store_in_order(model_ref, mask_ref[0], pair, low, values)


def gradient_kernel(mask_ref, *refs):
    ins, gradient_ref = refs[:-1], refs[-1]
    chains = [ins[: len(ins) // 2], ins[len(ins) // 2 :]]
    low = low_lanes((TILE, TILE))
    vectors = []
    factors = []
    for outer_ref, inner_ref, mine_ref, past_ref, *norms in chains:
        alphas, betas, _, _, factor = rotation(norms)
        parts = [(outer_ref, 2), (inner_ref, 1), (mine_ref, 1)]
        vectors.append(next_vector(parts, None, norms[-1], past_ref, norms[-2]))
        factors.append(factor)
    for ours, theirs in zip(*vectors):
        values = [factors[0] * ours[1], factors[1] * theirs[1]]
        store_in_order(gradient_ref, mask_ref[0], ours[0], low, values)


def last_call(body, mask, operands, shapes):
    return pl.pallas_call(
        body,
        in_specs=[SCALARS] + [WHOLE] * len(operands),
        out_specs=[WHOLE] * len(shapes),
        out_shape=[jax.ShapeDtypeStruct(shape, jnp.float32) for shape in shapes],
        compiler_params=pltpu.CompilerParams(vmem_limit_bytes=12 * 1024 * 1024),
        cost_estimate=pl.CostEstimate(
            flops=0, bytes_accessed=8 * shapes[0][0] * TILE, transcendentals=0
        ),
    )(mask, *operands)


def on_device(row_count, col_count, kernel, pattern, counts, delays):
    row_bits = list(range(row_count.bit_length() - 1))
    row_index = lax.axis_index("rows")
    core = lax.axis_index("cols") & 1

    orders = [row_bits, [row_bits[1], row_bits[0], *row_bits[2:]]]

    def swap_rows(value, level):
        pairs = []
        for row in range(row_count):
            for col in range(col_count):
                partner = row ^ (1 << orders[col & 1][level])
                pairs.append((row * col_count + col, partner * col_count + col))
        return lax.ppermute(value, ("rows", "cols"), pairs)

    bits = [(row_index >> bit) & 1 for bit in row_bits[:2]]
    outer_side = jnp.where(core == 0, bits[0], bits[1])
    inner_side = jnp.where(core == 0, bits[1], bits[0])
    mask = ((1 - outer_side) * 2 + (1 - inner_side)).astype(jnp.int32)
    blocks = jnp.arange(CB_DEV, dtype=jnp.int32)
    unit = CB_DEV // UNITS
    places = ((blocks // unit) ^ mask) * unit + blocks % unit
    mask = mask.reshape(1)

    dense, *lefts = fill_dense(kernel, pattern, counts, places, delays)

    def reduce_rows(send, keep):
        half = keep.shape[0]
        got = yield ROW_TIMES[0], swap_rows, send, 0
        keep = keep + got[:half]
        norm = send[half:] + got[half:]
        send, mine = keep[: half // 2], keep[half // 2 :]
        for level in range(1, len(row_bits)):
            message = jnp.concatenate([send, norm])
            got = yield ROW_TIMES[min(level, 2)], swap_rows, message, level
            norm = norm + got[half // 2 :]
            send = mine = mine + got[: half // 2]
        inner = yield ROW_TIMES[1], swap_rows, mine, 1
        outer = yield ROW_TIMES[0], swap_rows, jnp.concatenate([inner, mine]), 0
        return [outer, inner, mine], norm

    def sum_cols(value, turned_group):
        group = list(range(col_count))
        return lax.psum(value, "cols", axis_index_groups=[group[::-1] if turned_group else group])

    def chain(left, second):
        send, keep = back_product(dense, [left], True)
        totals, norm = yield from reduce_rows(send, keep)
        norms = [norm]
        rights = []
        for iteration in range(ITERS):
            past = [rights[-1], norms[-2]] if rights else []
            message, right = fore_product(dense, [*totals, norms[-1], *past], not rights)
            rights.append(right)
            total = yield COL_TIME, sum_cols, message, second
            norms.append(total[-NORM_ROWS:])
            send, keep, left = back_product(dense, [total, norms[-1], left, norms[-2]], False)
            totals, norm = yield from reduce_rows(send, keep)
            norms.append(norm)
        return rights, norms, totals

    def tied(value, other):
        return lax.optimization_barrier((value, other))[0]

    runs = [chain(left, second) for second, left in enumerate(lefts)]
    wanted = [next(run) for run in runs]
    chains = [None] * len(runs)
    gots = [None] * len(runs)
    length, transfer, latest, level = wanted[0]
    due = [length, length]
    gots[0] = transfer(latest, level)
    while None in chains:
        mine = due.index(min(due))
        if gots[mine] is None:
            length, transfer, value, level = wanted[mine]
            latest = tied(value, latest)
        else:
            try:
                length, transfer, latest, level = runs[mine].send(tied(gots[mine], latest))
            except StopIteration as stop:
                chains[mine] = stop.value
                due[mine] = float("inf")
                continue
        gots[mine] = transfer(latest, level)
        due[mine] += length

    cells = dense.shape[1]
    model, misfit = last_call(
        functools.partial(model_kernel, ITERS),
        mask,
        [operand for rights, norms, _ in chains for operand in [*rights, *norms]],
        [(cells, TILE), (NORM_ROWS, TILE)],
    )
    (gradient,) = last_call(
        gradient_kernel,
        mask,
        [operand for rights, norms, totals in chains for operand in [*totals, rights[-1], *norms]],
        [(cells, TILE)],
    )
    return (model, gradient, misfit[0])


def solution(mesh):
    placed = (P("rows", "cols", None, None), P("rows", "cols"), P("rows", "cols"), P("rows", None))

    def local(kernel, pattern, counts, delays):
        return on_device(
            mesh.shape["rows"], mesh.shape["cols"], kernel, pattern, counts, delays
        )

    return jax.shard_map(
        local,
        mesh=mesh,
        in_specs=placed,
        out_specs=(P("cols", None), P("cols", None), P()),
        check_vma=False,
    )
```

```python
import functools

import jax
import jax.numpy as jnp
from jax import lax
from jax.experimental import pallas as pl
from jax.experimental.pallas import tpu as pltpu
from jax.sharding import PartitionSpec as P

CB_DEV = 24
ITERS = 2
TILE = 128
PAIR = 2 * TILE
UNITS = 4
NORM_ROWS = 8
BEHIND = 1

tiny_eps = 1e-06

WHOLE = pl.BlockSpec(memory_space=pltpu.VMEM)
SCALARS = pl.BlockSpec(memory_space=pltpu.SMEM)


def low_lanes(shape):
    return lax.broadcasted_iota(jnp.int32, shape, 1) < shape[1] // 2


def turned(value):
    return pltpu.roll(value, value.shape[1] // 2, 1)


def rows_of(pair, size=TILE):
    return slice(pair * size, (pair + 1) * size)


def fill_kernel(
    place_ref, flip_ref, pattern_in, counts_in, delays_in, tiles_in,
    dense_ref, even_left_ref, odd_left_ref, pattern_ref, counts_ref, delays_ref, tiles_ref, arrived,
):
    flip = flip_ref[0]
    row_blocks = tiles_in.shape[0]
    small = [
        pltpu.make_async_copy(source, target, arrived.at[row_blocks + i])
        for i, (source, target) in enumerate(
            [(pattern_in, pattern_ref), (counts_in, counts_ref), (delays_in, delays_ref)]
        )
    ]
    for copy in small:
        copy.start()

    def fetch(position):
        return pltpu.make_async_copy(
            tiles_in.at[position ^ flip], tiles_ref.at[position], arrived.at[position]
        )

    for position in range(row_blocks):
        fetch(position).start()
    for copy in small:
        copy.wait()

    low = low_lanes((TILE, TILE))
    for pair in range(row_blocks // 2):
        source = (pair ^ (flip // 2)) * PAIR
        even = delays_ref[pl.ds(pl.multiple_of(source, TILE), TILE), :]
        odd = delays_ref[pl.ds(pl.multiple_of(source + TILE, TILE), TILE), :]
        even_left_ref[rows_of(pair), :] = jnp.where(low, even, turned(odd))
        odd_left_ref[rows_of(pair), :] = jnp.where(low, turned(even), odd)

    @pl.loop(0, row_blocks)
    def _(position):
        rows = pl.ds(pl.multiple_of(position * TILE, TILE), TILE)
        dense_ref[rows, :] = jnp.zeros((TILE, dense_ref.shape[1]), dense_ref.dtype)
        fetch(position).wait()
        block = position ^ flip

        @pl.loop(0, counts_ref[block])
        def _(tile):
            place = place_ref[pattern_ref[block, tile]]
            lanes = pl.ds(pl.multiple_of(place * TILE, TILE), TILE)
            dense_ref[rows, lanes] = tiles_ref[position, tile]


def fill_dense(kernel, pattern, counts, places, flip, delays):
    row_blocks = kernel.shape[0]
    rows = row_blocks * TILE
    left = jax.ShapeDtypeStruct((rows // 2, TILE), jnp.float32)
    return pl.pallas_call(
        fill_kernel,
        in_specs=[SCALARS] * 2 + [pl.BlockSpec(memory_space=pltpu.HBM)] * 4,
        out_specs=[WHOLE] * 3,
        out_shape=[jax.ShapeDtypeStruct((rows, CB_DEV * TILE), kernel.dtype), left, left],
        scratch_shapes=[
            pltpu.SMEM(pattern.shape, jnp.int32),
            pltpu.SMEM((row_blocks,), jnp.int32),
            pltpu.VMEM(delays.shape, delays.dtype),
            pltpu.VMEM(kernel.shape, kernel.dtype),
            pltpu.SemaphoreType.DMA((row_blocks + 3,)),
        ],
        compiler_params=pltpu.CompilerParams(vmem_limit_bytes=16 * 1024 * 1024),
        cost_estimate=pl.CostEstimate(
            flops=0, bytes_accessed=2 * kernel.size, transcendentals=0
        ),
    )(
        places,
        flip,
        *(pltpu.with_memory_space_constraint(x, pltpu.HBM) for x in (pattern, counts.reshape(-1), delays, kernel)),
    )


def norm_of(ref):
    return jnp.sqrt(ref[0:1, :] + tiny_eps)


def squares_row(sums):
    while len(sums) > 1:
        sums = [sums[i] + sums[i + 1] for i in range(0, len(sums), 2)]
    row = jnp.sum(sums[0], axis=0, keepdims=True)
    return row + turned(row)


def next_vector(parts, raw_ref, scale_ref, past_ref, past_scale_ref):
    if scale_ref is not None:
        scale = norm_of(scale_ref)
    if past_ref is not None:
        past_scale = norm_of(past_scale_ref)
    position = 0
    for part, units in parts:
        pairs = part.shape[0] // TILE // units
        for unit in range(units):
            squares = jnp.zeros((NORM_ROWS, TILE), jnp.float32)
            for pair in range(pairs):
                value = part[rows_of(unit * pairs + pair), :]
                if scale_ref is not None:
                    value = value / scale
                if past_ref is not None:
                    value = value - scale * (past_ref[rows_of(position), :] / past_scale)
                if raw_ref is not None:
                    raw_ref[rows_of(position), :] = value
                squares += jnp.sum((value * value).reshape(-1, NORM_ROWS, TILE), axis=0)
                yield position, value, squares if pair == pairs - 1 else None
                position += 1


def store_message(pair, value, send_ref, keep_ref):
    half = keep_ref.shape[0] // TILE
    if pair < half:
        send_ref[rows_of(pair), :] = value
    else:
        keep_ref[rows_of(pair - half), :] = value


def back_kernel(first, *refs):
    if first:
        dense_ref, own_ref, send_ref, keep_ref, turned_ref = refs
        parts, raw_ref, scales = [(own_ref, 2)], None, (None, None, None)
    else:
        (dense_ref, other_ref, own_ref, scale_ref, past_ref, past_scale_ref,
         send_ref, keep_ref, raw_ref, turned_ref) = refs
        parts, scales = [(other_ref, 1), (own_ref, 1)], (scale_ref, past_ref, past_scale_ref)
    sums = []
    half = turned_ref.shape[0]
    for pair, value, squares in next_vector(parts, raw_ref, *scales):
        flat = value.T.astype(turned_ref.dtype)
        turned_ref[:, rows_of(2 * pair)] = flat[:half]
        turned_ref[:, rows_of(2 * pair + 1)] = flat[half:]
        if squares is not None:
            sums.append(squares)
    send_ref[keep_ref.shape[0] :, :] = jnp.broadcast_to(squares_row(sums), (NORM_ROWS, TILE))
    for pair in range(dense_ref.shape[1] // PAIR):
        product = jnp.dot(
            turned_ref[...], dense_ref[:, rows_of(pair, PAIR)], preferred_element_type=jnp.float32
        )
        stacked = jnp.concatenate([product[:, :TILE], product[:, TILE:]], axis=0)
        store_message(pair, stacked.T, send_ref, keep_ref)


def fore_kernel(first, *refs):
    if first:
        (dense_ref, outer_ref, inner_ref, mine_ref, scale_ref,
         send_ref, keep_ref, raw_ref, wide_ref) = refs
        scales = (scale_ref, None, None)
    else:
        (dense_ref, outer_ref, inner_ref, mine_ref, scale_ref, past_ref, past_scale_ref,
         send_ref, keep_ref, raw_ref, wide_ref) = refs
        scales = (scale_ref, past_ref, past_scale_ref)
    parts = [(outer_ref, 2), (inner_ref, 1), (mine_ref, 1)]
    low = low_lanes((TILE, TILE))
    sums = []
    for pair, value, squares in next_vector(parts, raw_ref, *scales):
        other = turned(value)
        wide_ref[rows_of(2 * pair), :] = jnp.where(low, value, other).astype(wide_ref.dtype)
        wide_ref[rows_of(2 * pair + 1), :] = jnp.where(low, other, value).astype(wide_ref.dtype)
        if squares is not None:
            sums.append(squares)
    send_ref[keep_ref.shape[0] :, :] = jnp.broadcast_to(squares_row(sums), (NORM_ROWS, TILE))
    step = 4
    for start in range(0, dense_ref.shape[0] // TILE, step):
        product = jnp.dot(
            dense_ref[start * TILE : (start + step) * TILE, :],
            wide_ref[...],
            preferred_element_type=jnp.float32,
        )
        for pair in range(step // 2):
            even, odd = product[rows_of(2 * pair), :], product[rows_of(2 * pair + 1), :]
            store_message(start // 2 + pair, jnp.where(low, even, odd), send_ref, keep_ref)


def product_call(body, dense, operands, half, raw_rows, scratch):
    message = jax.ShapeDtypeStruct((half + NORM_ROWS, TILE), jnp.float32)
    kept = jax.ShapeDtypeStruct((half, TILE), jnp.float32)
    shapes = [message, kept]
    if raw_rows:
        shapes.append(jax.ShapeDtypeStruct((raw_rows, TILE), jnp.float32))
    return pl.pallas_call(
        body,
        in_specs=[WHOLE] * (1 + len(operands)),
        out_specs=[WHOLE] * len(shapes),
        out_shape=shapes,
        scratch_shapes=[scratch],
        compiler_params=pltpu.CompilerParams(vmem_limit_bytes=12 * 1024 * 1024),
        cost_estimate=pl.CostEstimate(
            flops=4 * TILE * dense.size, bytes_accessed=2 * dense.size, transcendentals=0
        ),
    )(dense, *operands)


def back_product(dense, operands, first):
    scratch = pltpu.VMEM((TILE // 2, dense.shape[0]), dense.dtype)
    raw_rows = 0 if first else dense.shape[0] // 2
    return product_call(
        functools.partial(back_kernel, first), dense, operands, dense.shape[1] // 4, raw_rows, scratch
    )


def fore_product(dense, operands, first):
    scratch = pltpu.VMEM((dense.shape[1], TILE), dense.dtype)
    return product_call(
        functools.partial(fore_kernel, first),
        dense, operands, dense.shape[0] // 4, dense.shape[1] // 2, scratch,
    )


def rotation(norms):
    betas, alphas = [norm_of(ref) for ref in norms[0::2]], [norm_of(ref) for ref in norms[1::2]]
    resid_bar, diag_bar = betas[0], alphas[0]
    steps = []
    for j in range(len(alphas)):
        radius = jnp.sqrt(diag_bar * diag_bar + betas[j + 1] * betas[j + 1])
        rotate_cos = diag_bar / radius
        rotate_sin = betas[j + 1] / radius
        step_size = rotate_cos * resid_bar
        resid_bar = rotate_sin * resid_bar
        coupling = None
        if j + 1 < len(alphas):
            coupling = rotate_sin * alphas[j + 1] / radius
            diag_bar = -rotate_cos * alphas[j + 1]
        steps.append((step_size / radius, coupling))
    misfit = resid_bar / betas[0]
    return alphas, betas, steps, misfit, misfit * rotate_cos


def store_in_order(out_ref, mask, pair, low, values):
    pairs = out_ref.shape[0] // PAIR // UNITS
    start = (((pair // pairs) ^ mask) * pairs + pair % pairs) * PAIR
    ours, theirs = values
    even = pl.ds(pl.multiple_of(start, TILE), TILE)
    odd = pl.ds(pl.multiple_of(start + TILE, TILE), TILE)
    out_ref[even, :] = jnp.where(low, ours, turned(theirs))
    out_ref[odd, :] = jnp.where(low, turned(ours), theirs)


def model_kernel(count, mask_ref, *refs):
    ins, (model_ref, misfit_ref) = refs[:-2], refs[-2:]
    chains = [ins[: len(ins) // 2], ins[len(ins) // 2 :]]
    low = low_lanes((TILE, TILE))
    rotations = [rotation(refs_[count:]) for refs_ in chains]
    misfits = [jnp.broadcast_to(r[3], misfit_ref.shape) for r in rotations]
    misfit_ref[...] = jnp.where(low_lanes(misfit_ref.shape), misfits[0], misfits[1])
    for pair in range(model_ref.shape[0] // PAIR):
        values = []
        for refs_, (alphas, _, steps, _, _) in zip(chains, rotations):
            search = total = None
            for j in range(count):
                right = refs_[j][rows_of(pair), :] / alphas[j]
                search = right if j == 0 else right - steps[j - 1][1] * search
                total = steps[j][0] * search if j == 0 else total + steps[j][0] * search
            values.append(total)
        store_in_order(model_ref, mask_ref[0], pair, low, values)


def gradient_kernel(mask_ref, *refs):
    ins, gradient_ref = refs[:-1], refs[-1]
    chains = [ins[: len(ins) // 2], ins[len(ins) // 2 :]]
    low = low_lanes((TILE, TILE))
    vectors = []
    factors = []
    for outer_ref, inner_ref, mine_ref, past_ref, *norms in chains:
        alphas, betas, _, _, factor = rotation(norms)
        parts = [(outer_ref, 2), (inner_ref, 1), (mine_ref, 1)]
        vectors.append(next_vector(parts, None, norms[-1], past_ref, norms[-2]))
        factors.append(factor)
    for ours, theirs in zip(*vectors):
        values = [factors[0] * ours[1], factors[1] * theirs[1]]
        store_in_order(gradient_ref, mask_ref[0], ours[0], low, values)


def last_call(body, mask, operands, shapes):
    return pl.pallas_call(
        body,
        in_specs=[SCALARS] + [WHOLE] * len(operands),
        out_specs=[WHOLE] * len(shapes),
        out_shape=[jax.ShapeDtypeStruct(shape, jnp.float32) for shape in shapes],
        compiler_params=pltpu.CompilerParams(vmem_limit_bytes=12 * 1024 * 1024),
        cost_estimate=pl.CostEstimate(
            flops=0, bytes_accessed=8 * shapes[0][0] * TILE, transcendentals=0
        ),
    )(mask, *operands)


def on_device(row_count, col_count, kernel, pattern, counts, delays):
    row_bits = list(range(row_count.bit_length() - 1))
    col_bits = list(range(col_count.bit_length() - 1))
    row_index = lax.axis_index("rows")
    core = lax.axis_index("cols") & 1

    orders = [row_bits, [row_bits[1], row_bits[0], *row_bits[2:]]]

    def swap_rows(value, level):
        pairs = []
        for row in range(row_count):
            for col in range(col_count):
                partner = row ^ (1 << orders[col & 1][level])
                pairs.append((row * col_count + col, partner * col_count + col))
        return lax.ppermute(value, ("rows", "cols"), pairs)

    def swap_cols(value, level):
        return lax.ppermute(value, "cols", [(i, i ^ (1 << level)) for i in range(col_count)])

    bits = [(row_index >> bit) & 1 for bit in row_bits[:2]]
    outer_side = jnp.where(core == 0, bits[0], bits[1])
    inner_side = jnp.where(core == 0, bits[1], bits[0])
    mask = ((1 - outer_side) * 2 + (1 - inner_side)).astype(jnp.int32)
    blocks = jnp.arange(CB_DEV, dtype=jnp.int32)
    unit = CB_DEV // UNITS
    places = ((blocks // unit) ^ mask) * unit + blocks % unit
    flip = ((1 - core) * (kernel.shape[0] // 2)).astype(jnp.int32).reshape(1)
    mask = mask.reshape(1)

    dense, *lefts = fill_dense(kernel, pattern, counts, places, flip, delays)

    def reduce_rows(send, keep):
        half = keep.shape[0]
        got = yield swap_rows, send, 0
        keep = keep + got[:half]
        norm = send[half:] + got[half:]
        send, mine = keep[: half // 2], keep[half // 2 :]
        for level in range(1, len(row_bits)):
            got = yield swap_rows, jnp.concatenate([send, norm]), level
            norm = norm + got[half // 2 :]
            send = mine = mine + got[: half // 2]
        inner = yield swap_rows, mine, 1
        outer = yield swap_rows, jnp.concatenate([inner, mine]), 0
        return [outer, inner, mine], norm

    def reduce_cols(send, keep):
        half = keep.shape[0]
        got = yield swap_cols, send, 0
        own = keep + got[:half]
        norm = send[half:] + got[half:]
        for bit in col_bits[1:]:
            got = yield swap_cols, jnp.concatenate([own, norm]), bit
            norm = norm + got[half:]
            own = own + got[:half]
        other = yield swap_cols, own, 0
        return [other, own], norm

    def chain(left):
        send, keep = back_product(dense, [left], True)
        totals, norm = yield from reduce_rows(send, keep)
        norms = [norm]
        rights = []
        for iteration in range(ITERS):
            past = [rights[-1], norms[-2]] if rights else []
            send, keep, right = fore_product(dense, [*totals, norms[-1], *past], not rights)
            rights.append(right)
            halves, norm = yield from reduce_cols(send, keep)
            norms.append(norm)
            send, keep, left = back_product(
                dense, [*halves, norms[-1], left, norms[-2]], False
            )
            totals, norm = yield from reduce_rows(send, keep)
            norms.append(norm)
        return rights, norms, totals

    def tied(value, other):
        return lax.optimization_barrier((value, other))[0]

    runs = [chain(left) for left in lefts]
    wanted = [next(run) for run in runs]
    chains = [None] * len(runs)
    gots = [None] * len(runs)
    swap, latest, level = wanted[0]
    gots[0] = swap(latest, level)
    turn = 0
    while None in chains:
        mine = 0 if turn < BEHIND else (turn - BEHIND) % 2
        turn += 1
        if chains[mine] is not None:
            continue
        if gots[mine] is None:
            swap, value, level = wanted[mine]
            latest = tied(value, latest)
        else:
            try:
                swap, latest, level = runs[mine].send(tied(gots[mine], latest))
            except StopIteration as stop:
                chains[mine] = stop.value
                continue
        gots[mine] = swap(latest, level)

    cells = dense.shape[1]
    model, misfit = last_call(
        functools.partial(model_kernel, ITERS),
        mask,
        [operand for rights, norms, _ in chains for operand in [*rights, *norms]],
        [(cells, TILE), (NORM_ROWS, TILE)],
    )
    (gradient,) = last_call(
        gradient_kernel,
        mask,
        [operand for rights, norms, totals in chains for operand in [*totals, rights[-1], *norms]],
        [(cells, TILE)],
    )
    return (model, gradient, misfit[0])


def solution(mesh):
    placed = (P("rows", "cols", None, None), P("rows", "cols"), P("rows", "cols"), P("rows", None))

    def local(kernel, pattern, counts, delays):
        return on_device(
            mesh.shape["rows"], mesh.shape["cols"], kernel, pattern, counts, delays
        )

    return jax.shard_map(
        local,
        mesh=mesh,
        in_specs=placed,
        out_specs=(P("cols", None), P("cols", None), P()),
        check_vma=False,
    )
```

```python
import functools

import jax
import jax.numpy as jnp
from jax import lax
from jax.experimental import pallas as pl
from jax.experimental.pallas import tpu as pltpu
from jax.sharding import PartitionSpec as P

CB_DEV = 24
ITERS = 2
TILE = 128
PAIR = 2 * TILE
UNITS = 4
NORM_ROWS = 8
ROW_TIMES = (7.5, 5.5, 10.5)
COL_TIMES = (3.0, 8.0)
FORE_TIME, BACK_TIME = 3.5, 2.5

tiny_eps = 1e-06

WHOLE = pl.BlockSpec(memory_space=pltpu.VMEM)
SCALARS = pl.BlockSpec(memory_space=pltpu.SMEM)


def low_lanes(shape):
    return lax.broadcasted_iota(jnp.int32, shape, 1) < shape[1] // 2


def turned(value):
    return pltpu.roll(value, value.shape[1] // 2, 1)


def rows_of(pair, size=TILE):
    return slice(pair * size, (pair + 1) * size)


def fill_kernel(
    place_ref, flip_ref, pattern_in, counts_in, delays_in, tiles_in,
    dense_ref, even_left_ref, odd_left_ref, pattern_ref, counts_ref, delays_ref, tiles_ref, arrived,
):
    flip = flip_ref[0]
    row_blocks = tiles_in.shape[0]
    small = [
        pltpu.make_async_copy(source, target, arrived.at[row_blocks + i])
        for i, (source, target) in enumerate(
            [(pattern_in, pattern_ref), (counts_in, counts_ref), (delays_in, delays_ref)]
        )
    ]
    for copy in small:
        copy.start()

    def fetch(position):
        return pltpu.make_async_copy(
            tiles_in.at[position ^ flip], tiles_ref.at[position], arrived.at[position]
        )

    for position in range(row_blocks):
        fetch(position).start()
    for copy in small:
        copy.wait()

    low = low_lanes((TILE, TILE))
    for pair in range(row_blocks // 2):
        source = (pair ^ (flip // 2)) * PAIR
        even = delays_ref[pl.ds(pl.multiple_of(source, TILE), TILE), :]
        odd = delays_ref[pl.ds(pl.multiple_of(source + TILE, TILE), TILE), :]
        even_left_ref[rows_of(pair), :] = jnp.where(low, even, turned(odd))
        odd_left_ref[rows_of(pair), :] = jnp.where(low, turned(even), odd)

    @pl.loop(0, row_blocks)
    def _(position):
        rows = pl.ds(pl.multiple_of(position * TILE, TILE), TILE)
        dense_ref[rows, :] = jnp.zeros((TILE, dense_ref.shape[1]), dense_ref.dtype)
        fetch(position).wait()
        block = position ^ flip

        @pl.loop(0, counts_ref[block])
        def _(tile):
            place = place_ref[pattern_ref[block, tile]]
            lanes = pl.ds(pl.multiple_of(place * TILE, TILE), TILE)
            dense_ref[rows, lanes] = tiles_ref[position, tile]


def fill_dense(kernel, pattern, counts, places, flip, delays):
    row_blocks = kernel.shape[0]
    rows = row_blocks * TILE
    left = jax.ShapeDtypeStruct((rows // 2, TILE), jnp.float32)
    return pl.pallas_call(
        fill_kernel,
        in_specs=[SCALARS] * 2 + [pl.BlockSpec(memory_space=pltpu.HBM)] * 4,
        out_specs=[WHOLE] * 3,
        out_shape=[jax.ShapeDtypeStruct((rows, CB_DEV * TILE), kernel.dtype), left, left],
        scratch_shapes=[
            pltpu.SMEM(pattern.shape, jnp.int32),
            pltpu.SMEM((row_blocks,), jnp.int32),
            pltpu.VMEM(delays.shape, delays.dtype),
            pltpu.VMEM(kernel.shape, kernel.dtype),
            pltpu.SemaphoreType.DMA((row_blocks + 3,)),
        ],
        compiler_params=pltpu.CompilerParams(vmem_limit_bytes=16 * 1024 * 1024),
        cost_estimate=pl.CostEstimate(
            flops=0, bytes_accessed=2 * kernel.size, transcendentals=0
        ),
    )(
        places,
        flip,
        *(pltpu.with_memory_space_constraint(x, pltpu.HBM) for x in (pattern, counts.reshape(-1), delays, kernel)),
    )


def norm_of(ref):
    return jnp.sqrt(ref[0:1, :] + tiny_eps)


def squares_row(sums):
    while len(sums) > 1:
        sums = [sums[i] + sums[i + 1] for i in range(0, len(sums), 2)]
    row = jnp.sum(sums[0], axis=0, keepdims=True)
    return row + turned(row)


def next_vector(parts, raw_ref, scale_ref, past_ref, past_scale_ref):
    if scale_ref is not None:
        scale = norm_of(scale_ref)
    if past_ref is not None:
        past_scale = norm_of(past_scale_ref)
    position = 0
    for part, units in parts:
        pairs = part.shape[0] // TILE // units
        for unit in range(units):
            squares = jnp.zeros((NORM_ROWS, TILE), jnp.float32)
            for pair in range(pairs):
                value = part[rows_of(unit * pairs + pair), :]
                if scale_ref is not None:
                    value = value / scale
                if past_ref is not None:
                    value = value - scale * (past_ref[rows_of(position), :] / past_scale)
                if raw_ref is not None:
                    raw_ref[rows_of(position), :] = value
                squares += jnp.sum((value * value).reshape(-1, NORM_ROWS, TILE), axis=0)
                yield position, value, squares if pair == pairs - 1 else None
                position += 1


def store_message(pair, value, send_ref, keep_ref):
    half = keep_ref.shape[0] // TILE
    if pair < half:
        send_ref[rows_of(pair), :] = value
    else:
        keep_ref[rows_of(pair - half), :] = value


def back_kernel(first, *refs):
    if first:
        dense_ref, own_ref, send_ref, keep_ref, turned_ref = refs
        parts, raw_ref, scales = [(own_ref, 2)], None, (None, None, None)
    else:
        (dense_ref, other_ref, own_ref, scale_ref, past_ref, past_scale_ref,
         send_ref, keep_ref, raw_ref, turned_ref) = refs
        parts, scales = [(other_ref, 1), (own_ref, 1)], (scale_ref, past_ref, past_scale_ref)
    sums = []
    half = turned_ref.shape[0]
    for pair, value, squares in next_vector(parts, raw_ref, *scales):
        flat = value.T.astype(turned_ref.dtype)
        turned_ref[:, rows_of(2 * pair)] = flat[:half]
        turned_ref[:, rows_of(2 * pair + 1)] = flat[half:]
        if squares is not None:
            sums.append(squares)
    send_ref[keep_ref.shape[0] :, :] = jnp.broadcast_to(squares_row(sums), (NORM_ROWS, TILE))
    for pair in range(dense_ref.shape[1] // PAIR):
        product = jnp.dot(
            turned_ref[...], dense_ref[:, rows_of(pair, PAIR)], preferred_element_type=jnp.float32
        )
        stacked = jnp.concatenate([product[:, :TILE], product[:, TILE:]], axis=0)
        store_message(pair, stacked.T, send_ref, keep_ref)


def fore_kernel(first, *refs):
    if first:
        (dense_ref, outer_ref, inner_ref, mine_ref, scale_ref,
         send_ref, keep_ref, raw_ref, wide_ref) = refs
        scales = (scale_ref, None, None)
    else:
        (dense_ref, outer_ref, inner_ref, mine_ref, scale_ref, past_ref, past_scale_ref,
         send_ref, keep_ref, raw_ref, wide_ref) = refs
        scales = (scale_ref, past_ref, past_scale_ref)
    parts = [(outer_ref, 2), (inner_ref, 1), (mine_ref, 1)]
    low = low_lanes((TILE, TILE))
    sums = []
    for pair, value, squares in next_vector(parts, raw_ref, *scales):
        other = turned(value)
        wide_ref[rows_of(2 * pair), :] = jnp.where(low, value, other).astype(wide_ref.dtype)
        wide_ref[rows_of(2 * pair + 1), :] = jnp.where(low, other, value).astype(wide_ref.dtype)
        if squares is not None:
            sums.append(squares)
    send_ref[keep_ref.shape[0] :, :] = jnp.broadcast_to(squares_row(sums), (NORM_ROWS, TILE))
    step = 4
    for start in range(0, dense_ref.shape[0] // TILE, step):
        product = jnp.dot(
            dense_ref[start * TILE : (start + step) * TILE, :],
            wide_ref[...],
            preferred_element_type=jnp.float32,
        )
        for pair in range(step // 2):
            even, odd = product[rows_of(2 * pair), :], product[rows_of(2 * pair + 1), :]
            store_message(start // 2 + pair, jnp.where(low, even, odd), send_ref, keep_ref)


def product_call(body, dense, operands, half, raw_rows, scratch):
    message = jax.ShapeDtypeStruct((half + NORM_ROWS, TILE), jnp.float32)
    kept = jax.ShapeDtypeStruct((half, TILE), jnp.float32)
    shapes = [message, kept]
    if raw_rows:
        shapes.append(jax.ShapeDtypeStruct((raw_rows, TILE), jnp.float32))
    return pl.pallas_call(
        body,
        in_specs=[WHOLE] * (1 + len(operands)),
        out_specs=[WHOLE] * len(shapes),
        out_shape=shapes,
        scratch_shapes=[scratch],
        compiler_params=pltpu.CompilerParams(vmem_limit_bytes=12 * 1024 * 1024),
        cost_estimate=pl.CostEstimate(
            flops=4 * TILE * dense.size, bytes_accessed=2 * dense.size, transcendentals=0
        ),
    )(dense, *operands)


def back_product(dense, operands, first):
    scratch = pltpu.VMEM((TILE // 2, dense.shape[0]), dense.dtype)
    raw_rows = 0 if first else dense.shape[0] // 2
    return product_call(
        functools.partial(back_kernel, first), dense, operands, dense.shape[1] // 4, raw_rows, scratch
    )


def fore_product(dense, operands, first):
    scratch = pltpu.VMEM((dense.shape[1], TILE), dense.dtype)
    return product_call(
        functools.partial(fore_kernel, first),
        dense, operands, dense.shape[0] // 4, dense.shape[1] // 2, scratch,
    )


def rotation(norms):
    betas, alphas = [norm_of(ref) for ref in norms[0::2]], [norm_of(ref) for ref in norms[1::2]]
    resid_bar, diag_bar = betas[0], alphas[0]
    steps = []
    for j in range(len(alphas)):
        radius = jnp.sqrt(diag_bar * diag_bar + betas[j + 1] * betas[j + 1])
        rotate_cos = diag_bar / radius
        rotate_sin = betas[j + 1] / radius
        step_size = rotate_cos * resid_bar
        resid_bar = rotate_sin * resid_bar
        coupling = None
        if j + 1 < len(alphas):
            coupling = rotate_sin * alphas[j + 1] / radius
            diag_bar = -rotate_cos * alphas[j + 1]
        steps.append((step_size / radius, coupling))
    misfit = resid_bar / betas[0]
    return alphas, betas, steps, misfit, misfit * rotate_cos


def store_in_order(out_ref, mask, pair, low, values):
    pairs = out_ref.shape[0] // PAIR // UNITS
    start = (((pair // pairs) ^ mask) * pairs + pair % pairs) * PAIR
    ours, theirs = values
    even = pl.ds(pl.multiple_of(start, TILE), TILE)
    odd = pl.ds(pl.multiple_of(start + TILE, TILE), TILE)
    out_ref[even, :] = jnp.where(low, ours, turned(theirs))
    out_ref[odd, :] = jnp.where(low, turned(ours), theirs)


def model_kernel(count, mask_ref, *refs):
    ins, (model_ref, misfit_ref) = refs[:-2], refs[-2:]
    chains = [ins[: len(ins) // 2], ins[len(ins) // 2 :]]
    low = low_lanes((TILE, TILE))
    rotations = [rotation(refs_[count:]) for refs_ in chains]
    misfits = [jnp.broadcast_to(r[3], misfit_ref.shape) for r in rotations]
    misfit_ref[...] = jnp.where(low_lanes(misfit_ref.shape), misfits[0], misfits[1])
    for pair in range(model_ref.shape[0] // PAIR):
        values = []
        for refs_, (alphas, _, steps, _, _) in zip(chains, rotations):
            search = total = None
            for j in range(count):
                right = refs_[j][rows_of(pair), :] / alphas[j]
                search = right if j == 0 else right - steps[j - 1][1] * search
                total = steps[j][0] * search if j == 0 else total + steps[j][0] * search
            values.append(total)
        store_in_order(model_ref, mask_ref[0], pair, low, values)


def gradient_kernel(mask_ref, *refs):
    ins, gradient_ref = refs[:-1], refs[-1]
    chains = [ins[: len(ins) // 2], ins[len(ins) // 2 :]]
    low = low_lanes((TILE, TILE))
    vectors = []
    factors = []
    for outer_ref, inner_ref, mine_ref, past_ref, *norms in chains:
        alphas, betas, _, _, factor = rotation(norms)
        parts = [(outer_ref, 2), (inner_ref, 1), (mine_ref, 1)]
        vectors.append(next_vector(parts, None, norms[-1], past_ref, norms[-2]))
        factors.append(factor)
    for ours, theirs in zip(*vectors):
        values = [factors[0] * ours[1], factors[1] * theirs[1]]
        store_in_order(gradient_ref, mask_ref[0], ours[0], low, values)


def last_call(body, mask, operands, shapes):
    return pl.pallas_call(
        body,
        in_specs=[SCALARS] + [WHOLE] * len(operands),
        out_specs=[WHOLE] * len(shapes),
        out_shape=[jax.ShapeDtypeStruct(shape, jnp.float32) for shape in shapes],
        compiler_params=pltpu.CompilerParams(vmem_limit_bytes=12 * 1024 * 1024),
        cost_estimate=pl.CostEstimate(
            flops=0, bytes_accessed=8 * shapes[0][0] * TILE, transcendentals=0
        ),
    )(mask, *operands)


def on_device(row_count, col_count, kernel, pattern, counts, delays):
    row_bits = list(range(row_count.bit_length() - 1))
    col_bits = list(range(col_count.bit_length() - 1))
    row_index = lax.axis_index("rows")
    core = lax.axis_index("cols") & 1

    orders = [row_bits, [row_bits[1], row_bits[0], *row_bits[2:]]]

    def swap_rows(value, level):
        pairs = []
        for row in range(row_count):
            for col in range(col_count):
                partner = row ^ (1 << orders[col & 1][level])
                pairs.append((row * col_count + col, partner * col_count + col))
        return lax.ppermute(value, ("rows", "cols"), pairs)

    def swap_cols(value, level):
        return lax.ppermute(value, "cols", [(i, i ^ (1 << level)) for i in range(col_count)])

    bits = [(row_index >> bit) & 1 for bit in row_bits[:2]]
    outer_side = jnp.where(core == 0, bits[0], bits[1])
    inner_side = jnp.where(core == 0, bits[1], bits[0])
    mask = ((1 - outer_side) * 2 + (1 - inner_side)).astype(jnp.int32)
    blocks = jnp.arange(CB_DEV, dtype=jnp.int32)
    unit = CB_DEV // UNITS
    places = ((blocks // unit) ^ mask) * unit + blocks % unit
    flip = ((1 - core) * (kernel.shape[0] // 2)).astype(jnp.int32).reshape(1)
    mask = mask.reshape(1)

    dense, *lefts = fill_dense(kernel, pattern, counts, places, flip, delays)

    def reduce_rows(send, keep):
        half = keep.shape[0]
        got = yield BACK_TIME + ROW_TIMES[0], swap_rows, send, 0
        keep = keep + got[:half]
        norm = send[half:] + got[half:]
        send, mine = keep[: half // 2], keep[half // 2 :]
        for level in range(1, len(row_bits)):
            message = jnp.concatenate([send, norm])
            got = yield ROW_TIMES[min(level, 2)], swap_rows, message, level
            norm = norm + got[half // 2 :]
            send = mine = mine + got[: half // 2]
        inner = yield ROW_TIMES[1], swap_rows, mine, 1
        outer = yield ROW_TIMES[0], swap_rows, jnp.concatenate([inner, mine]), 0
        return [outer, inner, mine], norm

    def reduce_cols(send, keep):
        half = keep.shape[0]
        got = yield FORE_TIME + COL_TIMES[0], swap_cols, send, 0
        own = keep + got[:half]
        norm = send[half:] + got[half:]
        for bit in col_bits[1:]:
            got = yield COL_TIMES[1], swap_cols, jnp.concatenate([own, norm]), bit
            norm = norm + got[half:]
            own = own + got[:half]
        other = yield COL_TIMES[0], swap_cols, own, 0
        return [other, own], norm

    def chain(left):
        send, keep = back_product(dense, [left], True)
        totals, norm = yield from reduce_rows(send, keep)
        norms = [norm]
        rights = []
        for iteration in range(ITERS):
            past = [rights[-1], norms[-2]] if rights else []
            send, keep, right = fore_product(dense, [*totals, norms[-1], *past], not rights)
            rights.append(right)
            halves, norm = yield from reduce_cols(send, keep)
            norms.append(norm)
            send, keep, left = back_product(
                dense, [*halves, norms[-1], left, norms[-2]], False
            )
            totals, norm = yield from reduce_rows(send, keep)
            norms.append(norm)
        return rights, norms, totals

    def tied(value, other):
        return lax.optimization_barrier((value, other))[0]

    runs = [chain(left) for left in lefts]
    wanted = [next(run) for run in runs]
    chains = [None] * len(runs)
    gots = [None] * len(runs)
    length, swap, latest, level = wanted[0]
    due = [length, length]
    gots[0] = swap(latest, level)
    while None in chains:
        mine = due.index(min(due))
        if gots[mine] is None:
            length, swap, value, level = wanted[mine]
            latest = tied(value, latest)
        else:
            try:
                length, swap, latest, level = runs[mine].send(tied(gots[mine], latest))
            except StopIteration as stop:
                chains[mine] = stop.value
                due[mine] = float("inf")
                continue
        gots[mine] = swap(latest, level)
        due[mine] += length

    cells = dense.shape[1]
    model, misfit = last_call(
        functools.partial(model_kernel, ITERS),
        mask,
        [operand for rights, norms, _ in chains for operand in [*rights, *norms]],
        [(cells, TILE), (NORM_ROWS, TILE)],
    )
    (gradient,) = last_call(
        gradient_kernel,
        mask,
        [operand for rights, norms, totals in chains for operand in [*totals, rights[-1], *norms]],
        [(cells, TILE)],
    )
    return (model, gradient, misfit[0])


def solution(mesh):
    placed = (P("rows", "cols", None, None), P("rows", "cols"), P("rows", "cols"), P("rows", None))

    def local(kernel, pattern, counts, delays):
        return on_device(
            mesh.shape["rows"], mesh.shape["cols"], kernel, pattern, counts, delays
        )

    return jax.shard_map(
        local,
        mesh=mesh,
        in_specs=placed,
        out_specs=(P("cols", None), P("cols", None), P()),
        check_vma=False,
    )
```

```python
import functools

import jax
import jax.numpy as jnp
from jax import lax
from jax.experimental import pallas as pl
from jax.experimental.pallas import tpu as pltpu
from jax.sharding import PartitionSpec as P

CB_DEV = 24
ITERS = 2
TILE = 128
PAIR = 2 * TILE
UNITS = 4
NORM_ROWS = 8
BEHIND = 0

tiny_eps = 1e-06

WHOLE = pl.BlockSpec(memory_space=pltpu.VMEM)
SCALARS = pl.BlockSpec(memory_space=pltpu.SMEM)


def low_lanes(shape):
    return lax.broadcasted_iota(jnp.int32, shape, 1) < shape[1] // 2


def turned(value):
    return pltpu.roll(value, value.shape[1] // 2, 1)


def rows_of(pair, size=TILE):
    return slice(pair * size, (pair + 1) * size)


def fill_kernel(
    place_ref, flip_ref, pattern_in, counts_in, delays_in, tiles_in,
    dense_ref, even_left_ref, odd_left_ref, pattern_ref, counts_ref, delays_ref, tiles_ref, arrived,
):
    flip = flip_ref[0]
    row_blocks = tiles_in.shape[0]
    small = [
        pltpu.make_async_copy(source, target, arrived.at[row_blocks + i])
        for i, (source, target) in enumerate(
            [(pattern_in, pattern_ref), (counts_in, counts_ref), (delays_in, delays_ref)]
        )
    ]
    for copy in small:
        copy.start()

    def fetch(position):
        return pltpu.make_async_copy(
            tiles_in.at[position ^ flip], tiles_ref.at[position], arrived.at[position]
        )

    for position in range(row_blocks):
        fetch(position).start()
    for copy in small:
        copy.wait()

    low = low_lanes((TILE, TILE))
    for pair in range(row_blocks // 2):
        source = (pair ^ (flip // 2)) * PAIR
        even = delays_ref[pl.ds(pl.multiple_of(source, TILE), TILE), :]
        odd = delays_ref[pl.ds(pl.multiple_of(source + TILE, TILE), TILE), :]
        even_left_ref[rows_of(pair), :] = jnp.where(low, even, turned(odd))
        odd_left_ref[rows_of(pair), :] = jnp.where(low, turned(even), odd)

    @pl.loop(0, row_blocks)
    def _(position):
        rows = pl.ds(pl.multiple_of(position * TILE, TILE), TILE)
        dense_ref[rows, :] = jnp.zeros((TILE, dense_ref.shape[1]), dense_ref.dtype)
        fetch(position).wait()
        block = position ^ flip

        @pl.loop(0, counts_ref[block])
        def _(tile):
            place = place_ref[pattern_ref[block, tile]]
            lanes = pl.ds(pl.multiple_of(place * TILE, TILE), TILE)
            dense_ref[rows, lanes] = tiles_ref[position, tile]


def fill_dense(kernel, pattern, counts, places, flip, delays):
    row_blocks = kernel.shape[0]
    rows = row_blocks * TILE
    left = jax.ShapeDtypeStruct((rows // 2, TILE), jnp.float32)
    return pl.pallas_call(
        fill_kernel,
        in_specs=[SCALARS] * 2 + [pl.BlockSpec(memory_space=pltpu.HBM)] * 4,
        out_specs=[WHOLE] * 3,
        out_shape=[jax.ShapeDtypeStruct((rows, CB_DEV * TILE), kernel.dtype), left, left],
        scratch_shapes=[
            pltpu.SMEM(pattern.shape, jnp.int32),
            pltpu.SMEM((row_blocks,), jnp.int32),
            pltpu.VMEM(delays.shape, delays.dtype),
            pltpu.VMEM(kernel.shape, kernel.dtype),
            pltpu.SemaphoreType.DMA((row_blocks + 3,)),
        ],
        compiler_params=pltpu.CompilerParams(vmem_limit_bytes=16 * 1024 * 1024),
        cost_estimate=pl.CostEstimate(
            flops=0, bytes_accessed=2 * kernel.size, transcendentals=0
        ),
    )(
        places,
        flip,
        *(pltpu.with_memory_space_constraint(x, pltpu.HBM) for x in (pattern, counts.reshape(-1), delays, kernel)),
    )


def norm_of(ref):
    return jnp.sqrt(ref[0:1, :] + tiny_eps)


def squares_row(sums):
    while len(sums) > 1:
        sums = [sums[i] + sums[i + 1] for i in range(0, len(sums), 2)]
    row = jnp.sum(sums[0], axis=0, keepdims=True)
    return row + turned(row)


def next_vector(parts, raw_ref, scale_ref, past_ref, past_scale_ref):
    if scale_ref is not None:
        scale = norm_of(scale_ref)
    if past_ref is not None:
        past_scale = norm_of(past_scale_ref)
    position = 0
    for part, units in parts:
        pairs = part.shape[0] // TILE // units
        for unit in range(units):
            squares = jnp.zeros((NORM_ROWS, TILE), jnp.float32)
            for pair in range(pairs):
                value = part[rows_of(unit * pairs + pair), :]
                if scale_ref is not None:
                    value = value / scale
                if past_ref is not None:
                    value = value - scale * (past_ref[rows_of(position), :] / past_scale)
                if raw_ref is not None:
                    raw_ref[rows_of(position), :] = value
                squares += jnp.sum((value * value).reshape(-1, NORM_ROWS, TILE), axis=0)
                yield position, value, squares if pair == pairs - 1 else None
                position += 1


def back_pairs(dense_ref, turned_ref, out_ref, start):
    for pair in range(out_ref.shape[0] // TILE):
        product = jnp.dot(
            turned_ref[...],
            dense_ref[:, rows_of(start + pair, PAIR)],
            preferred_element_type=jnp.float32,
        )
        stacked = jnp.concatenate([product[:, :TILE], product[:, TILE:]], axis=0)
        out_ref[rows_of(pair), :] = stacked.T


def back_send_kernel(first, *refs):
    if first:
        dense_ref, own_ref, send_ref, turned_ref = refs
        parts, raw_ref, scales = [(own_ref, 2)], None, (None, None, None)
    else:
        (dense_ref, other_ref, own_ref, scale_ref, past_ref, past_scale_ref,
         send_ref, turned_ref, raw_ref) = refs
        parts, scales = [(other_ref, 1), (own_ref, 1)], (scale_ref, past_ref, past_scale_ref)
    sums = []
    half = turned_ref.shape[0]
    for pair, value, squares in next_vector(parts, raw_ref, *scales):
        flat = value.T.astype(turned_ref.dtype)
        turned_ref[:, rows_of(2 * pair)] = flat[:half]
        turned_ref[:, rows_of(2 * pair + 1)] = flat[half:]
        if squares is not None:
            sums.append(squares)
    send_ref[-NORM_ROWS:, :] = jnp.broadcast_to(squares_row(sums), (NORM_ROWS, TILE))
    back_pairs(dense_ref, turned_ref, send_ref, 0)


def back_keep_kernel(dense_ref, turned_ref, keep_ref):
    back_pairs(dense_ref, turned_ref, keep_ref, keep_ref.shape[0] // TILE)


def fore_pairs(dense_ref, wide_ref, out_ref, start):
    low = low_lanes((TILE, TILE))
    step = 2
    for pair in range(0, out_ref.shape[0] // TILE, step):
        product = jnp.dot(
            dense_ref[(start + pair) * PAIR : (start + pair + step) * PAIR, :],
            wide_ref[...],
            preferred_element_type=jnp.float32,
        )
        for i in range(step):
            even, odd = product[rows_of(2 * i), :], product[rows_of(2 * i + 1), :]
            out_ref[rows_of(pair + i), :] = jnp.where(low, even, odd)


def fore_send_kernel(first, *refs):
    if first:
        (dense_ref, outer_ref, inner_ref, mine_ref, scale_ref, send_ref, wide_ref, raw_ref) = refs
        scales = (scale_ref, None, None)
    else:
        (dense_ref, outer_ref, inner_ref, mine_ref, scale_ref, past_ref, past_scale_ref,
         send_ref, wide_ref, raw_ref) = refs
        scales = (scale_ref, past_ref, past_scale_ref)
    parts = [(outer_ref, 2), (inner_ref, 1), (mine_ref, 1)]
    low = low_lanes((TILE, TILE))
    sums = []
    for pair, value, squares in next_vector(parts, raw_ref, *scales):
        other = turned(value)
        wide_ref[rows_of(2 * pair), :] = jnp.where(low, value, other).astype(wide_ref.dtype)
        wide_ref[rows_of(2 * pair + 1), :] = jnp.where(low, other, value).astype(wide_ref.dtype)
        if squares is not None:
            sums.append(squares)
    send_ref[-NORM_ROWS:, :] = jnp.broadcast_to(squares_row(sums), (NORM_ROWS, TILE))
    fore_pairs(dense_ref, wide_ref, send_ref, 0)


def fore_keep_kernel(dense_ref, wide_ref, keep_ref):
    fore_pairs(dense_ref, wide_ref, keep_ref, keep_ref.shape[0] // TILE)


def product_call(body, dense, operands, shapes):
    return pl.pallas_call(
        body,
        in_specs=[WHOLE] * (1 + len(operands)),
        out_specs=[WHOLE] * len(shapes),
        out_shape=shapes,
        compiler_params=pltpu.CompilerParams(vmem_limit_bytes=12 * 1024 * 1024),
        cost_estimate=pl.CostEstimate(
            flops=2 * TILE * dense.size, bytes_accessed=dense.size, transcendentals=0
        ),
    )(dense, *operands)


def float_rows(rows):
    return jax.ShapeDtypeStruct((rows, TILE), jnp.float32)


def back_product(dense, operands, first):
    rows, cells = dense.shape
    shapes = [float_rows(cells // 4 + NORM_ROWS), jax.ShapeDtypeStruct((TILE // 2, rows), dense.dtype)]
    shapes += [] if first else [float_rows(rows // 2)]
    send, flat, *raw = product_call(
        functools.partial(back_send_kernel, first), dense, operands, shapes
    )
    (keep,) = product_call(back_keep_kernel, dense, [flat], [float_rows(cells // 4)])
    return send, keep, *raw


def fore_product(dense, operands, first):
    rows, cells = dense.shape
    shapes = [
        float_rows(rows // 4 + NORM_ROWS),
        jax.ShapeDtypeStruct((cells, TILE), dense.dtype),
        float_rows(cells // 2),
    ]
    send, wide, raw = product_call(
        functools.partial(fore_send_kernel, first), dense, operands, shapes
    )
    (keep,) = product_call(fore_keep_kernel, dense, [wide], [float_rows(rows // 4)])
    return send, keep, raw


def rotation(norms):
    betas, alphas = [norm_of(ref) for ref in norms[0::2]], [norm_of(ref) for ref in norms[1::2]]
    resid_bar, diag_bar = betas[0], alphas[0]
    steps = []
    for j in range(len(alphas)):
        radius = jnp.sqrt(diag_bar * diag_bar + betas[j + 1] * betas[j + 1])
        rotate_cos = diag_bar / radius
        rotate_sin = betas[j + 1] / radius
        step_size = rotate_cos * resid_bar
        resid_bar = rotate_sin * resid_bar
        coupling = None
        if j + 1 < len(alphas):
            coupling = rotate_sin * alphas[j + 1] / radius
            diag_bar = -rotate_cos * alphas[j + 1]
        steps.append((step_size / radius, coupling))
    misfit = resid_bar / betas[0]
    return alphas, betas, steps, misfit, misfit * rotate_cos


def store_in_order(out_ref, mask, pair, low, values):
    pairs = out_ref.shape[0] // PAIR // UNITS
    start = (((pair // pairs) ^ mask) * pairs + pair % pairs) * PAIR
    ours, theirs = values
    even = pl.ds(pl.multiple_of(start, TILE), TILE)
    odd = pl.ds(pl.multiple_of(start + TILE, TILE), TILE)
    out_ref[even, :] = jnp.where(low, ours, turned(theirs))
    out_ref[odd, :] = jnp.where(low, turned(ours), theirs)


def model_kernel(count, mask_ref, *refs):
    ins, (model_ref, misfit_ref) = refs[:-2], refs[-2:]
    chains = [ins[: len(ins) // 2], ins[len(ins) // 2 :]]
    low = low_lanes((TILE, TILE))
    rotations = [rotation(refs_[count:]) for refs_ in chains]
    misfits = [jnp.broadcast_to(r[3], misfit_ref.shape) for r in rotations]
    misfit_ref[...] = jnp.where(low_lanes(misfit_ref.shape), misfits[0], misfits[1])
    for pair in range(model_ref.shape[0] // PAIR):
        values = []
        for refs_, (alphas, _, steps, _, _) in zip(chains, rotations):
            search = total = None
            for j in range(count):
                right = refs_[j][rows_of(pair), :] / alphas[j]
                search = right if j == 0 else right - steps[j - 1][1] * search
                total = steps[j][0] * search if j == 0 else total + steps[j][0] * search
            values.append(total)
        store_in_order(model_ref, mask_ref[0], pair, low, values)


def gradient_kernel(mask_ref, *refs):
    ins, gradient_ref = refs[:-1], refs[-1]
    chains = [ins[: len(ins) // 2], ins[len(ins) // 2 :]]
    low = low_lanes((TILE, TILE))
    vectors = []
    factors = []
    for outer_ref, inner_ref, mine_ref, past_ref, *norms in chains:
        alphas, betas, _, _, factor = rotation(norms)
        parts = [(outer_ref, 2), (inner_ref, 1), (mine_ref, 1)]
        vectors.append(next_vector(parts, None, norms[-1], past_ref, norms[-2]))
        factors.append(factor)
    for ours, theirs in zip(*vectors):
        values = [factors[0] * ours[1], factors[1] * theirs[1]]
        store_in_order(gradient_ref, mask_ref[0], ours[0], low, values)


def last_call(body, mask, operands, shapes):
    return pl.pallas_call(
        body,
        in_specs=[SCALARS] + [WHOLE] * len(operands),
        out_specs=[WHOLE] * len(shapes),
        out_shape=[jax.ShapeDtypeStruct(shape, jnp.float32) for shape in shapes],
        compiler_params=pltpu.CompilerParams(vmem_limit_bytes=12 * 1024 * 1024),
        cost_estimate=pl.CostEstimate(
            flops=0, bytes_accessed=8 * shapes[0][0] * TILE, transcendentals=0
        ),
    )(mask, *operands)


def on_device(row_count, col_count, kernel, pattern, counts, delays):
    row_bits = list(range(row_count.bit_length() - 1))
    col_bits = list(range(col_count.bit_length() - 1))
    row_index = lax.axis_index("rows")
    core = lax.axis_index("cols") & 1

    orders = [row_bits, [row_bits[1], row_bits[0], *row_bits[2:]]]

    def swap_rows(value, level):
        pairs = []
        for row in range(row_count):
            for col in range(col_count):
                partner = row ^ (1 << orders[col & 1][level])
                pairs.append((row * col_count + col, partner * col_count + col))
        return lax.ppermute(value, ("rows", "cols"), pairs)

    def swap_cols(value, level):
        return lax.ppermute(value, "cols", [(i, i ^ (1 << level)) for i in range(col_count)])

    bits = [(row_index >> bit) & 1 for bit in row_bits[:2]]
    outer_side = jnp.where(core == 0, bits[0], bits[1])
    inner_side = jnp.where(core == 0, bits[1], bits[0])
    mask = ((1 - outer_side) * 2 + (1 - inner_side)).astype(jnp.int32)
    blocks = jnp.arange(CB_DEV, dtype=jnp.int32)
    unit = CB_DEV // UNITS
    places = ((blocks // unit) ^ mask) * unit + blocks % unit
    flip = ((1 - core) * (kernel.shape[0] // 2)).astype(jnp.int32).reshape(1)
    mask = mask.reshape(1)

    dense, *lefts = fill_dense(kernel, pattern, counts, places, flip, delays)

    def reduce_rows(send, keep):
        half = keep.shape[0]
        got = yield swap_rows, send, 0
        keep = keep + got[:half]
        norm = send[half:] + got[half:]
        send, mine = keep[: half // 2], keep[half // 2 :]
        for level in range(1, len(row_bits)):
            got = yield swap_rows, jnp.concatenate([send, norm]), level
            norm = norm + got[half // 2 :]
            send = mine = mine + got[: half // 2]
        inner = yield swap_rows, mine, 1
        outer = yield swap_rows, jnp.concatenate([inner, mine]), 0
        return [outer, inner, mine], norm

    def reduce_cols(send, keep):
        half = keep.shape[0]
        got = yield swap_cols, send, 0
        own = keep + got[:half]
        norm = send[half:] + got[half:]
        for bit in col_bits[1:]:
            got = yield swap_cols, jnp.concatenate([own, norm]), bit
            norm = norm + got[half:]
            own = own + got[:half]
        other = yield swap_cols, own, 0
        return [other, own], norm

    def chain(left):
        send, keep = back_product(dense, [left], True)
        totals, norm = yield from reduce_rows(send, keep)
        norms = [norm]
        rights = []
        for iteration in range(ITERS):
            past = [rights[-1], norms[-2]] if rights else []
            send, keep, right = fore_product(dense, [*totals, norms[-1], *past], not rights)
            rights.append(right)
            halves, norm = yield from reduce_cols(send, keep)
            norms.append(norm)
            send, keep, left = back_product(
                dense, [*halves, norms[-1], left, norms[-2]], False
            )
            totals, norm = yield from reduce_rows(send, keep)
            norms.append(norm)
        return rights, norms, totals

    def tied(value, other):
        return lax.optimization_barrier((value, other))[0]

    runs = [chain(left) for left in lefts]
    wanted = [next(run) for run in runs]
    chains = [None] * len(runs)
    gots = [None] * len(runs)
    swap, latest, level = wanted[0]
    gots[0] = swap(latest, level)
    turn = 0
    while None in chains:
        mine = 0 if turn < BEHIND else (turn - BEHIND) % 2
        turn += 1
        if chains[mine] is not None:
            continue
        if gots[mine] is None:
            swap, value, level = wanted[mine]
            latest = tied(value, latest)
        else:
            try:
                swap, latest, level = runs[mine].send(tied(gots[mine], latest))
            except StopIteration as stop:
                chains[mine] = stop.value
                continue
        gots[mine] = swap(latest, level)

    cells = dense.shape[1]
    model, misfit = last_call(
        functools.partial(model_kernel, ITERS),
        mask,
        [operand for rights, norms, _ in chains for operand in [*rights, *norms]],
        [(cells, TILE), (NORM_ROWS, TILE)],
    )
    (gradient,) = last_call(
        gradient_kernel,
        mask,
        [operand for rights, norms, totals in chains for operand in [*totals, rights[-1], *norms]],
        [(cells, TILE)],
    )
    return (model, gradient, misfit[0])


def solution(mesh):
    placed = (P("rows", "cols", None, None), P("rows", "cols"), P("rows", "cols"), P("rows", None))

    def local(kernel, pattern, counts, delays):
        return on_device(
            mesh.shape["rows"], mesh.shape["cols"], kernel, pattern, counts, delays
        )

    return jax.shard_map(
        local,
        mesh=mesh,
        in_specs=placed,
        out_specs=(P("cols", None), P("cols", None), P()),
        check_vma=False,
    )
```

```python
import functools

import jax
import jax.numpy as jnp
from jax import lax
from jax.experimental import pallas as pl
from jax.experimental.pallas import tpu as pltpu
from jax.sharding import PartitionSpec as P

CB_DEV = 24
ITERS = 2
TILE = 128
PAIR = 2 * TILE
UNITS = 4
NORM_ROWS = 8
BEHIND = 0

tiny_eps = 1e-06

WHOLE = pl.BlockSpec(memory_space=pltpu.VMEM)
SCALARS = pl.BlockSpec(memory_space=pltpu.SMEM)


def low_lanes(shape):
    return lax.broadcasted_iota(jnp.int32, shape, 1) < shape[1] // 2


def turned(value):
    return pltpu.roll(value, value.shape[1] // 2, 1)


def rows_of(pair, size=TILE):
    return slice(pair * size, (pair + 1) * size)


def fill_kernel(
    place_ref, flip_ref, pattern_in, counts_in, delays_in, tiles_in,
    dense_ref, even_left_ref, odd_left_ref, pattern_ref, counts_ref, delays_ref, tiles_ref, arrived,
):
    flip = flip_ref[0]
    row_blocks = tiles_in.shape[0]
    small = [
        pltpu.make_async_copy(source, target, arrived.at[row_blocks + i])
        for i, (source, target) in enumerate(
            [(pattern_in, pattern_ref), (counts_in, counts_ref), (delays_in, delays_ref)]
        )
    ]
    for copy in small:
        copy.start()

    def fetch(position):
        return pltpu.make_async_copy(
            tiles_in.at[position ^ flip], tiles_ref.at[position], arrived.at[position]
        )

    for position in range(row_blocks):
        fetch(position).start()
    for copy in small:
        copy.wait()

    low = low_lanes((TILE, TILE))
    for pair in range(row_blocks // 2):
        source = (pair ^ (flip // 2)) * PAIR
        even = delays_ref[pl.ds(pl.multiple_of(source, TILE), TILE), :]
        odd = delays_ref[pl.ds(pl.multiple_of(source + TILE, TILE), TILE), :]
        even_left_ref[rows_of(pair), :] = jnp.where(low, even, turned(odd))
        odd_left_ref[rows_of(pair), :] = jnp.where(low, turned(even), odd)

    @pl.loop(0, row_blocks)
    def _(position):
        rows = pl.ds(pl.multiple_of(position * TILE, TILE), TILE)
        dense_ref[rows, :] = jnp.zeros((TILE, dense_ref.shape[1]), dense_ref.dtype)
        fetch(position).wait()
        block = position ^ flip

        @pl.loop(0, counts_ref[block])
        def _(tile):
            place = place_ref[pattern_ref[block, tile]]
            lanes = pl.ds(pl.multiple_of(place * TILE, TILE), TILE)
            dense_ref[rows, lanes] = tiles_ref[position, tile]


def fill_dense(kernel, pattern, counts, places, flip, delays):
    row_blocks = kernel.shape[0]
    rows = row_blocks * TILE
    left = jax.ShapeDtypeStruct((rows // 2, TILE), jnp.float32)
    return pl.pallas_call(
        fill_kernel,
        in_specs=[SCALARS] * 2 + [pl.BlockSpec(memory_space=pltpu.HBM)] * 4,
        out_specs=[WHOLE] * 3,
        out_shape=[jax.ShapeDtypeStruct((rows, CB_DEV * TILE), kernel.dtype), left, left],
        scratch_shapes=[
            pltpu.SMEM(pattern.shape, jnp.int32),
            pltpu.SMEM((row_blocks,), jnp.int32),
            pltpu.VMEM(delays.shape, delays.dtype),
            pltpu.VMEM(kernel.shape, kernel.dtype),
            pltpu.SemaphoreType.DMA((row_blocks + 3,)),
        ],
        compiler_params=pltpu.CompilerParams(vmem_limit_bytes=16 * 1024 * 1024),
        cost_estimate=pl.CostEstimate(
            flops=0, bytes_accessed=2 * kernel.size, transcendentals=0
        ),
    )(
        places,
        flip,
        *(pltpu.with_memory_space_constraint(x, pltpu.HBM) for x in (pattern, counts.reshape(-1), delays, kernel)),
    )


def norm_of(ref):
    return jnp.sqrt(ref[0:1, :] + tiny_eps)


def squares_row(sums):
    while len(sums) > 1:
        sums = [sums[i] + sums[i + 1] for i in range(0, len(sums), 2)]
    row = jnp.sum(sums[0], axis=0, keepdims=True)
    return row + turned(row)


def next_vector(parts, raw_ref, scale_ref, past_ref, past_scale_ref):
    if scale_ref is not None:
        scale = norm_of(scale_ref)
    if past_ref is not None:
        past_scale = norm_of(past_scale_ref)
    position = 0
    for part, units in parts:
        pairs = part.shape[0] // TILE // units
        for unit in range(units):
            squares = jnp.zeros((NORM_ROWS, TILE), jnp.float32)
            for pair in range(pairs):
                value = part[rows_of(unit * pairs + pair), :]
                if scale_ref is not None:
                    value = value / scale
                if past_ref is not None:
                    value = value - scale * (past_ref[rows_of(position), :] / past_scale)
                if raw_ref is not None:
                    raw_ref[rows_of(position), :] = value
                squares += jnp.sum((value * value).reshape(-1, NORM_ROWS, TILE), axis=0)
                yield position, value, squares if pair == pairs - 1 else None
                position += 1


def back_pairs(dense_ref, turned_ref, out_ref, start):
    for pair in range(out_ref.shape[0] // TILE):
        product = jnp.dot(
            turned_ref[...],
            dense_ref[:, rows_of(start + pair, PAIR)],
            preferred_element_type=jnp.float32,
        )
        stacked = jnp.concatenate([product[:, :TILE], product[:, TILE:]], axis=0)
        out_ref[rows_of(pair), :] = stacked.T


def back_send_kernel(first, *refs):
    if first:
        dense_ref, own_ref, send_ref, turned_ref = refs
        parts, raw_ref, scales = [(own_ref, 2)], None, (None, None, None)
    else:
        (dense_ref, other_ref, own_ref, scale_ref, past_ref, past_scale_ref,
         send_ref, turned_ref, raw_ref) = refs
        parts, scales = [(other_ref, 1), (own_ref, 1)], (scale_ref, past_ref, past_scale_ref)
    sums = []
    half = turned_ref.shape[0]
    for pair, value, squares in next_vector(parts, raw_ref, *scales):
        flat = value.T.astype(turned_ref.dtype)
        turned_ref[:, rows_of(2 * pair)] = flat[:half]
        turned_ref[:, rows_of(2 * pair + 1)] = flat[half:]
        if squares is not None:
            sums.append(squares)
    send_ref[-NORM_ROWS:, :] = jnp.broadcast_to(squares_row(sums), (NORM_ROWS, TILE))
    back_pairs(dense_ref, turned_ref, send_ref, 0)


def back_keep_kernel(dense_ref, turned_ref, keep_ref):
    back_pairs(dense_ref, turned_ref, keep_ref, keep_ref.shape[0] // TILE)


def fore_pairs(dense_ref, wide_ref, out_ref, start):
    low = low_lanes((TILE, TILE))
    step = 2
    for pair in range(0, out_ref.shape[0] // TILE, step):
        product = jnp.dot(
            dense_ref[(start + pair) * PAIR : (start + pair + step) * PAIR, :],
            wide_ref[...],
            preferred_element_type=jnp.float32,
        )
        for i in range(step):
            even, odd = product[rows_of(2 * i), :], product[rows_of(2 * i + 1), :]
            out_ref[rows_of(pair + i), :] = jnp.where(low, even, odd)


def pair_rows(unit_ref, pair, rows):
    pairs = rows // PAIR // UNITS
    start = (unit_ref[pair // pairs] * pairs + pair % pairs) * PAIR
    return [pl.ds(pl.multiple_of(start + half * TILE, TILE), TILE) for half in range(2)]


def fore_send_kernel(first, *refs):
    if first:
        (dense_ref, unit_ref, outer_ref, inner_ref, mine_ref, scale_ref,
         send_ref, wide_ref, raw_ref) = refs
        scales = (scale_ref, None, None)
    else:
        (dense_ref, unit_ref, outer_ref, inner_ref, mine_ref, scale_ref, past_ref, past_scale_ref,
         send_ref, wide_ref, raw_ref) = refs
        scales = (scale_ref, past_ref, past_scale_ref)
    parts = [(outer_ref, 2), (inner_ref, 1), (mine_ref, 1)]
    low = low_lanes((TILE, TILE))
    sums = []
    for pair, value, squares in next_vector(parts, raw_ref, *scales):
        other = turned(value)
        even, odd = pair_rows(unit_ref, pair, wide_ref.shape[0])
        wide_ref[even, :] = jnp.where(low, value, other).astype(wide_ref.dtype)
        wide_ref[odd, :] = jnp.where(low, other, value).astype(wide_ref.dtype)
        if squares is not None:
            sums.append(squares)
    send_ref[-NORM_ROWS:, :] = jnp.broadcast_to(squares_row(sums), (NORM_ROWS, TILE))
    fore_pairs(dense_ref, wide_ref, send_ref, 0)


def fore_keep_kernel(dense_ref, wide_ref, keep_ref):
    fore_pairs(dense_ref, wide_ref, keep_ref, keep_ref.shape[0] // TILE)


def product_call(body, dense, operands, shapes, units=None):
    scalars = [] if units is None else [units]
    return pl.pallas_call(
        body,
        in_specs=[WHOLE] + [SCALARS] * len(scalars) + [WHOLE] * len(operands),
        out_specs=[WHOLE] * len(shapes),
        out_shape=shapes,
        compiler_params=pltpu.CompilerParams(vmem_limit_bytes=12 * 1024 * 1024),
        cost_estimate=pl.CostEstimate(
            flops=2 * TILE * dense.size, bytes_accessed=dense.size, transcendentals=0
        ),
    )(dense, *scalars, *operands)


def float_rows(rows):
    return jax.ShapeDtypeStruct((rows, TILE), jnp.float32)


def back_product(dense, operands, first):
    rows, cells = dense.shape
    shapes = [float_rows(cells // 4 + NORM_ROWS), jax.ShapeDtypeStruct((TILE // 2, rows), dense.dtype)]
    shapes += [] if first else [float_rows(rows // 2)]
    send, flat, *raw = product_call(
        functools.partial(back_send_kernel, first), dense, operands, shapes
    )
    (keep,) = product_call(back_keep_kernel, dense, [flat], [float_rows(cells // 4)])
    return send, keep, *raw


def fore_product(dense, units, operands, first):
    rows, cells = dense.shape
    shapes = [
        float_rows(rows // 4 + NORM_ROWS),
        jax.ShapeDtypeStruct((cells, TILE), dense.dtype),
        float_rows(cells // 2),
    ]
    send, wide, raw = product_call(
        functools.partial(fore_send_kernel, first), dense, operands, shapes, units
    )
    (keep,) = product_call(fore_keep_kernel, dense, [wide], [float_rows(rows // 4)])
    return send, keep, raw


def rotation(norms):
    betas, alphas = [norm_of(ref) for ref in norms[0::2]], [norm_of(ref) for ref in norms[1::2]]
    resid_bar, diag_bar = betas[0], alphas[0]
    steps = []
    for j in range(len(alphas)):
        radius = jnp.sqrt(diag_bar * diag_bar + betas[j + 1] * betas[j + 1])
        rotate_cos = diag_bar / radius
        rotate_sin = betas[j + 1] / radius
        step_size = rotate_cos * resid_bar
        resid_bar = rotate_sin * resid_bar
        coupling = None
        if j + 1 < len(alphas):
            coupling = rotate_sin * alphas[j + 1] / radius
            diag_bar = -rotate_cos * alphas[j + 1]
        steps.append((step_size / radius, coupling))
    misfit = resid_bar / betas[0]
    return alphas, betas, steps, misfit, misfit * rotate_cos


def store_in_order(out_ref, unit_ref, pair, low, values):
    ours, theirs = values
    even, odd = pair_rows(unit_ref, pair, out_ref.shape[0])
    out_ref[even, :] = jnp.where(low, ours, turned(theirs))
    out_ref[odd, :] = jnp.where(low, turned(ours), theirs)


def model_kernel(count, unit_ref, *refs):
    ins, (model_ref, misfit_ref) = refs[:-2], refs[-2:]
    chains = [ins[: len(ins) // 2], ins[len(ins) // 2 :]]
    low = low_lanes((TILE, TILE))
    rotations = [rotation(refs_[count:]) for refs_ in chains]
    misfits = [jnp.broadcast_to(r[3], misfit_ref.shape) for r in rotations]
    misfit_ref[...] = jnp.where(low_lanes(misfit_ref.shape), misfits[0], misfits[1])
    for pair in range(model_ref.shape[0] // PAIR):
        values = []
        for refs_, (alphas, _, steps, _, _) in zip(chains, rotations):
            search = total = None
            for j in range(count):
                right = refs_[j][rows_of(pair), :] / alphas[j]
                search = right if j == 0 else right - steps[j - 1][1] * search
                total = steps[j][0] * search if j == 0 else total + steps[j][0] * search
            values.append(total)
        store_in_order(model_ref, unit_ref, pair, low, values)


def gradient_kernel(unit_ref, *refs):
    ins, gradient_ref = refs[:-1], refs[-1]
    chains = [ins[: len(ins) // 2], ins[len(ins) // 2 :]]
    low = low_lanes((TILE, TILE))
    vectors = []
    factors = []
    for outer_ref, inner_ref, mine_ref, past_ref, *norms in chains:
        alphas, betas, _, _, factor = rotation(norms)
        parts = [(outer_ref, 2), (inner_ref, 1), (mine_ref, 1)]
        vectors.append(next_vector(parts, None, norms[-1], past_ref, norms[-2]))
        factors.append(factor)
    for ours, theirs in zip(*vectors):
        values = [factors[0] * ours[1], factors[1] * theirs[1]]
        store_in_order(gradient_ref, unit_ref, ours[0], low, values)


def last_call(body, units, operands, shapes):
    return pl.pallas_call(
        body,
        in_specs=[SCALARS] + [WHOLE] * len(operands),
        out_specs=[WHOLE] * len(shapes),
        out_shape=[jax.ShapeDtypeStruct(shape, jnp.float32) for shape in shapes],
        compiler_params=pltpu.CompilerParams(vmem_limit_bytes=12 * 1024 * 1024),
        cost_estimate=pl.CostEstimate(
            flops=0, bytes_accessed=8 * shapes[0][0] * TILE, transcendentals=0
        ),
    )(units, *operands)


def on_device(row_count, col_count, kernel, pattern, counts, delays):
    row_bits = list(range(row_count.bit_length() - 1))
    col_bits = list(range(col_count.bit_length() - 1))
    row_index = lax.axis_index("rows")
    core = lax.axis_index("cols") & 1

    near, far, *rest = row_bits
    orders = [[near, far, *rest, far, near], [far, near, *rest, far, near]]
    steps = len(orders[0])

    def swap_rows(value, level):
        pairs = []
        for row in range(row_count):
            for col in range(col_count):
                partner = row ^ (1 << orders[col & 1][level])
                pairs.append((row * col_count + col, partner * col_count + col))
        return lax.ppermute(value, ("rows", "cols"), pairs)

    def swap_cols(value, level):
        return lax.ppermute(value, "cols", [(i, i ^ (1 << level)) for i in range(col_count)])

    bits = [(row_index >> bit) & 1 for bit in row_bits[:2]]
    outer_side = jnp.where(core == 0, bits[0], bits[1])
    inner_side = jnp.where(core == 0, bits[1], bits[0])
    mask = ((1 - outer_side) * 2 + (1 - inner_side)).astype(jnp.int32)
    blocks = jnp.arange(CB_DEV, dtype=jnp.int32)
    unit = CB_DEV // UNITS
    places = ((blocks // unit) ^ mask) * unit + blocks % unit
    flip = ((1 - core) * (kernel.shape[0] // 2)).astype(jnp.int32).reshape(1)
    units = jnp.where(core == 0, jnp.array([0, 1, 2, 3]), jnp.array([0, 2, 1, 3])).astype(jnp.int32)
    own_units = units ^ mask

    dense, *lefts = fill_dense(kernel, pattern, counts, places, flip, delays)

    def reduce_rows(send, keep):
        half = keep.shape[0]
        got = yield swap_rows, send, 0
        keep = keep + got[:half]
        norm = send[half:] + got[half:]
        send, mine = keep[: half // 2], keep[half // 2 :]
        for level in range(1, len(row_bits)):
            got = yield swap_rows, jnp.concatenate([send, norm]), level
            norm = norm + got[half // 2 :]
            send = mine = mine + got[: half // 2]
        inner = yield swap_rows, mine, steps - 2
        outer = yield swap_rows, jnp.concatenate([inner, mine]), steps - 1
        return [outer, inner, mine], norm

    def reduce_cols(send, keep):
        half = keep.shape[0]
        got = yield swap_cols, send, 0
        own = keep + got[:half]
        norm = send[half:] + got[half:]
        for bit in col_bits[1:]:
            got = yield swap_cols, jnp.concatenate([own, norm]), bit
            norm = norm + got[half:]
            own = own + got[:half]
        other = yield swap_cols, own, 0
        return [other, own], norm

    def chain(left):
        send, keep = back_product(dense, [left], True)
        totals, norm = yield from reduce_rows(send, keep)
        norms = [norm]
        rights = []
        for iteration in range(ITERS):
            past = [rights[-1], norms[-2]] if rights else []
            send, keep, right = fore_product(dense, units, [*totals, norms[-1], *past], not rights)
            rights.append(right)
            halves, norm = yield from reduce_cols(send, keep)
            norms.append(norm)
            send, keep, left = back_product(
                dense, [*halves, norms[-1], left, norms[-2]], False
            )
            totals, norm = yield from reduce_rows(send, keep)
            norms.append(norm)
        return rights, norms, totals

    def tied(value, other):
        return lax.optimization_barrier((value, other))[0]

    runs = [chain(left) for left in lefts]
    wanted = [next(run) for run in runs]
    chains = [None] * len(runs)
    gots = [None] * len(runs)
    swap, latest, level = wanted[0]
    gots[0] = swap(latest, level)
    turn = 0
    while None in chains:
        mine = 0 if turn < BEHIND else (turn - BEHIND) % 2
        turn += 1
        if chains[mine] is not None:
            continue
        if gots[mine] is None:
            swap, value, level = wanted[mine]
            latest = tied(value, latest)
        else:
            try:
                swap, latest, level = runs[mine].send(tied(gots[mine], latest))
            except StopIteration as stop:
                chains[mine] = stop.value
                continue
        gots[mine] = swap(latest, level)

    cells = dense.shape[1]
    model, misfit = last_call(
        functools.partial(model_kernel, ITERS),
        own_units,
        [operand for rights, norms, _ in chains for operand in [*rights, *norms]],
        [(cells, TILE), (NORM_ROWS, TILE)],
    )
    (gradient,) = last_call(
        gradient_kernel,
        own_units,
        [operand for rights, norms, totals in chains for operand in [*totals, rights[-1], *norms]],
        [(cells, TILE)],
    )
    return (model, gradient, misfit[0])


def solution(mesh):
    placed = (P("rows", "cols", None, None), P("rows", "cols"), P("rows", "cols"), P("rows", None))

    def local(kernel, pattern, counts, delays):
        return on_device(
            mesh.shape["rows"], mesh.shape["cols"], kernel, pattern, counts, delays
        )

    return jax.shard_map(
        local,
        mesh=mesh,
        in_specs=placed,
        out_specs=(P("cols", None), P("cols", None), P()),
        check_vma=False,
    )
```

```python
import functools

import jax
import jax.numpy as jnp
from jax import lax
from jax.experimental import pallas as pl
from jax.experimental.pallas import tpu as pltpu
from jax.sharding import PartitionSpec as P

CB_DEV = 24
ITERS = 2
TILE = 128
PAIR = 2 * TILE
UNITS = 4
NORM_ROWS = 8
BEHIND = 0

tiny_eps = 1e-06

WHOLE = pl.BlockSpec(memory_space=pltpu.VMEM)
SCALARS = pl.BlockSpec(memory_space=pltpu.SMEM)


def low_lanes(shape):
    return lax.broadcasted_iota(jnp.int32, shape, 1) < shape[1] // 2


def turned(value):
    return pltpu.roll(value, value.shape[1] // 2, 1)


def rows_of(pair, size=TILE):
    return slice(pair * size, (pair + 1) * size)


def fill_kernel(
    place_ref, flip_ref, pattern_in, counts_in, delays_in, tiles_in,
    dense_ref, even_left_ref, odd_left_ref, pattern_ref, counts_ref, delays_ref, tiles_ref, arrived,
):
    flip = flip_ref[0]
    row_blocks = tiles_in.shape[0]
    small = [
        pltpu.make_async_copy(source, target, arrived.at[row_blocks + i])
        for i, (source, target) in enumerate(
            [(pattern_in, pattern_ref), (counts_in, counts_ref), (delays_in, delays_ref)]
        )
    ]
    for copy in small:
        copy.start()

    def fetch(position):
        return pltpu.make_async_copy(
            tiles_in.at[position ^ flip], tiles_ref.at[position], arrived.at[position]
        )

    for position in range(row_blocks):
        fetch(position).start()
    for copy in small:
        copy.wait()

    low = low_lanes((TILE, TILE))
    for pair in range(row_blocks // 2):
        source = (pair ^ (flip // 2)) * PAIR
        even = delays_ref[pl.ds(pl.multiple_of(source, TILE), TILE), :]
        odd = delays_ref[pl.ds(pl.multiple_of(source + TILE, TILE), TILE), :]
        even_left_ref[rows_of(pair), :] = jnp.where(low, even, turned(odd))
        odd_left_ref[rows_of(pair), :] = jnp.where(low, turned(even), odd)

    @pl.loop(0, row_blocks)
    def _(position):
        rows = pl.ds(pl.multiple_of(position * TILE, TILE), TILE)
        dense_ref[rows, :] = jnp.zeros((TILE, dense_ref.shape[1]), dense_ref.dtype)
        fetch(position).wait()
        block = position ^ flip

        @pl.loop(0, counts_ref[block])
        def _(tile):
            place = place_ref[pattern_ref[block, tile]]
            lanes = pl.ds(pl.multiple_of(place * TILE, TILE), TILE)
            dense_ref[rows, lanes] = tiles_ref[position, tile]


def fill_dense(kernel, pattern, counts, places, flip, delays):
    row_blocks = kernel.shape[0]
    rows = row_blocks * TILE
    left = jax.ShapeDtypeStruct((rows // 2, TILE), jnp.float32)
    return pl.pallas_call(
        fill_kernel,
        in_specs=[SCALARS] * 2 + [pl.BlockSpec(memory_space=pltpu.HBM)] * 4,
        out_specs=[WHOLE] * 3,
        out_shape=[jax.ShapeDtypeStruct((rows, CB_DEV * TILE), kernel.dtype), left, left],
        scratch_shapes=[
            pltpu.SMEM(pattern.shape, jnp.int32),
            pltpu.SMEM((row_blocks,), jnp.int32),
            pltpu.VMEM(delays.shape, delays.dtype),
            pltpu.VMEM(kernel.shape, kernel.dtype),
            pltpu.SemaphoreType.DMA((row_blocks + 3,)),
        ],
        compiler_params=pltpu.CompilerParams(vmem_limit_bytes=16 * 1024 * 1024),
        cost_estimate=pl.CostEstimate(
            flops=0, bytes_accessed=2 * kernel.size, transcendentals=0
        ),
    )(
        places,
        flip,
        *(pltpu.with_memory_space_constraint(x, pltpu.HBM) for x in (pattern, counts.reshape(-1), delays, kernel)),
    )


def norm_of(ref):
    return jnp.sqrt(ref[0:1, :] + tiny_eps)


def squares_row(sums):
    while len(sums) > 1:
        sums = [sums[i] + sums[i + 1] for i in range(0, len(sums), 2)]
    row = jnp.sum(sums[0], axis=0, keepdims=True)
    return row + turned(row)


def next_vector(parts, raw_ref, scale_ref, past_ref, past_scale_ref):
    if scale_ref is not None:
        scale = norm_of(scale_ref)
    if past_ref is not None:
        past_scale = norm_of(past_scale_ref)
    position = 0
    for part, units in parts:
        pairs = part.shape[0] // TILE // units
        for unit in range(units):
            squares = jnp.zeros((NORM_ROWS, TILE), jnp.float32)
            for pair in range(pairs):
                value = part[rows_of(unit * pairs + pair), :]
                if scale_ref is not None:
                    value = value / scale
                if past_ref is not None:
                    value = value - scale * (past_ref[rows_of(position), :] / past_scale)
                if raw_ref is not None:
                    raw_ref[rows_of(position), :] = value
                squares += jnp.sum((value * value).reshape(-1, NORM_ROWS, TILE), axis=0)
                yield position, value, squares if pair == pairs - 1 else None
                position += 1


def back_pairs(dense_ref, turned_ref, out_ref, start):
    for pair in range(out_ref.shape[0] // TILE):
        product = jnp.dot(
            turned_ref[...],
            dense_ref[:, rows_of(start + pair, PAIR)],
            preferred_element_type=jnp.float32,
        )
        stacked = jnp.concatenate([product[:, :TILE], product[:, TILE:]], axis=0)
        out_ref[rows_of(pair), :] = stacked.T


def back_send_kernel(first, *refs):
    if first:
        dense_ref, own_ref, send_ref, turned_ref = refs
        parts, raw_ref, scales = [(own_ref, 2)], None, (None, None, None)
    else:
        (dense_ref, other_ref, own_ref, scale_ref, past_ref, past_scale_ref,
         send_ref, turned_ref, raw_ref) = refs
        parts, scales = [(other_ref, 1), (own_ref, 1)], (scale_ref, past_ref, past_scale_ref)
    sums = []
    half = turned_ref.shape[0]
    for pair, value, squares in next_vector(parts, raw_ref, *scales):
        flat = value.T.astype(turned_ref.dtype)
        turned_ref[:, rows_of(2 * pair)] = flat[:half]
        turned_ref[:, rows_of(2 * pair + 1)] = flat[half:]
        if squares is not None:
            sums.append(squares)
    send_ref[-NORM_ROWS:, :] = jnp.broadcast_to(squares_row(sums), (NORM_ROWS, TILE))
    back_pairs(dense_ref, turned_ref, send_ref, 0)


def back_keep_kernel(dense_ref, turned_ref, keep_ref):
    back_pairs(dense_ref, turned_ref, keep_ref, keep_ref.shape[0] // TILE)


def fore_pairs(dense_ref, wide_ref, out_ref, start):
    low = low_lanes((TILE, TILE))
    step = 2
    for pair in range(0, out_ref.shape[0] // TILE, step):
        product = jnp.dot(
            dense_ref[(start + pair) * PAIR : (start + pair + step) * PAIR, :],
            wide_ref[...],
            preferred_element_type=jnp.float32,
        )
        for i in range(step):
            even, odd = product[rows_of(2 * i), :], product[rows_of(2 * i + 1), :]
            out_ref[rows_of(pair + i), :] = jnp.where(low, even, odd)


def fore_send_kernel(first, *refs):
    if first:
        (dense_ref, outer_ref, inner_ref, mine_ref, scale_ref, send_ref, wide_ref, raw_ref) = refs
        scales = (scale_ref, None, None)
    else:
        (dense_ref, outer_ref, inner_ref, mine_ref, scale_ref, past_ref, past_scale_ref,
         send_ref, wide_ref, raw_ref) = refs
        scales = (scale_ref, past_ref, past_scale_ref)
    parts = [(outer_ref, 2), (inner_ref, 1), (mine_ref, 1)]
    low = low_lanes((TILE, TILE))
    sums = []
    for pair, value, squares in next_vector(parts, raw_ref, *scales):
        other = turned(value)
        wide_ref[rows_of(2 * pair), :] = jnp.where(low, value, other).astype(wide_ref.dtype)
        wide_ref[rows_of(2 * pair + 1), :] = jnp.where(low, other, value).astype(wide_ref.dtype)
        if squares is not None:
            sums.append(squares)
    send_ref[-NORM_ROWS:, :] = jnp.broadcast_to(squares_row(sums), (NORM_ROWS, TILE))
    fore_pairs(dense_ref, wide_ref, send_ref, 0)


def fore_keep_kernel(dense_ref, wide_ref, keep_ref):
    fore_pairs(dense_ref, wide_ref, keep_ref, keep_ref.shape[0] // TILE)


def product_call(body, dense, operands, shapes):
    return pl.pallas_call(
        body,
        in_specs=[WHOLE] * (1 + len(operands)),
        out_specs=[WHOLE] * len(shapes),
        out_shape=shapes,
        compiler_params=pltpu.CompilerParams(vmem_limit_bytes=12 * 1024 * 1024),
        cost_estimate=pl.CostEstimate(
            flops=2 * TILE * dense.size, bytes_accessed=dense.size, transcendentals=0
        ),
    )(dense, *operands)


def float_rows(rows):
    return jax.ShapeDtypeStruct((rows, TILE), jnp.float32)


def back_product(dense, operands, first):
    rows, cells = dense.shape
    shapes = [float_rows(cells // 4 + NORM_ROWS), jax.ShapeDtypeStruct((TILE // 2, rows), dense.dtype)]
    shapes += [] if first else [float_rows(rows // 2)]
    send, flat, *raw = product_call(
        functools.partial(back_send_kernel, first), dense, operands, shapes
    )


    def keep(flat):
        return product_call(back_keep_kernel, dense, [flat], [float_rows(cells // 4)])[0]

    return send, (keep, flat), *raw


def fore_product(dense, operands, first):
    rows, cells = dense.shape
    shapes = [
        float_rows(rows // 4 + NORM_ROWS),
        jax.ShapeDtypeStruct((cells, TILE), dense.dtype),
        float_rows(cells // 2),
    ]
    send, wide, raw = product_call(
        functools.partial(fore_send_kernel, first), dense, operands, shapes
    )


    def keep(wide):
        return product_call(fore_keep_kernel, dense, [wide], [float_rows(rows // 4)])[0]

    return send, (keep, wide), raw


def rotation(norms):
    betas, alphas = [norm_of(ref) for ref in norms[0::2]], [norm_of(ref) for ref in norms[1::2]]
    resid_bar, diag_bar = betas[0], alphas[0]
    steps = []
    for j in range(len(alphas)):
        radius = jnp.sqrt(diag_bar * diag_bar + betas[j + 1] * betas[j + 1])
        rotate_cos = diag_bar / radius
        rotate_sin = betas[j + 1] / radius
        step_size = rotate_cos * resid_bar
        resid_bar = rotate_sin * resid_bar
        coupling = None
        if j + 1 < len(alphas):
            coupling = rotate_sin * alphas[j + 1] / radius
            diag_bar = -rotate_cos * alphas[j + 1]
        steps.append((step_size / radius, coupling))
    misfit = resid_bar / betas[0]
    return alphas, betas, steps, misfit, misfit * rotate_cos


def store_in_order(out_ref, mask, pair, low, values):
    pairs = out_ref.shape[0] // PAIR // UNITS
    start = (((pair // pairs) ^ mask) * pairs + pair % pairs) * PAIR
    ours, theirs = values
    even = pl.ds(pl.multiple_of(start, TILE), TILE)
    odd = pl.ds(pl.multiple_of(start + TILE, TILE), TILE)
    out_ref[even, :] = jnp.where(low, ours, turned(theirs))
    out_ref[odd, :] = jnp.where(low, turned(ours), theirs)


def model_kernel(count, mask_ref, *refs):
    ins, (model_ref, misfit_ref) = refs[:-2], refs[-2:]
    chains = [ins[: len(ins) // 2], ins[len(ins) // 2 :]]
    low = low_lanes((TILE, TILE))
    rotations = [rotation(refs_[count:]) for refs_ in chains]
    misfits = [jnp.broadcast_to(r[3], misfit_ref.shape) for r in rotations]
    misfit_ref[...] = jnp.where(low_lanes(misfit_ref.shape), misfits[0], misfits[1])
    for pair in range(model_ref.shape[0] // PAIR):
        values = []
        for refs_, (alphas, _, steps, _, _) in zip(chains, rotations):
            search = total = None
            for j in range(count):
                right = refs_[j][rows_of(pair), :] / alphas[j]
                search = right if j == 0 else right - steps[j - 1][1] * search
                total = steps[j][0] * search if j == 0 else total + steps[j][0] * search
            values.append(total)
        store_in_order(model_ref, mask_ref[0], pair, low, values)


def gradient_kernel(mask_ref, *refs):
    ins, gradient_ref = refs[:-1], refs[-1]
    chains = [ins[: len(ins) // 2], ins[len(ins) // 2 :]]
    low = low_lanes((TILE, TILE))
    vectors = []
    factors = []
    for outer_ref, inner_ref, mine_ref, past_ref, *norms in chains:
        alphas, betas, _, _, factor = rotation(norms)
        parts = [(outer_ref, 2), (inner_ref, 1), (mine_ref, 1)]
        vectors.append(next_vector(parts, None, norms[-1], past_ref, norms[-2]))
        factors.append(factor)
    for ours, theirs in zip(*vectors):
        values = [factors[0] * ours[1], factors[1] * theirs[1]]
        store_in_order(gradient_ref, mask_ref[0], ours[0], low, values)


def last_call(body, mask, operands, shapes):
    return pl.pallas_call(
        body,
        in_specs=[SCALARS] + [WHOLE] * len(operands),
        out_specs=[WHOLE] * len(shapes),
        out_shape=[jax.ShapeDtypeStruct(shape, jnp.float32) for shape in shapes],
        compiler_params=pltpu.CompilerParams(vmem_limit_bytes=12 * 1024 * 1024),
        cost_estimate=pl.CostEstimate(
            flops=0, bytes_accessed=8 * shapes[0][0] * TILE, transcendentals=0
        ),
    )(mask, *operands)


def on_device(row_count, col_count, kernel, pattern, counts, delays):
    row_bits = list(range(row_count.bit_length() - 1))
    col_bits = list(range(col_count.bit_length() - 1))
    row_index = lax.axis_index("rows")
    core = lax.axis_index("cols") & 1

    orders = [row_bits, [row_bits[1], row_bits[0], *row_bits[2:]]]

    def swap_rows(value, level):
        pairs = []
        for row in range(row_count):
            for col in range(col_count):
                partner = row ^ (1 << orders[col & 1][level])
                pairs.append((row * col_count + col, partner * col_count + col))
        return lax.ppermute(value, ("rows", "cols"), pairs)

    def swap_cols(value, level):
        return lax.ppermute(value, "cols", [(i, i ^ (1 << level)) for i in range(col_count)])

    bits = [(row_index >> bit) & 1 for bit in row_bits[:2]]
    outer_side = jnp.where(core == 0, bits[0], bits[1])
    inner_side = jnp.where(core == 0, bits[1], bits[0])
    mask = ((1 - outer_side) * 2 + (1 - inner_side)).astype(jnp.int32)
    blocks = jnp.arange(CB_DEV, dtype=jnp.int32)
    unit = CB_DEV // UNITS
    places = ((blocks // unit) ^ mask) * unit + blocks % unit
    flip = ((1 - core) * (kernel.shape[0] // 2)).astype(jnp.int32).reshape(1)
    mask = mask.reshape(1)

    dense, *lefts = fill_dense(kernel, pattern, counts, places, flip, delays)

    def tied(value, other):
        return lax.optimization_barrier((value, other))[0]

    def kept_half(kept, ahead):
        half, operand = kept
        return half(tied(operand, ahead))

    def reduce_rows(send, kept):
        half = send.shape[0] - NORM_ROWS
        got, ahead = yield swap_rows, send, 0
        keep = kept_half(kept, ahead) + got[:half]
        norm = send[half:] + got[half:]
        send, mine = keep[: half // 2], keep[half // 2 :]
        for level in range(1, len(row_bits)):
            got, _ = yield swap_rows, jnp.concatenate([send, norm]), level
            norm = norm + got[half // 2 :]
            send = mine = mine + got[: half // 2]
        inner, _ = yield swap_rows, mine, 1
        outer, _ = yield swap_rows, jnp.concatenate([inner, mine]), 0
        return [outer, inner, mine], norm

    def reduce_cols(send, kept):
        half = send.shape[0] - NORM_ROWS
        got, ahead = yield swap_cols, send, 0
        own = kept_half(kept, ahead) + got[:half]
        norm = send[half:] + got[half:]
        for bit in col_bits[1:]:
            got, _ = yield swap_cols, jnp.concatenate([own, norm]), bit
            norm = norm + got[half:]
            own = own + got[:half]
        other, _ = yield swap_cols, own, 0
        return [other, own], norm

    def chain(left):
        send, keep = back_product(dense, [left], True)
        totals, norm = yield from reduce_rows(send, keep)
        norms = [norm]
        rights = []
        for iteration in range(ITERS):
            past = [rights[-1], norms[-2]] if rights else []
            send, keep, right = fore_product(dense, [*totals, norms[-1], *past], not rights)
            rights.append(right)
            halves, norm = yield from reduce_cols(send, keep)
            norms.append(norm)
            send, keep, left = back_product(
                dense, [*halves, norms[-1], left, norms[-2]], False
            )
            totals, norm = yield from reduce_rows(send, keep)
            norms.append(norm)
        return rights, norms, totals

    runs = [chain(left) for left in lefts]
    wanted = [next(run) for run in runs]
    chains = [None] * len(runs)
    gots = [None] * len(runs)
    swap, value, level = wanted[0]
    gots[0] = swap(value, level)
    latest = wanted[1][1]
    turn = 0
    while None in chains:
        mine = 0 if turn < BEHIND else (turn - BEHIND) % 2
        turn += 1
        if chains[mine] is not None:
            continue
        if gots[mine] is None:
            swap, value, level = wanted[mine]
            latest = tied(value, latest)
        else:
            try:
                swap, latest, level = runs[mine].send((tied(gots[mine], latest), latest))
            except StopIteration as stop:
                chains[mine] = stop.value
                continue
        gots[mine] = swap(latest, level)

    cells = dense.shape[1]
    model, misfit = last_call(
        functools.partial(model_kernel, ITERS),
        mask,
        [operand for rights, norms, _ in chains for operand in [*rights, *norms]],
        [(cells, TILE), (NORM_ROWS, TILE)],
    )
    (gradient,) = last_call(
        gradient_kernel,
        mask,
        [operand for rights, norms, totals in chains for operand in [*totals, rights[-1], *norms]],
        [(cells, TILE)],
    )
    return (model, gradient, misfit[0])


def solution(mesh):
    placed = (P("rows", "cols", None, None), P("rows", "cols"), P("rows", "cols"), P("rows", None))

    def local(kernel, pattern, counts, delays):
        return on_device(
            mesh.shape["rows"], mesh.shape["cols"], kernel, pattern, counts, delays
        )

    return jax.shard_map(
        local,
        mesh=mesh,
        in_specs=placed,
        out_specs=(P("cols", None), P("cols", None), P()),
        check_vma=False,
    )
```

```python
import functools

import jax
import jax.numpy as jnp
from jax import lax
from jax.experimental import pallas as pl
from jax.experimental.pallas import tpu as pltpu
from jax.sharding import PartitionSpec as P

CB_DEV = 24
ITERS = 2
TILE = 128
PAIR = 2 * TILE
UNITS = 4
NORM_ROWS = 8
BEHIND = 0

tiny_eps = 1e-06

WHOLE = pl.BlockSpec(memory_space=pltpu.VMEM)
SCALARS = pl.BlockSpec(memory_space=pltpu.SMEM)


def low_lanes(shape):
    return lax.broadcasted_iota(jnp.int32, shape, 1) < shape[1] // 2


def turned(value):
    return pltpu.roll(value, value.shape[1] // 2, 1)


def rows_of(pair, size=TILE):
    return slice(pair * size, (pair + 1) * size)


def fill_kernel(
    place_ref, flip_ref, pattern_in, counts_in, delays_in, tiles_in,
    dense_ref, even_left_ref, odd_left_ref, pattern_ref, counts_ref, delays_ref, tiles_ref, arrived,
):
    flip = flip_ref[0]
    row_blocks = tiles_in.shape[0]
    small = [
        pltpu.make_async_copy(source, target, arrived.at[row_blocks + i])
        for i, (source, target) in enumerate(
            [(pattern_in, pattern_ref), (counts_in, counts_ref), (delays_in, delays_ref)]
        )
    ]
    for copy in small:
        copy.start()

    def fetch(position):
        return pltpu.make_async_copy(
            tiles_in.at[position ^ flip], tiles_ref.at[position], arrived.at[position]
        )

    for position in range(row_blocks):
        fetch(position).start()
    for copy in small:
        copy.wait()

    low = low_lanes((TILE, TILE))
    for pair in range(row_blocks // 2):
        source = (pair ^ (flip // 2)) * PAIR
        even = delays_ref[pl.ds(pl.multiple_of(source, TILE), TILE), :]
        odd = delays_ref[pl.ds(pl.multiple_of(source + TILE, TILE), TILE), :]
        even_left_ref[rows_of(pair), :] = jnp.where(low, even, turned(odd))
        odd_left_ref[rows_of(pair), :] = jnp.where(low, turned(even), odd)

    @pl.loop(0, row_blocks)
    def _(position):
        rows = pl.ds(pl.multiple_of(position * TILE, TILE), TILE)
        dense_ref[rows, :] = jnp.zeros((TILE, dense_ref.shape[1]), dense_ref.dtype)
        fetch(position).wait()
        block = position ^ flip

        @pl.loop(0, counts_ref[block])
        def _(tile):
            place = place_ref[pattern_ref[block, tile]]
            lanes = pl.ds(pl.multiple_of(place * TILE, TILE), TILE)
            dense_ref[rows, lanes] = tiles_ref[position, tile]


def fill_dense(kernel, pattern, counts, places, flip, delays):
    row_blocks = kernel.shape[0]
    rows = row_blocks * TILE
    left = jax.ShapeDtypeStruct((rows // 2, TILE), jnp.float32)
    return pl.pallas_call(
        fill_kernel,
        in_specs=[SCALARS] * 2 + [pl.BlockSpec(memory_space=pltpu.HBM)] * 4,
        out_specs=[WHOLE] * 3,
        out_shape=[jax.ShapeDtypeStruct((rows, CB_DEV * TILE), kernel.dtype), left, left],
        scratch_shapes=[
            pltpu.SMEM(pattern.shape, jnp.int32),
            pltpu.SMEM((row_blocks,), jnp.int32),
            pltpu.VMEM(delays.shape, delays.dtype),
            pltpu.VMEM(kernel.shape, kernel.dtype),
            pltpu.SemaphoreType.DMA((row_blocks + 3,)),
        ],
        compiler_params=pltpu.CompilerParams(vmem_limit_bytes=16 * 1024 * 1024),
        cost_estimate=pl.CostEstimate(
            flops=0, bytes_accessed=2 * kernel.size, transcendentals=0
        ),
    )(
        places,
        flip,
        *(pltpu.with_memory_space_constraint(x, pltpu.HBM) for x in (pattern, counts.reshape(-1), delays, kernel)),
    )


def norm_of(ref):
    return jnp.sqrt(ref[0:1, :] + tiny_eps)


def squares_row(sums):
    while len(sums) > 1:
        sums = [sums[i] + sums[i + 1] for i in range(0, len(sums), 2)]
    row = jnp.sum(sums[0], axis=0, keepdims=True)
    return row + turned(row)


def next_vector(units, pairs, raw_ref, scale_ref, past_ref, past_scale_ref, other=False):
    if scale_ref is not None:
        scale = norm_of(scale_ref)
    if past_ref is not None:
        past_scale = norm_of(past_scale_ref)
    position = 0
    for places in units:
        squares = jnp.zeros((NORM_ROWS, TILE), jnp.float32)
        for pair in range(pairs):
            value, *others = [ref[rows_of(start + pair), :] for ref, start in places]
            if others:
                value = jnp.where(other, others[0], value)
            if scale_ref is not None:
                value = value / scale
            if past_ref is not None:
                value = value - scale * (past_ref[rows_of(position), :] / past_scale)
            if raw_ref is not None:
                raw_ref[rows_of(position), :] = value
            squares += jnp.sum((value * value).reshape(-1, NORM_ROWS, TILE), axis=0)
            yield position, value, squares if pair == pairs - 1 else None
            position += 1


def gathered_units(outer_ref, inner_ref, mine_ref, crossed):
    pairs = mine_ref.shape[0] // TILE
    second, third = (outer_ref, pairs), (inner_ref, 0)
    if crossed:
        middle = [(second, third), (third, second)]
    else:
        middle = [(second,), (third,)]
    return [((outer_ref, 0),), *middle, ((mine_ref, 0),)], pairs


def back_pairs(dense_ref, turned_ref, out_ref, start):
    for pair in range(out_ref.shape[0] // TILE):
        product = jnp.dot(
            turned_ref[...],
            dense_ref[:, rows_of(start + pair, PAIR)],
            preferred_element_type=jnp.float32,
        )
        stacked = jnp.concatenate([product[:, :TILE], product[:, TILE:]], axis=0)
        out_ref[rows_of(pair), :] = stacked.T


def back_send_kernel(first, *refs):
    if first:
        dense_ref, own_ref, send_ref, turned_ref = refs
        pairs = own_ref.shape[0] // PAIR
        units, raw_ref, scales = [((own_ref, 0),), ((own_ref, pairs),)], None, (None, None, None)
    else:
        (dense_ref, other_ref, own_ref, scale_ref, past_ref, past_scale_ref,
         send_ref, turned_ref, raw_ref) = refs
        pairs = own_ref.shape[0] // TILE
        units, scales = [((other_ref, 0),), ((own_ref, 0),)], (scale_ref, past_ref, past_scale_ref)
    sums = []
    half = turned_ref.shape[0]
    for pair, value, squares in next_vector(units, pairs, raw_ref, *scales):
        flat = value.T.astype(turned_ref.dtype)
        turned_ref[:, rows_of(2 * pair)] = flat[:half]
        turned_ref[:, rows_of(2 * pair + 1)] = flat[half:]
        if squares is not None:
            sums.append(squares)
    send_ref[-NORM_ROWS:, :] = jnp.broadcast_to(squares_row(sums), (NORM_ROWS, TILE))
    back_pairs(dense_ref, turned_ref, send_ref, 0)


def back_keep_kernel(dense_ref, turned_ref, keep_ref):
    back_pairs(dense_ref, turned_ref, keep_ref, keep_ref.shape[0] // TILE)


def fore_pairs(dense_ref, wide_ref, out_ref, start):
    low = low_lanes((TILE, TILE))
    step = 2
    for pair in range(0, out_ref.shape[0] // TILE, step):
        product = jnp.dot(
            dense_ref[(start + pair) * PAIR : (start + pair + step) * PAIR, :],
            wide_ref[...],
            preferred_element_type=jnp.float32,
        )
        for i in range(step):
            even, odd = product[rows_of(2 * i), :], product[rows_of(2 * i + 1), :]
            out_ref[rows_of(pair + i), :] = jnp.where(low, even, odd)


def fore_send_kernel(first, crossed, *refs):
    core_ref, dense_ref, outer_ref, inner_ref, mine_ref, scale_ref, *refs = refs
    past_ref, past_scale_ref = (None, None) if first else refs[:2]
    send_ref, wide_ref, raw_ref = refs[-3:]
    scales = (scale_ref, past_ref, past_scale_ref)
    units, pairs = gathered_units(outer_ref, inner_ref, mine_ref, crossed)
    low = low_lanes((TILE, TILE))
    sums = []
    vector = next_vector(units, pairs, raw_ref, *scales, other=core_ref[0] != 0)
    for pair, value, squares in vector:
        other = turned(value)
        wide_ref[rows_of(2 * pair), :] = jnp.where(low, value, other).astype(wide_ref.dtype)
        wide_ref[rows_of(2 * pair + 1), :] = jnp.where(low, other, value).astype(wide_ref.dtype)
        if squares is not None:
            sums.append(squares)
    send_ref[-NORM_ROWS:, :] = jnp.broadcast_to(squares_row(sums), (NORM_ROWS, TILE))
    fore_pairs(dense_ref, wide_ref, send_ref, 0)


def fore_keep_kernel(dense_ref, wide_ref, keep_ref):
    fore_pairs(dense_ref, wide_ref, keep_ref, keep_ref.shape[0] // TILE)


def product_call(body, dense, operands, shapes, scalars=()):
    return pl.pallas_call(
        body,
        in_specs=[SCALARS] * len(scalars) + [WHOLE] * (1 + len(operands)),
        out_specs=[WHOLE] * len(shapes),
        out_shape=shapes,
        compiler_params=pltpu.CompilerParams(vmem_limit_bytes=12 * 1024 * 1024),
        cost_estimate=pl.CostEstimate(
            flops=2 * TILE * dense.size, bytes_accessed=dense.size, transcendentals=0
        ),
    )(*scalars, dense, *operands)


def float_rows(rows):
    return jax.ShapeDtypeStruct((rows, TILE), jnp.float32)


def back_product(dense, operands, first):
    rows, cells = dense.shape
    shapes = [float_rows(cells // 4 + NORM_ROWS), jax.ShapeDtypeStruct((TILE // 2, rows), dense.dtype)]
    shapes += [] if first else [float_rows(rows // 2)]
    send, flat, *raw = product_call(
        functools.partial(back_send_kernel, first), dense, operands, shapes
    )


    def keep(flat):
        return product_call(back_keep_kernel, dense, [flat], [float_rows(cells // 4)])[0]

    return send, (keep, flat), *raw


def fore_product(core, dense, operands, first, crossed):
    rows, cells = dense.shape
    shapes = [
        float_rows(rows // 4 + NORM_ROWS),
        jax.ShapeDtypeStruct((cells, TILE), dense.dtype),
        float_rows(cells // 2),
    ]
    send, wide, raw = product_call(
        functools.partial(fore_send_kernel, first, crossed), dense, operands, shapes, [core]
    )


    def keep(wide):
        return product_call(fore_keep_kernel, dense, [wide], [float_rows(rows // 4)])[0]

    return send, (keep, wide), raw


def rotation(norms):
    betas, alphas = [norm_of(ref) for ref in norms[0::2]], [norm_of(ref) for ref in norms[1::2]]
    resid_bar, diag_bar = betas[0], alphas[0]
    steps = []
    for j in range(len(alphas)):
        radius = jnp.sqrt(diag_bar * diag_bar + betas[j + 1] * betas[j + 1])
        rotate_cos = diag_bar / radius
        rotate_sin = betas[j + 1] / radius
        step_size = rotate_cos * resid_bar
        resid_bar = rotate_sin * resid_bar
        coupling = None
        if j + 1 < len(alphas):
            coupling = rotate_sin * alphas[j + 1] / radius
            diag_bar = -rotate_cos * alphas[j + 1]
        steps.append((step_size / radius, coupling))
    misfit = resid_bar / betas[0]
    return alphas, betas, steps, misfit, misfit * rotate_cos


def store_in_order(out_ref, mask, pair, low, values):
    pairs = out_ref.shape[0] // PAIR // UNITS
    start = (((pair // pairs) ^ mask) * pairs + pair % pairs) * PAIR
    ours, theirs = values
    even = pl.ds(pl.multiple_of(start, TILE), TILE)
    odd = pl.ds(pl.multiple_of(start + TILE, TILE), TILE)
    out_ref[even, :] = jnp.where(low, ours, turned(theirs))
    out_ref[odd, :] = jnp.where(low, turned(ours), theirs)


def model_kernel(count, mask_ref, core_ref, *refs):
    ins, (model_ref, misfit_ref) = refs[:-2], refs[-2:]
    chains = [ins[: len(ins) // 2], ins[len(ins) // 2 :]]
    low = low_lanes((TILE, TILE))
    rotations = [rotation(refs_[count:]) for refs_ in chains]
    misfits = [jnp.broadcast_to(r[3], misfit_ref.shape) for r in rotations]
    misfit_ref[...] = jnp.where(low_lanes(misfit_ref.shape), misfits[0], misfits[1])
    for pair in range(model_ref.shape[0] // PAIR):
        values = []
        for refs_, (alphas, _, steps, _, _) in zip(chains, rotations):
            search = total = None
            for j in range(count):
                right = refs_[j][rows_of(pair), :] / alphas[j]
                search = right if j == 0 else right - steps[j - 1][1] * search
                total = steps[j][0] * search if j == 0 else total + steps[j][0] * search
            values.append(total)
        store_in_order(model_ref, mask_ref[0], pair, low, values)


def gradient_kernel(mask_ref, core_ref, *refs):
    ins, gradient_ref = refs[:-1], refs[-1]
    chains = [ins[: len(ins) // 2], ins[len(ins) // 2 :]]
    low = low_lanes((TILE, TILE))
    vectors = []
    factors = []
    for second, (outer_ref, inner_ref, mine_ref, past_ref, *norms) in enumerate(chains):
        units, pairs = gathered_units(outer_ref, inner_ref, mine_ref, not second)
        scales = (norms[-1], past_ref, norms[-2])
        vectors.append(next_vector(units, pairs, None, *scales, other=core_ref[0] != 0))
        factors.append(rotation(norms)[-1])
    for ours, theirs in zip(*vectors):
        values = [factors[0] * ours[1], factors[1] * theirs[1]]
        store_in_order(gradient_ref, mask_ref[0], ours[0], low, values)


def last_call(body, scalars, operands, shapes):
    return pl.pallas_call(
        body,
        in_specs=[SCALARS] * len(scalars) + [WHOLE] * len(operands),
        out_specs=[WHOLE] * len(shapes),
        out_shape=[jax.ShapeDtypeStruct(shape, jnp.float32) for shape in shapes],
        compiler_params=pltpu.CompilerParams(vmem_limit_bytes=12 * 1024 * 1024),
        cost_estimate=pl.CostEstimate(
            flops=0, bytes_accessed=8 * shapes[0][0] * TILE, transcendentals=0
        ),
    )(*scalars, *operands)


def on_device(row_count, col_count, kernel, pattern, counts, delays):
    row_bits = list(range(row_count.bit_length() - 1))
    col_bits = list(range(col_count.bit_length() - 1))
    row_index = lax.axis_index("rows")
    core = lax.axis_index("cols") & 1

    near, far, *rest = row_bits
    add_up = [[near, far, *rest], [far, near, *rest]]
    gather = [[[far, near], [far, near]], [[far, near], [near, far]]]
    steps = len(row_bits) + 2

    def swap_rows(second, value, level):
        pairs = []
        for row in range(row_count):
            for col in range(col_count):
                order = add_up[col & 1] + gather[second][col & 1]
                partner = row ^ (1 << order[level])
                pairs.append((row * col_count + col, partner * col_count + col))
        return lax.ppermute(value, ("rows", "cols"), pairs)

    def swap_cols(value, level):
        return lax.ppermute(value, "cols", [(i, i ^ (1 << level)) for i in range(col_count)])

    bits = [(row_index >> bit) & 1 for bit in row_bits[:2]]
    outer_side = jnp.where(core == 0, bits[0], bits[1])
    inner_side = jnp.where(core == 0, bits[1], bits[0])
    mask = ((1 - outer_side) * 2 + (1 - inner_side)).astype(jnp.int32)
    blocks = jnp.arange(CB_DEV, dtype=jnp.int32)
    unit = CB_DEV // UNITS
    places = ((blocks // unit) ^ mask) * unit + blocks % unit
    flip = ((1 - core) * (kernel.shape[0] // 2)).astype(jnp.int32).reshape(1)
    mask = mask.reshape(1)
    core_index = core.astype(jnp.int32).reshape(1)

    dense, *lefts = fill_dense(kernel, pattern, counts, places, flip, delays)

    def tied(value, other):
        return lax.optimization_barrier((value, other))[0]

    def kept_half(kept, ahead):
        half, operand = kept
        return half(tied(operand, ahead))

    def reduce_rows(swap_rows, send, kept):
        half = send.shape[0] - NORM_ROWS
        got, ahead = yield swap_rows, send, 0
        keep = kept_half(kept, ahead) + got[:half]
        norm = send[half:] + got[half:]
        send, mine = keep[: half // 2], keep[half // 2 :]
        for level in range(1, len(row_bits)):
            got, _ = yield swap_rows, jnp.concatenate([send, norm]), level
            norm = norm + got[half // 2 :]
            send = mine = mine + got[: half // 2]
        inner, _ = yield swap_rows, mine, steps - 2
        outer, _ = yield swap_rows, jnp.concatenate([inner, mine]), steps - 1
        return [outer, inner, mine], norm

    def reduce_cols(send, kept):
        half = send.shape[0] - NORM_ROWS
        got, ahead = yield swap_cols, send, 0
        own = kept_half(kept, ahead) + got[:half]
        norm = send[half:] + got[half:]
        for bit in col_bits[1:]:
            got, _ = yield swap_cols, jnp.concatenate([own, norm]), bit
            norm = norm + got[half:]
            own = own + got[:half]
        other, _ = yield swap_cols, own, 0
        return [other, own], norm

    def chain(second, left):
        swap = functools.partial(swap_rows, second)
        send, keep = back_product(dense, [left], True)
        totals, norm = yield from reduce_rows(swap, send, keep)
        norms = [norm]
        rights = []
        for iteration in range(ITERS):
            past = [rights[-1], norms[-2]] if rights else []
            send, keep, right = fore_product(
                core_index, dense, [*totals, norms[-1], *past], not rights, not second
            )
            rights.append(right)
            halves, norm = yield from reduce_cols(send, keep)
            norms.append(norm)
            send, keep, left = back_product(
                dense, [*halves, norms[-1], left, norms[-2]], False
            )
            totals, norm = yield from reduce_rows(swap, send, keep)
            norms.append(norm)
        return rights, norms, totals

    runs = [chain(second, left) for second, left in enumerate(lefts)]
    wanted = [next(run) for run in runs]
    chains = [None] * len(runs)
    gots = [None] * len(runs)
    swap, value, level = wanted[0]
    gots[0] = swap(value, level)
    latest = wanted[1][1]
    turn = 0
    while None in chains:
        mine = 0 if turn < BEHIND else (turn - BEHIND) % 2
        turn += 1
        if chains[mine] is not None:
            continue
        if gots[mine] is None:
            swap, value, level = wanted[mine]
            latest = tied(value, latest)
        else:
            try:
                swap, latest, level = runs[mine].send((tied(gots[mine], latest), latest))
            except StopIteration as stop:
                chains[mine] = stop.value
                continue
        gots[mine] = swap(latest, level)

    cells = dense.shape[1]
    model, misfit = last_call(
        functools.partial(model_kernel, ITERS),
        [mask, core_index],
        [operand for rights, norms, _ in chains for operand in [*rights, *norms]],
        [(cells, TILE), (NORM_ROWS, TILE)],
    )
    (gradient,) = last_call(
        gradient_kernel,
        [mask, core_index],
        [operand for rights, norms, totals in chains for operand in [*totals, rights[-1], *norms]],
        [(cells, TILE)],
    )
    return (model, gradient, misfit[0])


def solution(mesh):
    placed = (P("rows", "cols", None, None), P("rows", "cols"), P("rows", "cols"), P("rows", None))

    def local(kernel, pattern, counts, delays):
        return on_device(
            mesh.shape["rows"], mesh.shape["cols"], kernel, pattern, counts, delays
        )

    return jax.shard_map(
        local,
        mesh=mesh,
        in_specs=placed,
        out_specs=(P("cols", None), P("cols", None), P()),
        check_vma=False,
    )
```

```python
import functools

import jax
import jax.numpy as jnp
from jax import lax
from jax.experimental import pallas as pl
from jax.experimental.pallas import tpu as pltpu
from jax.sharding import PartitionSpec as P

CB_DEV = 24
ITERS = 2
TILE = 128
PAIR = 2 * TILE
UNITS = 4
NORM_ROWS = 8
BEHIND = 0

tiny_eps = 1e-06

WHOLE = pl.BlockSpec(memory_space=pltpu.VMEM)
SCALARS = pl.BlockSpec(memory_space=pltpu.SMEM)


def low_lanes(shape):
    return lax.broadcasted_iota(jnp.int32, shape, 1) < shape[1] // 2


def turned(value):
    return pltpu.roll(value, value.shape[1] // 2, 1)


def rows_of(pair, size=TILE):
    return slice(pair * size, (pair + 1) * size)


def fill_kernel(
    place_ref, flip_ref, pattern_in, counts_in, delays_in, tiles_in,
    dense_ref, even_left_ref, odd_left_ref, pattern_ref, counts_ref, delays_ref, tiles_ref, arrived,
):
    flip = flip_ref[0]
    row_blocks = tiles_in.shape[0]
    small = [
        pltpu.make_async_copy(source, target, arrived.at[2 * row_blocks + i])
        for i, (source, target) in enumerate(
            [(pattern_in, pattern_ref), (counts_in, counts_ref), (delays_in, delays_ref)]
        )
    ]
    for copy in small:
        copy.start()

    half = tiles_in.shape[1] // 2

    def fetch(position, upper):
        slots = pl.ds(upper * half, half)
        return pltpu.make_async_copy(
            tiles_in.at[position ^ flip, slots],
            tiles_ref.at[position, slots],
            arrived.at[upper * row_blocks + position],
        )

    for position in range(row_blocks):
        fetch(position, 0).start()
    for copy in small:
        copy.wait()
    for position in range(row_blocks):

        @pl.when(counts_ref[position ^ flip] > half)
        def _():
            fetch(position, 1).start()

    low = low_lanes((TILE, TILE))
    for pair in range(row_blocks // 2):
        source = (pair ^ (flip // 2)) * PAIR
        even = delays_ref[pl.ds(pl.multiple_of(source, TILE), TILE), :]
        odd = delays_ref[pl.ds(pl.multiple_of(source + TILE, TILE), TILE), :]
        even_left_ref[rows_of(pair), :] = jnp.where(low, even, turned(odd))
        odd_left_ref[rows_of(pair), :] = jnp.where(low, turned(even), odd)

    @pl.loop(0, row_blocks)
    def _(position):
        rows = pl.ds(pl.multiple_of(position * TILE, TILE), TILE)
        block = position ^ flip
        count = counts_ref[block]

        def place(tile):
            column = jnp.where(tile < count, place_ref[pattern_ref[block, tile]], CB_DEV)
            lanes = pl.ds(pl.multiple_of(column * TILE, TILE), TILE)
            dense_ref[rows, lanes] = tiles_ref[position, tile]

        dense_ref[rows, :] = jnp.zeros((TILE, dense_ref.shape[1]), dense_ref.dtype)
        fetch(position, 0).wait()
        for tile in range(half):
            place(tile)

        @pl.when(count > half)
        def _():
            fetch(position, 1).wait()
            for tile in range(half, 2 * half):
                place(tile)


def fill_dense(kernel, pattern, counts, places, flip, delays):
    row_blocks = kernel.shape[0]
    rows = row_blocks * TILE
    left = jax.ShapeDtypeStruct((rows // 2, TILE), jnp.float32)
    return pl.pallas_call(
        fill_kernel,
        in_specs=[SCALARS] * 2 + [pl.BlockSpec(memory_space=pltpu.HBM)] * 4,
        out_specs=[WHOLE] * 3,
        out_shape=[jax.ShapeDtypeStruct((rows, (CB_DEV + 1) * TILE), kernel.dtype), left, left],
        scratch_shapes=[
            pltpu.SMEM(pattern.shape, jnp.int32),
            pltpu.SMEM((row_blocks,), jnp.int32),
            pltpu.VMEM(delays.shape, delays.dtype),
            pltpu.VMEM(kernel.shape, kernel.dtype),
            pltpu.SemaphoreType.DMA((2 * row_blocks + 3,)),
        ],
        compiler_params=pltpu.CompilerParams(vmem_limit_bytes=16 * 1024 * 1024),
        cost_estimate=pl.CostEstimate(
            flops=0, bytes_accessed=2 * kernel.size, transcendentals=0
        ),
    )(
        places,
        flip,
        *(pltpu.with_memory_space_constraint(x, pltpu.HBM) for x in (pattern, counts.reshape(-1), delays, kernel)),
    )


def norm_of(ref):
    return jnp.sqrt(ref[0:1, :] + tiny_eps)


def squares_row(sums):
    while len(sums) > 1:
        sums = [sums[i] + sums[i + 1] for i in range(0, len(sums), 2)]
    row = jnp.sum(sums[0], axis=0, keepdims=True)
    return row + turned(row)


def next_vector(parts, raw_ref, scale_ref, past_ref, past_scale_ref):
    if scale_ref is not None:
        scale = norm_of(scale_ref)
    if past_ref is not None:
        past_scale = norm_of(past_scale_ref)
    position = 0
    for part, units in parts:
        pairs = part.shape[0] // TILE // units
        for unit in range(units):
            squares = jnp.zeros((NORM_ROWS, TILE), jnp.float32)
            for pair in range(pairs):
                value = part[rows_of(unit * pairs + pair), :]
                if scale_ref is not None:
                    value = value / scale
                if past_ref is not None:
                    value = value - scale * (past_ref[rows_of(position), :] / past_scale)
                if raw_ref is not None:
                    raw_ref[rows_of(position), :] = value
                squares += jnp.sum((value * value).reshape(-1, NORM_ROWS, TILE), axis=0)
                yield position, value, squares if pair == pairs - 1 else None
                position += 1


def back_pairs(dense_ref, turned_ref, out_ref, start):
    for pair in range(out_ref.shape[0] // TILE):
        product = jnp.dot(
            turned_ref[...],
            dense_ref[:, rows_of(start + pair, PAIR)],
            preferred_element_type=jnp.float32,
        )
        stacked = jnp.concatenate([product[:, :TILE], product[:, TILE:]], axis=0)
        out_ref[rows_of(pair), :] = stacked.T


def back_send_kernel(first, *refs):
    if first:
        dense_ref, own_ref, send_ref, turned_ref = refs
        parts, raw_ref, scales = [(own_ref, 2)], None, (None, None, None)
    else:
        (dense_ref, other_ref, own_ref, scale_ref, past_ref, past_scale_ref,
         send_ref, turned_ref, raw_ref) = refs
        parts, scales = [(other_ref, 1), (own_ref, 1)], (scale_ref, past_ref, past_scale_ref)
    sums = []
    half = turned_ref.shape[0]
    for pair, value, squares in next_vector(parts, raw_ref, *scales):
        flat = value.T.astype(turned_ref.dtype)
        turned_ref[:, rows_of(2 * pair)] = flat[:half]
        turned_ref[:, rows_of(2 * pair + 1)] = flat[half:]
        if squares is not None:
            sums.append(squares)
    send_ref[-NORM_ROWS:, :] = jnp.broadcast_to(squares_row(sums), (NORM_ROWS, TILE))
    back_pairs(dense_ref, turned_ref, send_ref, 0)


def back_keep_kernel(dense_ref, turned_ref, keep_ref):
    back_pairs(dense_ref, turned_ref, keep_ref, keep_ref.shape[0] // TILE)


def fore_pairs(dense_ref, cells, wide_ref, add_ref, out_ref, start):
    low = low_lanes((TILE, TILE))
    step = 2
    pairs = out_ref.shape[0] // TILE
    for pair in range(0, pairs, step):
        product = jnp.dot(
            dense_ref[(start + pair) * PAIR : (start + pair + step) * PAIR, cells],
            wide_ref[...],
            preferred_element_type=jnp.float32,
        )
        for i in range(step):
            even, odd = product[rows_of(2 * i), :], product[rows_of(2 * i + 1), :]
            value = jnp.where(low, even, odd)
            if add_ref is not None:
                value = value + add_ref[rows_of(start + pair + i), :]
            out_ref[rows_of(pair + i), :] = value


def fore_vector(parts, wide_ref, raw_ref, scales):
    low = low_lanes((TILE, TILE))
    sums = []
    for pair, value, squares in next_vector(parts, raw_ref, *scales):
        other = turned(value)
        wide_ref[rows_of(2 * pair), :] = jnp.where(low, value, other).astype(wide_ref.dtype)
        wide_ref[rows_of(2 * pair + 1), :] = jnp.where(low, other, value).astype(wide_ref.dtype)
        if squares is not None:
            sums.append(squares)
    return sums[0] + sums[1]


def fore_own_kernel(first, dense_ref, inner_ref, mine_ref, scale_ref, *refs):
    past_ref, past_scale_ref = (None, None) if first else refs[:2]
    part_ref, sum_ref, raw_ref, wide_ref = refs[-4:]
    parts = [(inner_ref, 1), (mine_ref, 1)]
    sum_ref[...] = fore_vector(parts, wide_ref, raw_ref, (scale_ref, past_ref, past_scale_ref))
    depth = wide_ref.shape[0]
    fore_pairs(dense_ref, slice(depth, 2 * depth), wide_ref, None, part_ref, 0)


def fore_send_kernel(first, dense_ref, outer_ref, part_ref, sum_ref, scale_ref, *refs):
    past_ref, past_scale_ref = (None, None) if first else refs[:2]
    send_ref, wide_ref, raw_ref = refs[-3:]
    squares = fore_vector([(outer_ref, 2)], wide_ref, raw_ref, (scale_ref, past_ref, past_scale_ref))
    row = squares_row([squares, sum_ref[...]])
    send_ref[-NORM_ROWS:, :] = jnp.broadcast_to(row, (NORM_ROWS, TILE))
    fore_pairs(dense_ref, slice(0, wide_ref.shape[0]), wide_ref, part_ref, send_ref, 0)


def fore_keep_kernel(dense_ref, wide_ref, part_ref, keep_ref):
    start = keep_ref.shape[0] // TILE
    fore_pairs(dense_ref, slice(0, wide_ref.shape[0]), wide_ref, part_ref, keep_ref, start)


def product_call(body, dense, operands, shapes, scratch=()):
    return pl.pallas_call(
        body,
        in_specs=[WHOLE] * (1 + len(operands)),
        out_specs=[WHOLE] * len(shapes),
        out_shape=shapes,
        scratch_shapes=scratch,
        compiler_params=pltpu.CompilerParams(vmem_limit_bytes=12 * 1024 * 1024),
        cost_estimate=pl.CostEstimate(
            flops=2 * TILE * dense.size, bytes_accessed=dense.size, transcendentals=0
        ),
    )(dense, *operands)


def float_rows(rows):
    return jax.ShapeDtypeStruct((rows, TILE), jnp.float32)


def back_product(dense, operands, first):
    rows, cells = dense.shape[0], CB_DEV * TILE
    shapes = [float_rows(cells // 4 + NORM_ROWS), jax.ShapeDtypeStruct((TILE // 2, rows), dense.dtype)]
    shapes += [] if first else [float_rows(rows // 2)]
    send, flat, *raw = product_call(
        functools.partial(back_send_kernel, first), dense, operands, shapes
    )


    def keep(flat):
        return product_call(back_keep_kernel, dense, [flat], [float_rows(cells // 4)])[0]

    return send, (keep, flat), *raw


def fore_own_product(dense, operands, first):
    rows, cells = dense.shape[0], CB_DEV * TILE
    return product_call(
        functools.partial(fore_own_kernel, first),
        dense,
        operands,
        [float_rows(rows // 2), float_rows(NORM_ROWS), float_rows(cells // 4)],
        [pltpu.VMEM((cells // 2, TILE), dense.dtype)],
    )


def fore_product(dense, operands, first):
    rows, cells = dense.shape[0], CB_DEV * TILE
    shapes = [
        float_rows(rows // 4 + NORM_ROWS),
        jax.ShapeDtypeStruct((cells // 2, TILE), dense.dtype),
        float_rows(cells // 4),
    ]
    send, wide, raw = product_call(
        functools.partial(fore_send_kernel, first), dense, operands, shapes
    )

    def keep(wide):
        return product_call(fore_keep_kernel, dense, [wide, operands[1]], [float_rows(rows // 4)])[0]

    return send, (keep, wide), raw


def rotation(norms):
    betas, alphas = [norm_of(ref) for ref in norms[0::2]], [norm_of(ref) for ref in norms[1::2]]
    resid_bar, diag_bar = betas[0], alphas[0]
    steps = []
    for j in range(len(alphas)):
        radius = jnp.sqrt(diag_bar * diag_bar + betas[j + 1] * betas[j + 1])
        rotate_cos = diag_bar / radius
        rotate_sin = betas[j + 1] / radius
        step_size = rotate_cos * resid_bar
        resid_bar = rotate_sin * resid_bar
        coupling = None
        if j + 1 < len(alphas):
            coupling = rotate_sin * alphas[j + 1] / radius
            diag_bar = -rotate_cos * alphas[j + 1]
        steps.append((step_size / radius, coupling))
    misfit = resid_bar / betas[0]
    return alphas, betas, steps, misfit, misfit * rotate_cos


def store_in_order(out_ref, mask, pair, low, values):
    pairs = out_ref.shape[0] // PAIR // UNITS
    start = (((pair // pairs) ^ mask) * pairs + pair % pairs) * PAIR
    ours, theirs = values
    even = pl.ds(pl.multiple_of(start, TILE), TILE)
    odd = pl.ds(pl.multiple_of(start + TILE, TILE), TILE)
    out_ref[even, :] = jnp.where(low, ours, turned(theirs))
    out_ref[odd, :] = jnp.where(low, turned(ours), theirs)


def model_kernel(count, mask_ref, *refs):
    ins, (model_ref, misfit_ref) = refs[:-2], refs[-2:]
    chains = [ins[: len(ins) // 2], ins[len(ins) // 2 :]]
    low = low_lanes((TILE, TILE))
    rotations = [rotation(refs_[2 * count :]) for refs_ in chains]
    half = model_ref.shape[0] // PAIR // 2
    misfits = [jnp.broadcast_to(r[3], misfit_ref.shape) for r in rotations]
    misfit_ref[...] = jnp.where(low_lanes(misfit_ref.shape), misfits[0], misfits[1])
    for pair in range(model_ref.shape[0] // PAIR):
        values = []
        for refs_, (alphas, _, steps, _, _) in zip(chains, rotations):
            search = total = None
            for j in range(count):
                right_ref = refs_[2 * j + pair // half]
                right = right_ref[rows_of(pair % half), :] / alphas[j]
                search = right if j == 0 else right - steps[j - 1][1] * search
                total = steps[j][0] * search if j == 0 else total + steps[j][0] * search
            values.append(total)
        store_in_order(model_ref, mask_ref[0], pair, low, values)


def gradient_kernel(mask_ref, *refs):
    ins, gradient_ref = refs[:-1], refs[-1]
    chains = [ins[: len(ins) // 2], ins[len(ins) // 2 :]]
    low = low_lanes((TILE, TILE))
    vectors = []
    factors = []
    for outer_ref, inner_ref, mine_ref, past_ref, own_past_ref, *norms in chains:
        halves = [
            next_vector(parts, None, norms[-1], past, norms[-2])
            for parts, past in [
                ([(outer_ref, 2)], past_ref),
                ([(inner_ref, 1), (mine_ref, 1)], own_past_ref),
            ]
        ]
        vectors.append([value for half in halves for _, value, _ in half])
        factors.append(rotation(norms)[-1])
    for pair, (ours, theirs) in enumerate(zip(*vectors)):
        values = [factors[0] * ours, factors[1] * theirs]
        store_in_order(gradient_ref, mask_ref[0], pair, low, values)


def last_call(body, mask, operands, shapes):
    return pl.pallas_call(
        body,
        in_specs=[SCALARS] + [WHOLE] * len(operands),
        out_specs=[WHOLE] * len(shapes),
        out_shape=[jax.ShapeDtypeStruct(shape, jnp.float32) for shape in shapes],
        compiler_params=pltpu.CompilerParams(vmem_limit_bytes=12 * 1024 * 1024),
        cost_estimate=pl.CostEstimate(
            flops=0, bytes_accessed=8 * shapes[0][0] * TILE, transcendentals=0
        ),
    )(mask, *operands)


def on_device(row_count, col_count, kernel, pattern, counts, delays):
    row_bits = list(range(row_count.bit_length() - 1))
    col_bits = list(range(col_count.bit_length() - 1))
    row_index = lax.axis_index("rows")
    core = lax.axis_index("cols") & 1

    orders = [row_bits, [row_bits[1], row_bits[0], *row_bits[2:]]]

    def swap_rows(value, level):
        pairs = []
        for row in range(row_count):
            for col in range(col_count):
                partner = row ^ (1 << orders[col & 1][level])
                pairs.append((row * col_count + col, partner * col_count + col))
        return lax.ppermute(value, ("rows", "cols"), pairs)

    def swap_cols(value, level):
        return lax.ppermute(value, "cols", [(i, i ^ (1 << level)) for i in range(col_count)])

    bits = [(row_index >> bit) & 1 for bit in row_bits[:2]]
    outer_side = jnp.where(core == 0, bits[0], bits[1])
    inner_side = jnp.where(core == 0, bits[1], bits[0])
    mask = ((1 - outer_side) * 2 + (1 - inner_side)).astype(jnp.int32)
    blocks = jnp.arange(CB_DEV, dtype=jnp.int32)
    unit = CB_DEV // UNITS
    places = ((blocks // unit) ^ mask) * unit + blocks % unit
    flip = ((1 - core) * (kernel.shape[0] // 2)).astype(jnp.int32).reshape(1)
    mask = mask.reshape(1)

    dense, *lefts = fill_dense(kernel, pattern, counts, places, flip, delays)

    def tied(value, other):
        return lax.optimization_barrier((value, other))[0]

    def kept_half(kept, ahead):
        half, operand = kept
        return half(tied(operand, ahead))

    def reduce_rows(send, kept):
        half = send.shape[0] - NORM_ROWS
        got, ahead = yield swap_rows, send, 0
        keep = kept_half(kept, ahead) + got[:half]
        norm = send[half:] + got[half:]
        send, mine = keep[: half // 2], keep[half // 2 :]
        for level in range(1, len(row_bits)):
            got, _ = yield swap_rows, jnp.concatenate([send, norm]), level
            norm = norm + got[half // 2 :]
            send = mine = mine + got[: half // 2]
        inner, _ = yield swap_rows, mine, 1
        outer, ahead = yield swap_rows, jnp.concatenate([inner, mine]), 0
        return [outer, inner, mine], norm, ahead

    def reduce_cols(send, kept):
        half = send.shape[0] - NORM_ROWS
        got, ahead = yield swap_cols, send, 0
        own = kept_half(kept, ahead) + got[:half]
        norm = send[half:] + got[half:]
        for bit in col_bits[1:]:
            got, _ = yield swap_cols, jnp.concatenate([own, norm]), bit
            norm = norm + got[half:]
            own = own + got[:half]
        other, _ = yield swap_cols, own, 0
        return [other, own], norm

    def chain(left):
        send, keep = back_product(dense, [left], True)
        totals, norm, ahead = yield from reduce_rows(send, keep)
        norms = [norm]
        rights = []
        for iteration in range(ITERS):
            outer, *own = totals
            pasts = [[right, norms[-2]] for right in rights[-1]] if rights else [[], []]
            own = [tied(own[0], ahead), own[1]]
            part, squares, own_right = fore_own_product(
                dense, [*own, norms[-1], *pasts[1]], not rights
            )
            send, keep, right = fore_product(
                dense, [outer, part, squares, norms[-1], *pasts[0]], not rights
            )
            rights.append([right, own_right])
            halves, norm = yield from reduce_cols(send, keep)
            norms.append(norm)
            send, keep, left = back_product(
                dense, [*halves, norms[-1], left, norms[-2]], False
            )
            totals, norm, ahead = yield from reduce_rows(send, keep)
            norms.append(norm)
        return rights, norms, totals

    runs = [chain(left) for left in lefts]
    wanted = [next(run) for run in runs]
    chains = [None] * len(runs)
    gots = [None] * len(runs)
    swap, value, level = wanted[0]
    gots[0] = swap(value, level)
    latest = wanted[1][1]
    turn = 0
    while None in chains:
        mine = 0 if turn < BEHIND else (turn - BEHIND) % 2
        turn += 1
        if chains[mine] is not None:
            continue
        if gots[mine] is None:
            swap, value, level = wanted[mine]
            latest = tied(value, latest)
        else:
            try:
                swap, latest, level = runs[mine].send((tied(gots[mine], latest), latest))
            except StopIteration as stop:
                chains[mine] = stop.value
                continue
        gots[mine] = swap(latest, level)

    cells = CB_DEV * TILE
    model, misfit = last_call(
        functools.partial(model_kernel, ITERS),
        mask,
        [operand for rights, norms, _ in chains for operand in [*sum(rights, []), *norms]],
        [(cells, TILE), (NORM_ROWS, TILE)],
    )
    (gradient,) = last_call(
        gradient_kernel,
        mask,
        [operand for rights, norms, totals in chains for operand in [*totals, *rights[-1], *norms]],
        [(cells, TILE)],
    )
    return (model, gradient, misfit[0])


def solution(mesh):
    placed = (P("rows", "cols", None, None), P("rows", "cols"), P("rows", "cols"), P("rows", None))

    def local(kernel, pattern, counts, delays):
        return on_device(
            mesh.shape["rows"], mesh.shape["cols"], kernel, pattern, counts, delays
        )

    return jax.shard_map(
        local,
        mesh=mesh,
        in_specs=placed,
        out_specs=(P("cols", None), P("cols", None), P()),
        check_vma=False,
    )
```

```python
import functools

import jax
import jax.numpy as jnp
from jax import lax
from jax.experimental import pallas as pl
from jax.experimental.pallas import tpu as pltpu
from jax.sharding import PartitionSpec as P

CB_DEV = 24
ITERS = 2
TILE = 128
PAIR = 2 * TILE
UNITS = 4
NORM_ROWS = 8
BEHIND = 0

tiny_eps = 1e-06

WHOLE = pl.BlockSpec(memory_space=pltpu.VMEM)
SCALARS = pl.BlockSpec(memory_space=pltpu.SMEM)


def low_lanes(shape):
    return lax.broadcasted_iota(jnp.int32, shape, 1) < shape[1] // 2


def turned(value):
    return pltpu.roll(value, value.shape[1] // 2, 1)


def rows_of(pair, size=TILE):
    return slice(pair * size, (pair + 1) * size)


def fill_kernel(
    place_ref, flip_ref, pattern_in, counts_in, delays_in, tiles_in,
    dense_ref, even_left_ref, odd_left_ref, pattern_ref, counts_ref, delays_ref, tiles_ref, arrived,
):
    flip = flip_ref[0]
    row_blocks = tiles_in.shape[0]
    small = [
        pltpu.make_async_copy(source, target, arrived.at[2 * row_blocks + i])
        for i, (source, target) in enumerate(
            [(pattern_in, pattern_ref), (counts_in, counts_ref), (delays_in, delays_ref)]
        )
    ]
    for copy in small:
        copy.start()

    half = tiles_in.shape[1] // 2

    def fetch(position, upper):
        slots = pl.ds(upper * half, half)
        return pltpu.make_async_copy(
            tiles_in.at[position ^ flip, slots],
            tiles_ref.at[position, slots],
            arrived.at[upper * row_blocks + position],
        )

    for position in range(row_blocks):
        fetch(position, 0).start()
    for copy in small:
        copy.wait()
    for position in range(row_blocks):

        @pl.when(counts_ref[position ^ flip] > half)
        def _():
            fetch(position, 1).start()

    low = low_lanes((TILE, TILE))
    for pair in range(row_blocks // 2):
        source = (pair ^ (flip // 2)) * PAIR
        even = delays_ref[pl.ds(pl.multiple_of(source, TILE), TILE), :]
        odd = delays_ref[pl.ds(pl.multiple_of(source + TILE, TILE), TILE), :]
        even_left_ref[rows_of(pair), :] = jnp.where(low, even, turned(odd))
        odd_left_ref[rows_of(pair), :] = jnp.where(low, turned(even), odd)

    @pl.loop(0, row_blocks)
    def _(position):
        rows = pl.ds(pl.multiple_of(position * TILE, TILE), TILE)
        block = position ^ flip
        count = counts_ref[block]

        def place(tile):
            column = jnp.where(tile < count, place_ref[pattern_ref[block, tile]], CB_DEV)
            lanes = pl.ds(pl.multiple_of(column * TILE, TILE), TILE)
            dense_ref[rows, lanes] = tiles_ref[position, tile]

        dense_ref[rows, :] = jnp.zeros((TILE, dense_ref.shape[1]), dense_ref.dtype)
        fetch(position, 0).wait()
        for tile in range(half):
            place(tile)

        @pl.when(count > half)
        def _():
            fetch(position, 1).wait()
            for tile in range(half, 2 * half):
                place(tile)


def fill_dense(kernel, pattern, counts, places, flip, delays):
    row_blocks = kernel.shape[0]
    rows = row_blocks * TILE
    left = jax.ShapeDtypeStruct((rows // 2, TILE), jnp.float32)
    return pl.pallas_call(
        fill_kernel,
        in_specs=[SCALARS] * 2 + [pl.BlockSpec(memory_space=pltpu.HBM)] * 4,
        out_specs=[WHOLE] * 3,
        out_shape=[jax.ShapeDtypeStruct((rows, (CB_DEV + 1) * TILE), kernel.dtype), left, left],
        scratch_shapes=[
            pltpu.SMEM(pattern.shape, jnp.int32),
            pltpu.SMEM((row_blocks,), jnp.int32),
            pltpu.VMEM(delays.shape, delays.dtype),
            pltpu.VMEM(kernel.shape, kernel.dtype),
            pltpu.SemaphoreType.DMA((2 * row_blocks + 3,)),
        ],
        compiler_params=pltpu.CompilerParams(vmem_limit_bytes=16 * 1024 * 1024),
        cost_estimate=pl.CostEstimate(
            flops=0, bytes_accessed=2 * kernel.size, transcendentals=0
        ),
    )(
        places,
        flip,
        *(pltpu.with_memory_space_constraint(x, pltpu.HBM) for x in (pattern, counts.reshape(-1), delays, kernel)),
    )


def norm_of(ref):
    return jnp.sqrt(ref[0:1, :] + tiny_eps)


def squares_row(sums):
    while len(sums) > 1:
        sums = [sums[i] + sums[i + 1] for i in range(0, len(sums), 2)]
    row = jnp.sum(sums[0], axis=0, keepdims=True)
    return row + turned(row)


def next_vector(parts, raw_ref, scale_ref, past_ref, past_scale_ref):
    if scale_ref is not None:
        scale = norm_of(scale_ref)
    if past_ref is not None:
        past_scale = norm_of(past_scale_ref)
    position = 0
    for part, units in parts:
        pairs = part.shape[0] // TILE // units
        for unit in range(units):
            squares = jnp.zeros((NORM_ROWS, TILE), jnp.float32)
            for pair in range(pairs):
                value = part[rows_of(unit * pairs + pair), :]
                if scale_ref is not None:
                    value = value / scale
                if past_ref is not None:
                    value = value - scale * (past_ref[rows_of(position), :] / past_scale)
                if raw_ref is not None:
                    raw_ref[rows_of(position), :] = value
                squares += jnp.sum((value * value).reshape(-1, NORM_ROWS, TILE), axis=0)
                yield position, value, squares if pair == pairs - 1 else None
                position += 1


def back_pairs(dense_ref, turned_ref, out_ref, start):
    for pair in range(out_ref.shape[0] // TILE):
        product = jnp.dot(
            turned_ref[...],
            dense_ref[:, rows_of(start + pair, PAIR)],
            preferred_element_type=jnp.float32,
        )
        stacked = jnp.concatenate([product[:, :TILE], product[:, TILE:]], axis=0)
        out_ref[rows_of(pair), :] = stacked.T


def back_send_kernel(first, *refs):
    if first:
        dense_ref, own_ref, send_ref, turned_ref = refs
        parts, raw_ref, scales = [(own_ref, 2)], None, (None, None, None)
    else:
        (dense_ref, other_ref, own_ref, scale_ref, past_ref, past_scale_ref,
         send_ref, turned_ref, raw_ref) = refs
        parts, scales = [(other_ref, 1), (own_ref, 1)], (scale_ref, past_ref, past_scale_ref)
    sums = []
    half = turned_ref.shape[0]
    for pair, value, squares in next_vector(parts, raw_ref, *scales):
        flat = value.T.astype(turned_ref.dtype)
        turned_ref[:, rows_of(2 * pair)] = flat[:half]
        turned_ref[:, rows_of(2 * pair + 1)] = flat[half:]
        if squares is not None:
            sums.append(squares)
    send_ref[-NORM_ROWS:, :] = jnp.broadcast_to(squares_row(sums), (NORM_ROWS, TILE))
    back_pairs(dense_ref, turned_ref, send_ref, 0)


def back_keep_kernel(dense_ref, turned_ref, keep_ref):
    back_pairs(dense_ref, turned_ref, keep_ref, keep_ref.shape[0] // TILE)


def fore_pairs(dense_ref, cells, wide_ref, add_ref, out_ref, start):
    low = low_lanes((TILE, TILE))
    step = 2
    pairs = out_ref.shape[0] // TILE
    for pair in range(0, pairs, step):
        product = jnp.dot(
            dense_ref[(start + pair) * PAIR : (start + pair + step) * PAIR, cells],
            wide_ref[...],
            preferred_element_type=jnp.float32,
        )
        for i in range(step):
            even, odd = product[rows_of(2 * i), :], product[rows_of(2 * i + 1), :]
            value = jnp.where(low, even, odd)
            if add_ref is not None:
                value = value + add_ref[rows_of(start + pair + i), :]
            out_ref[rows_of(pair + i), :] = value


def fore_vector(parts, wide_ref, raw_ref, scales):
    low = low_lanes((TILE, TILE))
    sums = []
    for pair, value, squares in next_vector(parts, raw_ref, *scales):
        other = turned(value)
        wide_ref[rows_of(2 * pair), :] = jnp.where(low, value, other).astype(wide_ref.dtype)
        wide_ref[rows_of(2 * pair + 1), :] = jnp.where(low, other, value).astype(wide_ref.dtype)
        if squares is not None:
            sums.append(squares)
    return sums[0] + sums[1]


def fore_own_kernel(first, dense_ref, inner_ref, mine_ref, scale_ref, *refs):
    past_ref, past_scale_ref = (None, None) if first else refs[:2]
    part_ref, sum_ref, raw_ref, wide_ref = refs[-4:]
    parts = [(inner_ref, 1), (mine_ref, 1)]
    sum_ref[...] = fore_vector(parts, wide_ref, raw_ref, (scale_ref, past_ref, past_scale_ref))
    depth = wide_ref.shape[0]
    fore_pairs(dense_ref, slice(depth, 2 * depth), wide_ref, None, part_ref, 0)


def fore_send_kernel(first, dense_ref, outer_ref, part_ref, sum_ref, scale_ref, *refs):
    past_ref, past_scale_ref = (None, None) if first else refs[:2]
    send_ref, wide_ref, raw_ref = refs[-3:]
    squares = fore_vector([(outer_ref, 2)], wide_ref, raw_ref, (scale_ref, past_ref, past_scale_ref))
    row = squares_row([squares, sum_ref[...]])
    send_ref[-NORM_ROWS:, :] = jnp.broadcast_to(row, (NORM_ROWS, TILE))
    fore_pairs(dense_ref, slice(0, wide_ref.shape[0]), wide_ref, part_ref, send_ref, 0)


def fore_keep_kernel(dense_ref, wide_ref, part_ref, keep_ref):
    start = keep_ref.shape[0] // TILE
    fore_pairs(dense_ref, slice(0, wide_ref.shape[0]), wide_ref, part_ref, keep_ref, start)


def product_call(body, dense, operands, shapes, scratch=()):
    return pl.pallas_call(
        body,
        in_specs=[WHOLE] * (1 + len(operands)),
        out_specs=[WHOLE] * len(shapes),
        out_shape=shapes,
        scratch_shapes=scratch,
        compiler_params=pltpu.CompilerParams(vmem_limit_bytes=12 * 1024 * 1024),
        cost_estimate=pl.CostEstimate(
            flops=2 * TILE * dense.size, bytes_accessed=dense.size, transcendentals=0
        ),
    )(dense, *operands)


def float_rows(rows):
    return jax.ShapeDtypeStruct((rows, TILE), jnp.float32)


def back_product(dense, operands, first):
    rows, cells = dense.shape[0], CB_DEV * TILE
    shapes = [float_rows(cells // 4 + NORM_ROWS), jax.ShapeDtypeStruct((TILE // 2, rows), dense.dtype)]
    shapes += [] if first else [float_rows(rows // 2)]
    send, flat, *raw = product_call(
        functools.partial(back_send_kernel, first), dense, operands, shapes
    )


    (keep,) = product_call(back_keep_kernel, dense, [flat], [float_rows(cells // 4)])
    return send, keep, *raw


def fore_own_product(dense, operands, first):
    rows, cells = dense.shape[0], CB_DEV * TILE
    return product_call(
        functools.partial(fore_own_kernel, first),
        dense,
        operands,
        [float_rows(rows // 2), float_rows(NORM_ROWS), float_rows(cells // 4)],
        [pltpu.VMEM((cells // 2, TILE), dense.dtype)],
    )


def fore_product(dense, operands, first):
    rows, cells = dense.shape[0], CB_DEV * TILE
    shapes = [
        float_rows(rows // 4 + NORM_ROWS),
        jax.ShapeDtypeStruct((cells // 2, TILE), dense.dtype),
        float_rows(cells // 4),
    ]
    send, wide, raw = product_call(
        functools.partial(fore_send_kernel, first), dense, operands, shapes
    )

    def keep(wide):
        return product_call(fore_keep_kernel, dense, [wide, operands[1]], [float_rows(rows // 4)])[0]

    return send, (keep, wide), raw


def rotation(norms):
    betas, alphas = [norm_of(ref) for ref in norms[0::2]], [norm_of(ref) for ref in norms[1::2]]
    resid_bar, diag_bar = betas[0], alphas[0]
    steps = []
    for j in range(len(alphas)):
        radius = jnp.sqrt(diag_bar * diag_bar + betas[j + 1] * betas[j + 1])
        rotate_cos = diag_bar / radius
        rotate_sin = betas[j + 1] / radius
        step_size = rotate_cos * resid_bar
        resid_bar = rotate_sin * resid_bar
        coupling = None
        if j + 1 < len(alphas):
            coupling = rotate_sin * alphas[j + 1] / radius
            diag_bar = -rotate_cos * alphas[j + 1]
        steps.append((step_size / radius, coupling))
    misfit = resid_bar / betas[0]
    return alphas, betas, steps, misfit, misfit * rotate_cos


def store_in_order(out_ref, mask, pair, low, values):
    pairs = out_ref.shape[0] // PAIR // UNITS
    start = (((pair // pairs) ^ mask) * pairs + pair % pairs) * PAIR
    ours, theirs = values
    even = pl.ds(pl.multiple_of(start, TILE), TILE)
    odd = pl.ds(pl.multiple_of(start + TILE, TILE), TILE)
    out_ref[even, :] = jnp.where(low, ours, turned(theirs))
    out_ref[odd, :] = jnp.where(low, turned(ours), theirs)


def model_kernel(count, mask_ref, *refs):
    ins, (model_ref, misfit_ref) = refs[:-2], refs[-2:]
    chains = [ins[: len(ins) // 2], ins[len(ins) // 2 :]]
    low = low_lanes((TILE, TILE))
    rotations = [rotation(refs_[2 * count :]) for refs_ in chains]
    half = model_ref.shape[0] // PAIR // 2
    misfits = [jnp.broadcast_to(r[3], misfit_ref.shape) for r in rotations]
    misfit_ref[...] = jnp.where(low_lanes(misfit_ref.shape), misfits[0], misfits[1])
    for pair in range(model_ref.shape[0] // PAIR):
        values = []
        for refs_, (alphas, _, steps, _, _) in zip(chains, rotations):
            search = total = None
            for j in range(count):
                right_ref = refs_[2 * j + pair // half]
                right = right_ref[rows_of(pair % half), :] / alphas[j]
                search = right if j == 0 else right - steps[j - 1][1] * search
                total = steps[j][0] * search if j == 0 else total + steps[j][0] * search
            values.append(total)
        store_in_order(model_ref, mask_ref[0], pair, low, values)


def gradient_kernel(mask_ref, *refs):
    ins, gradient_ref = refs[:-1], refs[-1]
    chains = [ins[: len(ins) // 2], ins[len(ins) // 2 :]]
    low = low_lanes((TILE, TILE))
    vectors = []
    factors = []
    for outer_ref, inner_ref, mine_ref, past_ref, own_past_ref, *norms in chains:
        halves = [
            next_vector(parts, None, norms[-1], past, norms[-2])
            for parts, past in [
                ([(outer_ref, 2)], past_ref),
                ([(inner_ref, 1), (mine_ref, 1)], own_past_ref),
            ]
        ]
        vectors.append([value for half in halves for _, value, _ in half])
        factors.append(rotation(norms)[-1])
    for pair, (ours, theirs) in enumerate(zip(*vectors)):
        values = [factors[0] * ours, factors[1] * theirs]
        store_in_order(gradient_ref, mask_ref[0], pair, low, values)


def last_call(body, mask, operands, shapes):
    return pl.pallas_call(
        body,
        in_specs=[SCALARS] + [WHOLE] * len(operands),
        out_specs=[WHOLE] * len(shapes),
        out_shape=[jax.ShapeDtypeStruct(shape, jnp.float32) for shape in shapes],
        compiler_params=pltpu.CompilerParams(vmem_limit_bytes=12 * 1024 * 1024),
        cost_estimate=pl.CostEstimate(
            flops=0, bytes_accessed=8 * shapes[0][0] * TILE, transcendentals=0
        ),
    )(mask, *operands)


def on_device(row_count, col_count, kernel, pattern, counts, delays):
    row_bits = list(range(row_count.bit_length() - 1))
    col_bits = list(range(col_count.bit_length() - 1))
    row_index = lax.axis_index("rows")
    core = lax.axis_index("cols") & 1

    orders = [row_bits, [row_bits[1], row_bits[0], *row_bits[2:]]]

    def swap_rows(value, level):
        pairs = []
        for row in range(row_count):
            for col in range(col_count):
                partner = row ^ (1 << orders[col & 1][level])
                pairs.append((row * col_count + col, partner * col_count + col))
        return lax.ppermute(value, ("rows", "cols"), pairs)

    def swap_cols(value, level):
        return lax.ppermute(value, "cols", [(i, i ^ (1 << level)) for i in range(col_count)])

    bits = [(row_index >> bit) & 1 for bit in row_bits[:2]]
    outer_side = jnp.where(core == 0, bits[0], bits[1])
    inner_side = jnp.where(core == 0, bits[1], bits[0])
    mask = ((1 - outer_side) * 2 + (1 - inner_side)).astype(jnp.int32)
    blocks = jnp.arange(CB_DEV, dtype=jnp.int32)
    unit = CB_DEV // UNITS
    places = ((blocks // unit) ^ mask) * unit + blocks % unit
    flip = ((1 - core) * (kernel.shape[0] // 2)).astype(jnp.int32).reshape(1)
    mask = mask.reshape(1)

    dense, *lefts = fill_dense(kernel, pattern, counts, places, flip, delays)

    def tied(value, other):
        return lax.optimization_barrier((value, other))[0]

    def kept_half(kept, ahead):
        half, operand = kept
        return half(tied(operand, ahead))

    def reduce_rows(send, keep):
        half = keep.shape[0]
        got, _ = yield swap_rows, send, 0
        keep = keep + got[:half]
        norm = send[half:] + got[half:]
        send, mine = keep[: half // 2], keep[half // 2 :]
        for level in range(1, len(row_bits)):
            got, _ = yield swap_rows, jnp.concatenate([send, norm]), level
            norm = norm + got[half // 2 :]
            send = mine = mine + got[: half // 2]
        inner, _ = yield swap_rows, mine, 1
        outer, ahead = yield swap_rows, jnp.concatenate([inner, mine]), 0
        return [outer, inner, mine], norm, ahead

    def reduce_cols(send, kept):
        half = send.shape[0] - NORM_ROWS
        got, ahead = yield swap_cols, send, 0
        own = kept_half(kept, ahead) + got[:half]
        norm = send[half:] + got[half:]
        for bit in col_bits[1:]:
            got, _ = yield swap_cols, jnp.concatenate([own, norm]), bit
            norm = norm + got[half:]
            own = own + got[:half]
        other, _ = yield swap_cols, own, 0
        return [other, own], norm

    def chain(left):
        send, keep = back_product(dense, [left], True)
        totals, norm, ahead = yield from reduce_rows(send, keep)
        norms = [norm]
        rights = []
        for iteration in range(ITERS):
            outer, *own = totals
            pasts = [[right, norms[-2]] for right in rights[-1]] if rights else [[], []]
            own = [tied(own[0], ahead), own[1]]
            part, squares, own_right = fore_own_product(
                dense, [*own, norms[-1], *pasts[1]], not rights
            )
            send, keep, right = fore_product(
                dense, [outer, part, squares, norms[-1], *pasts[0]], not rights
            )
            rights.append([right, own_right])
            halves, norm = yield from reduce_cols(send, keep)
            norms.append(norm)
            send, keep, left = back_product(
                dense, [*halves, norms[-1], left, norms[-2]], False
            )
            totals, norm, ahead = yield from reduce_rows(send, keep)
            norms.append(norm)
        return rights, norms, totals

    runs = [chain(left) for left in lefts]
    wanted = [next(run) for run in runs]
    chains = [None] * len(runs)
    gots = [None] * len(runs)
    swap, value, level = wanted[0]
    gots[0] = swap(value, level)
    latest = wanted[1][1]
    turn = 0
    while None in chains:
        mine = 0 if turn < BEHIND else (turn - BEHIND) % 2
        turn += 1
        if chains[mine] is not None:
            continue
        if gots[mine] is None:
            swap, value, level = wanted[mine]
            latest = tied(value, latest)
        else:
            try:
                swap, latest, level = runs[mine].send((tied(gots[mine], latest), latest))
            except StopIteration as stop:
                chains[mine] = stop.value
                continue
        gots[mine] = swap(latest, level)

    cells = CB_DEV * TILE
    model, misfit = last_call(
        functools.partial(model_kernel, ITERS),
        mask,
        [operand for rights, norms, _ in chains for operand in [*sum(rights, []), *norms]],
        [(cells, TILE), (NORM_ROWS, TILE)],
    )
    (gradient,) = last_call(
        gradient_kernel,
        mask,
        [operand for rights, norms, totals in chains for operand in [*totals, *rights[-1], *norms]],
        [(cells, TILE)],
    )
    return (model, gradient, misfit[0])


def solution(mesh):
    placed = (P("rows", "cols", None, None), P("rows", "cols"), P("rows", "cols"), P("rows", None))

    def local(kernel, pattern, counts, delays):
        return on_device(
            mesh.shape["rows"], mesh.shape["cols"], kernel, pattern, counts, delays
        )

    return jax.shard_map(
        local,
        mesh=mesh,
        in_specs=placed,
        out_specs=(P("cols", None), P("cols", None), P()),
        check_vma=False,
    )
```

```python
import functools

import jax
import jax.numpy as jnp
from jax import lax
from jax.experimental import pallas as pl
from jax.experimental.pallas import tpu as pltpu
from jax.sharding import PartitionSpec as P

CB_DEV = 24
ITERS = 2
TILE = 128
PAIR = 2 * TILE
UNITS = 4
NORM_ROWS = 8
UNIT_ORDERS = ((0, 1, 2, 3), (0, 2, 1, 3))
BEHIND = 0

tiny_eps = 1e-06

WHOLE = pl.BlockSpec(memory_space=pltpu.VMEM)
SCALARS = pl.BlockSpec(memory_space=pltpu.SMEM)


def low_lanes(shape):
    return lax.broadcasted_iota(jnp.int32, shape, 1) < shape[1] // 2


def turned(value):
    return pltpu.roll(value, value.shape[1] // 2, 1)


def rows_of(pair, size=TILE):
    return slice(pair * size, (pair + 1) * size)


def fill_kernel(
    place_ref, flip_ref, pattern_in, counts_in, delays_in, tiles_in,
    dense_ref, even_left_ref, odd_left_ref, pattern_ref, counts_ref, delays_ref, tiles_ref, arrived,
):
    flip = flip_ref[0]
    row_blocks = tiles_in.shape[0]
    small = [
        pltpu.make_async_copy(source, target, arrived.at[2 * row_blocks + i])
        for i, (source, target) in enumerate(
            [(pattern_in, pattern_ref), (counts_in, counts_ref), (delays_in, delays_ref)]
        )
    ]
    for copy in small:
        copy.start()

    half = tiles_in.shape[1] // 2

    def fetch(position, upper):
        slots = pl.ds(upper * half, half)
        return pltpu.make_async_copy(
            tiles_in.at[position ^ flip, slots],
            tiles_ref.at[position, slots],
            arrived.at[upper * row_blocks + position],
        )

    for position in range(row_blocks):
        fetch(position, 0).start()
    for copy in small:
        copy.wait()
    for position in range(row_blocks):

        @pl.when(counts_ref[position ^ flip] > half)
        def _():
            fetch(position, 1).start()

    low = low_lanes((TILE, TILE))
    for pair in range(row_blocks // 2):
        source = (pair ^ (flip // 2)) * PAIR
        even = delays_ref[pl.ds(pl.multiple_of(source, TILE), TILE), :]
        odd = delays_ref[pl.ds(pl.multiple_of(source + TILE, TILE), TILE), :]
        even_left_ref[rows_of(pair), :] = jnp.where(low, even, turned(odd))
        odd_left_ref[rows_of(pair), :] = jnp.where(low, turned(even), odd)

    @pl.loop(0, row_blocks)
    def _(position):
        rows = pl.ds(pl.multiple_of(position * TILE, TILE), TILE)
        block = position ^ flip
        count = counts_ref[block]

        def place(tile):
            column = jnp.where(tile < count, place_ref[pattern_ref[block, tile]], CB_DEV)
            lanes = pl.ds(pl.multiple_of(column * TILE, TILE), TILE)
            dense_ref[rows, lanes] = tiles_ref[position, tile]

        dense_ref[rows, :] = jnp.zeros((TILE, dense_ref.shape[1]), dense_ref.dtype)
        fetch(position, 0).wait()
        for tile in range(half):
            place(tile)

        @pl.when(count > half)
        def _():
            fetch(position, 1).wait()
            for tile in range(half, 2 * half):
                place(tile)


def fill_dense(kernel, pattern, counts, places, flip, delays):
    row_blocks = kernel.shape[0]
    rows = row_blocks * TILE
    left = jax.ShapeDtypeStruct((rows // 2, TILE), jnp.float32)
    return pl.pallas_call(
        fill_kernel,
        in_specs=[SCALARS] * 2 + [pl.BlockSpec(memory_space=pltpu.HBM)] * 4,
        out_specs=[WHOLE] * 3,
        out_shape=[jax.ShapeDtypeStruct((rows, (CB_DEV + 1) * TILE), kernel.dtype), left, left],
        scratch_shapes=[
            pltpu.SMEM(pattern.shape, jnp.int32),
            pltpu.SMEM((row_blocks,), jnp.int32),
            pltpu.VMEM(delays.shape, delays.dtype),
            pltpu.VMEM(kernel.shape, kernel.dtype),
            pltpu.SemaphoreType.DMA((2 * row_blocks + 3,)),
        ],
        compiler_params=pltpu.CompilerParams(vmem_limit_bytes=16 * 1024 * 1024),
        cost_estimate=pl.CostEstimate(
            flops=0, bytes_accessed=2 * kernel.size, transcendentals=0
        ),
    )(
        places,
        flip,
        *(pltpu.with_memory_space_constraint(x, pltpu.HBM) for x in (pattern, counts.reshape(-1), delays, kernel)),
    )


def norm_of(ref):
    return jnp.sqrt(ref[0:1, :] + tiny_eps)


def squares_row(sums):
    while len(sums) > 1:
        sums = [sums[i] + sums[i + 1] for i in range(0, len(sums), 2)]
    row = jnp.sum(sums[0], axis=0, keepdims=True)
    return row + turned(row)


def next_vector(parts, raw_ref, scale_ref, past_ref, past_scale_ref):
    if scale_ref is not None:
        scale = norm_of(scale_ref)
    if past_ref is not None:
        past_scale = norm_of(past_scale_ref)
    position = 0
    for part, units in parts:
        pairs = part.shape[0] // TILE // units
        for unit in range(units):
            squares = jnp.zeros((NORM_ROWS, TILE), jnp.float32)
            for pair in range(pairs):
                value = part[rows_of(unit * pairs + pair), :]
                if scale_ref is not None:
                    value = value / scale
                if past_ref is not None:
                    value = value - scale * (past_ref[rows_of(position), :] / past_scale)
                if raw_ref is not None:
                    raw_ref[rows_of(position), :] = value
                squares += jnp.sum((value * value).reshape(-1, NORM_ROWS, TILE), axis=0)
                yield position, value, squares if pair == pairs - 1 else None
                position += 1


def back_pairs(dense_ref, turned_ref, out_ref, units):
    pairs = CB_DEV // 2 // UNITS
    for pair in range(pairs * len(units)):
        column = units[pair // pairs] * pairs + pair % pairs
        product = jnp.dot(
            turned_ref[...],
            dense_ref[:, rows_of(column, PAIR)],
            preferred_element_type=jnp.float32,
        )
        stacked = jnp.concatenate([product[:, :TILE], product[:, TILE:]], axis=0)
        out_ref[rows_of(pair), :] = stacked.T


def back_send_kernel(first, units, *refs):
    if first:
        dense_ref, own_ref, send_ref, turned_ref = refs
        parts, raw_ref, scales = [(own_ref, 2)], None, (None, None, None)
    else:
        (dense_ref, other_ref, own_ref, scale_ref, past_ref, past_scale_ref,
         send_ref, turned_ref, raw_ref) = refs
        parts, scales = [(other_ref, 1), (own_ref, 1)], (scale_ref, past_ref, past_scale_ref)
    sums = []
    half = turned_ref.shape[0]
    for pair, value, squares in next_vector(parts, raw_ref, *scales):
        flat = value.T.astype(turned_ref.dtype)
        turned_ref[:, rows_of(2 * pair)] = flat[:half]
        turned_ref[:, rows_of(2 * pair + 1)] = flat[half:]
        if squares is not None:
            sums.append(squares)
    send_ref[-NORM_ROWS:, :] = jnp.broadcast_to(squares_row(sums), (NORM_ROWS, TILE))
    back_pairs(dense_ref, turned_ref, send_ref, units)


def back_keep_kernel(units, dense_ref, turned_ref, keep_ref):
    back_pairs(dense_ref, turned_ref, keep_ref, units)


def fore_pairs(dense_ref, units, wide_ref, add_ref, out_ref, start):
    depth = wide_ref.shape[0] // len(units)
    runs = [(unit * depth, i * depth, depth) for i, unit in enumerate(units)]
    if units[1] == units[0] + 1:
        runs = [(units[0] * depth, 0, 2 * depth)]
    low = low_lanes((TILE, TILE))
    step = 2
    pairs = out_ref.shape[0] // TILE
    for pair in range(0, pairs, step):
        rows = slice((start + pair) * PAIR, (start + pair + step) * PAIR)
        product = sum(
            jnp.dot(
                dense_ref[rows, cell : cell + size],
                wide_ref[row : row + size, :],
                preferred_element_type=jnp.float32,
            )
            for cell, row, size in runs
        )
        for i in range(step):
            even, odd = product[rows_of(2 * i), :], product[rows_of(2 * i + 1), :]
            value = jnp.where(low, even, odd)
            if add_ref is not None:
                value = value + add_ref[rows_of(start + pair + i), :]
            out_ref[rows_of(pair + i), :] = value


def fore_vector(parts, wide_ref, raw_ref, scales):
    low = low_lanes((TILE, TILE))
    sums = []
    for pair, value, squares in next_vector(parts, raw_ref, *scales):
        other = turned(value)
        wide_ref[rows_of(2 * pair), :] = jnp.where(low, value, other).astype(wide_ref.dtype)
        wide_ref[rows_of(2 * pair + 1), :] = jnp.where(low, other, value).astype(wide_ref.dtype)
        if squares is not None:
            sums.append(squares)
    return sums[0] + sums[1]


def fore_own_kernel(first, units, dense_ref, inner_ref, mine_ref, scale_ref, *refs):
    past_ref, past_scale_ref = (None, None) if first else refs[:2]
    part_ref, sum_ref, raw_ref, wide_ref = refs[-4:]
    parts = [(inner_ref, 1), (mine_ref, 1)]
    sum_ref[...] = fore_vector(parts, wide_ref, raw_ref, (scale_ref, past_ref, past_scale_ref))
    fore_pairs(dense_ref, units, wide_ref, None, part_ref, 0)


def fore_send_kernel(first, units, dense_ref, outer_ref, part_ref, sum_ref, scale_ref, *refs):
    past_ref, past_scale_ref = (None, None) if first else refs[:2]
    send_ref, wide_ref, raw_ref = refs[-3:]
    squares = fore_vector([(outer_ref, 2)], wide_ref, raw_ref, (scale_ref, past_ref, past_scale_ref))
    row = squares_row([squares, sum_ref[...]])
    send_ref[-NORM_ROWS:, :] = jnp.broadcast_to(row, (NORM_ROWS, TILE))
    fore_pairs(dense_ref, units, wide_ref, part_ref, send_ref, 0)


def fore_keep_kernel(units, dense_ref, wide_ref, part_ref, keep_ref):
    start = keep_ref.shape[0] // TILE
    fore_pairs(dense_ref, units, wide_ref, part_ref, keep_ref, start)


def product_call(body, dense, operands, shapes, scratch=()):
    return pl.pallas_call(
        body,
        in_specs=[WHOLE] * (1 + len(operands)),
        out_specs=[WHOLE] * len(shapes),
        out_shape=shapes,
        scratch_shapes=scratch,
        compiler_params=pltpu.CompilerParams(vmem_limit_bytes=12 * 1024 * 1024),
        cost_estimate=pl.CostEstimate(
            flops=2 * TILE * dense.size, bytes_accessed=dense.size, transcendentals=0
        ),
    )(dense, *operands)


def float_rows(rows):
    return jax.ShapeDtypeStruct((rows, TILE), jnp.float32)


def back_product(order, dense, operands, first):
    rows, cells = dense.shape[0], CB_DEV * TILE
    shapes = [float_rows(cells // 4 + NORM_ROWS), jax.ShapeDtypeStruct((TILE // 2, rows), dense.dtype)]
    shapes += [] if first else [float_rows(rows // 2)]
    send, flat, *raw = product_call(
        functools.partial(back_send_kernel, first, order[:2]), dense, operands, shapes
    )


    body = functools.partial(back_keep_kernel, order[2:])
    (keep,) = product_call(body, dense, [flat], [float_rows(cells // 4)])
    return send, keep, *raw


def fore_own_product(order, dense, operands, first):
    rows, cells = dense.shape[0], CB_DEV * TILE
    return product_call(
        functools.partial(fore_own_kernel, first, order[2:]),
        dense,
        operands,
        [float_rows(rows // 2), float_rows(NORM_ROWS), float_rows(cells // 4)],
        [pltpu.VMEM((cells // 2, TILE), dense.dtype)],
    )


def fore_product(order, dense, operands, first):
    rows, cells = dense.shape[0], CB_DEV * TILE
    shapes = [
        float_rows(rows // 4 + NORM_ROWS),
        jax.ShapeDtypeStruct((cells // 2, TILE), dense.dtype),
        float_rows(cells // 4),
    ]
    send, wide, raw = product_call(
        functools.partial(fore_send_kernel, first, order[:2]), dense, operands, shapes
    )

    def keep(wide):
        body = functools.partial(fore_keep_kernel, order[:2])
        return product_call(body, dense, [wide, operands[1]], [float_rows(rows // 4)])[0]

    return send, (keep, wide), raw


def rotation(norms):
    betas, alphas = [norm_of(ref) for ref in norms[0::2]], [norm_of(ref) for ref in norms[1::2]]
    resid_bar, diag_bar = betas[0], alphas[0]
    steps = []
    for j in range(len(alphas)):
        radius = jnp.sqrt(diag_bar * diag_bar + betas[j + 1] * betas[j + 1])
        rotate_cos = diag_bar / radius
        rotate_sin = betas[j + 1] / radius
        step_size = rotate_cos * resid_bar
        resid_bar = rotate_sin * resid_bar
        coupling = None
        if j + 1 < len(alphas):
            coupling = rotate_sin * alphas[j + 1] / radius
            diag_bar = -rotate_cos * alphas[j + 1]
        steps.append((step_size / radius, coupling))
    misfit = resid_bar / betas[0]
    return alphas, betas, steps, misfit, misfit * rotate_cos


def store_in_order(out_ref, mask, pair, low, values):
    pairs = out_ref.shape[0] // PAIR // UNITS
    start = (((pair // pairs) ^ mask) * pairs + pair % pairs) * PAIR
    ours, theirs = values
    even = pl.ds(pl.multiple_of(start, TILE), TILE)
    odd = pl.ds(pl.multiple_of(start + TILE, TILE), TILE)
    out_ref[even, :] = jnp.where(low, ours, turned(theirs))
    out_ref[odd, :] = jnp.where(low, turned(ours), theirs)


def model_kernel(count, mask_ref, *refs):
    ins, (model_ref, misfit_ref) = refs[:-2], refs[-2:]
    chains = [ins[: len(ins) // 2], ins[len(ins) // 2 :]]
    low = low_lanes((TILE, TILE))
    rotations = [rotation(refs_[2 * count :]) for refs_ in chains]
    misfits = [jnp.broadcast_to(r[3], misfit_ref.shape) for r in rotations]
    misfit_ref[...] = jnp.where(low_lanes(misfit_ref.shape), misfits[0], misfits[1])
    pairs = model_ref.shape[0] // PAIR // UNITS
    for pair in range(model_ref.shape[0] // PAIR):
        values = []
        for order, refs_, (alphas, _, steps, _, _) in zip(UNIT_ORDERS, chains, rotations):
            slot = order.index(pair // pairs)
            rows = rows_of(slot % 2 * pairs + pair % pairs)
            search = total = None
            for j in range(count):
                right = refs_[2 * j + slot // 2][rows, :] / alphas[j]
                search = right if j == 0 else right - steps[j - 1][1] * search
                total = steps[j][0] * search if j == 0 else total + steps[j][0] * search
            values.append(total)
        store_in_order(model_ref, mask_ref[0], pair, low, values)


def gradient_kernel(mask_ref, *refs):
    ins, gradient_ref = refs[:-1], refs[-1]
    chains = [ins[: len(ins) // 2], ins[len(ins) // 2 :]]
    low = low_lanes((TILE, TILE))
    vectors = []
    factors = []
    for outer_ref, inner_ref, mine_ref, past_ref, own_past_ref, *norms in chains:
        halves = [
            next_vector(parts, None, norms[-1], past, norms[-2])
            for parts, past in [
                ([(outer_ref, 2)], past_ref),
                ([(inner_ref, 1), (mine_ref, 1)], own_past_ref),
            ]
        ]
        vectors.append([value for half in halves for _, value, _ in half])
        factors.append(rotation(norms)[-1])
    pairs = gradient_ref.shape[0] // PAIR // UNITS
    for pair in range(gradient_ref.shape[0] // PAIR):
        values = []
        for order, vector, factor in zip(UNIT_ORDERS, vectors, factors):
            slot = order.index(pair // pairs)
            values.append(factor * vector[slot * pairs + pair % pairs])
        store_in_order(gradient_ref, mask_ref[0], pair, low, values)


def last_call(body, mask, operands, shapes):
    return pl.pallas_call(
        body,
        in_specs=[SCALARS] + [WHOLE] * len(operands),
        out_specs=[WHOLE] * len(shapes),
        out_shape=[jax.ShapeDtypeStruct(shape, jnp.float32) for shape in shapes],
        compiler_params=pltpu.CompilerParams(vmem_limit_bytes=12 * 1024 * 1024),
        cost_estimate=pl.CostEstimate(
            flops=0, bytes_accessed=8 * shapes[0][0] * TILE, transcendentals=0
        ),
    )(mask, *operands)


def on_device(row_count, col_count, kernel, pattern, counts, delays):
    row_bits = list(range(row_count.bit_length() - 1))
    col_bits = list(range(col_count.bit_length() - 1))
    row_index = lax.axis_index("rows")
    core = lax.axis_index("cols") & 1

    near, far, *rest = row_bits
    orders = [[near, far, *rest, far, near], [far, near, *rest, near, far]]
    steps = len(orders[0])

    def swap_rows(second, value, level):
        pairs = []
        for row in range(row_count):
            for col in range(col_count):
                partner = row ^ (1 << orders[col & 1 ^ second][level])
                pairs.append((row * col_count + col, partner * col_count + col))
        return lax.ppermute(value, ("rows", "cols"), pairs)

    def swap_cols(value, level):
        return lax.ppermute(value, "cols", [(i, i ^ (1 << level)) for i in range(col_count)])

    bits = [(row_index >> bit) & 1 for bit in row_bits[:2]]
    outer_side = jnp.where(core == 0, bits[0], bits[1])
    inner_side = jnp.where(core == 0, bits[1], bits[0])
    mask = ((1 - outer_side) * 2 + (1 - inner_side)).astype(jnp.int32)
    blocks = jnp.arange(CB_DEV, dtype=jnp.int32)
    unit = CB_DEV // UNITS
    places = ((blocks // unit) ^ mask) * unit + blocks % unit
    flip = ((1 - core) * (kernel.shape[0] // 2)).astype(jnp.int32).reshape(1)
    mask = mask.reshape(1)

    dense, *lefts = fill_dense(kernel, pattern, counts, places, flip, delays)

    def tied(value, other):
        return lax.optimization_barrier((value, other))[0]

    def kept_half(kept, ahead):
        half, operand = kept
        return half(tied(operand, ahead))

    def reduce_rows(swap_rows, send, keep):
        half = keep.shape[0]
        got, _ = yield swap_rows, send, 0
        keep = keep + got[:half]
        norm = send[half:] + got[half:]
        send, mine = keep[: half // 2], keep[half // 2 :]
        for level in range(1, len(row_bits)):
            got, _ = yield swap_rows, jnp.concatenate([send, norm]), level
            norm = norm + got[half // 2 :]
            send = mine = mine + got[: half // 2]
        inner, _ = yield swap_rows, mine, steps - 2
        outer, ahead = yield swap_rows, jnp.concatenate([inner, mine]), steps - 1
        return [outer, inner, mine], norm, ahead

    def reduce_cols(send, kept):
        half = send.shape[0] - NORM_ROWS
        got, ahead = yield swap_cols, send, 0
        own = kept_half(kept, ahead) + got[:half]
        norm = send[half:] + got[half:]
        for bit in col_bits[1:]:
            got, _ = yield swap_cols, jnp.concatenate([own, norm]), bit
            norm = norm + got[half:]
            own = own + got[:half]
        other, _ = yield swap_cols, own, 0
        return [other, own], norm

    def chain(second, left):
        order = UNIT_ORDERS[second]
        swap = functools.partial(swap_rows, second)
        send, keep = back_product(order, dense, [left], True)
        totals, norm, ahead = yield from reduce_rows(swap, send, keep)
        norms = [norm]
        rights = []
        for iteration in range(ITERS):
            outer, *own = totals
            pasts = [[right, norms[-2]] for right in rights[-1]] if rights else [[], []]
            own = [tied(own[0], ahead), own[1]]
            part, squares, own_right = fore_own_product(
                order, dense, [*own, norms[-1], *pasts[1]], not rights
            )
            send, keep, right = fore_product(
                order, dense, [outer, part, squares, norms[-1], *pasts[0]], not rights
            )
            rights.append([right, own_right])
            halves, norm = yield from reduce_cols(send, keep)
            norms.append(norm)
            send, keep, left = back_product(
                order, dense, [*halves, norms[-1], left, norms[-2]], False
            )
            totals, norm, ahead = yield from reduce_rows(swap, send, keep)
            norms.append(norm)
        return rights, norms, totals

    runs = [chain(second, left) for second, left in enumerate(lefts)]
    wanted = [next(run) for run in runs]
    chains = [None] * len(runs)
    gots = [None] * len(runs)
    swap, value, level = wanted[0]
    gots[0] = swap(value, level)
    latest = wanted[1][1]
    turn = 0
    while None in chains:
        mine = 0 if turn < BEHIND else (turn - BEHIND) % 2
        turn += 1
        if chains[mine] is not None:
            continue
        if gots[mine] is None:
            swap, value, level = wanted[mine]
            latest = tied(value, latest)
        else:
            try:
                swap, latest, level = runs[mine].send((tied(gots[mine], latest), latest))
            except StopIteration as stop:
                chains[mine] = stop.value
                continue
        gots[mine] = swap(latest, level)

    cells = CB_DEV * TILE
    model, misfit = last_call(
        functools.partial(model_kernel, ITERS),
        mask,
        [operand for rights, norms, _ in chains for operand in [*sum(rights, []), *norms]],
        [(cells, TILE), (NORM_ROWS, TILE)],
    )
    (gradient,) = last_call(
        gradient_kernel,
        mask,
        [operand for rights, norms, totals in chains for operand in [*totals, *rights[-1], *norms]],
        [(cells, TILE)],
    )
    return (model, gradient, misfit[0])


def solution(mesh):
    placed = (P("rows", "cols", None, None), P("rows", "cols"), P("rows", "cols"), P("rows", None))

    def local(kernel, pattern, counts, delays):
        return on_device(
            mesh.shape["rows"], mesh.shape["cols"], kernel, pattern, counts, delays
        )

    return jax.shard_map(
        local,
        mesh=mesh,
        in_specs=placed,
        out_specs=(P("cols", None), P("cols", None), P()),
        check_vma=False,
    )
```

```python
import functools

import jax
import jax.numpy as jnp
from jax import lax
from jax.experimental import pallas as pl
from jax.experimental.pallas import tpu as pltpu
from jax.sharding import PartitionSpec as P

CB_DEV = 24
ITERS = 2
TILE = 128
PAIR = 2 * TILE
UNITS = 4
NORM_ROWS = 8
UNIT_ORDERS = ((0, 1, 2, 3), (0, 2, 1, 3))

tiny_eps = 1e-06

WHOLE = pl.BlockSpec(memory_space=pltpu.VMEM)
SCALARS = pl.BlockSpec(memory_space=pltpu.SMEM)


def low_lanes(shape):
    return lax.broadcasted_iota(jnp.int32, shape, 1) < shape[1] // 2


def turned(value):
    return pltpu.roll(value, value.shape[1] // 2, 1)


def rows_of(pair, size=TILE):
    return slice(pair * size, (pair + 1) * size)


def fill_kernel(
    place_ref, flip_ref, pattern_in, counts_in, delays_in, tiles_in,
    dense_ref, even_left_ref, odd_left_ref, pattern_ref, counts_ref, delays_ref, tiles_ref, arrived,
):
    flip = flip_ref[0]
    row_blocks = tiles_in.shape[0]
    small = [
        pltpu.make_async_copy(source, target, arrived.at[2 * row_blocks + i])
        for i, (source, target) in enumerate(
            [(pattern_in, pattern_ref), (counts_in, counts_ref), (delays_in, delays_ref)]
        )
    ]
    for copy in small:
        copy.start()

    half = tiles_in.shape[1] // 2

    def fetch(position, upper):
        slots = pl.ds(upper * half, half)
        return pltpu.make_async_copy(
            tiles_in.at[position ^ flip, slots],
            tiles_ref.at[position, slots],
            arrived.at[upper * row_blocks + position],
        )

    for position in range(row_blocks):
        fetch(position, 0).start()
    for copy in small:
        copy.wait()
    for position in range(row_blocks):

        @pl.when(counts_ref[position ^ flip] > half)
        def _():
            fetch(position, 1).start()

    low = low_lanes((TILE, TILE))
    for pair in range(row_blocks // 2):
        source = (pair ^ (flip // 2)) * PAIR
        even = delays_ref[pl.ds(pl.multiple_of(source, TILE), TILE), :]
        odd = delays_ref[pl.ds(pl.multiple_of(source + TILE, TILE), TILE), :]
        even_left_ref[rows_of(pair), :] = jnp.where(low, even, turned(odd))
        odd_left_ref[rows_of(pair), :] = jnp.where(low, turned(even), odd)

    @pl.loop(0, row_blocks)
    def _(position):
        rows = pl.ds(pl.multiple_of(position * TILE, TILE), TILE)
        block = position ^ flip
        count = counts_ref[block]

        def place(tile):
            column = jnp.where(tile < count, place_ref[pattern_ref[block, tile]], CB_DEV)
            lanes = pl.ds(pl.multiple_of(column * TILE, TILE), TILE)
            dense_ref[rows, lanes] = tiles_ref[position, tile]

        dense_ref[rows, :] = jnp.zeros((TILE, dense_ref.shape[1]), dense_ref.dtype)
        fetch(position, 0).wait()
        for tile in range(half):
            place(tile)

        @pl.when(count > half)
        def _():
            fetch(position, 1).wait()
            for tile in range(half, 2 * half):
                place(tile)


def fill_dense(kernel, pattern, counts, places, flip, delays):
    row_blocks = kernel.shape[0]
    rows = row_blocks * TILE
    left = jax.ShapeDtypeStruct((rows // 2, TILE), jnp.float32)
    return pl.pallas_call(
        fill_kernel,
        in_specs=[SCALARS] * 2 + [pl.BlockSpec(memory_space=pltpu.HBM)] * 4,
        out_specs=[WHOLE] * 3,
        out_shape=[jax.ShapeDtypeStruct((rows, (CB_DEV + 1) * TILE), kernel.dtype), left, left],
        scratch_shapes=[
            pltpu.SMEM(pattern.shape, jnp.int32),
            pltpu.SMEM((row_blocks,), jnp.int32),
            pltpu.VMEM(delays.shape, delays.dtype),
            pltpu.VMEM(kernel.shape, kernel.dtype),
            pltpu.SemaphoreType.DMA((2 * row_blocks + 3,)),
        ],
        compiler_params=pltpu.CompilerParams(vmem_limit_bytes=16 * 1024 * 1024),
        cost_estimate=pl.CostEstimate(
            flops=0, bytes_accessed=2 * kernel.size, transcendentals=0
        ),
    )(
        places,
        flip,
        *(pltpu.with_memory_space_constraint(x, pltpu.HBM) for x in (pattern, counts.reshape(-1), delays, kernel)),
    )


def norm_of(ref):
    return jnp.sqrt(ref[0:1, :] + tiny_eps)


def squares_row(sums):
    while len(sums) > 1:
        sums = [sums[i] + sums[i + 1] for i in range(0, len(sums), 2)]
    row = jnp.sum(sums[0], axis=0, keepdims=True)
    return row + turned(row)


def next_vector(parts, raw_ref, scale_ref, past_ref, past_scale_ref):
    if scale_ref is not None:
        scale = norm_of(scale_ref)
    if past_ref is not None:
        past_scale = norm_of(past_scale_ref)
    position = 0
    for part, units in parts:
        pairs = part.shape[0] // TILE // units
        for unit in range(units):
            squares = jnp.zeros((NORM_ROWS, TILE), jnp.float32)
            for pair in range(pairs):
                value = part[rows_of(unit * pairs + pair), :]
                if scale_ref is not None:
                    value = value / scale
                if past_ref is not None:
                    value = value - scale * (past_ref[rows_of(position), :] / past_scale)
                if raw_ref is not None:
                    raw_ref[rows_of(position), :] = value
                squares += jnp.sum((value * value).reshape(-1, NORM_ROWS, TILE), axis=0)
                yield position, value, squares if pair == pairs - 1 else None
                position += 1


def back_pairs(dense_ref, turned_ref, out_ref, units):
    pairs = CB_DEV // 2 // UNITS
    for pair in range(pairs * len(units)):
        column = units[pair // pairs] * pairs + pair % pairs
        product = jnp.dot(
            turned_ref[...],
            dense_ref[:, rows_of(column, PAIR)],
            preferred_element_type=jnp.float32,
        )
        stacked = jnp.concatenate([product[:, :TILE], product[:, TILE:]], axis=0)
        out_ref[rows_of(pair), :] = stacked.T


def back_send_kernel(first, units, *refs):
    if first:
        dense_ref, own_ref, send_ref, turned_ref = refs
        parts, raw_ref, scales = [(own_ref, 2)], None, (None, None, None)
    else:
        (dense_ref, other_ref, own_ref, scale_ref, past_ref, past_scale_ref,
         send_ref, turned_ref, raw_ref) = refs
        parts, scales = [(other_ref, 1), (own_ref, 1)], (scale_ref, past_ref, past_scale_ref)
    sums = []
    half = turned_ref.shape[0]
    for pair, value, squares in next_vector(parts, raw_ref, *scales):
        flat = value.T.astype(turned_ref.dtype)
        turned_ref[:, rows_of(2 * pair)] = flat[:half]
        turned_ref[:, rows_of(2 * pair + 1)] = flat[half:]
        if squares is not None:
            sums.append(squares)
    send_ref[-NORM_ROWS:, :] = jnp.broadcast_to(squares_row(sums), (NORM_ROWS, TILE))
    back_pairs(dense_ref, turned_ref, send_ref, units)


def back_keep_kernel(units, dense_ref, turned_ref, keep_ref):
    back_pairs(dense_ref, turned_ref, keep_ref, units)


def fore_pairs(dense_ref, units, wide_ref, add_ref, out_ref, start):
    depth = wide_ref.shape[0] // len(units)
    runs = [(unit * depth, i * depth, depth) for i, unit in enumerate(units)]
    if units[1] == units[0] + 1:
        runs = [(units[0] * depth, 0, 2 * depth)]
    low = low_lanes((TILE, TILE))
    step = 2
    pairs = out_ref.shape[0] // TILE
    for pair in range(0, pairs, step):
        rows = slice((start + pair) * PAIR, (start + pair + step) * PAIR)
        product = sum(
            jnp.dot(
                dense_ref[rows, cell : cell + size],
                wide_ref[row : row + size, :],
                preferred_element_type=jnp.float32,
            )
            for cell, row, size in runs
        )
        for i in range(step):
            even, odd = product[rows_of(2 * i), :], product[rows_of(2 * i + 1), :]
            value = jnp.where(low, even, odd)
            if add_ref is not None:
                value = value + add_ref[rows_of(start + pair + i), :]
            out_ref[rows_of(pair + i), :] = value


def fore_vector(parts, wide_ref, raw_ref, scales):
    low = low_lanes((TILE, TILE))
    sums = []
    for pair, value, squares in next_vector(parts, raw_ref, *scales):
        other = turned(value)
        wide_ref[rows_of(2 * pair), :] = jnp.where(low, value, other).astype(wide_ref.dtype)
        wide_ref[rows_of(2 * pair + 1), :] = jnp.where(low, other, value).astype(wide_ref.dtype)
        if squares is not None:
            sums.append(squares)
    return sums[0] + sums[1]


def fore_own_kernel(first, units, dense_ref, inner_ref, mine_ref, scale_ref, *refs):
    past_ref, past_scale_ref = (None, None) if first else refs[:2]
    part_ref, sum_ref, raw_ref, wide_ref = refs[-4:]
    parts = [(inner_ref, 1), (mine_ref, 1)]
    sum_ref[...] = fore_vector(parts, wide_ref, raw_ref, (scale_ref, past_ref, past_scale_ref))
    fore_pairs(dense_ref, units, wide_ref, None, part_ref, 0)


def fore_send_kernel(first, units, dense_ref, outer_ref, part_ref, sum_ref, scale_ref, *refs):
    past_ref, past_scale_ref = (None, None) if first else refs[:2]
    send_ref, wide_ref, raw_ref = refs[-3:]
    squares = fore_vector([(outer_ref, 2)], wide_ref, raw_ref, (scale_ref, past_ref, past_scale_ref))
    row = squares_row([squares, sum_ref[...]])
    send_ref[-NORM_ROWS:, :] = jnp.broadcast_to(row, (NORM_ROWS, TILE))
    fore_pairs(dense_ref, units, wide_ref, part_ref, send_ref, 0)


def fore_keep_kernel(units, dense_ref, wide_ref, part_ref, keep_ref):
    start = keep_ref.shape[0] // TILE
    fore_pairs(dense_ref, units, wide_ref, part_ref, keep_ref, start)


def product_call(body, dense, operands, shapes, scratch=()):
    return pl.pallas_call(
        body,
        in_specs=[WHOLE] * (1 + len(operands)),
        out_specs=[WHOLE] * len(shapes),
        out_shape=shapes,
        scratch_shapes=scratch,
        compiler_params=pltpu.CompilerParams(vmem_limit_bytes=12 * 1024 * 1024),
        cost_estimate=pl.CostEstimate(
            flops=2 * TILE * dense.size, bytes_accessed=dense.size, transcendentals=0
        ),
    )(dense, *operands)


def float_rows(rows):
    return jax.ShapeDtypeStruct((rows, TILE), jnp.float32)


def back_product(order, dense, operands, first):
    rows, cells = dense.shape[0], CB_DEV * TILE
    shapes = [float_rows(cells // 4 + NORM_ROWS), jax.ShapeDtypeStruct((TILE // 2, rows), dense.dtype)]
    shapes += [] if first else [float_rows(rows // 2)]
    send, flat, *raw = product_call(
        functools.partial(back_send_kernel, first, order[:2]), dense, operands, shapes
    )


    body = functools.partial(back_keep_kernel, order[2:])
    (keep,) = product_call(body, dense, [flat], [float_rows(cells // 4)])
    return send, keep, *raw


def fore_own_product(order, dense, operands, first):
    rows, cells = dense.shape[0], CB_DEV * TILE
    return product_call(
        functools.partial(fore_own_kernel, first, order[2:]),
        dense,
        operands,
        [float_rows(rows // 2), float_rows(NORM_ROWS), float_rows(cells // 4)],
        [pltpu.VMEM((cells // 2, TILE), dense.dtype)],
    )


def fore_product(order, dense, operands, first):
    rows, cells = dense.shape[0], CB_DEV * TILE
    shapes = [
        float_rows(rows // 4 + NORM_ROWS),
        jax.ShapeDtypeStruct((cells // 2, TILE), dense.dtype),
        float_rows(cells // 4),
    ]
    send, wide, raw = product_call(
        functools.partial(fore_send_kernel, first, order[:2]), dense, operands, shapes
    )

    def keep(wide):
        body = functools.partial(fore_keep_kernel, order[:2])
        return product_call(body, dense, [wide, operands[1]], [float_rows(rows // 4)])[0]

    return send, (keep, wide), raw


def rotation(norms):
    betas, alphas = [norm_of(ref) for ref in norms[0::2]], [norm_of(ref) for ref in norms[1::2]]
    resid_bar, diag_bar = betas[0], alphas[0]
    steps = []
    for j in range(len(alphas)):
        radius = jnp.sqrt(diag_bar * diag_bar + betas[j + 1] * betas[j + 1])
        rotate_cos = diag_bar / radius
        rotate_sin = betas[j + 1] / radius
        step_size = rotate_cos * resid_bar
        resid_bar = rotate_sin * resid_bar
        coupling = None
        if j + 1 < len(alphas):
            coupling = rotate_sin * alphas[j + 1] / radius
            diag_bar = -rotate_cos * alphas[j + 1]
        steps.append((step_size / radius, coupling))
    misfit = resid_bar / betas[0]
    return alphas, betas, steps, misfit, misfit * rotate_cos


def store_in_order(out_ref, mask, pair, low, values):
    pairs = out_ref.shape[0] // PAIR // UNITS
    start = (((pair // pairs) ^ mask) * pairs + pair % pairs) * PAIR
    ours, theirs = values
    even = pl.ds(pl.multiple_of(start, TILE), TILE)
    odd = pl.ds(pl.multiple_of(start + TILE, TILE), TILE)
    out_ref[even, :] = jnp.where(low, ours, turned(theirs))
    out_ref[odd, :] = jnp.where(low, turned(ours), theirs)


def model_kernel(count, mask_ref, *refs):
    ins, (model_ref, misfit_ref) = refs[:-2], refs[-2:]
    chains = [ins[: len(ins) // 2], ins[len(ins) // 2 :]]
    low = low_lanes((TILE, TILE))
    rotations = [rotation(refs_[2 * count :]) for refs_ in chains]
    misfits = [jnp.broadcast_to(r[3], misfit_ref.shape) for r in rotations]
    misfit_ref[...] = jnp.where(low_lanes(misfit_ref.shape), misfits[0], misfits[1])
    pairs = model_ref.shape[0] // PAIR // UNITS
    for pair in range(model_ref.shape[0] // PAIR):
        values = []
        for order, refs_, (alphas, _, steps, _, _) in zip(UNIT_ORDERS, chains, rotations):
            slot = order.index(pair // pairs)
            rows = rows_of(slot % 2 * pairs + pair % pairs)
            search = total = None
            for j in range(count):
                right = refs_[2 * j + slot // 2][rows, :] / alphas[j]
                search = right if j == 0 else right - steps[j - 1][1] * search
                total = steps[j][0] * search if j == 0 else total + steps[j][0] * search
            values.append(total)
        store_in_order(model_ref, mask_ref[0], pair, low, values)


def gradient_kernel(mask_ref, *refs):
    ins, gradient_ref = refs[:-1], refs[-1]
    chains = [ins[: len(ins) // 2], ins[len(ins) // 2 :]]
    low = low_lanes((TILE, TILE))
    vectors = []
    factors = []
    for outer_ref, inner_ref, mine_ref, past_ref, own_past_ref, *norms in chains:
        halves = [
            next_vector(parts, None, norms[-1], past, norms[-2])
            for parts, past in [
                ([(outer_ref, 2)], past_ref),
                ([(inner_ref, 1), (mine_ref, 1)], own_past_ref),
            ]
        ]
        vectors.append([value for half in halves for _, value, _ in half])
        factors.append(rotation(norms)[-1])
    pairs = gradient_ref.shape[0] // PAIR // UNITS
    for pair in range(gradient_ref.shape[0] // PAIR):
        values = []
        for order, vector, factor in zip(UNIT_ORDERS, vectors, factors):
            slot = order.index(pair // pairs)
            values.append(factor * vector[slot * pairs + pair % pairs])
        store_in_order(gradient_ref, mask_ref[0], pair, low, values)


def last_call(body, mask, operands, shapes):
    return pl.pallas_call(
        body,
        in_specs=[SCALARS] + [WHOLE] * len(operands),
        out_specs=[WHOLE] * len(shapes),
        out_shape=[jax.ShapeDtypeStruct(shape, jnp.float32) for shape in shapes],
        compiler_params=pltpu.CompilerParams(vmem_limit_bytes=12 * 1024 * 1024),
        cost_estimate=pl.CostEstimate(
            flops=0, bytes_accessed=8 * shapes[0][0] * TILE, transcendentals=0
        ),
    )(mask, *operands)


def on_device(row_count, col_count, kernel, pattern, counts, delays):
    row_bits = list(range(row_count.bit_length() - 1))
    col_bits = list(range(col_count.bit_length() - 1))
    row_index = lax.axis_index("rows")
    core = lax.axis_index("cols") & 1

    near, far, *rest = row_bits
    orders = [[near, far, *rest, far, near], [far, near, *rest, near, far]]
    steps = len(orders[0])

    def swap_rows(second, value, level):
        pairs = []
        for row in range(row_count):
            for col in range(col_count):
                partner = row ^ (1 << orders[col & 1 ^ second][level])
                pairs.append((row * col_count + col, partner * col_count + col))
        return lax.ppermute(value, ("rows", "cols"), pairs)

    def swap_cols(value, level):
        return lax.ppermute(value, "cols", [(i, i ^ (1 << level)) for i in range(col_count)])

    bits = [(row_index >> bit) & 1 for bit in row_bits[:2]]
    outer_side = jnp.where(core == 0, bits[0], bits[1])
    inner_side = jnp.where(core == 0, bits[1], bits[0])
    mask = ((1 - outer_side) * 2 + (1 - inner_side)).astype(jnp.int32)
    blocks = jnp.arange(CB_DEV, dtype=jnp.int32)
    unit = CB_DEV // UNITS
    places = ((blocks // unit) ^ mask) * unit + blocks % unit
    flip = ((1 - core) * (kernel.shape[0] // 2)).astype(jnp.int32).reshape(1)
    mask = mask.reshape(1)

    dense, *lefts = fill_dense(kernel, pattern, counts, places, flip, delays)

    def tied(value, other):
        return lax.optimization_barrier((value, other))[0]

    def kept_half(kept, ahead):
        half, operand = kept
        return half(tied(operand, ahead))

    def reduce_rows(swap_rows, send, keep):
        half = keep.shape[0]
        got, _ = yield swap_rows, send, 0
        keep = keep + got[:half]
        norm = send[half:] + got[half:]
        send, mine = keep[: half // 2], keep[half // 2 :]
        for level in range(1, len(row_bits)):
            got, _ = yield swap_rows, jnp.concatenate([send, norm]), level
            norm = norm + got[half // 2 :]
            send = mine = mine + got[: half // 2]
        inner, _ = yield swap_rows, mine, steps - 2
        outer, ahead = yield swap_rows, jnp.concatenate([inner, mine]), steps - 1
        return [outer, inner, mine], norm, ahead

    def reduce_cols(send, kept):
        half = send.shape[0] - NORM_ROWS
        got, ahead = yield swap_cols, send, 0
        own = kept_half(kept, ahead) + got[:half]
        norm = send[half:] + got[half:]
        for bit in col_bits[1:]:
            got, _ = yield swap_cols, jnp.concatenate([own, norm]), bit
            norm = norm + got[half:]
            own = own + got[:half]
        other, _ = yield swap_cols, own, 0
        return [other, own], norm

    def chain(second, left):
        order = UNIT_ORDERS[second]
        swap = functools.partial(swap_rows, second)
        send, keep = back_product(order, dense, [left], True)
        totals, norm, ahead = yield from reduce_rows(swap, send, keep)
        norms = [norm]
        rights = []
        for iteration in range(ITERS):
            outer, *own = totals
            pasts = [[right, norms[-2]] for right in rights[-1]] if rights else [[], []]
            own = [tied(own[0], ahead), own[1]]
            part, squares, own_right = fore_own_product(
                order, dense, [*own, norms[-1], *pasts[1]], not rights
            )
            send, keep, right = fore_product(
                order, dense, [outer, part, squares, norms[-1], *pasts[0]], not rights
            )
            rights.append([right, own_right])
            halves, norm = yield from reduce_cols(send, keep)
            norms.append(norm)
            send, keep, left = back_product(
                order, dense, [*halves, norms[-1], left, norms[-2]], False
            )
            totals, norm, ahead = yield from reduce_rows(swap, send, keep)
            norms.append(norm)
        return rights, norms, totals

    runs = [chain(second, left) for second, left in enumerate(lefts)]
    wanted = [next(run) for run in runs]
    chains = [None] * len(runs)
    gots = [None] * len(runs)
    latest = None
    for mine, (swap, value, level) in enumerate(wanted):
        latest = value if latest is None else tied(value, latest)
        gots[mine] = swap(latest, level)
    turn = 0
    while None in chains:
        mine = turn % 2
        turn += 1
        if chains[mine] is not None:
            continue
        try:
            swap, latest, level = runs[mine].send((tied(gots[mine], latest), latest))
        except StopIteration as stop:
            chains[mine] = stop.value
            continue
        gots[mine] = swap(latest, level)

    cells = CB_DEV * TILE
    model, misfit = last_call(
        functools.partial(model_kernel, ITERS),
        mask,
        [operand for rights, norms, _ in chains for operand in [*sum(rights, []), *norms]],
        [(cells, TILE), (NORM_ROWS, TILE)],
    )
    (gradient,) = last_call(
        gradient_kernel,
        mask,
        [operand for rights, norms, totals in chains for operand in [*totals, *rights[-1], *norms]],
        [(cells, TILE)],
    )
    return (model, gradient, misfit[0])


def solution(mesh):
    placed = (P("rows", "cols", None, None), P("rows", "cols"), P("rows", "cols"), P("rows", None))

    def local(kernel, pattern, counts, delays):
        return on_device(
            mesh.shape["rows"], mesh.shape["cols"], kernel, pattern, counts, delays
        )

    return jax.shard_map(
        local,
        mesh=mesh,
        in_specs=placed,
        out_specs=(P("cols", None), P("cols", None), P()),
        check_vma=False,
    )
```

```python
import functools

import jax
import jax.numpy as jnp
from jax import lax
from jax.experimental import pallas as pl
from jax.experimental.pallas import tpu as pltpu
from jax.sharding import PartitionSpec as P

CB_DEV = 24
ITERS = 2
TILE = 128
PAIR = 2 * TILE
UNITS = 4
NORM_ROWS = 8
UNIT_ORDERS = ((0, 1, 2, 3), (0, 2, 1, 3))
BEHIND = 1

tiny_eps = 1e-06

WHOLE = pl.BlockSpec(memory_space=pltpu.VMEM)
SCALARS = pl.BlockSpec(memory_space=pltpu.SMEM)


def low_lanes(shape):
    return lax.broadcasted_iota(jnp.int32, shape, 1) < shape[1] // 2


def turned(value):
    return pltpu.roll(value, value.shape[1] // 2, 1)


def rows_of(pair, size=TILE):
    return slice(pair * size, (pair + 1) * size)


def fill_kernel(
    place_ref, flip_ref, pattern_in, counts_in, delays_in, tiles_in,
    dense_ref, even_left_ref, odd_left_ref, pattern_ref, counts_ref, delays_ref, tiles_ref, arrived,
):
    flip = flip_ref[0]
    row_blocks = tiles_in.shape[0]
    small = [
        pltpu.make_async_copy(source, target, arrived.at[2 * row_blocks + i])
        for i, (source, target) in enumerate(
            [(pattern_in, pattern_ref), (counts_in, counts_ref), (delays_in, delays_ref)]
        )
    ]
    for copy in small:
        copy.start()

    half = tiles_in.shape[1] // 2

    def fetch(position, upper):
        slots = pl.ds(upper * half, half)
        return pltpu.make_async_copy(
            tiles_in.at[position ^ flip, slots],
            tiles_ref.at[position, slots],
            arrived.at[upper * row_blocks + position],
        )

    for position in range(row_blocks):
        fetch(position, 0).start()
    for copy in small:
        copy.wait()
    for position in range(row_blocks):

        @pl.when(counts_ref[position ^ flip] > half)
        def _():
            fetch(position, 1).start()

    low = low_lanes((TILE, TILE))
    for pair in range(row_blocks // 2):
        source = (pair ^ (flip // 2)) * PAIR
        even = delays_ref[pl.ds(pl.multiple_of(source, TILE), TILE), :]
        odd = delays_ref[pl.ds(pl.multiple_of(source + TILE, TILE), TILE), :]
        even_left_ref[rows_of(pair), :] = jnp.where(low, even, turned(odd))
        odd_left_ref[rows_of(pair), :] = jnp.where(low, turned(even), odd)

    @pl.loop(0, row_blocks)
    def _(position):
        rows = pl.ds(pl.multiple_of(position * TILE, TILE), TILE)
        block = position ^ flip
        count = counts_ref[block]

        def place(tile):
            column = jnp.where(tile < count, place_ref[pattern_ref[block, tile]], CB_DEV)
            lanes = pl.ds(pl.multiple_of(column * TILE, TILE), TILE)
            dense_ref[rows, lanes] = tiles_ref[position, tile]

        dense_ref[rows, :] = jnp.zeros((TILE, dense_ref.shape[1]), dense_ref.dtype)
        fetch(position, 0).wait()
        for tile in range(half):
            place(tile)

        @pl.when(count > half)
        def _():
            fetch(position, 1).wait()
            for tile in range(half, 2 * half):
                place(tile)


def fill_dense(kernel, pattern, counts, places, flip, delays):
    row_blocks = kernel.shape[0]
    rows = row_blocks * TILE
    left = jax.ShapeDtypeStruct((rows // 2, TILE), jnp.float32)
    return pl.pallas_call(
        fill_kernel,
        in_specs=[SCALARS] * 2 + [pl.BlockSpec(memory_space=pltpu.HBM)] * 4,
        out_specs=[WHOLE] * 3,
        out_shape=[jax.ShapeDtypeStruct((rows, (CB_DEV + 1) * TILE), kernel.dtype), left, left],
        scratch_shapes=[
            pltpu.SMEM(pattern.shape, jnp.int32),
            pltpu.SMEM((row_blocks,), jnp.int32),
            pltpu.VMEM(delays.shape, delays.dtype),
            pltpu.VMEM(kernel.shape, kernel.dtype),
            pltpu.SemaphoreType.DMA((2 * row_blocks + 3,)),
        ],
        compiler_params=pltpu.CompilerParams(vmem_limit_bytes=16 * 1024 * 1024),
        cost_estimate=pl.CostEstimate(
            flops=0, bytes_accessed=2 * kernel.size, transcendentals=0
        ),
    )(
        places,
        flip,
        *(pltpu.with_memory_space_constraint(x, pltpu.HBM) for x in (pattern, counts.reshape(-1), delays, kernel)),
    )


def norm_of(ref):
    return jnp.sqrt(ref[0:1, :] + tiny_eps)


def squares_row(sums):
    while len(sums) > 1:
        sums = [sums[i] + sums[i + 1] for i in range(0, len(sums), 2)]
    row = jnp.sum(sums[0], axis=0, keepdims=True)
    return row + turned(row)


def next_vector(parts, raw_ref, scale_ref, past_ref, past_scale_ref):
    if scale_ref is not None:
        scale = norm_of(scale_ref)
    if past_ref is not None:
        past_scale = norm_of(past_scale_ref)
    position = 0
    for part, units in parts:
        pairs = part.shape[0] // TILE // units
        for unit in range(units):
            squares = jnp.zeros((NORM_ROWS, TILE), jnp.float32)
            for pair in range(pairs):
                value = part[rows_of(unit * pairs + pair), :]
                if scale_ref is not None:
                    value = value / scale
                if past_ref is not None:
                    value = value - scale * (past_ref[rows_of(position), :] / past_scale)
                if raw_ref is not None:
                    raw_ref[rows_of(position), :] = value
                squares += jnp.sum((value * value).reshape(-1, NORM_ROWS, TILE), axis=0)
                yield position, value, squares if pair == pairs - 1 else None
                position += 1


def back_pairs(dense_ref, turned_ref, out_ref, units):
    pairs = CB_DEV // 2 // UNITS
    for pair in range(pairs * len(units)):
        column = units[pair // pairs] * pairs + pair % pairs
        product = jnp.dot(
            turned_ref[...],
            dense_ref[:, rows_of(column, PAIR)],
            preferred_element_type=jnp.float32,
        )
        stacked = jnp.concatenate([product[:, :TILE], product[:, TILE:]], axis=0)
        out_ref[rows_of(pair), :] = stacked.T


def back_send_kernel(first, units, *refs):
    if first:
        dense_ref, own_ref, send_ref, turned_ref = refs
        parts, raw_ref, scales = [(own_ref, 2)], None, (None, None, None)
    else:
        (dense_ref, other_ref, own_ref, scale_ref, past_ref, past_scale_ref,
         send_ref, turned_ref, raw_ref) = refs
        parts, scales = [(other_ref, 1), (own_ref, 1)], (scale_ref, past_ref, past_scale_ref)
    sums = []
    half = turned_ref.shape[0]
    for pair, value, squares in next_vector(parts, raw_ref, *scales):
        flat = value.T.astype(turned_ref.dtype)
        turned_ref[:, rows_of(2 * pair)] = flat[:half]
        turned_ref[:, rows_of(2 * pair + 1)] = flat[half:]
        if squares is not None:
            sums.append(squares)
    send_ref[-NORM_ROWS:, :] = jnp.broadcast_to(squares_row(sums), (NORM_ROWS, TILE))
    back_pairs(dense_ref, turned_ref, send_ref, units)


def back_keep_kernel(units, dense_ref, turned_ref, keep_ref):
    back_pairs(dense_ref, turned_ref, keep_ref, units)


def fore_pairs(dense_ref, units, wide_ref, add_ref, out_ref, start):
    depth = wide_ref.shape[0] // len(units)
    runs = [(unit * depth, i * depth, depth) for i, unit in enumerate(units)]
    if units[1] == units[0] + 1:
        runs = [(units[0] * depth, 0, 2 * depth)]
    low = low_lanes((TILE, TILE))
    step = 2
    pairs = out_ref.shape[0] // TILE
    for pair in range(0, pairs, step):
        rows = slice((start + pair) * PAIR, (start + pair + step) * PAIR)
        product = sum(
            jnp.dot(
                dense_ref[rows, cell : cell + size],
                wide_ref[row : row + size, :],
                preferred_element_type=jnp.float32,
            )
            for cell, row, size in runs
        )
        for i in range(step):
            even, odd = product[rows_of(2 * i), :], product[rows_of(2 * i + 1), :]
            value = jnp.where(low, even, odd)
            if add_ref is not None:
                value = value + add_ref[rows_of(start + pair + i), :]
            out_ref[rows_of(pair + i), :] = value


def fore_vector(parts, wide_ref, raw_ref, scales):
    low = low_lanes((TILE, TILE))
    sums = []
    for pair, value, squares in next_vector(parts, raw_ref, *scales):
        other = turned(value)
        wide_ref[rows_of(2 * pair), :] = jnp.where(low, value, other).astype(wide_ref.dtype)
        wide_ref[rows_of(2 * pair + 1), :] = jnp.where(low, other, value).astype(wide_ref.dtype)
        if squares is not None:
            sums.append(squares)
    return sums[0] + sums[1]


def fore_own_kernel(first, units, dense_ref, inner_ref, mine_ref, scale_ref, *refs):
    past_ref, past_scale_ref = (None, None) if first else refs[:2]
    part_ref, sum_ref, raw_ref, wide_ref = refs[-4:]
    parts = [(inner_ref, 1), (mine_ref, 1)]
    sum_ref[...] = fore_vector(parts, wide_ref, raw_ref, (scale_ref, past_ref, past_scale_ref))
    fore_pairs(dense_ref, units, wide_ref, None, part_ref, 0)


def fore_send_kernel(first, units, dense_ref, outer_ref, part_ref, sum_ref, scale_ref, *refs):
    past_ref, past_scale_ref = (None, None) if first else refs[:2]
    send_ref, wide_ref, raw_ref = refs[-3:]
    squares = fore_vector([(outer_ref, 2)], wide_ref, raw_ref, (scale_ref, past_ref, past_scale_ref))
    row = squares_row([squares, sum_ref[...]])
    send_ref[-NORM_ROWS:, :] = jnp.broadcast_to(row, (NORM_ROWS, TILE))
    fore_pairs(dense_ref, units, wide_ref, part_ref, send_ref, 0)


def fore_keep_kernel(units, dense_ref, wide_ref, part_ref, keep_ref):
    start = keep_ref.shape[0] // TILE
    fore_pairs(dense_ref, units, wide_ref, part_ref, keep_ref, start)


def product_call(body, dense, operands, shapes, scratch=()):
    return pl.pallas_call(
        body,
        in_specs=[WHOLE] * (1 + len(operands)),
        out_specs=[WHOLE] * len(shapes),
        out_shape=shapes,
        scratch_shapes=scratch,
        compiler_params=pltpu.CompilerParams(vmem_limit_bytes=12 * 1024 * 1024),
        cost_estimate=pl.CostEstimate(
            flops=2 * TILE * dense.size, bytes_accessed=dense.size, transcendentals=0
        ),
    )(dense, *operands)


def float_rows(rows):
    return jax.ShapeDtypeStruct((rows, TILE), jnp.float32)


def back_product(order, dense, operands, first):
    rows, cells = dense.shape[0], CB_DEV * TILE
    shapes = [float_rows(cells // 4 + NORM_ROWS), jax.ShapeDtypeStruct((TILE // 2, rows), dense.dtype)]
    shapes += [] if first else [float_rows(rows // 2)]
    send, flat, *raw = product_call(
        functools.partial(back_send_kernel, first, order[:2]), dense, operands, shapes
    )


    body = functools.partial(back_keep_kernel, order[2:])
    (keep,) = product_call(body, dense, [flat], [float_rows(cells // 4)])
    return send, keep, *raw


def fore_own_product(order, dense, operands, first):
    rows, cells = dense.shape[0], CB_DEV * TILE
    return product_call(
        functools.partial(fore_own_kernel, first, order[2:]),
        dense,
        operands,
        [float_rows(rows // 2), float_rows(NORM_ROWS), float_rows(cells // 4)],
        [pltpu.VMEM((cells // 2, TILE), dense.dtype)],
    )


def fore_product(order, dense, operands, first):
    rows, cells = dense.shape[0], CB_DEV * TILE
    shapes = [
        float_rows(rows // 4 + NORM_ROWS),
        jax.ShapeDtypeStruct((cells // 2, TILE), dense.dtype),
        float_rows(cells // 4),
    ]
    send, wide, raw = product_call(
        functools.partial(fore_send_kernel, first, order[:2]), dense, operands, shapes
    )

    def keep(wide):
        body = functools.partial(fore_keep_kernel, order[:2])
        return product_call(body, dense, [wide, operands[1]], [float_rows(rows // 4)])[0]

    return send, (keep, wide), raw


def rotation(norms):
    betas, alphas = [norm_of(ref) for ref in norms[0::2]], [norm_of(ref) for ref in norms[1::2]]
    resid_bar, diag_bar = betas[0], alphas[0]
    steps = []
    for j in range(len(alphas)):
        radius = jnp.sqrt(diag_bar * diag_bar + betas[j + 1] * betas[j + 1])
        rotate_cos = diag_bar / radius
        rotate_sin = betas[j + 1] / radius
        step_size = rotate_cos * resid_bar
        resid_bar = rotate_sin * resid_bar
        coupling = None
        if j + 1 < len(alphas):
            coupling = rotate_sin * alphas[j + 1] / radius
            diag_bar = -rotate_cos * alphas[j + 1]
        steps.append((step_size / radius, coupling))
    misfit = resid_bar / betas[0]
    return alphas, betas, steps, misfit, misfit * rotate_cos


def store_in_order(out_ref, mask, pair, low, values):
    pairs = out_ref.shape[0] // PAIR // UNITS
    start = (((pair // pairs) ^ mask) * pairs + pair % pairs) * PAIR
    ours, theirs = values
    even = pl.ds(pl.multiple_of(start, TILE), TILE)
    odd = pl.ds(pl.multiple_of(start + TILE, TILE), TILE)
    out_ref[even, :] = jnp.where(low, ours, turned(theirs))
    out_ref[odd, :] = jnp.where(low, turned(ours), theirs)


def model_kernel(count, mask_ref, *refs):
    ins, (model_ref, misfit_ref) = refs[:-2], refs[-2:]
    chains = [ins[: len(ins) // 2], ins[len(ins) // 2 :]]
    low = low_lanes((TILE, TILE))
    rotations = [rotation(refs_[2 * count :]) for refs_ in chains]
    misfits = [jnp.broadcast_to(r[3], misfit_ref.shape) for r in rotations]
    misfit_ref[...] = jnp.where(low_lanes(misfit_ref.shape), misfits[0], misfits[1])
    pairs = model_ref.shape[0] // PAIR // UNITS
    for pair in range(model_ref.shape[0] // PAIR):
        values = []
        for order, refs_, (alphas, _, steps, _, _) in zip(UNIT_ORDERS, chains, rotations):
            slot = order.index(pair // pairs)
            rows = rows_of(slot % 2 * pairs + pair % pairs)
            search = total = None
            for j in range(count):
                right = refs_[2 * j + slot // 2][rows, :] / alphas[j]
                search = right if j == 0 else right - steps[j - 1][1] * search
                total = steps[j][0] * search if j == 0 else total + steps[j][0] * search
            values.append(total)
        store_in_order(model_ref, mask_ref[0], pair, low, values)


def gradient_kernel(mask_ref, *refs):
    ins, gradient_ref = refs[:-1], refs[-1]
    chains = [ins[: len(ins) // 2], ins[len(ins) // 2 :]]
    low = low_lanes((TILE, TILE))
    vectors = []
    factors = []
    for outer_ref, inner_ref, mine_ref, past_ref, own_past_ref, *norms in chains:
        halves = [
            next_vector(parts, None, norms[-1], past, norms[-2])
            for parts, past in [
                ([(outer_ref, 2)], past_ref),
                ([(inner_ref, 1), (mine_ref, 1)], own_past_ref),
            ]
        ]
        vectors.append([value for half in halves for _, value, _ in half])
        factors.append(rotation(norms)[-1])
    pairs = gradient_ref.shape[0] // PAIR // UNITS
    for pair in range(gradient_ref.shape[0] // PAIR):
        values = []
        for order, vector, factor in zip(UNIT_ORDERS, vectors, factors):
            slot = order.index(pair // pairs)
            values.append(factor * vector[slot * pairs + pair % pairs])
        store_in_order(gradient_ref, mask_ref[0], pair, low, values)


def last_call(body, mask, operands, shapes):
    return pl.pallas_call(
        body,
        in_specs=[SCALARS] + [WHOLE] * len(operands),
        out_specs=[WHOLE] * len(shapes),
        out_shape=[jax.ShapeDtypeStruct(shape, jnp.float32) for shape in shapes],
        compiler_params=pltpu.CompilerParams(vmem_limit_bytes=12 * 1024 * 1024),
        cost_estimate=pl.CostEstimate(
            flops=0, bytes_accessed=8 * shapes[0][0] * TILE, transcendentals=0
        ),
    )(mask, *operands)


def on_device(row_count, col_count, kernel, pattern, counts, delays):
    row_bits = list(range(row_count.bit_length() - 1))
    col_bits = list(range(col_count.bit_length() - 1))
    row_index = lax.axis_index("rows")
    core = lax.axis_index("cols") & 1

    near, far, *rest = row_bits
    orders = [[near, far, *rest, far, near], [far, near, *rest, near, far]]
    steps = len(orders[0])

    def swap_rows(second, value, level):
        pairs = []
        for row in range(row_count):
            for col in range(col_count):
                partner = row ^ (1 << orders[col & 1 ^ second][level])
                pairs.append((row * col_count + col, partner * col_count + col))
        return lax.ppermute(value, ("rows", "cols"), pairs)

    def swap_cols(value, level):
        return lax.ppermute(value, "cols", [(i, i ^ (1 << level)) for i in range(col_count)])

    bits = [(row_index >> bit) & 1 for bit in row_bits[:2]]
    outer_side = jnp.where(core == 0, bits[0], bits[1])
    inner_side = jnp.where(core == 0, bits[1], bits[0])
    mask = ((1 - outer_side) * 2 + (1 - inner_side)).astype(jnp.int32)
    blocks = jnp.arange(CB_DEV, dtype=jnp.int32)
    unit = CB_DEV // UNITS
    places = ((blocks // unit) ^ mask) * unit + blocks % unit
    flip = ((1 - core) * (kernel.shape[0] // 2)).astype(jnp.int32).reshape(1)
    mask = mask.reshape(1)

    dense, *lefts = fill_dense(kernel, pattern, counts, places, flip, delays)

    def tied(value, other):
        return lax.optimization_barrier((value, other))[0]

    def kept_half(kept, ahead):
        half, operand = kept
        return half(tied(operand, ahead))

    def reduce_rows(swap_rows, send, keep):
        half = keep.shape[0]
        got, _ = yield swap_rows, send, 0
        keep = keep + got[:half]
        norm = send[half:] + got[half:]
        send, mine = keep[: half // 2], keep[half // 2 :]
        for level in range(1, len(row_bits)):
            got, _ = yield swap_rows, jnp.concatenate([send, norm]), level
            norm = norm + got[half // 2 :]
            send = mine = mine + got[: half // 2]
        inner, _ = yield swap_rows, mine, steps - 2
        outer, ahead = yield swap_rows, jnp.concatenate([inner, mine]), steps - 1
        return [outer, inner, mine], norm, ahead

    def reduce_cols(send, kept):
        half = send.shape[0] - NORM_ROWS
        got, ahead = yield swap_cols, send, 0
        own = kept_half(kept, ahead) + got[:half]
        norm = send[half:] + got[half:]
        for bit in col_bits[1:]:
            got, _ = yield swap_cols, jnp.concatenate([own, norm]), bit
            norm = norm + got[half:]
            own = own + got[:half]
        other, _ = yield swap_cols, own, 0
        return [other, own], norm

    def chain(second, left):
        order = UNIT_ORDERS[second]
        swap = functools.partial(swap_rows, second)
        send, keep = back_product(order, dense, [left], True)
        totals, norm, ahead = yield from reduce_rows(swap, send, keep)
        norms = [norm]
        rights = []
        for iteration in range(ITERS):
            outer, *own = totals
            pasts = [[right, norms[-2]] for right in rights[-1]] if rights else [[], []]
            own = [tied(own[0], ahead), own[1]]
            part, squares, own_right = fore_own_product(
                order, dense, [*own, norms[-1], *pasts[1]], not rights
            )
            send, keep, right = fore_product(
                order, dense, [outer, part, squares, norms[-1], *pasts[0]], not rights
            )
            rights.append([right, own_right])
            halves, norm = yield from reduce_cols(send, keep)
            norms.append(norm)
            send, keep, left = back_product(
                order, dense, [*halves, norms[-1], left, norms[-2]], False
            )
            totals, norm, ahead = yield from reduce_rows(swap, send, keep)
            norms.append(norm)
        return rights, norms, totals

    runs = [chain(second, left) for second, left in enumerate(lefts)]
    wanted = [next(run) for run in runs]
    chains = [None] * len(runs)
    gots = [None] * len(runs)
    swap, value, level = wanted[0]
    gots[0] = swap(value, level)
    latest = wanted[1][1]
    turn = 0
    while None in chains:
        mine = 0 if turn < BEHIND else (turn - BEHIND) % 2
        turn += 1
        if chains[mine] is not None:
            continue
        if gots[mine] is None:
            swap, value, level = wanted[mine]
            latest = tied(value, latest)
        else:
            try:
                swap, latest, level = runs[mine].send((tied(gots[mine], latest), latest))
            except StopIteration as stop:
                chains[mine] = stop.value
                continue
        gots[mine] = swap(latest, level)

    cells = CB_DEV * TILE
    model, misfit = last_call(
        functools.partial(model_kernel, ITERS),
        mask,
        [operand for rights, norms, _ in chains for operand in [*sum(rights, []), *norms]],
        [(cells, TILE), (NORM_ROWS, TILE)],
    )
    (gradient,) = last_call(
        gradient_kernel,
        mask,
        [operand for rights, norms, totals in chains for operand in [*totals, *rights[-1], *norms]],
        [(cells, TILE)],
    )
    return (model, gradient, misfit[0])


def solution(mesh):
    placed = (P("rows", "cols", None, None), P("rows", "cols"), P("rows", "cols"), P("rows", None))

    def local(kernel, pattern, counts, delays):
        return on_device(
            mesh.shape["rows"], mesh.shape["cols"], kernel, pattern, counts, delays
        )

    return jax.shard_map(
        local,
        mesh=mesh,
        in_specs=placed,
        out_specs=(P("cols", None), P("cols", None), P()),
        check_vma=False,
    )
```

```python
import functools

import jax
import jax.numpy as jnp
from jax import lax
from jax.experimental import pallas as pl
from jax.experimental.pallas import tpu as pltpu
from jax.sharding import PartitionSpec as P

CB_DEV = 24
ITERS = 2
TILE = 128
PAIR = 2 * TILE
UNITS = 4
NORM_ROWS = 8
UNIT_ORDERS = ((0, 1, 2, 3), (0, 2, 1, 3))
BEHIND = 0

tiny_eps = 1e-06

WHOLE = pl.BlockSpec(memory_space=pltpu.VMEM)
SCALARS = pl.BlockSpec(memory_space=pltpu.SMEM)


def low_lanes(shape):
    return lax.broadcasted_iota(jnp.int32, shape, 1) < shape[1] // 2


def turned(value):
    return pltpu.roll(value, value.shape[1] // 2, 1)


def rows_of(pair, size=TILE):
    return slice(pair * size, (pair + 1) * size)


def fill_kernel(
    place_ref, flip_ref, pattern_in, counts_in, delays_in, tiles_in,
    dense_ref, even_left_ref, odd_left_ref, pattern_ref, counts_ref, delays_ref, tiles_ref, arrived,
):
    flip = flip_ref[0]
    row_blocks = tiles_in.shape[0]
    small = [
        pltpu.make_async_copy(source, target, arrived.at[2 * row_blocks + i])
        for i, (source, target) in enumerate(
            [(pattern_in, pattern_ref), (counts_in, counts_ref), (delays_in, delays_ref)]
        )
    ]
    for copy in small:
        copy.start()

    half = tiles_in.shape[1] // 2

    def fetch(position, upper):
        slots = pl.ds(upper * half, half)
        return pltpu.make_async_copy(
            tiles_in.at[position ^ flip, slots],
            tiles_ref.at[position, slots],
            arrived.at[upper * row_blocks + position],
        )

    for position in range(row_blocks):
        fetch(position, 0).start()
    for copy in small[:2]:
        copy.wait()
    for position in range(row_blocks):

        @pl.when(counts_ref[position ^ flip] > half)
        def _():
            fetch(position, 1).start()

    @pl.loop(0, row_blocks)
    def _(position):
        rows = pl.ds(pl.multiple_of(position * TILE, TILE), TILE)
        dense_ref[rows, :] = jnp.zeros((TILE, dense_ref.shape[1]), dense_ref.dtype)

    @pl.loop(0, row_blocks)
    def _(position):
        rows = pl.ds(pl.multiple_of(position * TILE, TILE), TILE)
        block = position ^ flip
        count = counts_ref[block]

        def place(tile):
            column = jnp.where(tile < count, place_ref[pattern_ref[block, tile]], CB_DEV)
            lanes = pl.ds(pl.multiple_of(column * TILE, TILE), TILE)
            dense_ref[rows, lanes] = tiles_ref[position, tile]

        fetch(position, 0).wait()
        for tile in range(half):
            place(tile)

        @pl.when(count > half)
        def _():
            fetch(position, 1).wait()
            for tile in range(half, 2 * half):
                place(tile)

    small[2].wait()
    low = low_lanes((TILE, TILE))
    for pair in range(row_blocks // 2):
        source = (pair ^ (flip // 2)) * PAIR
        even = delays_ref[pl.ds(pl.multiple_of(source, TILE), TILE), :]
        odd = delays_ref[pl.ds(pl.multiple_of(source + TILE, TILE), TILE), :]
        even_left_ref[rows_of(pair), :] = jnp.where(low, even, turned(odd))
        odd_left_ref[rows_of(pair), :] = jnp.where(low, turned(even), odd)


def fill_dense(kernel, pattern, counts, places, flip, delays):
    row_blocks = kernel.shape[0]
    rows = row_blocks * TILE
    left = jax.ShapeDtypeStruct((rows // 2, TILE), jnp.float32)
    return pl.pallas_call(
        fill_kernel,
        in_specs=[SCALARS] * 2 + [pl.BlockSpec(memory_space=pltpu.HBM)] * 4,
        out_specs=[WHOLE] * 3,
        out_shape=[jax.ShapeDtypeStruct((rows, (CB_DEV + 1) * TILE), kernel.dtype), left, left],
        scratch_shapes=[
            pltpu.SMEM(pattern.shape, jnp.int32),
            pltpu.SMEM((row_blocks,), jnp.int32),
            pltpu.VMEM(delays.shape, delays.dtype),
            pltpu.VMEM(kernel.shape, kernel.dtype),
            pltpu.SemaphoreType.DMA((2 * row_blocks + 3,)),
        ],
        compiler_params=pltpu.CompilerParams(vmem_limit_bytes=16 * 1024 * 1024),
        cost_estimate=pl.CostEstimate(
            flops=0, bytes_accessed=2 * kernel.size, transcendentals=0
        ),
    )(
        places,
        flip,
        *(pltpu.with_memory_space_constraint(x, pltpu.HBM) for x in (pattern, counts.reshape(-1), delays, kernel)),
    )


def norm_of(ref):
    return jnp.sqrt(ref[0:1, :] + tiny_eps)


def squares_row(sums):
    while len(sums) > 1:
        sums = [sums[i] + sums[i + 1] for i in range(0, len(sums), 2)]
    row = jnp.sum(sums[0], axis=0, keepdims=True)
    return row + turned(row)


def next_vector(parts, raw_ref, scale_ref, past_ref, past_scale_ref):
    if scale_ref is not None:
        scale = norm_of(scale_ref)
    if past_ref is not None:
        past_scale = norm_of(past_scale_ref)
    position = 0
    for part, units in parts:
        pairs = part.shape[0] // TILE // units
        for unit in range(units):
            squares = jnp.zeros((NORM_ROWS, TILE), jnp.float32)
            for pair in range(pairs):
                value = part[rows_of(unit * pairs + pair), :]
                if scale_ref is not None:
                    value = value / scale
                if past_ref is not None:
                    value = value - scale * (past_ref[rows_of(position), :] / past_scale)
                if raw_ref is not None:
                    raw_ref[rows_of(position), :] = value
                squares += jnp.sum((value * value).reshape(-1, NORM_ROWS, TILE), axis=0)
                yield position, value, squares if pair == pairs - 1 else None
                position += 1


def back_pairs(dense_ref, turned_ref, out_ref, units):
    pairs = CB_DEV // 2 // UNITS
    for pair in range(pairs * len(units)):
        column = units[pair // pairs] * pairs + pair % pairs
        product = jnp.dot(
            turned_ref[...],
            dense_ref[:, rows_of(column, PAIR)],
            preferred_element_type=jnp.float32,
        )
        stacked = jnp.concatenate([product[:, :TILE], product[:, TILE:]], axis=0)
        out_ref[rows_of(pair), :] = stacked.T


def back_send_kernel(first, units, *refs):
    if first:
        dense_ref, own_ref, send_ref, turned_ref = refs
        parts, raw_ref, scales = [(own_ref, 2)], None, (None, None, None)
    else:
        (dense_ref, other_ref, own_ref, scale_ref, past_ref, past_scale_ref,
         send_ref, turned_ref, raw_ref) = refs
        parts, scales = [(other_ref, 1), (own_ref, 1)], (scale_ref, past_ref, past_scale_ref)
    sums = []
    half = turned_ref.shape[0]
    for pair, value, squares in next_vector(parts, raw_ref, *scales):
        flat = value.T.astype(turned_ref.dtype)
        turned_ref[:, rows_of(2 * pair)] = flat[:half]
        turned_ref[:, rows_of(2 * pair + 1)] = flat[half:]
        if squares is not None:
            sums.append(squares)
    send_ref[-NORM_ROWS:, :] = jnp.broadcast_to(squares_row(sums), (NORM_ROWS, TILE))
    back_pairs(dense_ref, turned_ref, send_ref, units)


def back_keep_kernel(units, dense_ref, turned_ref, keep_ref):
    back_pairs(dense_ref, turned_ref, keep_ref, units)


def fore_pairs(dense_ref, units, wide_ref, add_ref, out_ref, start):
    depth = wide_ref.shape[0] // len(units)
    runs = [(unit * depth, i * depth, depth) for i, unit in enumerate(units)]
    if units[1] == units[0] + 1:
        runs = [(units[0] * depth, 0, 2 * depth)]
    low = low_lanes((TILE, TILE))
    step = 2
    pairs = out_ref.shape[0] // TILE
    for pair in range(0, pairs, step):
        rows = slice((start + pair) * PAIR, (start + pair + step) * PAIR)
        product = sum(
            jnp.dot(
                dense_ref[rows, cell : cell + size],
                wide_ref[row : row + size, :],
                preferred_element_type=jnp.float32,
            )
            for cell, row, size in runs
        )
        for i in range(step):
            even, odd = product[rows_of(2 * i), :], product[rows_of(2 * i + 1), :]
            value = jnp.where(low, even, odd)
            if add_ref is not None:
                value = value + add_ref[rows_of(start + pair + i), :]
            out_ref[rows_of(pair + i), :] = value


def fore_vector(parts, wide_ref, raw_ref, scales):
    low = low_lanes((TILE, TILE))
    sums = []
    for pair, value, squares in next_vector(parts, raw_ref, *scales):
        other = turned(value)
        wide_ref[rows_of(2 * pair), :] = jnp.where(low, value, other).astype(wide_ref.dtype)
        wide_ref[rows_of(2 * pair + 1), :] = jnp.where(low, other, value).astype(wide_ref.dtype)
        if squares is not None:
            sums.append(squares)
    return sums[0] + sums[1]


def fore_own_kernel(first, units, dense_ref, inner_ref, mine_ref, scale_ref, *refs):
    past_ref, past_scale_ref = (None, None) if first else refs[:2]
    part_ref, sum_ref, raw_ref, wide_ref = refs[-4:]
    parts = [(inner_ref, 1), (mine_ref, 1)]
    sum_ref[...] = fore_vector(parts, wide_ref, raw_ref, (scale_ref, past_ref, past_scale_ref))
    fore_pairs(dense_ref, units, wide_ref, None, part_ref, 0)


def fore_send_kernel(first, units, dense_ref, outer_ref, part_ref, sum_ref, scale_ref, *refs):
    past_ref, past_scale_ref = (None, None) if first else refs[:2]
    send_ref, wide_ref, raw_ref = refs[-3:]
    squares = fore_vector([(outer_ref, 2)], wide_ref, raw_ref, (scale_ref, past_ref, past_scale_ref))
    row = squares_row([squares, sum_ref[...]])
    send_ref[-NORM_ROWS:, :] = jnp.broadcast_to(row, (NORM_ROWS, TILE))
    fore_pairs(dense_ref, units, wide_ref, part_ref, send_ref, 0)


def fore_keep_kernel(units, dense_ref, wide_ref, part_ref, keep_ref):
    start = keep_ref.shape[0] // TILE
    fore_pairs(dense_ref, units, wide_ref, part_ref, keep_ref, start)


def product_call(body, dense, operands, shapes, scratch=()):
    return pl.pallas_call(
        body,
        in_specs=[WHOLE] * (1 + len(operands)),
        out_specs=[WHOLE] * len(shapes),
        out_shape=shapes,
        scratch_shapes=scratch,
        compiler_params=pltpu.CompilerParams(vmem_limit_bytes=12 * 1024 * 1024),
        cost_estimate=pl.CostEstimate(
            flops=2 * TILE * dense.size, bytes_accessed=dense.size, transcendentals=0
        ),
    )(dense, *operands)


def float_rows(rows):
    return jax.ShapeDtypeStruct((rows, TILE), jnp.float32)


def back_product(order, dense, operands, first):
    rows, cells = dense.shape[0], CB_DEV * TILE
    shapes = [float_rows(cells // 4 + NORM_ROWS), jax.ShapeDtypeStruct((TILE // 2, rows), dense.dtype)]
    shapes += [] if first else [float_rows(rows // 2)]
    send, flat, *raw = product_call(
        functools.partial(back_send_kernel, first, order[:2]), dense, operands, shapes
    )


    body = functools.partial(back_keep_kernel, order[2:])
    (keep,) = product_call(body, dense, [flat], [float_rows(cells // 4)])
    return send, keep, *raw


def fore_own_product(order, dense, operands, first):
    rows, cells = dense.shape[0], CB_DEV * TILE
    return product_call(
        functools.partial(fore_own_kernel, first, order[2:]),
        dense,
        operands,
        [float_rows(rows // 2), float_rows(NORM_ROWS), float_rows(cells // 4)],
        [pltpu.VMEM((cells // 2, TILE), dense.dtype)],
    )


def fore_product(order, dense, operands, first):
    rows, cells = dense.shape[0], CB_DEV * TILE
    shapes = [
        float_rows(rows // 4 + NORM_ROWS),
        jax.ShapeDtypeStruct((cells // 2, TILE), dense.dtype),
        float_rows(cells // 4),
    ]
    send, wide, raw = product_call(
        functools.partial(fore_send_kernel, first, order[:2]), dense, operands, shapes
    )

    def keep(wide):
        body = functools.partial(fore_keep_kernel, order[:2])
        return product_call(body, dense, [wide, operands[1]], [float_rows(rows // 4)])[0]

    return send, (keep, wide), raw


def rotation(norms):
    betas, alphas = [norm_of(ref) for ref in norms[0::2]], [norm_of(ref) for ref in norms[1::2]]
    resid_bar, diag_bar = betas[0], alphas[0]
    steps = []
    for j in range(len(alphas)):
        radius = jnp.sqrt(diag_bar * diag_bar + betas[j + 1] * betas[j + 1])
        rotate_cos = diag_bar / radius
        rotate_sin = betas[j + 1] / radius
        step_size = rotate_cos * resid_bar
        resid_bar = rotate_sin * resid_bar
        coupling = None
        if j + 1 < len(alphas):
            coupling = rotate_sin * alphas[j + 1] / radius
            diag_bar = -rotate_cos * alphas[j + 1]
        steps.append((step_size / radius, coupling))
    misfit = resid_bar / betas[0]
    return alphas, betas, steps, misfit, misfit * rotate_cos


def store_in_order(out_ref, mask, pair, low, values):
    pairs = out_ref.shape[0] // PAIR // UNITS
    start = (((pair // pairs) ^ mask) * pairs + pair % pairs) * PAIR
    ours, theirs = values
    even = pl.ds(pl.multiple_of(start, TILE), TILE)
    odd = pl.ds(pl.multiple_of(start + TILE, TILE), TILE)
    out_ref[even, :] = jnp.where(low, ours, turned(theirs))
    out_ref[odd, :] = jnp.where(low, turned(ours), theirs)


def model_kernel(count, mask_ref, *refs):
    ins, (model_ref, misfit_ref) = refs[:-2], refs[-2:]
    chains = [ins[: len(ins) // 2], ins[len(ins) // 2 :]]
    low = low_lanes((TILE, TILE))
    rotations = [rotation(refs_[2 * count :]) for refs_ in chains]
    misfits = [jnp.broadcast_to(r[3], misfit_ref.shape) for r in rotations]
    misfit_ref[...] = jnp.where(low_lanes(misfit_ref.shape), misfits[0], misfits[1])
    pairs = model_ref.shape[0] // PAIR // UNITS
    for pair in range(model_ref.shape[0] // PAIR):
        values = []
        for order, refs_, (alphas, _, steps, _, _) in zip(UNIT_ORDERS, chains, rotations):
            slot = order.index(pair // pairs)
            rows = rows_of(slot % 2 * pairs + pair % pairs)
            search = total = None
            for j in range(count):
                right = refs_[2 * j + slot // 2][rows, :] / alphas[j]
                search = right if j == 0 else right - steps[j - 1][1] * search
                total = steps[j][0] * search if j == 0 else total + steps[j][0] * search
            values.append(total)
        store_in_order(model_ref, mask_ref[0], pair, low, values)


def gathered_values(outer, own, norms):
    factor = rotation(norms)[-1]
    values = []
    for half in (outer, own):
        if half is not None:
            parts, past_ref = half
            vector = next_vector(parts, None, norms[-1], past_ref, norms[-2])
            values += [factor * value for _, value, _ in vector]
    return values


def store_pair(ref, pair, low, ours, theirs):
    ref[rows_of(2 * pair), :] = jnp.where(low, ours, turned(theirs))
    ref[rows_of(2 * pair + 1), :] = jnp.where(low, turned(ours), theirs)


def ready_kernel(outer_ref, inner_ref, mine_ref, past_ref, own_past_ref, *refs):
    norms, refs = refs[: 2 * ITERS + 1], refs[2 * ITERS + 1 :]
    second_inner_ref, second_mine_ref, second_past_ref, *second_norms, ready_ref, ours_ref = refs
    low = low_lanes((TILE, TILE))
    ours = gathered_values(
        ([(outer_ref, 2)], past_ref), ([(inner_ref, 1), (mine_ref, 1)], own_past_ref), norms
    )
    theirs = gathered_values(
        None, ([(second_inner_ref, 1), (second_mine_ref, 1)], second_past_ref), second_norms
    )
    pairs = mine_ref.shape[0] // TILE
    for slot, unit in enumerate(UNIT_ORDERS[1]):
        start = UNIT_ORDERS[0].index(unit) * pairs
        for pair in range(pairs):
            if slot < 2:
                ours_ref[rows_of(slot * pairs + pair), :] = ours[start + pair]
            else:
                done = (slot - 2) * pairs + pair
                store_pair(ready_ref, done, low, ours[start + pair], theirs[done])


def gradient_kernel(mask_ref, ready_ref, ours_ref, outer_ref, past_ref, *refs):
    *norms, gradient_ref, last_ref, sent = refs
    low = low_lanes((TILE, TILE))
    size = gradient_ref.shape[0] // UNITS

    def send(slot, source_ref):
        rows = pl.ds(pl.multiple_of((UNIT_ORDERS[1][slot] ^ mask_ref[0]) * size, TILE), size)
        source = source_ref.at[pl.ds(slot % 2 * size, size)]
        return pltpu.make_async_copy(source, gradient_ref.at[rows], sent.at[slot])

    copies = [send(slot, last_ref if slot < 2 else ready_ref) for slot in range(UNITS)]
    for copy in copies[2:]:
        copy.start()
    theirs = gathered_values(([(outer_ref, 2)], past_ref), None, norms)
    for slot, copy in enumerate(copies[:2]):
        pairs = size // PAIR
        for pair in range(slot * pairs, (slot + 1) * pairs):
            store_pair(last_ref, pair, low, ours_ref[rows_of(pair), :], theirs[pair])
        copy.start()
    for copy in copies:
        copy.wait()


def gradient_of(mask, first, second):
    (rights, norms, totals), (second_rights, second_norms, second_totals) = first, second
    half = totals[0].shape[0]
    cost = pl.CostEstimate(flops=0, bytes_accessed=16 * half * TILE, transcendentals=0)
    params = pltpu.CompilerParams(vmem_limit_bytes=12 * 1024 * 1024)
    operands = [*totals, *rights[-1], *norms]
    operands += [*second_totals[1:], second_rights[-1][1], *second_norms]
    ready, ours = pl.pallas_call(
        ready_kernel,
        in_specs=[WHOLE] * len(operands),
        out_specs=[WHOLE] * 2,
        out_shape=[float_rows(2 * half), float_rows(half)],
        compiler_params=params,
        cost_estimate=cost,
    )(*operands)
    operands = [ready, ours, second_totals[0], second_rights[-1][0], *second_norms]
    return pl.pallas_call(
        gradient_kernel,
        in_specs=[SCALARS] + [WHOLE] * len(operands),
        out_specs=pl.BlockSpec(memory_space=pl.ANY),
        out_shape=float_rows(4 * half),
        scratch_shapes=[
            pltpu.VMEM((2 * half, TILE), jnp.float32),
            pltpu.SemaphoreType.DMA((UNITS,)),
        ],
        compiler_params=params,
        cost_estimate=cost,
    )(mask, *operands)


def last_call(body, mask, operands, shapes):
    return pl.pallas_call(
        body,
        in_specs=[SCALARS] + [WHOLE] * len(operands),
        out_specs=[WHOLE] * len(shapes),
        out_shape=[jax.ShapeDtypeStruct(shape, jnp.float32) for shape in shapes],
        compiler_params=pltpu.CompilerParams(vmem_limit_bytes=12 * 1024 * 1024),
        cost_estimate=pl.CostEstimate(
            flops=0, bytes_accessed=8 * shapes[0][0] * TILE, transcendentals=0
        ),
    )(mask, *operands)


def on_device(row_count, col_count, kernel, pattern, counts, delays):
    row_bits = list(range(row_count.bit_length() - 1))
    col_bits = list(range(col_count.bit_length() - 1))
    row_index = lax.axis_index("rows")
    core = lax.axis_index("cols") & 1

    near, far, *rest = row_bits
    orders = [[near, far, *rest, far, near], [far, near, *rest, near, far]]
    steps = len(orders[0])

    def swap_rows(second, value, level):
        pairs = []
        for row in range(row_count):
            for col in range(col_count):
                partner = row ^ (1 << orders[col & 1 ^ second][level])
                pairs.append((row * col_count + col, partner * col_count + col))
        return lax.ppermute(value, ("rows", "cols"), pairs)

    def swap_cols(value, level):
        return lax.ppermute(value, "cols", [(i, i ^ (1 << level)) for i in range(col_count)])

    bits = [(row_index >> bit) & 1 for bit in row_bits[:2]]
    outer_side = jnp.where(core == 0, bits[0], bits[1])
    inner_side = jnp.where(core == 0, bits[1], bits[0])
    mask = ((1 - outer_side) * 2 + (1 - inner_side)).astype(jnp.int32)
    blocks = jnp.arange(CB_DEV, dtype=jnp.int32)
    unit = CB_DEV // UNITS
    places = ((blocks // unit) ^ mask) * unit + blocks % unit
    flip = ((1 - core) * (kernel.shape[0] // 2)).astype(jnp.int32).reshape(1)
    mask = mask.reshape(1)

    dense, *lefts = fill_dense(kernel, pattern, counts, places, flip, delays)

    def tied(value, other):
        return lax.optimization_barrier((value, other))[0]

    def kept_half(kept, ahead):
        half, operand = kept
        return half(tied(operand, ahead))

    def reduce_rows(swap_rows, send, keep):
        half = keep.shape[0]
        got, _ = yield swap_rows, send, 0
        keep = keep + got[:half]
        norm = send[half:] + got[half:]
        send, mine = keep[: half // 2], keep[half // 2 :]
        for level in range(1, len(row_bits)):
            got, _ = yield swap_rows, jnp.concatenate([send, norm]), level
            norm = norm + got[half // 2 :]
            send = mine = mine + got[: half // 2]
        inner, _ = yield swap_rows, mine, steps - 2
        outer, ahead = yield swap_rows, jnp.concatenate([inner, mine]), steps - 1
        return [outer, inner, mine], norm, ahead

    def reduce_cols(send, kept):
        half = send.shape[0] - NORM_ROWS
        got, ahead = yield swap_cols, send, 0
        own = kept_half(kept, ahead) + got[:half]
        norm = send[half:] + got[half:]
        for bit in col_bits[1:]:
            got, _ = yield swap_cols, jnp.concatenate([own, norm]), bit
            norm = norm + got[half:]
            own = own + got[:half]
        other, _ = yield swap_cols, own, 0
        return [other, own], norm

    def chain(second, left):
        order = UNIT_ORDERS[second]
        swap = functools.partial(swap_rows, second)
        send, keep = back_product(order, dense, [left], True)
        totals, norm, ahead = yield from reduce_rows(swap, send, keep)
        norms = [norm]
        rights = []
        for iteration in range(ITERS):
            outer, *own = totals
            pasts = [[right, norms[-2]] for right in rights[-1]] if rights else [[], []]
            own = [tied(own[0], ahead), own[1]]
            part, squares, own_right = fore_own_product(
                order, dense, [*own, norms[-1], *pasts[1]], not rights
            )
            send, keep, right = fore_product(
                order, dense, [outer, part, squares, norms[-1], *pasts[0]], not rights
            )
            rights.append([right, own_right])
            halves, norm = yield from reduce_cols(send, keep)
            norms.append(norm)
            send, keep, left = back_product(
                order, dense, [*halves, norms[-1], left, norms[-2]], False
            )
            totals, norm, ahead = yield from reduce_rows(swap, send, keep)
            norms.append(norm)
        return rights, norms, totals

    runs = [chain(second, left) for second, left in enumerate(lefts)]
    wanted = [next(run) for run in runs]
    chains = [None] * len(runs)
    gots = [None] * len(runs)
    swap, value, level = wanted[0]
    gots[0] = swap(value, level)
    latest = wanted[1][1]
    turn = 0
    while None in chains:
        mine = 0 if turn < BEHIND else (turn - BEHIND) % 2
        turn += 1
        if chains[mine] is not None:
            continue
        if gots[mine] is None:
            swap, value, level = wanted[mine]
            latest = tied(value, latest)
        else:
            try:
                swap, latest, level = runs[mine].send((tied(gots[mine], latest), latest))
            except StopIteration as stop:
                chains[mine] = stop.value
                continue
        gots[mine] = swap(latest, level)

    cells = CB_DEV * TILE
    model, misfit = last_call(
        functools.partial(model_kernel, ITERS),
        mask,
        [operand for rights, norms, _ in chains for operand in [*sum(rights, []), *norms]],
        [(cells, TILE), (NORM_ROWS, TILE)],
    )
    gradient = gradient_of(mask, *chains)
    return (model, gradient, misfit[0])


def solution(mesh):
    placed = (P("rows", "cols", None, None), P("rows", "cols"), P("rows", "cols"), P("rows", None))

    def local(kernel, pattern, counts, delays):
        return on_device(
            mesh.shape["rows"], mesh.shape["cols"], kernel, pattern, counts, delays
        )

    return jax.shard_map(
        local,
        mesh=mesh,
        in_specs=placed,
        out_specs=(P("cols", None), P("cols", None), P()),
        check_vma=False,
    )
```

```python
import functools

import jax
import jax.numpy as jnp
from jax import lax
from jax.experimental import pallas as pl
from jax.experimental.pallas import tpu as pltpu
from jax.sharding import PartitionSpec as P

CB_DEV = 24
ITERS = 2
TILE = 128
PAIR = 2 * TILE
UNITS = 4
NORM_ROWS = 8
UNIT_ORDERS = ((0, 1, 2, 3), (0, 2, 1, 3))
BEHIND = 0

tiny_eps = 1e-06

WHOLE = pl.BlockSpec(memory_space=pltpu.VMEM)
SCALARS = pl.BlockSpec(memory_space=pltpu.SMEM)


def low_lanes(shape):
    return lax.broadcasted_iota(jnp.int32, shape, 1) < shape[1] // 2


def turned(value):
    return pltpu.roll(value, value.shape[1] // 2, 1)


def rows_of(pair, size=TILE):
    return slice(pair * size, (pair + 1) * size)


def fill_kernel(
    place_ref, flip_ref, pattern_in, counts_in, delays_in, tiles_in,
    dense_ref, even_left_ref, odd_left_ref, pattern_ref, counts_ref, delays_ref, tiles_ref, arrived,
):
    flip = flip_ref[0]
    row_blocks = tiles_in.shape[0]
    small = [
        pltpu.make_async_copy(source, target, arrived.at[2 * row_blocks + i])
        for i, (source, target) in enumerate(
            [(pattern_in, pattern_ref), (counts_in, counts_ref), (delays_in, delays_ref)]
        )
    ]
    for copy in small:
        copy.start()

    half = tiles_in.shape[1] // 2

    def fetch(position, upper):
        slots = pl.ds(upper * half, half)
        return pltpu.make_async_copy(
            tiles_in.at[position ^ flip, slots],
            tiles_ref.at[position, slots],
            arrived.at[upper * row_blocks + position],
        )

    for position in range(row_blocks):
        fetch(position, 0).start()
    for copy in small[:2]:
        copy.wait()
    for position in range(row_blocks):

        @pl.when(counts_ref[position ^ flip] > half)
        def _():
            fetch(position, 1).start()

    @pl.loop(0, row_blocks)
    def _(position):
        rows = pl.ds(pl.multiple_of(position * TILE, TILE), TILE)
        dense_ref[rows, :] = jnp.zeros((TILE, dense_ref.shape[1]), dense_ref.dtype)

    @pl.loop(0, row_blocks)
    def _(position):
        rows = pl.ds(pl.multiple_of(position * TILE, TILE), TILE)
        block = position ^ flip
        count = counts_ref[block]

        def place(tile):
            column = jnp.where(tile < count, place_ref[pattern_ref[block, tile]], CB_DEV)
            lanes = pl.ds(pl.multiple_of(column * TILE, TILE), TILE)
            dense_ref[rows, lanes] = tiles_ref[position, tile]

        fetch(position, 0).wait()
        for tile in range(half):
            place(tile)

        @pl.when(count > half)
        def _():
            fetch(position, 1).wait()
            for tile in range(half, 2 * half):
                place(tile)

    small[2].wait()
    low = low_lanes((TILE, TILE))
    for pair in range(row_blocks // 2):
        source = (pair ^ (flip // 2)) * PAIR
        even = delays_ref[pl.ds(pl.multiple_of(source, TILE), TILE), :]
        odd = delays_ref[pl.ds(pl.multiple_of(source + TILE, TILE), TILE), :]
        even_left_ref[rows_of(pair), :] = jnp.where(low, even, turned(odd))
        odd_left_ref[rows_of(pair), :] = jnp.where(low, turned(even), odd)


def fill_dense(kernel, pattern, counts, places, flip, delays):
    row_blocks = kernel.shape[0]
    rows = row_blocks * TILE
    left = jax.ShapeDtypeStruct((rows // 2, TILE), jnp.float32)
    return pl.pallas_call(
        fill_kernel,
        in_specs=[SCALARS] * 2 + [pl.BlockSpec(memory_space=pltpu.HBM)] * 4,
        out_specs=[WHOLE] * 3,
        out_shape=[jax.ShapeDtypeStruct((rows, (CB_DEV + 1) * TILE), kernel.dtype), left, left],
        scratch_shapes=[
            pltpu.SMEM(pattern.shape, jnp.int32),
            pltpu.SMEM((row_blocks,), jnp.int32),
            pltpu.VMEM(delays.shape, delays.dtype),
            pltpu.VMEM(kernel.shape, kernel.dtype),
            pltpu.SemaphoreType.DMA((2 * row_blocks + 3,)),
        ],
        compiler_params=pltpu.CompilerParams(vmem_limit_bytes=16 * 1024 * 1024),
        cost_estimate=pl.CostEstimate(
            flops=0, bytes_accessed=2 * kernel.size, transcendentals=0
        ),
    )(
        places,
        flip,
        *(pltpu.with_memory_space_constraint(x, pltpu.HBM) for x in (pattern, counts.reshape(-1), delays, kernel)),
    )


def norm_of(ref):
    return jnp.sqrt(ref[0:1, :] + tiny_eps)


def squares_row(sums):
    while len(sums) > 1:
        sums = [sums[i] + sums[i + 1] for i in range(0, len(sums), 2)]
    row = jnp.sum(sums[0], axis=0, keepdims=True)
    return row + turned(row)


def next_vector(parts, raw_ref, scale_ref, past_ref, past_scale_ref):
    if scale_ref is not None:
        scale = norm_of(scale_ref)
        shrink = 1.0 / scale
    if past_ref is not None:
        past_share = scale / norm_of(past_scale_ref)
    position = 0
    for part, units in parts:
        pairs = part.shape[0] // TILE // units
        for unit in range(units):
            squares = jnp.zeros((NORM_ROWS, TILE), jnp.float32)
            for pair in range(pairs):
                value = part[rows_of(unit * pairs + pair), :]
                if scale_ref is not None:
                    value = value * shrink
                if past_ref is not None:
                    value = value - past_share * past_ref[rows_of(position), :]
                if raw_ref is not None:
                    raw_ref[rows_of(position), :] = value
                squares += jnp.sum((value * value).reshape(-1, NORM_ROWS, TILE), axis=0)
                yield position, value, squares if pair == pairs - 1 else None
                position += 1


def back_pairs(dense_ref, turned_ref, out_ref, units):
    pairs = CB_DEV // 2 // UNITS
    for pair in range(pairs * len(units)):
        column = units[pair // pairs] * pairs + pair % pairs
        product = jnp.dot(
            turned_ref[...],
            dense_ref[:, rows_of(column, PAIR)],
            preferred_element_type=jnp.float32,
        )
        stacked = jnp.concatenate([product[:, :TILE], product[:, TILE:]], axis=0)
        out_ref[rows_of(pair), :] = stacked.T


def back_send_kernel(first, units, *refs):
    if first:
        dense_ref, own_ref, send_ref, turned_ref = refs
        parts, raw_ref, scales = [(own_ref, 2)], None, (None, None, None)
    else:
        (dense_ref, other_ref, own_ref, scale_ref, past_ref, past_scale_ref,
         send_ref, turned_ref, raw_ref) = refs
        parts, scales = [(other_ref, 1), (own_ref, 1)], (scale_ref, past_ref, past_scale_ref)
    sums = []
    half = turned_ref.shape[0]
    for pair, value, squares in next_vector(parts, raw_ref, *scales):
        flat = value.T.astype(turned_ref.dtype)
        turned_ref[:, rows_of(2 * pair)] = flat[:half]
        turned_ref[:, rows_of(2 * pair + 1)] = flat[half:]
        if squares is not None:
            sums.append(squares)
    send_ref[-NORM_ROWS:, :] = jnp.broadcast_to(squares_row(sums), (NORM_ROWS, TILE))
    back_pairs(dense_ref, turned_ref, send_ref, units)


def back_keep_kernel(units, dense_ref, turned_ref, keep_ref):
    back_pairs(dense_ref, turned_ref, keep_ref, units)


def fore_pairs(dense_ref, units, wide_ref, add_ref, out_ref, start):
    depth = wide_ref.shape[0] // len(units)
    runs = [(unit * depth, i * depth, depth) for i, unit in enumerate(units)]
    if units[1] == units[0] + 1:
        runs = [(units[0] * depth, 0, 2 * depth)]
    low = low_lanes((TILE, TILE))
    step = 4
    pairs = out_ref.shape[0] // TILE
    for pair in range(0, pairs, step):
        rows = slice((start + pair) * PAIR, (start + pair + step) * PAIR)
        product = sum(
            jnp.dot(
                dense_ref[rows, cell : cell + size],
                wide_ref[row : row + size, :],
                preferred_element_type=jnp.float32,
            )
            for cell, row, size in runs
        )
        for i in range(step):
            even, odd = product[rows_of(2 * i), :], product[rows_of(2 * i + 1), :]
            value = jnp.where(low, even, odd)
            if add_ref is not None:
                value = value + add_ref[rows_of(start + pair + i), :]
            out_ref[rows_of(pair + i), :] = value


def fore_vector(parts, wide_ref, raw_ref, scales):
    low = low_lanes((TILE, TILE))
    sums = []
    for pair, value, squares in next_vector(parts, raw_ref, *scales):
        other = turned(value)
        wide_ref[rows_of(2 * pair), :] = jnp.where(low, value, other).astype(wide_ref.dtype)
        wide_ref[rows_of(2 * pair + 1), :] = jnp.where(low, other, value).astype(wide_ref.dtype)
        if squares is not None:
            sums.append(squares)
    return sums[0] + sums[1]


def fore_own_kernel(first, units, dense_ref, inner_ref, mine_ref, scale_ref, *refs):
    past_ref, past_scale_ref = (None, None) if first else refs[:2]
    part_ref, sum_ref, raw_ref, wide_ref = refs[-4:]
    parts = [(inner_ref, 1), (mine_ref, 1)]
    sum_ref[...] = fore_vector(parts, wide_ref, raw_ref, (scale_ref, past_ref, past_scale_ref))
    fore_pairs(dense_ref, units, wide_ref, None, part_ref, 0)


def fore_send_kernel(first, units, dense_ref, outer_ref, part_ref, sum_ref, scale_ref, *refs):
    past_ref, past_scale_ref = (None, None) if first else refs[:2]
    send_ref, wide_ref, raw_ref = refs[-3:]
    squares = fore_vector([(outer_ref, 2)], wide_ref, raw_ref, (scale_ref, past_ref, past_scale_ref))
    row = squares_row([squares, sum_ref[...]])
    send_ref[-NORM_ROWS:, :] = jnp.broadcast_to(row, (NORM_ROWS, TILE))
    fore_pairs(dense_ref, units, wide_ref, part_ref, send_ref, 0)


def fore_keep_kernel(units, dense_ref, wide_ref, part_ref, keep_ref):
    start = keep_ref.shape[0] // TILE
    fore_pairs(dense_ref, units, wide_ref, part_ref, keep_ref, start)


def product_call(body, dense, operands, shapes, scratch=()):
    return pl.pallas_call(
        body,
        in_specs=[WHOLE] * (1 + len(operands)),
        out_specs=[WHOLE] * len(shapes),
        out_shape=shapes,
        scratch_shapes=scratch,
        compiler_params=pltpu.CompilerParams(vmem_limit_bytes=12 * 1024 * 1024),
        cost_estimate=pl.CostEstimate(
            flops=2 * TILE * dense.size, bytes_accessed=dense.size, transcendentals=0
        ),
    )(dense, *operands)


def float_rows(rows):
    return jax.ShapeDtypeStruct((rows, TILE), jnp.float32)


def back_product(order, dense, operands, first):
    rows, cells = dense.shape[0], CB_DEV * TILE
    shapes = [float_rows(cells // 4 + NORM_ROWS), jax.ShapeDtypeStruct((TILE // 2, rows), dense.dtype)]
    shapes += [] if first else [float_rows(rows // 2)]
    send, flat, *raw = product_call(
        functools.partial(back_send_kernel, first, order[:2]), dense, operands, shapes
    )


    body = functools.partial(back_keep_kernel, order[2:])
    (keep,) = product_call(body, dense, [flat], [float_rows(cells // 4)])
    return send, keep, *raw


def fore_own_product(order, dense, operands, first):
    rows, cells = dense.shape[0], CB_DEV * TILE
    return product_call(
        functools.partial(fore_own_kernel, first, order[2:]),
        dense,
        operands,
        [float_rows(rows // 2), float_rows(NORM_ROWS), float_rows(cells // 4)],
        [pltpu.VMEM((cells // 2, TILE), dense.dtype)],
    )


def fore_product(order, dense, operands, first):
    rows, cells = dense.shape[0], CB_DEV * TILE
    shapes = [
        float_rows(rows // 4 + NORM_ROWS),
        jax.ShapeDtypeStruct((cells // 2, TILE), dense.dtype),
        float_rows(cells // 4),
    ]
    send, wide, raw = product_call(
        functools.partial(fore_send_kernel, first, order[:2]), dense, operands, shapes
    )

    def keep(wide):
        body = functools.partial(fore_keep_kernel, order[:2])
        return product_call(body, dense, [wide, operands[1]], [float_rows(rows // 4)])[0]

    return send, (keep, wide), raw


def rotation(norms):
    betas, alphas = [norm_of(ref) for ref in norms[0::2]], [norm_of(ref) for ref in norms[1::2]]
    resid_bar, diag_bar = betas[0], alphas[0]
    steps = []
    for j in range(len(alphas)):
        radius = jnp.sqrt(diag_bar * diag_bar + betas[j + 1] * betas[j + 1])
        rotate_cos = diag_bar / radius
        rotate_sin = betas[j + 1] / radius
        step_size = rotate_cos * resid_bar
        resid_bar = rotate_sin * resid_bar
        coupling = None
        if j + 1 < len(alphas):
            coupling = rotate_sin * alphas[j + 1] / radius
            diag_bar = -rotate_cos * alphas[j + 1]
        steps.append((step_size / radius, coupling))
    misfit = resid_bar / betas[0]
    return alphas, betas, steps, misfit, misfit * rotate_cos


def store_in_order(out_ref, mask, pair, low, values):
    pairs = out_ref.shape[0] // PAIR // UNITS
    start = (((pair // pairs) ^ mask) * pairs + pair % pairs) * PAIR
    ours, theirs = values
    even = pl.ds(pl.multiple_of(start, TILE), TILE)
    odd = pl.ds(pl.multiple_of(start + TILE, TILE), TILE)
    out_ref[even, :] = jnp.where(low, ours, turned(theirs))
    out_ref[odd, :] = jnp.where(low, turned(ours), theirs)


def model_kernel(count, mask_ref, *refs):
    ins, (model_ref, misfit_ref) = refs[:-2], refs[-2:]
    chains = [ins[: len(ins) // 2], ins[len(ins) // 2 :]]
    low = low_lanes((TILE, TILE))
    rotations = [rotation(refs_[2 * count :]) for refs_ in chains]
    misfits = [jnp.broadcast_to(r[3], misfit_ref.shape) for r in rotations]
    misfit_ref[...] = jnp.where(low_lanes(misfit_ref.shape), misfits[0], misfits[1])
    pairs = model_ref.shape[0] // PAIR // UNITS
    for pair in range(model_ref.shape[0] // PAIR):
        values = []
        for order, refs_, (alphas, _, steps, _, _) in zip(UNIT_ORDERS, chains, rotations):
            slot = order.index(pair // pairs)
            rows = rows_of(slot % 2 * pairs + pair % pairs)
            search = total = None
            for j in range(count):
                right = refs_[2 * j + slot // 2][rows, :] / alphas[j]
                search = right if j == 0 else right - steps[j - 1][1] * search
                total = steps[j][0] * search if j == 0 else total + steps[j][0] * search
            values.append(total)
        store_in_order(model_ref, mask_ref[0], pair, low, values)


def gathered_values(outer, own, norms):
    factor = rotation(norms)[-1]
    values = []
    for half in (outer, own):
        if half is not None:
            parts, past_ref = half
            vector = next_vector(parts, None, norms[-1], past_ref, norms[-2])
            values += [factor * value for _, value, _ in vector]
    return values


def store_pair(ref, pair, low, ours, theirs):
    ref[rows_of(2 * pair), :] = jnp.where(low, ours, turned(theirs))
    ref[rows_of(2 * pair + 1), :] = jnp.where(low, turned(ours), theirs)


def ready_kernel(outer_ref, inner_ref, mine_ref, past_ref, own_past_ref, *refs):
    norms, refs = refs[: 2 * ITERS + 1], refs[2 * ITERS + 1 :]
    second_inner_ref, second_mine_ref, second_past_ref, *second_norms, ready_ref, ours_ref = refs
    low = low_lanes((TILE, TILE))
    ours = gathered_values(
        ([(outer_ref, 2)], past_ref), ([(inner_ref, 1), (mine_ref, 1)], own_past_ref), norms
    )
    theirs = gathered_values(
        None, ([(second_inner_ref, 1), (second_mine_ref, 1)], second_past_ref), second_norms
    )
    pairs = mine_ref.shape[0] // TILE
    for slot, unit in enumerate(UNIT_ORDERS[1]):
        start = UNIT_ORDERS[0].index(unit) * pairs
        for pair in range(pairs):
            if slot < 2:
                ours_ref[rows_of(slot * pairs + pair), :] = ours[start + pair]
            else:
                done = (slot - 2) * pairs + pair
                store_pair(ready_ref, done, low, ours[start + pair], theirs[done])


def gradient_kernel(mask_ref, ready_ref, ours_ref, outer_ref, past_ref, *refs):
    *norms, gradient_ref, last_ref, sent = refs
    low = low_lanes((TILE, TILE))
    size = gradient_ref.shape[0] // UNITS

    def send(slot, source_ref):
        rows = pl.ds(pl.multiple_of((UNIT_ORDERS[1][slot] ^ mask_ref[0]) * size, TILE), size)
        source = source_ref.at[pl.ds(slot % 2 * size, size)]
        return pltpu.make_async_copy(source, gradient_ref.at[rows], sent.at[slot])

    copies = [send(slot, last_ref if slot < 2 else ready_ref) for slot in range(UNITS)]
    for copy in copies[2:]:
        copy.start()
    theirs = gathered_values(([(outer_ref, 2)], past_ref), None, norms)
    for slot, copy in enumerate(copies[:2]):
        pairs = size // PAIR
        for pair in range(slot * pairs, (slot + 1) * pairs):
            store_pair(last_ref, pair, low, ours_ref[rows_of(pair), :], theirs[pair])
        copy.start()
    for copy in copies:
        copy.wait()


def gradient_of(mask, first, second):
    (rights, norms, totals), (second_rights, second_norms, second_totals) = first, second
    half = totals[0].shape[0]
    cost = pl.CostEstimate(flops=0, bytes_accessed=16 * half * TILE, transcendentals=0)
    params = pltpu.CompilerParams(vmem_limit_bytes=12 * 1024 * 1024)
    operands = [*totals, *rights[-1], *norms]
    operands += [*second_totals[1:], second_rights[-1][1], *second_norms]
    ready, ours = pl.pallas_call(
        ready_kernel,
        in_specs=[WHOLE] * len(operands),
        out_specs=[WHOLE] * 2,
        out_shape=[float_rows(2 * half), float_rows(half)],
        compiler_params=params,
        cost_estimate=cost,
    )(*operands)
    operands = [ready, ours, second_totals[0], second_rights[-1][0], *second_norms]
    return pl.pallas_call(
        gradient_kernel,
        in_specs=[SCALARS] + [WHOLE] * len(operands),
        out_specs=pl.BlockSpec(memory_space=pl.ANY),
        out_shape=float_rows(4 * half),
        scratch_shapes=[
            pltpu.VMEM((2 * half, TILE), jnp.float32),
            pltpu.SemaphoreType.DMA((UNITS,)),
        ],
        compiler_params=params,
        cost_estimate=cost,
    )(mask, *operands)


def last_call(body, mask, operands, shapes):
    return pl.pallas_call(
        body,
        in_specs=[SCALARS] + [WHOLE] * len(operands),
        out_specs=[WHOLE] * len(shapes),
        out_shape=[jax.ShapeDtypeStruct(shape, jnp.float32) for shape in shapes],
        compiler_params=pltpu.CompilerParams(vmem_limit_bytes=12 * 1024 * 1024),
        cost_estimate=pl.CostEstimate(
            flops=0, bytes_accessed=8 * shapes[0][0] * TILE, transcendentals=0
        ),
    )(mask, *operands)


def on_device(row_count, col_count, kernel, pattern, counts, delays):
    row_bits = list(range(row_count.bit_length() - 1))
    col_bits = list(range(col_count.bit_length() - 1))
    row_index = lax.axis_index("rows")
    core = lax.axis_index("cols") & 1

    near, far, *rest = row_bits
    orders = [[near, far, *rest, far, near], [far, near, *rest, near, far]]
    steps = len(orders[0])

    def swap_rows(second, value, level):
        pairs = []
        for row in range(row_count):
            for col in range(col_count):
                partner = row ^ (1 << orders[col & 1 ^ second][level])
                pairs.append((row * col_count + col, partner * col_count + col))
        return lax.ppermute(value, ("rows", "cols"), pairs)

    def swap_cols(value, level):
        return lax.ppermute(value, "cols", [(i, i ^ (1 << level)) for i in range(col_count)])

    bits = [(row_index >> bit) & 1 for bit in row_bits[:2]]
    outer_side = jnp.where(core == 0, bits[0], bits[1])
    inner_side = jnp.where(core == 0, bits[1], bits[0])
    mask = ((1 - outer_side) * 2 + (1 - inner_side)).astype(jnp.int32)
    blocks = jnp.arange(CB_DEV, dtype=jnp.int32)
    unit = CB_DEV // UNITS
    places = ((blocks // unit) ^ mask) * unit + blocks % unit
    flip = ((1 - core) * (kernel.shape[0] // 2)).astype(jnp.int32).reshape(1)
    mask = mask.reshape(1)

    dense, *lefts = fill_dense(kernel, pattern, counts, places, flip, delays)

    def tied(value, other):
        return lax.optimization_barrier((value, other))[0]

    def kept_half(kept, ahead):
        half, operand = kept
        return half(tied(operand, ahead))

    def reduce_rows(swap_rows, send, keep):
        half = keep.shape[0]
        got, _ = yield swap_rows, send, 0
        keep = keep + got[:half]
        norm = send[half:] + got[half:]
        send, mine = keep[: half // 2], keep[half // 2 :]
        for level in range(1, len(row_bits)):
            got, _ = yield swap_rows, jnp.concatenate([send, norm]), level
            norm = norm + got[half // 2 :]
            send = mine = mine + got[: half // 2]
        inner, _ = yield swap_rows, mine, steps - 2
        outer, ahead = yield swap_rows, jnp.concatenate([inner, mine]), steps - 1
        return [outer, inner, mine], norm, ahead

    def reduce_cols(send, kept):
        half = send.shape[0] - NORM_ROWS
        got, ahead = yield swap_cols, send, 0
        own = kept_half(kept, ahead) + got[:half]
        norm = send[half:] + got[half:]
        for bit in col_bits[1:]:
            got, _ = yield swap_cols, jnp.concatenate([own, norm]), bit
            norm = norm + got[half:]
            own = own + got[:half]
        other, _ = yield swap_cols, own, 0
        return [other, own], norm

    def chain(second, left):
        order = UNIT_ORDERS[second]
        swap = functools.partial(swap_rows, second)
        send, keep = back_product(order, dense, [left], True)
        totals, norm, ahead = yield from reduce_rows(swap, send, keep)
        norms = [norm]
        rights = []
        for iteration in range(ITERS):
            outer, *own = totals
            pasts = [[right, norms[-2]] for right in rights[-1]] if rights else [[], []]
            own = [tied(own[0], ahead), own[1]]
            part, squares, own_right = fore_own_product(
                order, dense, [*own, norms[-1], *pasts[1]], not rights
            )
            send, keep, right = fore_product(
                order, dense, [outer, part, squares, norms[-1], *pasts[0]], not rights
            )
            rights.append([right, own_right])
            halves, norm = yield from reduce_cols(send, keep)
            norms.append(norm)
            send, keep, left = back_product(
                order, dense, [*halves, norms[-1], left, norms[-2]], False
            )
            totals, norm, ahead = yield from reduce_rows(swap, send, keep)
            norms.append(norm)
        return rights, norms, totals

    runs = [chain(second, left) for second, left in enumerate(lefts)]
    wanted = [next(run) for run in runs]
    chains = [None] * len(runs)
    gots = [None] * len(runs)
    swap, value, level = wanted[0]
    gots[0] = swap(value, level)
    latest = wanted[1][1]
    turn = 0
    while None in chains:
        mine = 0 if turn < BEHIND else (turn - BEHIND) % 2
        turn += 1
        if chains[mine] is not None:
            continue
        if gots[mine] is None:
            swap, value, level = wanted[mine]
            latest = tied(value, latest)
        else:
            try:
                swap, latest, level = runs[mine].send((tied(gots[mine], latest), latest))
            except StopIteration as stop:
                chains[mine] = stop.value
                continue
        gots[mine] = swap(latest, level)

    cells = CB_DEV * TILE
    model, misfit = last_call(
        functools.partial(model_kernel, ITERS),
        mask,
        [operand for rights, norms, _ in chains for operand in [*sum(rights, []), *norms]],
        [(cells, TILE), (NORM_ROWS, TILE)],
    )
    gradient = gradient_of(mask, *chains)
    return (model, gradient, misfit[0])


def solution(mesh):
    placed = (P("rows", "cols", None, None), P("rows", "cols"), P("rows", "cols"), P("rows", None))

    def local(kernel, pattern, counts, delays):
        return on_device(
            mesh.shape["rows"], mesh.shape["cols"], kernel, pattern, counts, delays
        )

    return jax.shard_map(
        local,
        mesh=mesh,
        in_specs=placed,
        out_specs=(P("cols", None), P("cols", None), P()),
        check_vma=False,
    )
```

```python
import functools

import jax
import jax.numpy as jnp
from jax import lax
from jax.experimental import pallas as pl
from jax.experimental.pallas import tpu as pltpu
from jax.sharding import PartitionSpec as P

CB_DEV = 24
ITERS = 2
TILE = 128
PAIR = 2 * TILE
UNITS = 4
NORM_ROWS = 8
UNIT_ORDERS = ((0, 1, 2, 3), (0, 2, 1, 3))
BEHIND = 0

tiny_eps = 1e-06

WHOLE = pl.BlockSpec(memory_space=pltpu.VMEM)
SCALARS = pl.BlockSpec(memory_space=pltpu.SMEM)


def low_lanes(shape):
    return lax.broadcasted_iota(jnp.int32, shape, 1) < shape[1] // 2


def turned(value):
    return pltpu.roll(value, value.shape[1] // 2, 1)


def rows_of(pair, size=TILE):
    return slice(pair * size, (pair + 1) * size)


def fill_kernel(
    place_ref, flip_ref, pattern_in, counts_in, delays_in, tiles_in,
    dense_ref, even_left_ref, odd_left_ref, pattern_ref, counts_ref, delays_ref, tiles_ref, arrived,
):
    flip = flip_ref[0]
    row_blocks = tiles_in.shape[0]
    small = [
        pltpu.make_async_copy(source, target, arrived.at[2 * row_blocks + i])
        for i, (source, target) in enumerate(
            [(pattern_in, pattern_ref), (counts_in, counts_ref), (delays_in, delays_ref)]
        )
    ]
    for copy in small:
        copy.start()

    half = tiles_in.shape[1] // 2

    def fetch(position, upper):
        slots = pl.ds(upper * half, half)
        return pltpu.make_async_copy(
            tiles_in.at[position ^ flip, slots],
            tiles_ref.at[position, slots],
            arrived.at[upper * row_blocks + position],
        )

    for position in range(row_blocks):
        fetch(position, 0).start()
    for copy in small[:2]:
        copy.wait()
    for position in range(row_blocks):

        @pl.when(counts_ref[position ^ flip] > half)
        def _():
            fetch(position, 1).start()

    @pl.loop(0, row_blocks)
    def _(position):
        rows = pl.ds(pl.multiple_of(position * TILE, TILE), TILE)
        dense_ref[rows, :] = jnp.zeros((TILE, dense_ref.shape[1]), dense_ref.dtype)

    @pl.loop(0, row_blocks)
    def _(position):
        rows = pl.ds(pl.multiple_of(position * TILE, TILE), TILE)
        block = position ^ flip
        count = counts_ref[block]

        def place(tile):
            column = jnp.where(tile < count, place_ref[pattern_ref[block, tile]], CB_DEV)
            lanes = pl.ds(pl.multiple_of(column * TILE, TILE), TILE)
            dense_ref[rows, lanes] = tiles_ref[position, tile]

        fetch(position, 0).wait()
        for tile in range(half):
            place(tile)

        @pl.when(count > half)
        def _():
            fetch(position, 1).wait()
            for tile in range(half, 2 * half):
                place(tile)

    small[2].wait()
    low = low_lanes((TILE, TILE))
    for pair in range(row_blocks // 2):
        source = (pair ^ (flip // 2)) * PAIR
        even = delays_ref[pl.ds(pl.multiple_of(source, TILE), TILE), :]
        odd = delays_ref[pl.ds(pl.multiple_of(source + TILE, TILE), TILE), :]
        even_left_ref[rows_of(pair), :] = jnp.where(low, even, turned(odd))
        odd_left_ref[rows_of(pair), :] = jnp.where(low, turned(even), odd)


def fill_dense(kernel, pattern, counts, places, flip, delays):
    row_blocks = kernel.shape[0]
    rows = row_blocks * TILE
    left = jax.ShapeDtypeStruct((rows // 2, TILE), jnp.float32)
    return pl.pallas_call(
        fill_kernel,
        in_specs=[SCALARS] * 2 + [pl.BlockSpec(memory_space=pltpu.HBM)] * 4,
        out_specs=[WHOLE] * 3,
        out_shape=[jax.ShapeDtypeStruct((rows, (CB_DEV + 1) * TILE), kernel.dtype), left, left],
        scratch_shapes=[
            pltpu.SMEM(pattern.shape, jnp.int32),
            pltpu.SMEM((row_blocks,), jnp.int32),
            pltpu.VMEM(delays.shape, delays.dtype),
            pltpu.VMEM(kernel.shape, kernel.dtype),
            pltpu.SemaphoreType.DMA((2 * row_blocks + 3,)),
        ],
        compiler_params=pltpu.CompilerParams(vmem_limit_bytes=16 * 1024 * 1024),
        cost_estimate=pl.CostEstimate(
            flops=0, bytes_accessed=2 * kernel.size, transcendentals=0
        ),
    )(
        places,
        flip,
        *(pltpu.with_memory_space_constraint(x, pltpu.HBM) for x in (pattern, counts.reshape(-1), delays, kernel)),
    )


def norm_of(ref):
    return jnp.sqrt(ref[0:1, :] + tiny_eps)


def squares_row(sums):
    while len(sums) > 1:
        sums = [sums[i] + sums[i + 1] for i in range(0, len(sums), 2)]
    row = jnp.sum(sums[0], axis=0, keepdims=True)
    return row + turned(row)


def next_vector(parts, raw_ref, scale_ref, past_ref, past_scale_ref):
    if scale_ref is not None:
        scale = norm_of(scale_ref)
        shrink = 1.0 / scale
    if past_ref is not None:
        past_share = scale / norm_of(past_scale_ref)
    position = 0
    for part, units in parts:
        pairs = part.shape[0] // TILE // units
        for unit in range(units):
            squares = jnp.zeros((NORM_ROWS, TILE), jnp.float32)
            for pair in range(pairs):
                value = part[rows_of(unit * pairs + pair), :]
                if scale_ref is not None:
                    value = value * shrink
                if past_ref is not None:
                    value = value - past_share * past_ref[rows_of(position), :]
                if raw_ref is not None:
                    raw_ref[rows_of(position), :] = value
                squares += jnp.sum((value * value).reshape(-1, NORM_ROWS, TILE), axis=0)
                yield position, value, squares if pair == pairs - 1 else None
                position += 1


def back_pairs(dense_ref, turned_ref, out_ref, units):
    pairs = CB_DEV // 2 // UNITS
    for pair in range(pairs * len(units)):
        column = units[pair // pairs] * pairs + pair % pairs
        product = jnp.dot(
            turned_ref[...],
            dense_ref[:, rows_of(column, PAIR)],
            preferred_element_type=jnp.float32,
        )
        stacked = jnp.concatenate([product[:, :TILE], product[:, TILE:]], axis=0)
        out_ref[rows_of(pair), :] = stacked.T


def back_send_kernel(first, units, *refs):
    if first:
        dense_ref, own_ref, send_ref, turned_ref = refs
        parts, raw_ref, scales = [(own_ref, 2)], None, (None, None, None)
    else:
        (dense_ref, other_ref, own_ref, scale_ref, past_ref, past_scale_ref,
         send_ref, turned_ref, raw_ref) = refs
        parts, scales = [(other_ref, 1), (own_ref, 1)], (scale_ref, past_ref, past_scale_ref)
    sums = []
    half = turned_ref.shape[0]
    for pair, value, squares in next_vector(parts, raw_ref, *scales):
        flat = value.T.astype(turned_ref.dtype)
        turned_ref[:, rows_of(2 * pair)] = flat[:half]
        turned_ref[:, rows_of(2 * pair + 1)] = flat[half:]
        if squares is not None:
            sums.append(squares)
    send_ref[-NORM_ROWS:, :] = jnp.broadcast_to(squares_row(sums), (NORM_ROWS, TILE))
    back_pairs(dense_ref, turned_ref, send_ref, units)


def back_keep_kernel(units, dense_ref, turned_ref, keep_ref):
    back_pairs(dense_ref, turned_ref, keep_ref, units)


def fore_pairs(dense_ref, units, flat_ref, add_ref, out_ref, start):
    depth = flat_ref.shape[1] // len(units)
    runs = [(unit * depth, i * depth, depth) for i, unit in enumerate(units)]
    if units[1] == units[0] + 1:
        runs = [(units[0] * depth, 0, 2 * depth)]
    for pair in range(out_ref.shape[0] // TILE):
        product = sum(
            lax.dot_general(
                flat_ref[:, place : place + size],
                dense_ref[rows_of(start + pair, PAIR), cell : cell + size],
                (((1,), (1,)), ((), ())),
                preferred_element_type=jnp.float32,
            )
            for cell, place, size in runs
        )
        value = jnp.concatenate([product[:, :TILE], product[:, TILE:]], axis=0).T
        if add_ref is not None:
            value = value + add_ref[rows_of(start + pair), :]
        out_ref[rows_of(pair), :] = value


def fore_vector(parts, flat_ref, raw_ref, scales):
    half = flat_ref.shape[0]
    sums = []
    for pair, value, squares in next_vector(parts, raw_ref, *scales):
        flat = value.T.astype(flat_ref.dtype)
        flat_ref[:, rows_of(2 * pair)] = flat[:half]
        flat_ref[:, rows_of(2 * pair + 1)] = flat[half:]
        if squares is not None:
            sums.append(squares)
    return sums[0] + sums[1]


def fore_own_kernel(first, units, dense_ref, inner_ref, mine_ref, scale_ref, *refs):
    past_ref, past_scale_ref = (None, None) if first else refs[:2]
    part_ref, sum_ref, raw_ref, flat_ref = refs[-4:]
    parts = [(inner_ref, 1), (mine_ref, 1)]
    sum_ref[...] = fore_vector(parts, flat_ref, raw_ref, (scale_ref, past_ref, past_scale_ref))
    fore_pairs(dense_ref, units, flat_ref, None, part_ref, 0)


def fore_send_kernel(first, units, dense_ref, outer_ref, part_ref, sum_ref, scale_ref, *refs):
    past_ref, past_scale_ref = (None, None) if first else refs[:2]
    send_ref, flat_ref, raw_ref = refs[-3:]
    squares = fore_vector([(outer_ref, 2)], flat_ref, raw_ref, (scale_ref, past_ref, past_scale_ref))
    row = squares_row([squares, sum_ref[...]])
    send_ref[-NORM_ROWS:, :] = jnp.broadcast_to(row, (NORM_ROWS, TILE))
    fore_pairs(dense_ref, units, flat_ref, part_ref, send_ref, 0)


def fore_keep_kernel(units, dense_ref, flat_ref, part_ref, keep_ref):
    start = keep_ref.shape[0] // TILE
    fore_pairs(dense_ref, units, flat_ref, part_ref, keep_ref, start)


def product_call(body, dense, operands, shapes, scratch=()):
    return pl.pallas_call(
        body,
        in_specs=[WHOLE] * (1 + len(operands)),
        out_specs=[WHOLE] * len(shapes),
        out_shape=shapes,
        scratch_shapes=scratch,
        compiler_params=pltpu.CompilerParams(vmem_limit_bytes=12 * 1024 * 1024),
        cost_estimate=pl.CostEstimate(
            flops=2 * TILE * dense.size, bytes_accessed=dense.size, transcendentals=0
        ),
    )(dense, *operands)


def float_rows(rows):
    return jax.ShapeDtypeStruct((rows, TILE), jnp.float32)


def back_product(order, dense, operands, first):
    rows, cells = dense.shape[0], CB_DEV * TILE
    shapes = [float_rows(cells // 4 + NORM_ROWS), jax.ShapeDtypeStruct((TILE // 2, rows), dense.dtype)]
    shapes += [] if first else [float_rows(rows // 2)]
    send, flat, *raw = product_call(
        functools.partial(back_send_kernel, first, order[:2]), dense, operands, shapes
    )


    body = functools.partial(back_keep_kernel, order[2:])
    (keep,) = product_call(body, dense, [flat], [float_rows(cells // 4)])
    return send, keep, *raw


def fore_own_product(order, dense, operands, first):
    rows, cells = dense.shape[0], CB_DEV * TILE
    return product_call(
        functools.partial(fore_own_kernel, first, order[2:]),
        dense,
        operands,
        [float_rows(rows // 2), float_rows(NORM_ROWS), float_rows(cells // 4)],
        [pltpu.VMEM((TILE // 2, cells // 2), dense.dtype)],
    )


def fore_product(order, dense, operands, first):
    rows, cells = dense.shape[0], CB_DEV * TILE
    shapes = [
        float_rows(rows // 4 + NORM_ROWS),
        jax.ShapeDtypeStruct((TILE // 2, cells // 2), dense.dtype),
        float_rows(cells // 4),
    ]
    send, flat, raw = product_call(
        functools.partial(fore_send_kernel, first, order[:2]), dense, operands, shapes
    )

    def keep(flat):
        body = functools.partial(fore_keep_kernel, order[:2])
        return product_call(body, dense, [flat, operands[1]], [float_rows(rows // 4)])[0]

    return send, (keep, flat), raw


def rotation(norms):
    betas, alphas = [norm_of(ref) for ref in norms[0::2]], [norm_of(ref) for ref in norms[1::2]]
    resid_bar, diag_bar = betas[0], alphas[0]
    steps = []
    for j in range(len(alphas)):
        radius = jnp.sqrt(diag_bar * diag_bar + betas[j + 1] * betas[j + 1])
        rotate_cos = diag_bar / radius
        rotate_sin = betas[j + 1] / radius
        step_size = rotate_cos * resid_bar
        resid_bar = rotate_sin * resid_bar
        coupling = None
        if j + 1 < len(alphas):
            coupling = rotate_sin * alphas[j + 1] / radius
            diag_bar = -rotate_cos * alphas[j + 1]
        steps.append((step_size / radius, coupling))
    misfit = resid_bar / betas[0]
    return alphas, betas, steps, misfit, misfit * rotate_cos


def store_in_order(out_ref, mask, pair, low, values):
    pairs = out_ref.shape[0] // PAIR // UNITS
    start = (((pair // pairs) ^ mask) * pairs + pair % pairs) * PAIR
    ours, theirs = values
    even = pl.ds(pl.multiple_of(start, TILE), TILE)
    odd = pl.ds(pl.multiple_of(start + TILE, TILE), TILE)
    out_ref[even, :] = jnp.where(low, ours, turned(theirs))
    out_ref[odd, :] = jnp.where(low, turned(ours), theirs)


def model_kernel(count, mask_ref, *refs):
    ins, (model_ref, misfit_ref) = refs[:-2], refs[-2:]
    chains = [ins[: len(ins) // 2], ins[len(ins) // 2 :]]
    low = low_lanes((TILE, TILE))
    rotations = [rotation(refs_[2 * count :]) for refs_ in chains]
    misfits = [jnp.broadcast_to(r[3], misfit_ref.shape) for r in rotations]
    misfit_ref[...] = jnp.where(low_lanes(misfit_ref.shape), misfits[0], misfits[1])
    pairs = model_ref.shape[0] // PAIR // UNITS
    for pair in range(model_ref.shape[0] // PAIR):
        values = []
        for order, refs_, (alphas, _, steps, _, _) in zip(UNIT_ORDERS, chains, rotations):
            slot = order.index(pair // pairs)
            rows = rows_of(slot % 2 * pairs + pair % pairs)
            search = total = None
            for j in range(count):
                right = refs_[2 * j + slot // 2][rows, :] / alphas[j]
                search = right if j == 0 else right - steps[j - 1][1] * search
                total = steps[j][0] * search if j == 0 else total + steps[j][0] * search
            values.append(total)
        store_in_order(model_ref, mask_ref[0], pair, low, values)


def gathered_values(outer, own, norms):
    factor = rotation(norms)[-1]
    values = []
    for half in (outer, own):
        if half is not None:
            parts, past_ref = half
            vector = next_vector(parts, None, norms[-1], past_ref, norms[-2])
            values += [factor * value for _, value, _ in vector]
    return values


def store_pair(ref, pair, low, ours, theirs):
    ref[rows_of(2 * pair), :] = jnp.where(low, ours, turned(theirs))
    ref[rows_of(2 * pair + 1), :] = jnp.where(low, turned(ours), theirs)


def ready_kernel(outer_ref, inner_ref, mine_ref, past_ref, own_past_ref, *refs):
    norms, refs = refs[: 2 * ITERS + 1], refs[2 * ITERS + 1 :]
    second_inner_ref, second_mine_ref, second_past_ref, *second_norms, ready_ref, ours_ref = refs
    low = low_lanes((TILE, TILE))
    ours = gathered_values(
        ([(outer_ref, 2)], past_ref), ([(inner_ref, 1), (mine_ref, 1)], own_past_ref), norms
    )
    theirs = gathered_values(
        None, ([(second_inner_ref, 1), (second_mine_ref, 1)], second_past_ref), second_norms
    )
    pairs = mine_ref.shape[0] // TILE
    for slot, unit in enumerate(UNIT_ORDERS[1]):
        start = UNIT_ORDERS[0].index(unit) * pairs
        for pair in range(pairs):
            if slot < 2:
                ours_ref[rows_of(slot * pairs + pair), :] = ours[start + pair]
            else:
                done = (slot - 2) * pairs + pair
                store_pair(ready_ref, done, low, ours[start + pair], theirs[done])


def gradient_kernel(mask_ref, ready_ref, ours_ref, outer_ref, past_ref, *refs):
    *norms, gradient_ref, last_ref, sent = refs
    low = low_lanes((TILE, TILE))
    size = gradient_ref.shape[0] // UNITS

    def send(slot, source_ref):
        rows = pl.ds(pl.multiple_of((UNIT_ORDERS[1][slot] ^ mask_ref[0]) * size, TILE), size)
        source = source_ref.at[pl.ds(slot % 2 * size, size)]
        return pltpu.make_async_copy(source, gradient_ref.at[rows], sent.at[slot])

    copies = [send(slot, last_ref if slot < 2 else ready_ref) for slot in range(UNITS)]
    for copy in copies[2:]:
        copy.start()
    theirs = gathered_values(([(outer_ref, 2)], past_ref), None, norms)
    for slot, copy in enumerate(copies[:2]):
        pairs = size // PAIR
        for pair in range(slot * pairs, (slot + 1) * pairs):
            store_pair(last_ref, pair, low, ours_ref[rows_of(pair), :], theirs[pair])
        copy.start()
    for copy in copies:
        copy.wait()


def gradient_of(mask, first, second):
    (rights, norms, totals), (second_rights, second_norms, second_totals) = first, second
    half = totals[0].shape[0]
    cost = pl.CostEstimate(flops=0, bytes_accessed=16 * half * TILE, transcendentals=0)
    params = pltpu.CompilerParams(vmem_limit_bytes=12 * 1024 * 1024)
    operands = [*totals, *rights[-1], *norms]
    operands += [*second_totals[1:], second_rights[-1][1], *second_norms]
    ready, ours = pl.pallas_call(
        ready_kernel,
        in_specs=[WHOLE] * len(operands),
        out_specs=[WHOLE] * 2,
        out_shape=[float_rows(2 * half), float_rows(half)],
        compiler_params=params,
        cost_estimate=cost,
    )(*operands)
    operands = [ready, ours, second_totals[0], second_rights[-1][0], *second_norms]
    return pl.pallas_call(
        gradient_kernel,
        in_specs=[SCALARS] + [WHOLE] * len(operands),
        out_specs=pl.BlockSpec(memory_space=pl.ANY),
        out_shape=float_rows(4 * half),
        scratch_shapes=[
            pltpu.VMEM((2 * half, TILE), jnp.float32),
            pltpu.SemaphoreType.DMA((UNITS,)),
        ],
        compiler_params=params,
        cost_estimate=cost,
    )(mask, *operands)


def last_call(body, mask, operands, shapes):
    return pl.pallas_call(
        body,
        in_specs=[SCALARS] + [WHOLE] * len(operands),
        out_specs=[WHOLE] * len(shapes),
        out_shape=[jax.ShapeDtypeStruct(shape, jnp.float32) for shape in shapes],
        compiler_params=pltpu.CompilerParams(vmem_limit_bytes=12 * 1024 * 1024),
        cost_estimate=pl.CostEstimate(
            flops=0, bytes_accessed=8 * shapes[0][0] * TILE, transcendentals=0
        ),
    )(mask, *operands)


def on_device(row_count, col_count, kernel, pattern, counts, delays):
    row_bits = list(range(row_count.bit_length() - 1))
    col_bits = list(range(col_count.bit_length() - 1))
    row_index = lax.axis_index("rows")
    core = lax.axis_index("cols") & 1

    near, far, *rest = row_bits
    orders = [[near, far, *rest, far, near], [far, near, *rest, near, far]]
    steps = len(orders[0])

    def swap_rows(second, value, level):
        pairs = []
        for row in range(row_count):
            for col in range(col_count):
                partner = row ^ (1 << orders[col & 1 ^ second][level])
                pairs.append((row * col_count + col, partner * col_count + col))
        return lax.ppermute(value, ("rows", "cols"), pairs)

    def swap_cols(value, level):
        return lax.ppermute(value, "cols", [(i, i ^ (1 << level)) for i in range(col_count)])

    bits = [(row_index >> bit) & 1 for bit in row_bits[:2]]
    outer_side = jnp.where(core == 0, bits[0], bits[1])
    inner_side = jnp.where(core == 0, bits[1], bits[0])
    mask = ((1 - outer_side) * 2 + (1 - inner_side)).astype(jnp.int32)
    blocks = jnp.arange(CB_DEV, dtype=jnp.int32)
    unit = CB_DEV // UNITS
    places = ((blocks // unit) ^ mask) * unit + blocks % unit
    flip = ((1 - core) * (kernel.shape[0] // 2)).astype(jnp.int32).reshape(1)
    mask = mask.reshape(1)

    dense, *lefts = fill_dense(kernel, pattern, counts, places, flip, delays)

    def tied(value, other):
        return lax.optimization_barrier((value, other))[0]

    def kept_half(kept, ahead):
        half, operand = kept
        return half(tied(operand, ahead))

    def reduce_rows(swap_rows, send, keep):
        half = keep.shape[0]
        got, _ = yield swap_rows, send, 0
        keep = keep + got[:half]
        norm = send[half:] + got[half:]
        send, mine = keep[: half // 2], keep[half // 2 :]
        for level in range(1, len(row_bits)):
            got, _ = yield swap_rows, jnp.concatenate([send, norm]), level
            norm = norm + got[half // 2 :]
            send = mine = mine + got[: half // 2]
        inner, _ = yield swap_rows, mine, steps - 2
        outer, ahead = yield swap_rows, jnp.concatenate([inner, mine]), steps - 1
        return [outer, inner, mine], norm, ahead

    def reduce_cols(send, kept):
        half = send.shape[0] - NORM_ROWS
        got, ahead = yield swap_cols, send, 0
        own = kept_half(kept, ahead) + got[:half]
        norm = send[half:] + got[half:]
        for bit in col_bits[1:]:
            got, _ = yield swap_cols, jnp.concatenate([own, norm]), bit
            norm = norm + got[half:]
            own = own + got[:half]
        other, _ = yield swap_cols, own, 0
        return [other, own], norm

    def chain(second, left):
        order = UNIT_ORDERS[second]
        swap = functools.partial(swap_rows, second)
        send, keep = back_product(order, dense, [left], True)
        totals, norm, ahead = yield from reduce_rows(swap, send, keep)
        norms = [norm]
        rights = []
        for iteration in range(ITERS):
            outer, *own = totals
            pasts = [[right, norms[-2]] for right in rights[-1]] if rights else [[], []]
            own = [tied(own[0], ahead), own[1]]
            part, squares, own_right = fore_own_product(
                order, dense, [*own, norms[-1], *pasts[1]], not rights
            )
            send, keep, right = fore_product(
                order, dense, [outer, part, squares, norms[-1], *pasts[0]], not rights
            )
            rights.append([right, own_right])
            halves, norm = yield from reduce_cols(send, keep)
            norms.append(norm)
            send, keep, left = back_product(
                order, dense, [*halves, norms[-1], left, norms[-2]], False
            )
            totals, norm, ahead = yield from reduce_rows(swap, send, keep)
            norms.append(norm)
        return rights, norms, totals

    runs = [chain(second, left) for second, left in enumerate(lefts)]
    wanted = [next(run) for run in runs]
    chains = [None] * len(runs)
    gots = [None] * len(runs)
    swap, value, level = wanted[0]
    gots[0] = swap(value, level)
    latest = wanted[1][1]
    turn = 0
    while None in chains:
        mine = 0 if turn < BEHIND else (turn - BEHIND) % 2
        turn += 1
        if chains[mine] is not None:
            continue
        if gots[mine] is None:
            swap, value, level = wanted[mine]
            latest = tied(value, latest)
        else:
            try:
                swap, latest, level = runs[mine].send((tied(gots[mine], latest), latest))
            except StopIteration as stop:
                chains[mine] = stop.value
                continue
        gots[mine] = swap(latest, level)

    cells = CB_DEV * TILE
    model, misfit = last_call(
        functools.partial(model_kernel, ITERS),
        mask,
        [operand for rights, norms, _ in chains for operand in [*sum(rights, []), *norms]],
        [(cells, TILE), (NORM_ROWS, TILE)],
    )
    gradient = gradient_of(mask, *chains)
    return (model, gradient, misfit[0])


def solution(mesh):
    placed = (P("rows", "cols", None, None), P("rows", "cols"), P("rows", "cols"), P("rows", None))

    def local(kernel, pattern, counts, delays):
        return on_device(
            mesh.shape["rows"], mesh.shape["cols"], kernel, pattern, counts, delays
        )

    return jax.shard_map(
        local,
        mesh=mesh,
        in_specs=placed,
        out_specs=(P("cols", None), P("cols", None), P()),
        check_vma=False,
    )
```

```python
import functools

import jax
import jax.numpy as jnp
from jax import lax
from jax.experimental import pallas as pl
from jax.experimental.pallas import tpu as pltpu
from jax.sharding import PartitionSpec as P

CB_DEV = 24
ITERS = 2
TILE = 128
PAIR = 2 * TILE
UNITS = 4
NORM_ROWS = 8
UNIT_ORDERS = ((0, 1, 2, 3), (0, 2, 1, 3))
BEHIND = 0

tiny_eps = 1e-06

WHOLE = pl.BlockSpec(memory_space=pltpu.VMEM)
SCALARS = pl.BlockSpec(memory_space=pltpu.SMEM)


def low_lanes(shape):
    return lax.broadcasted_iota(jnp.int32, shape, 1) < shape[1] // 2


def turned(value):
    return pltpu.roll(value, value.shape[1] // 2, 1)


def rows_of(pair, size=TILE):
    return slice(pair * size, (pair + 1) * size)


def fill_kernel(
    place_ref, flip_ref, pattern_in, counts_in, delays_in, tiles_in,
    dense_ref, even_left_ref, odd_left_ref, pattern_ref, counts_ref, delays_ref, tiles_ref, arrived,
):
    flip = flip_ref[0]
    row_blocks = tiles_in.shape[0]
    small = [
        pltpu.make_async_copy(source, target, arrived.at[2 * row_blocks + i])
        for i, (source, target) in enumerate(
            [(pattern_in, pattern_ref), (counts_in, counts_ref), (delays_in, delays_ref)]
        )
    ]
    for copy in small:
        copy.start()

    half = tiles_in.shape[1] // 2

    def fetch(position, upper):
        slots = pl.ds(upper * half, half)
        return pltpu.make_async_copy(
            tiles_in.at[position ^ flip, slots],
            tiles_ref.at[position, slots],
            arrived.at[upper * row_blocks + position],
        )

    for position in range(row_blocks):
        fetch(position, 0).start()
    @pl.loop(0, row_blocks)
    def _(position):
        rows = pl.ds(pl.multiple_of(position * TILE, TILE), TILE)
        dense_ref[rows, :] = jnp.zeros((TILE, dense_ref.shape[1]), dense_ref.dtype)

    for copy in small[:2]:
        copy.wait()
    for position in range(row_blocks):

        @pl.when(counts_ref[position ^ flip] > half)
        def _():
            fetch(position, 1).start()

    small[2].wait()
    low = low_lanes((TILE, TILE))
    for pair in range(row_blocks // 2):
        source = (pair ^ (flip // 2)) * PAIR
        even = delays_ref[pl.ds(pl.multiple_of(source, TILE), TILE), :]
        odd = delays_ref[pl.ds(pl.multiple_of(source + TILE, TILE), TILE), :]
        even_left_ref[rows_of(pair), :] = jnp.where(low, even, turned(odd))
        odd_left_ref[rows_of(pair), :] = jnp.where(low, turned(even), odd)

    @pl.loop(0, row_blocks)
    def _(position):
        rows = pl.ds(pl.multiple_of(position * TILE, TILE), TILE)
        block = position ^ flip
        count = counts_ref[block]

        def place(tile):
            column = jnp.where(tile < count, place_ref[pattern_ref[block, tile]], CB_DEV)
            lanes = pl.ds(pl.multiple_of(column * TILE, TILE), TILE)
            dense_ref[rows, lanes] = tiles_ref[position, tile]

        fetch(position, 0).wait()
        for tile in range(half):
            place(tile)

        @pl.when(count > half)
        def _():
            fetch(position, 1).wait()
            for tile in range(half, 2 * half):
                place(tile)


def fill_dense(kernel, pattern, counts, places, flip, delays):
    row_blocks = kernel.shape[0]
    rows = row_blocks * TILE
    left = jax.ShapeDtypeStruct((rows // 2, TILE), jnp.float32)
    return pl.pallas_call(
        fill_kernel,
        in_specs=[SCALARS] * 2 + [pl.BlockSpec(memory_space=pltpu.HBM)] * 4,
        out_specs=[WHOLE] * 3,
        out_shape=[jax.ShapeDtypeStruct((rows, (CB_DEV + 1) * TILE), kernel.dtype), left, left],
        scratch_shapes=[
            pltpu.SMEM(pattern.shape, jnp.int32),
            pltpu.SMEM((row_blocks,), jnp.int32),
            pltpu.VMEM(delays.shape, delays.dtype),
            pltpu.VMEM(kernel.shape, kernel.dtype),
            pltpu.SemaphoreType.DMA((2 * row_blocks + 3,)),
        ],
        compiler_params=pltpu.CompilerParams(vmem_limit_bytes=16 * 1024 * 1024),
        cost_estimate=pl.CostEstimate(
            flops=0, bytes_accessed=2 * kernel.size, transcendentals=0
        ),
    )(
        places,
        flip,
        *(pltpu.with_memory_space_constraint(x, pltpu.HBM) for x in (pattern, counts.reshape(-1), delays, kernel)),
    )


def norm_of(ref):
    return jnp.sqrt(ref[0:1, :] + tiny_eps)


def squares_row(sums):
    while len(sums) > 1:
        sums = [sums[i] + sums[i + 1] for i in range(0, len(sums), 2)]
    row = jnp.sum(sums[0], axis=0, keepdims=True)
    return row + turned(row)


def next_vector(parts, raw_ref, scale_ref, past_ref, past_scale_ref):
    if scale_ref is not None:
        scale = norm_of(scale_ref)
        shrink = 1.0 / scale
    if past_ref is not None:
        past_share = scale / norm_of(past_scale_ref)
    position = 0
    for part, units in parts:
        pairs = part.shape[0] // TILE // units
        for unit in range(units):
            squares = jnp.zeros((NORM_ROWS, TILE), jnp.float32)
            for pair in range(pairs):
                value = part[rows_of(unit * pairs + pair), :]
                if scale_ref is not None:
                    value = value * shrink
                if past_ref is not None:
                    value = value - past_share * past_ref[rows_of(position), :]
                if raw_ref is not None:
                    raw_ref[rows_of(position), :] = value
                squares += jnp.sum((value * value).reshape(-1, NORM_ROWS, TILE), axis=0)
                yield position, value, squares if pair == pairs - 1 else None
                position += 1


def back_pairs(dense_ref, turned_ref, out_ref, units):
    pairs = CB_DEV // 2 // UNITS
    for pair in range(pairs * len(units)):
        column = units[pair // pairs] * pairs + pair % pairs
        product = jnp.dot(
            turned_ref[...],
            dense_ref[:, rows_of(column, PAIR)],
            preferred_element_type=jnp.float32,
        )
        stacked = jnp.concatenate([product[:, :TILE], product[:, TILE:]], axis=0)
        out_ref[rows_of(pair), :] = stacked.T


def back_send_kernel(first, units, *refs):
    if first:
        dense_ref, own_ref, send_ref, turned_ref = refs
        parts, raw_ref, scales = [(own_ref, 2)], None, (None, None, None)
    else:
        (dense_ref, other_ref, own_ref, scale_ref, past_ref, past_scale_ref,
         send_ref, turned_ref, raw_ref) = refs
        parts, scales = [(other_ref, 1), (own_ref, 1)], (scale_ref, past_ref, past_scale_ref)
    sums = []
    half = turned_ref.shape[0]
    for pair, value, squares in next_vector(parts, raw_ref, *scales):
        flat = value.T.astype(turned_ref.dtype)
        turned_ref[:, rows_of(2 * pair)] = flat[:half]
        turned_ref[:, rows_of(2 * pair + 1)] = flat[half:]
        if squares is not None:
            sums.append(squares)
    send_ref[-NORM_ROWS:, :] = jnp.broadcast_to(squares_row(sums), (NORM_ROWS, TILE))
    back_pairs(dense_ref, turned_ref, send_ref, units)


def back_keep_kernel(units, dense_ref, turned_ref, keep_ref):
    back_pairs(dense_ref, turned_ref, keep_ref, units)


def fore_pairs(dense_ref, units, wide_ref, add_ref, out_ref, start):
    depth = wide_ref.shape[0] // len(units)
    runs = [(unit * depth, i * depth, depth) for i, unit in enumerate(units)]
    if units[1] == units[0] + 1:
        runs = [(units[0] * depth, 0, 2 * depth)]
    low = low_lanes((TILE, TILE))
    step = 4
    pairs = out_ref.shape[0] // TILE
    for pair in range(0, pairs, step):
        rows = slice((start + pair) * PAIR, (start + pair + step) * PAIR)
        product = sum(
            jnp.dot(
                dense_ref[rows, cell : cell + size],
                wide_ref[row : row + size, :],
                preferred_element_type=jnp.float32,
            )
            for cell, row, size in runs
        )
        for i in range(step):
            even, odd = product[rows_of(2 * i), :], product[rows_of(2 * i + 1), :]
            value = jnp.where(low, even, odd)
            if add_ref is not None:
                value = value + add_ref[rows_of(start + pair + i), :]
            out_ref[rows_of(pair + i), :] = value


def fore_vector(parts, wide_ref, raw_ref, scales):
    low = low_lanes((TILE, TILE))
    sums = []
    for pair, value, squares in next_vector(parts, raw_ref, *scales):
        other = turned(value)
        wide_ref[rows_of(2 * pair), :] = jnp.where(low, value, other).astype(wide_ref.dtype)
        wide_ref[rows_of(2 * pair + 1), :] = jnp.where(low, other, value).astype(wide_ref.dtype)
        if squares is not None:
            sums.append(squares)
    return sums[0] + sums[1]


def fore_own_kernel(first, units, dense_ref, inner_ref, mine_ref, scale_ref, *refs):
    past_ref, past_scale_ref = (None, None) if first else refs[:2]
    part_ref, sum_ref, raw_ref, wide_ref = refs[-4:]
    parts = [(inner_ref, 1), (mine_ref, 1)]
    sum_ref[...] = fore_vector(parts, wide_ref, raw_ref, (scale_ref, past_ref, past_scale_ref))
    fore_pairs(dense_ref, units, wide_ref, None, part_ref, 0)


def fore_send_kernel(first, units, dense_ref, outer_ref, part_ref, sum_ref, scale_ref, *refs):
    past_ref, past_scale_ref = (None, None) if first else refs[:2]
    send_ref, wide_ref, raw_ref = refs[-3:]
    squares = fore_vector([(outer_ref, 2)], wide_ref, raw_ref, (scale_ref, past_ref, past_scale_ref))
    row = squares_row([squares, sum_ref[...]])
    send_ref[-NORM_ROWS:, :] = jnp.broadcast_to(row, (NORM_ROWS, TILE))
    fore_pairs(dense_ref, units, wide_ref, part_ref, send_ref, 0)


def fore_keep_kernel(units, dense_ref, wide_ref, part_ref, keep_ref):
    start = keep_ref.shape[0] // TILE
    fore_pairs(dense_ref, units, wide_ref, part_ref, keep_ref, start)


def product_call(body, dense, operands, shapes, scratch=()):
    return pl.pallas_call(
        body,
        in_specs=[WHOLE] * (1 + len(operands)),
        out_specs=[WHOLE] * len(shapes),
        out_shape=shapes,
        scratch_shapes=scratch,
        compiler_params=pltpu.CompilerParams(vmem_limit_bytes=12 * 1024 * 1024),
        cost_estimate=pl.CostEstimate(
            flops=2 * TILE * dense.size, bytes_accessed=dense.size, transcendentals=0
        ),
    )(dense, *operands)


def float_rows(rows):
    return jax.ShapeDtypeStruct((rows, TILE), jnp.float32)


def back_product(order, dense, operands, first):
    rows, cells = dense.shape[0], CB_DEV * TILE
    shapes = [float_rows(cells // 4 + NORM_ROWS), jax.ShapeDtypeStruct((TILE // 2, rows), dense.dtype)]
    shapes += [] if first else [float_rows(rows // 2)]
    send, flat, *raw = product_call(
        functools.partial(back_send_kernel, first, order[:2]), dense, operands, shapes
    )


    body = functools.partial(back_keep_kernel, order[2:])
    (keep,) = product_call(body, dense, [flat], [float_rows(cells // 4)])
    return send, keep, *raw


def fore_own_product(order, dense, operands, first):
    rows, cells = dense.shape[0], CB_DEV * TILE
    return product_call(
        functools.partial(fore_own_kernel, first, order[2:]),
        dense,
        operands,
        [float_rows(rows // 2), float_rows(NORM_ROWS), float_rows(cells // 4)],
        [pltpu.VMEM((cells // 2, TILE), dense.dtype)],
    )


def fore_product(order, dense, operands, first):
    rows, cells = dense.shape[0], CB_DEV * TILE
    shapes = [
        float_rows(rows // 4 + NORM_ROWS),
        jax.ShapeDtypeStruct((cells // 2, TILE), dense.dtype),
        float_rows(cells // 4),
    ]
    send, wide, raw = product_call(
        functools.partial(fore_send_kernel, first, order[:2]), dense, operands, shapes
    )

    def keep(wide):
        body = functools.partial(fore_keep_kernel, order[:2])
        return product_call(body, dense, [wide, operands[1]], [float_rows(rows // 4)])[0]

    return send, (keep, wide), raw


def rotation(norms):
    betas, alphas = [norm_of(ref) for ref in norms[0::2]], [norm_of(ref) for ref in norms[1::2]]
    resid_bar, diag_bar = betas[0], alphas[0]
    steps = []
    for j in range(len(alphas)):
        radius = jnp.sqrt(diag_bar * diag_bar + betas[j + 1] * betas[j + 1])
        rotate_cos = diag_bar / radius
        rotate_sin = betas[j + 1] / radius
        step_size = rotate_cos * resid_bar
        resid_bar = rotate_sin * resid_bar
        coupling = None
        if j + 1 < len(alphas):
            coupling = rotate_sin * alphas[j + 1] / radius
            diag_bar = -rotate_cos * alphas[j + 1]
        steps.append((step_size / radius, coupling))
    misfit = resid_bar / betas[0]
    return alphas, betas, steps, misfit, misfit * rotate_cos


def store_in_order(out_ref, mask, pair, low, values):
    pairs = out_ref.shape[0] // PAIR // UNITS
    start = (((pair // pairs) ^ mask) * pairs + pair % pairs) * PAIR
    ours, theirs = values
    even = pl.ds(pl.multiple_of(start, TILE), TILE)
    odd = pl.ds(pl.multiple_of(start + TILE, TILE), TILE)
    out_ref[even, :] = jnp.where(low, ours, turned(theirs))
    out_ref[odd, :] = jnp.where(low, turned(ours), theirs)


def model_kernel(count, mask_ref, *refs):
    ins, (model_ref, misfit_ref) = refs[:-2], refs[-2:]
    chains = [ins[: len(ins) // 2], ins[len(ins) // 2 :]]
    low = low_lanes((TILE, TILE))
    rotations = [rotation(refs_[2 * count :]) for refs_ in chains]
    misfits = [jnp.broadcast_to(r[3], misfit_ref.shape) for r in rotations]
    misfit_ref[...] = jnp.where(low_lanes(misfit_ref.shape), misfits[0], misfits[1])
    pairs = model_ref.shape[0] // PAIR // UNITS
    for pair in range(model_ref.shape[0] // PAIR):
        values = []
        for order, refs_, (alphas, _, steps, _, _) in zip(UNIT_ORDERS, chains, rotations):
            slot = order.index(pair // pairs)
            rows = rows_of(slot % 2 * pairs + pair % pairs)
            search = total = None
            for j in range(count):
                right = refs_[2 * j + slot // 2][rows, :] / alphas[j]
                search = right if j == 0 else right - steps[j - 1][1] * search
                total = steps[j][0] * search if j == 0 else total + steps[j][0] * search
            values.append(total)
        store_in_order(model_ref, mask_ref[0], pair, low, values)


def gathered_values(outer, own, norms):
    factor = rotation(norms)[-1]
    values = []
    for half in (outer, own):
        if half is not None:
            parts, past_ref = half
            vector = next_vector(parts, None, norms[-1], past_ref, norms[-2])
            values += [factor * value for _, value, _ in vector]
    return values


def store_pair(ref, pair, low, ours, theirs):
    ref[rows_of(2 * pair), :] = jnp.where(low, ours, turned(theirs))
    ref[rows_of(2 * pair + 1), :] = jnp.where(low, turned(ours), theirs)


def ready_kernel(outer_ref, inner_ref, mine_ref, past_ref, own_past_ref, *refs):
    norms, refs = refs[: 2 * ITERS + 1], refs[2 * ITERS + 1 :]
    second_inner_ref, second_mine_ref, second_past_ref, *second_norms, ready_ref, ours_ref = refs
    low = low_lanes((TILE, TILE))
    ours = gathered_values(
        ([(outer_ref, 2)], past_ref), ([(inner_ref, 1), (mine_ref, 1)], own_past_ref), norms
    )
    theirs = gathered_values(
        None, ([(second_inner_ref, 1), (second_mine_ref, 1)], second_past_ref), second_norms
    )
    pairs = mine_ref.shape[0] // TILE
    for slot, unit in enumerate(UNIT_ORDERS[1]):
        start = UNIT_ORDERS[0].index(unit) * pairs
        for pair in range(pairs):
            if slot < 2:
                ours_ref[rows_of(slot * pairs + pair), :] = ours[start + pair]
            else:
                done = (slot - 2) * pairs + pair
                store_pair(ready_ref, done, low, ours[start + pair], theirs[done])


def gradient_kernel(mask_ref, ready_ref, ours_ref, outer_ref, past_ref, *refs):
    *norms, gradient_ref, last_ref, sent = refs
    low = low_lanes((TILE, TILE))
    size = gradient_ref.shape[0] // UNITS

    def send(slot, source_ref):
        rows = pl.ds(pl.multiple_of((UNIT_ORDERS[1][slot] ^ mask_ref[0]) * size, TILE), size)
        source = source_ref.at[pl.ds(slot % 2 * size, size)]
        return pltpu.make_async_copy(source, gradient_ref.at[rows], sent.at[slot])

    copies = [send(slot, last_ref if slot < 2 else ready_ref) for slot in range(UNITS)]
    for copy in copies[2:]:
        copy.start()
    theirs = gathered_values(([(outer_ref, 2)], past_ref), None, norms)
    for slot, copy in enumerate(copies[:2]):
        pairs = size // PAIR
        for pair in range(slot * pairs, (slot + 1) * pairs):
            store_pair(last_ref, pair, low, ours_ref[rows_of(pair), :], theirs[pair])
        copy.start()
    for copy in copies:
        copy.wait()


def gradient_of(mask, first, second):
    (rights, norms, totals), (second_rights, second_norms, second_totals) = first, second
    half = totals[0].shape[0]
    cost = pl.CostEstimate(flops=0, bytes_accessed=16 * half * TILE, transcendentals=0)
    params = pltpu.CompilerParams(vmem_limit_bytes=12 * 1024 * 1024)
    operands = [*totals, *rights[-1], *norms]
    operands += [*second_totals[1:], second_rights[-1][1], *second_norms]
    ready, ours = pl.pallas_call(
        ready_kernel,
        in_specs=[WHOLE] * len(operands),
        out_specs=[WHOLE] * 2,
        out_shape=[float_rows(2 * half), float_rows(half)],
        compiler_params=params,
        cost_estimate=cost,
    )(*operands)
    operands = [ready, ours, second_totals[0], second_rights[-1][0], *second_norms]
    return pl.pallas_call(
        gradient_kernel,
        in_specs=[SCALARS] + [WHOLE] * len(operands),
        out_specs=pl.BlockSpec(memory_space=pl.ANY),
        out_shape=float_rows(4 * half),
        scratch_shapes=[
            pltpu.VMEM((2 * half, TILE), jnp.float32),
            pltpu.SemaphoreType.DMA((UNITS,)),
        ],
        compiler_params=params,
        cost_estimate=cost,
    )(mask, *operands)


def last_call(body, mask, operands, shapes):
    return pl.pallas_call(
        body,
        in_specs=[SCALARS] + [WHOLE] * len(operands),
        out_specs=[WHOLE] * len(shapes),
        out_shape=[jax.ShapeDtypeStruct(shape, jnp.float32) for shape in shapes],
        compiler_params=pltpu.CompilerParams(vmem_limit_bytes=12 * 1024 * 1024),
        cost_estimate=pl.CostEstimate(
            flops=0, bytes_accessed=8 * shapes[0][0] * TILE, transcendentals=0
        ),
    )(mask, *operands)


def on_device(row_count, col_count, kernel, pattern, counts, delays):
    row_bits = list(range(row_count.bit_length() - 1))
    col_bits = list(range(col_count.bit_length() - 1))
    row_index = lax.axis_index("rows")
    core = lax.axis_index("cols") & 1

    near, far, *rest = row_bits
    orders = [[near, far, *rest, far, near], [far, near, *rest, near, far]]
    steps = len(orders[0])

    def swap_rows(second, value, level):
        pairs = []
        for row in range(row_count):
            for col in range(col_count):
                partner = row ^ (1 << orders[col & 1 ^ second][level])
                pairs.append((row * col_count + col, partner * col_count + col))
        return lax.ppermute(value, ("rows", "cols"), pairs)

    def swap_cols(value, level):
        return lax.ppermute(value, "cols", [(i, i ^ (1 << level)) for i in range(col_count)])

    bits = [(row_index >> bit) & 1 for bit in row_bits[:2]]
    outer_side = jnp.where(core == 0, bits[0], bits[1])
    inner_side = jnp.where(core == 0, bits[1], bits[0])
    mask = ((1 - outer_side) * 2 + (1 - inner_side)).astype(jnp.int32)
    blocks = jnp.arange(CB_DEV, dtype=jnp.int32)
    unit = CB_DEV // UNITS
    places = ((blocks // unit) ^ mask) * unit + blocks % unit
    flip = ((1 - core) * (kernel.shape[0] // 2)).astype(jnp.int32).reshape(1)
    mask = mask.reshape(1)

    dense, *lefts = fill_dense(kernel, pattern, counts, places, flip, delays)

    def tied(value, other):
        return lax.optimization_barrier((value, other))[0]

    def kept_half(kept, ahead):
        half, operand = kept
        return half(tied(operand, ahead))

    def reduce_rows(swap_rows, send, keep):
        half = keep.shape[0]
        got, _ = yield swap_rows, send, 0
        keep = keep + got[:half]
        norm = send[half:] + got[half:]
        send, mine = keep[: half // 2], keep[half // 2 :]
        for level in range(1, len(row_bits)):
            got, _ = yield swap_rows, jnp.concatenate([send, norm]), level
            norm = norm + got[half // 2 :]
            send = mine = mine + got[: half // 2]
        inner, _ = yield swap_rows, mine, steps - 2
        outer, ahead = yield swap_rows, jnp.concatenate([inner, mine]), steps - 1
        return [outer, inner, mine], norm, ahead

    def reduce_cols(send, kept):
        half = send.shape[0] - NORM_ROWS
        got, ahead = yield swap_cols, send, 0
        own = kept_half(kept, ahead) + got[:half]
        norm = send[half:] + got[half:]
        for bit in col_bits[1:]:
            got, _ = yield swap_cols, jnp.concatenate([own, norm]), bit
            norm = norm + got[half:]
            own = own + got[:half]
        other, _ = yield swap_cols, own, 0
        return [other, own], norm

    def chain(second, left):
        order = UNIT_ORDERS[second]
        swap = functools.partial(swap_rows, second)
        send, keep = back_product(order, dense, [left], True)
        totals, norm, ahead = yield from reduce_rows(swap, send, keep)
        norms = [norm]
        rights = []
        for iteration in range(ITERS):
            outer, *own = totals
            pasts = [[right, norms[-2]] for right in rights[-1]] if rights else [[], []]
            own = [tied(own[0], ahead), own[1]]
            part, squares, own_right = fore_own_product(
                order, dense, [*own, norms[-1], *pasts[1]], not rights
            )
            send, keep, right = fore_product(
                order, dense, [outer, part, squares, norms[-1], *pasts[0]], not rights
            )
            rights.append([right, own_right])
            halves, norm = yield from reduce_cols(send, keep)
            norms.append(norm)
            send, keep, left = back_product(
                order, dense, [*halves, norms[-1], left, norms[-2]], False
            )
            totals, norm, ahead = yield from reduce_rows(swap, send, keep)
            norms.append(norm)
        return rights, norms, totals

    runs = [chain(second, left) for second, left in enumerate(lefts)]
    wanted = [next(run) for run in runs]
    chains = [None] * len(runs)
    gots = [None] * len(runs)
    swap, value, level = wanted[0]
    gots[0] = swap(value, level)
    latest = wanted[1][1]
    turn = 0
    while None in chains:
        mine = 0 if turn < BEHIND else (turn - BEHIND) % 2
        turn += 1
        if chains[mine] is not None:
            continue
        if gots[mine] is None:
            swap, value, level = wanted[mine]
            latest = tied(value, latest)
        else:
            try:
                swap, latest, level = runs[mine].send((tied(gots[mine], latest), latest))
            except StopIteration as stop:
                chains[mine] = stop.value
                continue
        gots[mine] = swap(latest, level)

    cells = CB_DEV * TILE
    model, misfit = last_call(
        functools.partial(model_kernel, ITERS),
        mask,
        [operand for rights, norms, _ in chains for operand in [*sum(rights, []), *norms]],
        [(cells, TILE), (NORM_ROWS, TILE)],
    )
    gradient = gradient_of(mask, *chains)
    return (model, gradient, misfit[0])


def solution(mesh):
    placed = (P("rows", "cols", None, None), P("rows", "cols"), P("rows", "cols"), P("rows", None))

    def local(kernel, pattern, counts, delays):
        return on_device(
            mesh.shape["rows"], mesh.shape["cols"], kernel, pattern, counts, delays
        )

    return jax.shard_map(
        local,
        mesh=mesh,
        in_specs=placed,
        out_specs=(P("cols", None), P("cols", None), P()),
        check_vma=False,
    )
```

```python
import functools

import jax
import jax.numpy as jnp
from jax import lax
from jax.experimental import pallas as pl
from jax.experimental.pallas import tpu as pltpu
from jax.sharding import PartitionSpec as P

CB_DEV = 24
ITERS = 2
TILE = 128
PAIR = 2 * TILE
UNITS = 4
NORM_ROWS = 8
FETCHES = 4
UNIT_ORDERS = ((0, 1, 2, 3), (0, 2, 1, 3))
BEHIND = 0

tiny_eps = 1e-06

WHOLE = pl.BlockSpec(memory_space=pltpu.VMEM)
SCALARS = pl.BlockSpec(memory_space=pltpu.SMEM)


def low_lanes(shape):
    return lax.broadcasted_iota(jnp.int32, shape, 1) < shape[1] // 2


def turned(value):
    return pltpu.roll(value, value.shape[1] // 2, 1)


def rows_of(pair, size=TILE):
    return slice(pair * size, (pair + 1) * size)


def fill_kernel(
    place_ref, flip_ref, pattern_in, counts_in, delays_in, tiles_in,
    dense_ref, even_left_ref, odd_left_ref, pattern_ref, counts_ref, delays_ref, tiles_ref, arrived,
):
    flip = flip_ref[0]
    row_blocks = tiles_in.shape[0]
    small = [
        pltpu.make_async_copy(source, target, arrived.at[FETCHES * row_blocks + i])
        for i, (source, target) in enumerate(
            [(pattern_in, pattern_ref), (counts_in, counts_ref), (delays_in, delays_ref)]
        )
    ]
    for copy in small:
        copy.start()

    size = tiles_in.shape[1] // FETCHES

    def fetch(position, part):
        slots = pl.ds(part * size, size)
        return pltpu.make_async_copy(
            tiles_in.at[position ^ flip, slots],
            tiles_ref.at[position, slots],
            arrived.at[part * row_blocks + position],
        )

    for position in range(row_blocks):
        fetch(position, 0).start()
    @pl.loop(0, row_blocks)
    def _(position):
        rows = pl.ds(pl.multiple_of(position * TILE, TILE), TILE)
        dense_ref[rows, :] = jnp.zeros((TILE, dense_ref.shape[1]), dense_ref.dtype)

    for copy in small[:2]:
        copy.wait()
    for position in range(row_blocks):
        for part in range(1, FETCHES):

            @pl.when(counts_ref[position ^ flip] > part * size)
            def _():
                fetch(position, part).start()

    small[2].wait()
    low = low_lanes((TILE, TILE))
    for pair in range(row_blocks // 2):
        source = (pair ^ (flip // 2)) * PAIR
        even = delays_ref[pl.ds(pl.multiple_of(source, TILE), TILE), :]
        odd = delays_ref[pl.ds(pl.multiple_of(source + TILE, TILE), TILE), :]
        even_left_ref[rows_of(pair), :] = jnp.where(low, even, turned(odd))
        odd_left_ref[rows_of(pair), :] = jnp.where(low, turned(even), odd)

    @pl.loop(0, row_blocks)
    def _(position):
        rows = pl.ds(pl.multiple_of(position * TILE, TILE), TILE)
        block = position ^ flip
        count = counts_ref[block]

        def place(tile):
            column = jnp.where(tile < count, place_ref[pattern_ref[block, tile]], CB_DEV)
            lanes = pl.ds(pl.multiple_of(column * TILE, TILE), TILE)
            dense_ref[rows, lanes] = tiles_ref[position, tile]

        for part in range(FETCHES):

            @pl.when(count > part * size)
            def _():
                fetch(position, part).wait()
                for tile in range(part * size, (part + 1) * size):
                    place(tile)


def fill_dense(kernel, pattern, counts, places, flip, delays):
    row_blocks = kernel.shape[0]
    rows = row_blocks * TILE
    left = jax.ShapeDtypeStruct((rows // 2, TILE), jnp.float32)
    return pl.pallas_call(
        fill_kernel,
        in_specs=[SCALARS] * 2 + [pl.BlockSpec(memory_space=pltpu.HBM)] * 4,
        out_specs=[WHOLE] * 3,
        out_shape=[jax.ShapeDtypeStruct((rows, (CB_DEV + 1) * TILE), kernel.dtype), left, left],
        scratch_shapes=[
            pltpu.SMEM(pattern.shape, jnp.int32),
            pltpu.SMEM((row_blocks,), jnp.int32),
            pltpu.VMEM(delays.shape, delays.dtype),
            pltpu.VMEM(kernel.shape, kernel.dtype),
            pltpu.SemaphoreType.DMA((FETCHES * row_blocks + 3,)),
        ],
        compiler_params=pltpu.CompilerParams(vmem_limit_bytes=16 * 1024 * 1024),
        cost_estimate=pl.CostEstimate(
            flops=0, bytes_accessed=2 * kernel.size, transcendentals=0
        ),
    )(
        places,
        flip,
        *(pltpu.with_memory_space_constraint(x, pltpu.HBM) for x in (pattern, counts.reshape(-1), delays, kernel)),
    )


def norm_of(ref):
    return jnp.sqrt(ref[0:1, :] + tiny_eps)


def squares_row(sums):
    while len(sums) > 1:
        sums = [sums[i] + sums[i + 1] for i in range(0, len(sums), 2)]
    row = jnp.sum(sums[0], axis=0, keepdims=True)
    return row + turned(row)


def next_vector(parts, raw_ref, scale_ref, past_ref, past_scale_ref):
    if scale_ref is not None:
        scale = norm_of(scale_ref)
        shrink = 1.0 / scale
    if past_ref is not None:
        past_share = scale / norm_of(past_scale_ref)
    position = 0
    for part, units in parts:
        pairs = part.shape[0] // TILE // units
        for unit in range(units):
            squares = jnp.zeros((NORM_ROWS, TILE), jnp.float32)
            for pair in range(pairs):
                value = part[rows_of(unit * pairs + pair), :]
                if scale_ref is not None:
                    value = value * shrink
                if past_ref is not None:
                    value = value - past_share * past_ref[rows_of(position), :]
                if raw_ref is not None:
                    raw_ref[rows_of(position), :] = value
                squares += jnp.sum((value * value).reshape(-1, NORM_ROWS, TILE), axis=0)
                yield position, value, squares if pair == pairs - 1 else None
                position += 1


def back_pairs(dense_ref, turned_ref, out_ref, units):
    pairs = CB_DEV // 2 // UNITS
    for pair in range(pairs * len(units)):
        column = units[pair // pairs] * pairs + pair % pairs
        product = jnp.dot(
            turned_ref[...],
            dense_ref[:, rows_of(column, PAIR)],
            preferred_element_type=jnp.float32,
        )
        stacked = jnp.concatenate([product[:, :TILE], product[:, TILE:]], axis=0)
        out_ref[rows_of(pair), :] = stacked.T


def back_send_kernel(first, units, *refs):
    if first:
        dense_ref, own_ref, send_ref, turned_ref = refs
        parts, raw_ref, scales = [(own_ref, 2)], None, (None, None, None)
    else:
        (dense_ref, other_ref, own_ref, scale_ref, past_ref, past_scale_ref,
         send_ref, turned_ref, raw_ref) = refs
        parts, scales = [(other_ref, 1), (own_ref, 1)], (scale_ref, past_ref, past_scale_ref)
    sums = []
    half = turned_ref.shape[0]
    for pair, value, squares in next_vector(parts, raw_ref, *scales):
        flat = value.T.astype(turned_ref.dtype)
        turned_ref[:, rows_of(2 * pair)] = flat[:half]
        turned_ref[:, rows_of(2 * pair + 1)] = flat[half:]
        if squares is not None:
            sums.append(squares)
    send_ref[-NORM_ROWS:, :] = jnp.broadcast_to(squares_row(sums), (NORM_ROWS, TILE))
    back_pairs(dense_ref, turned_ref, send_ref, units)


def back_keep_kernel(units, dense_ref, turned_ref, keep_ref):
    back_pairs(dense_ref, turned_ref, keep_ref, units)


def fore_pairs(dense_ref, units, wide_ref, add_ref, out_ref, start):
    depth = wide_ref.shape[0] // len(units)
    runs = [(unit * depth, i * depth, depth) for i, unit in enumerate(units)]
    if units[1] == units[0] + 1:
        runs = [(units[0] * depth, 0, 2 * depth)]
    low = low_lanes((TILE, TILE))
    step = 4
    pairs = out_ref.shape[0] // TILE
    for pair in range(0, pairs, step):
        rows = slice((start + pair) * PAIR, (start + pair + step) * PAIR)
        product = sum(
            jnp.dot(
                dense_ref[rows, cell : cell + size],
                wide_ref[row : row + size, :],
                preferred_element_type=jnp.float32,
            )
            for cell, row, size in runs
        )
        for i in range(step):
            even, odd = product[rows_of(2 * i), :], product[rows_of(2 * i + 1), :]
            value = jnp.where(low, even, odd)
            if add_ref is not None:
                value = value + add_ref[rows_of(start + pair + i), :]
            out_ref[rows_of(pair + i), :] = value


def fore_vector(parts, wide_ref, raw_ref, scales):
    low = low_lanes((TILE, TILE))
    sums = []
    for pair, value, squares in next_vector(parts, raw_ref, *scales):
        other = turned(value)
        wide_ref[rows_of(2 * pair), :] = jnp.where(low, value, other).astype(wide_ref.dtype)
        wide_ref[rows_of(2 * pair + 1), :] = jnp.where(low, other, value).astype(wide_ref.dtype)
        if squares is not None:
            sums.append(squares)
    return sums[0] + sums[1]


def fore_own_kernel(first, units, dense_ref, inner_ref, mine_ref, scale_ref, *refs):
    past_ref, past_scale_ref = (None, None) if first else refs[:2]
    part_ref, sum_ref, raw_ref, wide_ref = refs[-4:]
    parts = [(inner_ref, 1), (mine_ref, 1)]
    sum_ref[...] = fore_vector(parts, wide_ref, raw_ref, (scale_ref, past_ref, past_scale_ref))
    fore_pairs(dense_ref, units, wide_ref, None, part_ref, 0)


def fore_send_kernel(first, units, dense_ref, outer_ref, part_ref, sum_ref, scale_ref, *refs):
    past_ref, past_scale_ref = (None, None) if first else refs[:2]
    send_ref, wide_ref, raw_ref = refs[-3:]
    squares = fore_vector([(outer_ref, 2)], wide_ref, raw_ref, (scale_ref, past_ref, past_scale_ref))
    row = squares_row([squares, sum_ref[...]])
    send_ref[-NORM_ROWS:, :] = jnp.broadcast_to(row, (NORM_ROWS, TILE))
    fore_pairs(dense_ref, units, wide_ref, part_ref, send_ref, 0)


def fore_keep_kernel(units, dense_ref, wide_ref, part_ref, keep_ref):
    start = keep_ref.shape[0] // TILE
    fore_pairs(dense_ref, units, wide_ref, part_ref, keep_ref, start)


def product_call(body, dense, operands, shapes, scratch=()):
    return pl.pallas_call(
        body,
        in_specs=[WHOLE] * (1 + len(operands)),
        out_specs=[WHOLE] * len(shapes),
        out_shape=shapes,
        scratch_shapes=scratch,
        compiler_params=pltpu.CompilerParams(vmem_limit_bytes=12 * 1024 * 1024),
        cost_estimate=pl.CostEstimate(
            flops=2 * TILE * dense.size, bytes_accessed=dense.size, transcendentals=0
        ),
    )(dense, *operands)


def float_rows(rows):
    return jax.ShapeDtypeStruct((rows, TILE), jnp.float32)


def back_product(order, dense, operands, first):
    rows, cells = dense.shape[0], CB_DEV * TILE
    shapes = [float_rows(cells // 4 + NORM_ROWS), jax.ShapeDtypeStruct((TILE // 2, rows), dense.dtype)]
    shapes += [] if first else [float_rows(rows // 2)]
    send, flat, *raw = product_call(
        functools.partial(back_send_kernel, first, order[:2]), dense, operands, shapes
    )


    body = functools.partial(back_keep_kernel, order[2:])
    (keep,) = product_call(body, dense, [flat], [float_rows(cells // 4)])
    return send, keep, *raw


def fore_own_product(order, dense, operands, first):
    rows, cells = dense.shape[0], CB_DEV * TILE
    return product_call(
        functools.partial(fore_own_kernel, first, order[2:]),
        dense,
        operands,
        [float_rows(rows // 2), float_rows(NORM_ROWS), float_rows(cells // 4)],
        [pltpu.VMEM((cells // 2, TILE), dense.dtype)],
    )


def fore_product(order, dense, operands, first):
    rows, cells = dense.shape[0], CB_DEV * TILE
    shapes = [
        float_rows(rows // 4 + NORM_ROWS),
        jax.ShapeDtypeStruct((cells // 2, TILE), dense.dtype),
        float_rows(cells // 4),
    ]
    send, wide, raw = product_call(
        functools.partial(fore_send_kernel, first, order[:2]), dense, operands, shapes
    )

    def keep(wide):
        body = functools.partial(fore_keep_kernel, order[:2])
        return product_call(body, dense, [wide, operands[1]], [float_rows(rows // 4)])[0]

    return send, (keep, wide), raw


def rotation(norms):
    betas, alphas = [norm_of(ref) for ref in norms[0::2]], [norm_of(ref) for ref in norms[1::2]]
    resid_bar, diag_bar = betas[0], alphas[0]
    steps = []
    for j in range(len(alphas)):
        radius = jnp.sqrt(diag_bar * diag_bar + betas[j + 1] * betas[j + 1])
        rotate_cos = diag_bar / radius
        rotate_sin = betas[j + 1] / radius
        step_size = rotate_cos * resid_bar
        resid_bar = rotate_sin * resid_bar
        coupling = None
        if j + 1 < len(alphas):
            coupling = rotate_sin * alphas[j + 1] / radius
            diag_bar = -rotate_cos * alphas[j + 1]
        steps.append((step_size / radius, coupling))
    misfit = resid_bar / betas[0]
    return alphas, betas, steps, misfit, misfit * rotate_cos


def store_in_order(out_ref, mask, pair, low, values):
    pairs = out_ref.shape[0] // PAIR // UNITS
    start = (((pair // pairs) ^ mask) * pairs + pair % pairs) * PAIR
    ours, theirs = values
    even = pl.ds(pl.multiple_of(start, TILE), TILE)
    odd = pl.ds(pl.multiple_of(start + TILE, TILE), TILE)
    out_ref[even, :] = jnp.where(low, ours, turned(theirs))
    out_ref[odd, :] = jnp.where(low, turned(ours), theirs)


def model_kernel(count, mask_ref, *refs):
    ins, (model_ref, misfit_ref) = refs[:-2], refs[-2:]
    chains = [ins[: len(ins) // 2], ins[len(ins) // 2 :]]
    low = low_lanes((TILE, TILE))
    rotations = [rotation(refs_[2 * count :]) for refs_ in chains]
    misfits = [jnp.broadcast_to(r[3], misfit_ref.shape) for r in rotations]
    misfit_ref[...] = jnp.where(low_lanes(misfit_ref.shape), misfits[0], misfits[1])
    pairs = model_ref.shape[0] // PAIR // UNITS
    for pair in range(model_ref.shape[0] // PAIR):
        values = []
        for order, refs_, (alphas, _, steps, _, _) in zip(UNIT_ORDERS, chains, rotations):
            slot = order.index(pair // pairs)
            rows = rows_of(slot % 2 * pairs + pair % pairs)
            search = total = None
            for j in range(count):
                right = refs_[2 * j + slot // 2][rows, :] / alphas[j]
                search = right if j == 0 else right - steps[j - 1][1] * search
                total = steps[j][0] * search if j == 0 else total + steps[j][0] * search
            values.append(total)
        store_in_order(model_ref, mask_ref[0], pair, low, values)


def gathered_values(outer, own, norms):
    factor = rotation(norms)[-1]
    values = []
    for half in (outer, own):
        if half is not None:
            parts, past_ref = half
            vector = next_vector(parts, None, norms[-1], past_ref, norms[-2])
            values += [factor * value for _, value, _ in vector]
    return values


def store_pair(ref, pair, low, ours, theirs):
    ref[rows_of(2 * pair), :] = jnp.where(low, ours, turned(theirs))
    ref[rows_of(2 * pair + 1), :] = jnp.where(low, turned(ours), theirs)


def ready_kernel(outer_ref, inner_ref, mine_ref, past_ref, own_past_ref, *refs):
    norms, refs = refs[: 2 * ITERS + 1], refs[2 * ITERS + 1 :]
    second_inner_ref, second_mine_ref, second_past_ref, *second_norms, ready_ref, ours_ref = refs
    low = low_lanes((TILE, TILE))
    ours = gathered_values(
        ([(outer_ref, 2)], past_ref), ([(inner_ref, 1), (mine_ref, 1)], own_past_ref), norms
    )
    theirs = gathered_values(
        None, ([(second_inner_ref, 1), (second_mine_ref, 1)], second_past_ref), second_norms
    )
    pairs = mine_ref.shape[0] // TILE
    for slot, unit in enumerate(UNIT_ORDERS[1]):
        start = UNIT_ORDERS[0].index(unit) * pairs
        for pair in range(pairs):
            if slot < 2:
                ours_ref[rows_of(slot * pairs + pair), :] = ours[start + pair]
            else:
                done = (slot - 2) * pairs + pair
                store_pair(ready_ref, done, low, ours[start + pair], theirs[done])


def gradient_kernel(mask_ref, ready_ref, ours_ref, outer_ref, past_ref, *refs):
    *norms, gradient_ref, last_ref, sent = refs
    low = low_lanes((TILE, TILE))
    size = gradient_ref.shape[0] // UNITS

    def send(slot, source_ref):
        rows = pl.ds(pl.multiple_of((UNIT_ORDERS[1][slot] ^ mask_ref[0]) * size, TILE), size)
        source = source_ref.at[pl.ds(slot % 2 * size, size)]
        return pltpu.make_async_copy(source, gradient_ref.at[rows], sent.at[slot])

    copies = [send(slot, last_ref if slot < 2 else ready_ref) for slot in range(UNITS)]
    for copy in copies[2:]:
        copy.start()
    theirs = gathered_values(([(outer_ref, 2)], past_ref), None, norms)
    for slot, copy in enumerate(copies[:2]):
        pairs = size // PAIR
        for pair in range(slot * pairs, (slot + 1) * pairs):
            store_pair(last_ref, pair, low, ours_ref[rows_of(pair), :], theirs[pair])
        copy.start()
    for copy in copies:
        copy.wait()


def gradient_of(mask, first, second):
    (rights, norms, totals), (second_rights, second_norms, second_totals) = first, second
    half = totals[0].shape[0]
    cost = pl.CostEstimate(flops=0, bytes_accessed=16 * half * TILE, transcendentals=0)
    params = pltpu.CompilerParams(vmem_limit_bytes=12 * 1024 * 1024)
    operands = [*totals, *rights[-1], *norms]
    operands += [*second_totals[1:], second_rights[-1][1], *second_norms]
    ready, ours = pl.pallas_call(
        ready_kernel,
        in_specs=[WHOLE] * len(operands),
        out_specs=[WHOLE] * 2,
        out_shape=[float_rows(2 * half), float_rows(half)],
        compiler_params=params,
        cost_estimate=cost,
    )(*operands)
    operands = [ready, ours, second_totals[0], second_rights[-1][0], *second_norms]
    return pl.pallas_call(
        gradient_kernel,
        in_specs=[SCALARS] + [WHOLE] * len(operands),
        out_specs=pl.BlockSpec(memory_space=pl.ANY),
        out_shape=float_rows(4 * half),
        scratch_shapes=[
            pltpu.VMEM((2 * half, TILE), jnp.float32),
            pltpu.SemaphoreType.DMA((UNITS,)),
        ],
        compiler_params=params,
        cost_estimate=cost,
    )(mask, *operands)


def last_call(body, mask, operands, shapes):
    return pl.pallas_call(
        body,
        in_specs=[SCALARS] + [WHOLE] * len(operands),
        out_specs=[WHOLE] * len(shapes),
        out_shape=[jax.ShapeDtypeStruct(shape, jnp.float32) for shape in shapes],
        compiler_params=pltpu.CompilerParams(vmem_limit_bytes=12 * 1024 * 1024),
        cost_estimate=pl.CostEstimate(
            flops=0, bytes_accessed=8 * shapes[0][0] * TILE, transcendentals=0
        ),
    )(mask, *operands)


def on_device(row_count, col_count, kernel, pattern, counts, delays):
    row_bits = list(range(row_count.bit_length() - 1))
    col_bits = list(range(col_count.bit_length() - 1))
    row_index = lax.axis_index("rows")
    core = lax.axis_index("cols") & 1

    near, far, *rest = row_bits
    orders = [[near, far, *rest, far, near], [far, near, *rest, near, far]]
    steps = len(orders[0])

    def swap_rows(second, value, level):
        pairs = []
        for row in range(row_count):
            for col in range(col_count):
                partner = row ^ (1 << orders[col & 1 ^ second][level])
                pairs.append((row * col_count + col, partner * col_count + col))
        return lax.ppermute(value, ("rows", "cols"), pairs)

    def swap_cols(value, level):
        return lax.ppermute(value, "cols", [(i, i ^ (1 << level)) for i in range(col_count)])

    bits = [(row_index >> bit) & 1 for bit in row_bits[:2]]
    outer_side = jnp.where(core == 0, bits[0], bits[1])
    inner_side = jnp.where(core == 0, bits[1], bits[0])
    mask = ((1 - outer_side) * 2 + (1 - inner_side)).astype(jnp.int32)
    blocks = jnp.arange(CB_DEV, dtype=jnp.int32)
    unit = CB_DEV // UNITS
    places = ((blocks // unit) ^ mask) * unit + blocks % unit
    flip = ((1 - core) * (kernel.shape[0] // 2)).astype(jnp.int32).reshape(1)
    mask = mask.reshape(1)

    dense, *lefts = fill_dense(kernel, pattern, counts, places, flip, delays)

    def tied(value, other):
        return lax.optimization_barrier((value, other))[0]

    def kept_half(kept, ahead):
        half, operand = kept
        return half(tied(operand, ahead))

    def reduce_rows(swap_rows, send, keep):
        half = keep.shape[0]
        got, _ = yield swap_rows, send, 0
        keep = keep + got[:half]
        norm = send[half:] + got[half:]
        send, mine = keep[: half // 2], keep[half // 2 :]
        for level in range(1, len(row_bits)):
            got, _ = yield swap_rows, jnp.concatenate([send, norm]), level
            norm = norm + got[half // 2 :]
            send = mine = mine + got[: half // 2]
        inner, _ = yield swap_rows, mine, steps - 2
        outer, ahead = yield swap_rows, jnp.concatenate([inner, mine]), steps - 1
        return [outer, inner, mine], norm, ahead

    def reduce_cols(send, kept):
        half = send.shape[0] - NORM_ROWS
        got, ahead = yield swap_cols, send, 0
        own = kept_half(kept, ahead) + got[:half]
        norm = send[half:] + got[half:]
        for bit in col_bits[1:]:
            got, _ = yield swap_cols, jnp.concatenate([own, norm]), bit
            norm = norm + got[half:]
            own = own + got[:half]
        other, _ = yield swap_cols, own, 0
        return [other, own], norm

    def chain(second, left):
        order = UNIT_ORDERS[second]
        swap = functools.partial(swap_rows, second)
        send, keep = back_product(order, dense, [left], True)
        totals, norm, ahead = yield from reduce_rows(swap, send, keep)
        norms = [norm]
        rights = []
        for iteration in range(ITERS):
            outer, *own = totals
            pasts = [[right, norms[-2]] for right in rights[-1]] if rights else [[], []]
            own = [tied(own[0], ahead), own[1]]
            part, squares, own_right = fore_own_product(
                order, dense, [*own, norms[-1], *pasts[1]], not rights
            )
            send, keep, right = fore_product(
                order, dense, [outer, part, squares, norms[-1], *pasts[0]], not rights
            )
            rights.append([right, own_right])
            halves, norm = yield from reduce_cols(send, keep)
            norms.append(norm)
            send, keep, left = back_product(
                order, dense, [*halves, norms[-1], left, norms[-2]], False
            )
            totals, norm, ahead = yield from reduce_rows(swap, send, keep)
            norms.append(norm)
        return rights, norms, totals

    runs = [chain(second, left) for second, left in enumerate(lefts)]
    wanted = [next(run) for run in runs]
    chains = [None] * len(runs)
    gots = [None] * len(runs)
    swap, value, level = wanted[0]
    gots[0] = swap(value, level)
    latest = wanted[1][1]
    turn = 0
    while None in chains:
        mine = 0 if turn < BEHIND else (turn - BEHIND) % 2
        turn += 1
        if chains[mine] is not None:
            continue
        if gots[mine] is None:
            swap, value, level = wanted[mine]
            latest = tied(value, latest)
        else:
            try:
                swap, latest, level = runs[mine].send((tied(gots[mine], latest), latest))
            except StopIteration as stop:
                chains[mine] = stop.value
                continue
        gots[mine] = swap(latest, level)

    cells = CB_DEV * TILE
    model, misfit = last_call(
        functools.partial(model_kernel, ITERS),
        mask,
        [operand for rights, norms, _ in chains for operand in [*sum(rights, []), *norms]],
        [(cells, TILE), (NORM_ROWS, TILE)],
    )
    gradient = gradient_of(mask, *chains)
    return (model, gradient, misfit[0])


def solution(mesh):
    placed = (P("rows", "cols", None, None), P("rows", "cols"), P("rows", "cols"), P("rows", None))

    def local(kernel, pattern, counts, delays):
        return on_device(
            mesh.shape["rows"], mesh.shape["cols"], kernel, pattern, counts, delays
        )

    return jax.shard_map(
        local,
        mesh=mesh,
        in_specs=placed,
        out_specs=(P("cols", None), P("cols", None), P()),
        check_vma=False,
    )
```

```python
import functools

import jax
import jax.numpy as jnp
from jax import lax
from jax.experimental import pallas as pl
from jax.experimental.pallas import tpu as pltpu
from jax.sharding import PartitionSpec as P

CB_DEV = 24
ITERS = 2
TILE = 128
PAIR = 2 * TILE
UNITS = 4
NORM_ROWS = 8
UNIT_ORDERS = ((0, 1, 2, 3), (0, 2, 1, 3))
BEHIND = 0

tiny_eps = 1e-06

WHOLE = pl.BlockSpec(memory_space=pltpu.VMEM)
SCALARS = pl.BlockSpec(memory_space=pltpu.SMEM)


def low_lanes(shape):
    return lax.broadcasted_iota(jnp.int32, shape, 1) < shape[1] // 2


def turned(value):
    return pltpu.roll(value, value.shape[1] // 2, 1)


def rows_of(pair, size=TILE):
    return slice(pair * size, (pair + 1) * size)


def fill_kernel(
    place_ref, flip_ref, pattern_in, counts_in, delays_in, tiles_in,
    dense_ref, even_left_ref, odd_left_ref, pattern_ref, counts_ref, delays_ref, tiles_ref, arrived,
):
    flip = flip_ref[0]
    row_blocks = tiles_in.shape[0]
    small = [
        pltpu.make_async_copy(source, target, arrived.at[2 * row_blocks + i])
        for i, (source, target) in enumerate(
            [(pattern_in, pattern_ref), (counts_in, counts_ref), (delays_in, delays_ref)]
        )
    ]
    for copy in small:
        copy.start()

    half = tiles_in.shape[1] // 2

    def fetch(position, upper):
        slots = pl.ds(upper * half, half)
        return pltpu.make_async_copy(
            tiles_in.at[position ^ flip, slots],
            tiles_ref.at[position, slots],
            arrived.at[upper * row_blocks + position],
        )

    for position in range(row_blocks):
        fetch(position, 0).start()
    @pl.loop(0, row_blocks)
    def _(position):
        rows = pl.ds(pl.multiple_of(position * TILE, TILE), TILE)
        dense_ref[rows, :] = jnp.zeros((TILE, dense_ref.shape[1]), dense_ref.dtype)

    for copy in small[:2]:
        copy.wait()
    for position in range(row_blocks):

        @pl.when(counts_ref[position ^ flip] > half)
        def _():
            fetch(position, 1).start()

    small[2].wait()
    low = low_lanes((TILE, TILE))
    for pair in range(row_blocks // 2):
        source = (pair ^ (flip // 2)) * PAIR
        even = delays_ref[pl.ds(pl.multiple_of(source, TILE), TILE), :]
        odd = delays_ref[pl.ds(pl.multiple_of(source + TILE, TILE), TILE), :]
        even_left_ref[rows_of(pair), :] = jnp.where(low, even, turned(odd))
        odd_left_ref[rows_of(pair), :] = jnp.where(low, turned(even), odd)

    @pl.loop(0, row_blocks)
    def _(position):
        rows = pl.ds(pl.multiple_of(position * TILE, TILE), TILE)
        block = position ^ flip
        count = counts_ref[block]

        def place(tile):
            column = jnp.where(tile < count, place_ref[pattern_ref[block, tile]], CB_DEV)
            lanes = pl.ds(pl.multiple_of(column * TILE, TILE), TILE)
            dense_ref[rows, lanes] = tiles_ref[position, tile]

        fetch(position, 0).wait()
        for tile in range(half):
            place(tile)

        @pl.when(count > half)
        def _():
            fetch(position, 1).wait()
            for tile in range(half, 2 * half):
                place(tile)


def fill_dense(kernel, pattern, counts, places, flip, delays):
    row_blocks = kernel.shape[0]
    rows = row_blocks * TILE
    left = jax.ShapeDtypeStruct((rows // 2, TILE), jnp.float32)
    return pl.pallas_call(
        fill_kernel,
        in_specs=[SCALARS] * 2 + [pl.BlockSpec(memory_space=pltpu.HBM)] * 4,
        out_specs=[WHOLE] * 3,
        out_shape=[jax.ShapeDtypeStruct((rows, (CB_DEV + 1) * TILE), kernel.dtype), left, left],
        scratch_shapes=[
            pltpu.SMEM(pattern.shape, jnp.int32),
            pltpu.SMEM((row_blocks,), jnp.int32),
            pltpu.VMEM(delays.shape, delays.dtype),
            pltpu.VMEM(kernel.shape, kernel.dtype),
            pltpu.SemaphoreType.DMA((2 * row_blocks + 3,)),
        ],
        compiler_params=pltpu.CompilerParams(vmem_limit_bytes=16 * 1024 * 1024),
        cost_estimate=pl.CostEstimate(
            flops=0, bytes_accessed=2 * kernel.size, transcendentals=0
        ),
    )(
        places,
        flip,
        *(pltpu.with_memory_space_constraint(x, pltpu.HBM) for x in (pattern, counts.reshape(-1), delays, kernel)),
    )


def norm_of(ref):
    return jnp.sqrt(ref[0:1, :] + tiny_eps)


def squares_row(sums):
    while len(sums) > 1:
        sums = [sums[i] + sums[i + 1] for i in range(0, len(sums), 2)]
    row = jnp.sum(sums[0], axis=0, keepdims=True)
    return row + turned(row)


def next_vector(parts, raw_ref, scale_ref, past_ref, past_scale_ref):
    if scale_ref is not None:
        scale = norm_of(scale_ref)
        shrink = 1.0 / scale
    if past_ref is not None:
        past_share = scale / norm_of(past_scale_ref)
    position = 0
    for part, units in parts:
        pairs = part.shape[0] // TILE // units
        for unit in range(units):
            squares = jnp.zeros((NORM_ROWS, TILE), jnp.float32)
            for pair in range(pairs):
                value = part[rows_of(unit * pairs + pair), :]
                if scale_ref is not None:
                    value = value * shrink
                if past_ref is not None:
                    value = value - past_share * past_ref[rows_of(position), :]
                if raw_ref is not None:
                    raw_ref[rows_of(position), :] = value
                squares += jnp.sum((value * value).reshape(-1, NORM_ROWS, TILE), axis=0)
                yield position, value, squares if pair == pairs - 1 else None
                position += 1


def back_pairs(dense_ref, turned_ref, out_ref, units):
    pairs = CB_DEV // 2 // UNITS
    for pair in range(pairs * len(units)):
        column = units[pair // pairs] * pairs + pair % pairs
        product = jnp.dot(
            turned_ref[...],
            dense_ref[:, rows_of(column, PAIR)],
            preferred_element_type=jnp.float32,
        )
        stacked = jnp.concatenate([product[:, :TILE], product[:, TILE:]], axis=0)
        out_ref[rows_of(pair), :] = stacked.T


def back_send_kernel(first, units, *refs):
    if first:
        dense_ref, own_ref, send_ref, turned_ref = refs
        parts, raw_ref, scales = [(own_ref, 2)], None, (None, None, None)
    else:
        (dense_ref, other_ref, own_ref, scale_ref, past_ref, past_scale_ref,
         send_ref, turned_ref, raw_ref) = refs
        parts, scales = [(other_ref, 1), (own_ref, 1)], (scale_ref, past_ref, past_scale_ref)
    sums = []
    half = turned_ref.shape[0]
    for pair, value, squares in next_vector(parts, raw_ref, *scales):
        flat = value.T.astype(turned_ref.dtype)
        turned_ref[:, rows_of(2 * pair)] = flat[:half]
        turned_ref[:, rows_of(2 * pair + 1)] = flat[half:]
        if squares is not None:
            sums.append(squares)
    send_ref[-NORM_ROWS:, :] = jnp.broadcast_to(squares_row(sums), (NORM_ROWS, TILE))
    back_pairs(dense_ref, turned_ref, send_ref, units)


def back_keep_kernel(units, dense_ref, turned_ref, keep_ref):
    back_pairs(dense_ref, turned_ref, keep_ref, units)


def fore_pairs(dense_ref, units, wide_ref, add_ref, out_ref, start):
    depth = wide_ref.shape[0] // len(units)
    runs = [(unit * depth, i * depth, depth) for i, unit in enumerate(units)]
    if units[1] == units[0] + 1:
        runs = [(units[0] * depth, 0, 2 * depth)]
    low = low_lanes((TILE, TILE))
    step = 4
    pairs = out_ref.shape[0] // TILE
    for pair in range(0, pairs, step):
        rows = slice((start + pair) * PAIR, (start + pair + step) * PAIR)
        product = sum(
            jnp.dot(
                dense_ref[rows, cell : cell + size],
                wide_ref[row : row + size, :],
                preferred_element_type=jnp.float32,
            )
            for cell, row, size in runs
        )
        for i in range(step):
            even, odd = product[rows_of(2 * i), :], product[rows_of(2 * i + 1), :]
            value = jnp.where(low, even, odd)
            if add_ref is not None:
                value = value + add_ref[rows_of(start + pair + i), :]
            out_ref[rows_of(pair + i), :] = value


def fore_vector(parts, wide_ref, raw_ref, scales):
    low = low_lanes((TILE, TILE))
    sums = []
    for pair, value, squares in next_vector(parts, raw_ref, *scales):
        other = turned(value)
        wide_ref[rows_of(2 * pair), :] = jnp.where(low, value, other).astype(wide_ref.dtype)
        wide_ref[rows_of(2 * pair + 1), :] = jnp.where(low, other, value).astype(wide_ref.dtype)
        if squares is not None:
            sums.append(squares)
    return sums[0] + sums[1]


def fore_own_kernel(first, units, dense_ref, inner_ref, mine_ref, scale_ref, *refs):
    past_ref, past_scale_ref = (None, None) if first else refs[:2]
    part_ref, sum_ref, raw_ref, wide_ref = refs[-4:]
    parts = [(inner_ref, 1), (mine_ref, 1)]
    sum_ref[...] = fore_vector(parts, wide_ref, raw_ref, (scale_ref, past_ref, past_scale_ref))
    fore_pairs(dense_ref, units, wide_ref, None, part_ref, 0)


def fore_send_kernel(first, units, dense_ref, outer_ref, part_ref, sum_ref, scale_ref, *refs):
    past_ref, past_scale_ref = (None, None) if first else refs[:2]
    send_ref, wide_ref, raw_ref = refs[-3:]
    squares = fore_vector([(outer_ref, 2)], wide_ref, raw_ref, (scale_ref, past_ref, past_scale_ref))
    row = squares_row([squares, sum_ref[...]])
    send_ref[-NORM_ROWS:, :] = jnp.broadcast_to(row, (NORM_ROWS, TILE))
    fore_pairs(dense_ref, units, wide_ref, part_ref, send_ref, 0)


def fore_keep_kernel(units, dense_ref, wide_ref, part_ref, keep_ref):
    start = keep_ref.shape[0] // TILE
    fore_pairs(dense_ref, units, wide_ref, part_ref, keep_ref, start)


def product_call(body, dense, operands, shapes, scratch=()):
    return pl.pallas_call(
        body,
        in_specs=[WHOLE] * (1 + len(operands)),
        out_specs=[WHOLE] * len(shapes),
        out_shape=shapes,
        scratch_shapes=scratch,
        compiler_params=pltpu.CompilerParams(vmem_limit_bytes=12 * 1024 * 1024),
        cost_estimate=pl.CostEstimate(
            flops=2 * TILE * dense.size, bytes_accessed=dense.size, transcendentals=0
        ),
    )(dense, *operands)


def float_rows(rows):
    return jax.ShapeDtypeStruct((rows, TILE), jnp.float32)


def back_product(order, dense, operands, first):
    rows, cells = dense.shape[0], CB_DEV * TILE
    shapes = [float_rows(cells // 4 + NORM_ROWS), jax.ShapeDtypeStruct((TILE // 2, rows), dense.dtype)]
    shapes += [] if first else [float_rows(rows // 2)]
    send, flat, *raw = product_call(
        functools.partial(back_send_kernel, first, order[:2]), dense, operands, shapes
    )


    body = functools.partial(back_keep_kernel, order[2:])
    (keep,) = product_call(body, dense, [flat], [float_rows(cells // 4)])
    return send, keep, *raw


def fore_own_product(order, dense, operands, first):
    rows, cells = dense.shape[0], CB_DEV * TILE
    return product_call(
        functools.partial(fore_own_kernel, first, order[2:]),
        dense,
        operands,
        [float_rows(rows // 2), float_rows(NORM_ROWS), float_rows(cells // 4)],
        [pltpu.VMEM((cells // 2, TILE), dense.dtype)],
    )


def fore_product(order, dense, operands, first):
    rows, cells = dense.shape[0], CB_DEV * TILE
    shapes = [
        float_rows(rows // 4 + NORM_ROWS),
        jax.ShapeDtypeStruct((cells // 2, TILE), dense.dtype),
        float_rows(cells // 4),
    ]
    send, wide, raw = product_call(
        functools.partial(fore_send_kernel, first, order[:2]), dense, operands, shapes
    )

    def keep(wide):
        body = functools.partial(fore_keep_kernel, order[:2])
        return product_call(body, dense, [wide, operands[1]], [float_rows(rows // 4)])[0]

    return send, (keep, wide), raw


def rotation(norms):
    betas, alphas = [norm_of(ref) for ref in norms[0::2]], [norm_of(ref) for ref in norms[1::2]]
    resid_bar, diag_bar = betas[0], alphas[0]
    steps = []
    for j in range(len(alphas)):
        radius = jnp.sqrt(diag_bar * diag_bar + betas[j + 1] * betas[j + 1])
        rotate_cos = diag_bar / radius
        rotate_sin = betas[j + 1] / radius
        step_size = rotate_cos * resid_bar
        resid_bar = rotate_sin * resid_bar
        coupling = None
        if j + 1 < len(alphas):
            coupling = rotate_sin * alphas[j + 1] / radius
            diag_bar = -rotate_cos * alphas[j + 1]
        steps.append((step_size / radius, coupling))
    misfit = resid_bar / betas[0]
    return alphas, betas, steps, misfit, misfit * rotate_cos


def store_in_order(out_ref, mask, pair, low, values):
    pairs = out_ref.shape[0] // PAIR // UNITS
    start = (((pair // pairs) ^ mask) * pairs + pair % pairs) * PAIR
    ours, theirs = values
    even = pl.ds(pl.multiple_of(start, TILE), TILE)
    odd = pl.ds(pl.multiple_of(start + TILE, TILE), TILE)
    out_ref[even, :] = jnp.where(low, ours, turned(theirs))
    out_ref[odd, :] = jnp.where(low, turned(ours), theirs)


def model_kernel(count, mask_ref, *refs):
    ins, (model_ref, misfit_ref) = refs[:-2], refs[-2:]
    chains = [ins[: len(ins) // 2], ins[len(ins) // 2 :]]
    low = low_lanes((TILE, TILE))
    rotations = [rotation(refs_[2 * count :]) for refs_ in chains]
    misfits = [jnp.broadcast_to(r[3], misfit_ref.shape) for r in rotations]
    misfit_ref[...] = jnp.where(low_lanes(misfit_ref.shape), misfits[0], misfits[1])
    pairs = model_ref.shape[0] // PAIR // UNITS
    for pair in range(model_ref.shape[0] // PAIR):
        values = []
        for order, refs_, (alphas, _, steps, _, _) in zip(UNIT_ORDERS, chains, rotations):
            slot = order.index(pair // pairs)
            rows = rows_of(slot % 2 * pairs + pair % pairs)
            search = total = None
            for j in range(count):
                right = refs_[2 * j + slot // 2][rows, :] / alphas[j]
                search = right if j == 0 else right - steps[j - 1][1] * search
                total = steps[j][0] * search if j == 0 else total + steps[j][0] * search
            values.append(total)
        store_in_order(model_ref, mask_ref[0], pair, low, values)


def gathered_values(outer, own, norms):
    factor = rotation(norms)[-1]
    values = []
    for half in (outer, own):
        if half is not None:
            parts, past_ref = half
            vector = next_vector(parts, None, norms[-1], past_ref, norms[-2])
            values += [factor * value for _, value, _ in vector]
    return values


def store_pair(ref, pair, low, ours, theirs):
    ref[rows_of(2 * pair), :] = jnp.where(low, ours, turned(theirs))
    ref[rows_of(2 * pair + 1), :] = jnp.where(low, turned(ours), theirs)


def ready_kernel(outer_ref, inner_ref, mine_ref, past_ref, own_past_ref, *refs):
    norms, refs = refs[: 2 * ITERS + 1], refs[2 * ITERS + 1 :]
    second_inner_ref, second_mine_ref, second_past_ref, *second_norms, ready_ref, ours_ref = refs
    low = low_lanes((TILE, TILE))
    ours = gathered_values(
        ([(outer_ref, 2)], past_ref), ([(inner_ref, 1), (mine_ref, 1)], own_past_ref), norms
    )
    theirs = gathered_values(
        None, ([(second_inner_ref, 1), (second_mine_ref, 1)], second_past_ref), second_norms
    )
    pairs = mine_ref.shape[0] // TILE
    for slot, unit in enumerate(UNIT_ORDERS[1]):
        start = UNIT_ORDERS[0].index(unit) * pairs
        for pair in range(pairs):
            if slot < 2:
                ours_ref[rows_of(slot * pairs + pair), :] = ours[start + pair]
            else:
                done = (slot - 2) * pairs + pair
                store_pair(ready_ref, done, low, ours[start + pair], theirs[done])


def gradient_kernel(mask_ref, ready_ref, ours_ref, outer_ref, past_ref, *refs):
    *norms, gradient_ref, last_ref, sent = refs
    low = low_lanes((TILE, TILE))
    size = gradient_ref.shape[0] // UNITS

    def send(slot, source_ref):
        rows = pl.ds(pl.multiple_of((UNIT_ORDERS[1][slot] ^ mask_ref[0]) * size, TILE), size)
        source = source_ref.at[pl.ds(slot % 2 * size, size)]
        return pltpu.make_async_copy(source, gradient_ref.at[rows], sent.at[slot])

    copies = [send(slot, last_ref if slot < 2 else ready_ref) for slot in range(UNITS)]
    for copy in copies[2:]:
        copy.start()
    theirs = gathered_values(([(outer_ref, 2)], past_ref), None, norms)
    for slot, copy in enumerate(copies[:2]):
        pairs = size // PAIR
        for pair in range(slot * pairs, (slot + 1) * pairs):
            store_pair(last_ref, pair, low, ours_ref[rows_of(pair), :], theirs[pair])
        copy.start()
    for copy in copies:
        copy.wait()


def gradient_of(mask, first, second):
    (rights, norms, totals), (second_rights, second_norms, second_totals) = first, second
    half = totals[0].shape[0]
    cost = pl.CostEstimate(flops=0, bytes_accessed=16 * half * TILE, transcendentals=0)
    params = pltpu.CompilerParams(vmem_limit_bytes=12 * 1024 * 1024)
    operands = [*totals, *rights[-1], *norms]
    operands += [*second_totals[1:], second_rights[-1][1], *second_norms]
    ready, ours = pl.pallas_call(
        ready_kernel,
        in_specs=[WHOLE] * len(operands),
        out_specs=[WHOLE] * 2,
        out_shape=[float_rows(2 * half), float_rows(half)],
        compiler_params=params,
        cost_estimate=cost,
    )(*operands)
    operands = [ready, ours, second_totals[0], second_rights[-1][0], *second_norms]
    return pl.pallas_call(
        gradient_kernel,
        in_specs=[SCALARS] + [WHOLE] * len(operands),
        out_specs=pl.BlockSpec(memory_space=pl.ANY),
        out_shape=float_rows(4 * half),
        scratch_shapes=[
            pltpu.VMEM((2 * half, TILE), jnp.float32),
            pltpu.SemaphoreType.DMA((UNITS,)),
        ],
        compiler_params=params,
        cost_estimate=cost,
    )(mask, *operands)


def last_call(body, mask, operands, shapes):
    return pl.pallas_call(
        body,
        in_specs=[SCALARS] + [WHOLE] * len(operands),
        out_specs=[WHOLE] * len(shapes),
        out_shape=[jax.ShapeDtypeStruct(shape, jnp.float32) for shape in shapes],
        compiler_params=pltpu.CompilerParams(vmem_limit_bytes=12 * 1024 * 1024),
        cost_estimate=pl.CostEstimate(
            flops=0, bytes_accessed=8 * shapes[0][0] * TILE, transcendentals=0
        ),
    )(mask, *operands)


def on_device(row_count, col_count, kernel, pattern, counts, delays):
    row_bits = list(range(row_count.bit_length() - 1))
    col_bits = list(range(col_count.bit_length() - 1))
    row_index = lax.axis_index("rows")
    core = lax.axis_index("cols") & 1

    near, far, *rest = row_bits
    orders = [[near, far, *rest, far, near], [far, near, *rest, near, far]]
    steps = len(orders[0])

    def swap_rows(second, value, level):
        pairs = []
        for row in range(row_count):
            for col in range(col_count):
                partner = row ^ (1 << orders[col & 1 ^ second][level])
                pairs.append((row * col_count + col, partner * col_count + col))
        return lax.ppermute(value, ("rows", "cols"), pairs)

    def swap_cols(value, level):
        return lax.ppermute(value, "cols", [(i, i ^ (1 << level)) for i in range(col_count)])

    bits = [(row_index >> bit) & 1 for bit in row_bits[:2]]
    outer_side = jnp.where(core == 0, bits[0], bits[1])
    inner_side = jnp.where(core == 0, bits[1], bits[0])
    mask = ((1 - outer_side) * 2 + (1 - inner_side)).astype(jnp.int32)
    blocks = jnp.arange(CB_DEV, dtype=jnp.int32)
    unit = CB_DEV // UNITS
    places = ((blocks // unit) ^ mask) * unit + blocks % unit
    flip = ((1 - core) * (kernel.shape[0] // 2)).astype(jnp.int32).reshape(1)
    mask = mask.reshape(1)

    dense, *lefts = fill_dense(kernel, pattern, counts, places, flip, delays)

    def tied(value, other):
        return lax.optimization_barrier((value, other))[0]

    def kept_half(kept, ahead):
        half, operand = kept
        return half(tied(operand, ahead))

    def reduce_rows(swap_rows, send, keep):
        half = keep.shape[0]
        got, _ = yield swap_rows, send, 0
        keep = keep + got[:half]
        norm = send[half:] + got[half:]
        send, mine = keep[: half // 2], keep[half // 2 :]
        for level in range(1, len(row_bits)):
            got, _ = yield swap_rows, jnp.concatenate([send, norm]), level
            norm = norm + got[half // 2 :]
            send = mine = mine + got[: half // 2]
        inner, _ = yield swap_rows, mine, steps - 2
        outer, ahead = yield swap_rows, jnp.concatenate([inner, mine]), steps - 1
        return [outer, inner, mine], norm, ahead

    def reduce_cols(send, kept):
        half = send.shape[0] - NORM_ROWS
        got, ahead = yield swap_cols, send, 0
        own = kept_half(kept, ahead) + got[:half]
        norm = send[half:] + got[half:]
        for bit in col_bits[1:]:
            got, _ = yield swap_cols, jnp.concatenate([own, norm]), bit
            norm = norm + got[half:]
            own = own + got[:half]
        other, _ = yield swap_cols, own, 0
        return [other, own], norm

    def chain(second, left):
        order = UNIT_ORDERS[second]
        swap = functools.partial(swap_rows, second)
        send, keep = back_product(order, dense, [left], True)
        totals, norm, ahead = yield from reduce_rows(swap, send, keep)
        norms = [norm]
        rights = []
        for iteration in range(ITERS):
            outer, *own = totals
            pasts = [[right, norms[-2]] for right in rights[-1]] if rights else [[], []]
            if second:
                own = [tied(own[0], ahead), own[1]]
            part, squares, own_right = fore_own_product(
                order, dense, [*own, norms[-1], *pasts[1]], not rights
            )
            send, keep, right = fore_product(
                order, dense, [outer, part, squares, norms[-1], *pasts[0]], not rights
            )
            rights.append([right, own_right])
            halves, norm = yield from reduce_cols(send, keep)
            norms.append(norm)
            send, keep, left = back_product(
                order, dense, [*halves, norms[-1], left, norms[-2]], False
            )
            totals, norm, ahead = yield from reduce_rows(swap, send, keep)
            norms.append(norm)
        return rights, norms, totals

    runs = [chain(second, left) for second, left in enumerate(lefts)]
    wanted = [next(run) for run in runs]
    chains = [None] * len(runs)
    gots = [None] * len(runs)
    swap, value, level = wanted[0]
    gots[0] = swap(value, level)
    latest = wanted[1][1]
    turn = 0
    while None in chains:
        mine = 0 if turn < BEHIND else (turn - BEHIND) % 2
        turn += 1
        if chains[mine] is not None:
            continue
        if gots[mine] is None:
            swap, value, level = wanted[mine]
            latest = tied(value, latest)
        else:
            try:
                swap, latest, level = runs[mine].send((tied(gots[mine], latest), latest))
            except StopIteration as stop:
                chains[mine] = stop.value
                continue
        gots[mine] = swap(latest, level)

    cells = CB_DEV * TILE
    model, misfit = last_call(
        functools.partial(model_kernel, ITERS),
        mask,
        [operand for rights, norms, _ in chains for operand in [*sum(rights, []), *norms]],
        [(cells, TILE), (NORM_ROWS, TILE)],
    )
    gradient = gradient_of(mask, *chains)
    return (model, gradient, misfit[0])


def solution(mesh):
    placed = (P("rows", "cols", None, None), P("rows", "cols"), P("rows", "cols"), P("rows", None))

    def local(kernel, pattern, counts, delays):
        return on_device(
            mesh.shape["rows"], mesh.shape["cols"], kernel, pattern, counts, delays
        )

    return jax.shard_map(
        local,
        mesh=mesh,
        in_specs=placed,
        out_specs=(P("cols", None), P("cols", None), P()),
        check_vma=False,
    )
```
